32 devices in a mesh: blk: 2 (over y), ctx: 4 (over x, core), tp: 4 (over z).
Axes of the slice: x: 2, y: 2, z: 4, core: 2. Of those that a mesh axis runs over, the one named last changes fastest.
Arguments:
- inputs: bfloat16 [2, 1024, 1024], P(None, ('blk', 'ctx')), may hold values from -6 to 6
- cotangent: bfloat16 [2, 1024, 1024], P(None, ('blk', 'ctx')), may hold values from -6 to 6
- matrices: float32 [192, 65536], P('tp', 'blk')
- momenta: float32 [192, 65536], P('tp', 'blk'), may hold values from -80 to 80
- small: float32 [13312], replicated
- small_first: float32 [13312], replicated, may hold values from -28 to 28
- small_second: float32 [13312], replicated, may hold values from 20.48 to 409.6
- segments: int32 [2, 1024], replicated, may hold values from 0 to 1023, as said below
- positions: int32 [2, 1024], P(None, ('blk', 'ctx')), may hold values from 0 to 2046, as said below
Outputs:
- block_output: float32 [2, 1024, 1024], P(None, ('blk', 'ctx'))
- input_grad: float32 [2, 1024, 1024], P(None, ('blk', 'ctx'))
- matrix_grads: float32 [192, 65536], P('tp', 'blk')
- new_matrices: float32 [192, 65536], P('tp', 'blk')
- new_momenta: float32 [192, 65536], P('tp', 'blk')
- small_grads: float32 [13312], replicated
- new_first: float32 [13312], replicated
- new_second: float32 [13312], replicated
- new_small: float32 [13312], replicated
The draws below stay inside these ranges and needn't reach their ends.
Inputs may be any that keep to these rules, and one draw needn't show every extreme that they name: `segments`: along a sequence the numbers never fall; each token's number is the index of its document's first token; the last token of a sequence starts a document of its own. Within a document positions rise by one from token to token; the first token of a sequence has 0.
All inputs are finite; a program needn't handle non-finite values.
Results may differ from the reference program's by a relative error of at most 0.012.
Values may be sent and summed in bfloat16 or wider, within the bound.
No kernel may reach another device: no remote copies, remote signals or barrier semaphores. Data moves between devices by JAX's collectives and lax.ppermute only.
A program may use at most 256 MiB of HBM per device.

```python
import math
import jax
import jax.numpy as jnp
from jax import lax

MODEL_DIM = 1024
H = 16
HD = 64
FF = 4096
ROTARY = 16
SEQS = 2
DOC_MIN = 200
DOC_MAX = 2000
NEWTON = 5
STEP = 10
BLOCK = 512
LENGTH = 1024
TOKENS = 2048
MATS = 192
SMALL = 13312
N_TP = 4


def document_layout(key):
    choose_key, lead_key, tail_key, length_key, offset_key = jax.random.split(key, 5)
    doc_count = LENGTH // DOC_MIN + 2
    sequence_ids = jnp.arange(SEQS, dtype=jnp.int32)[:, None]
    spanning = jax.random.randint(choose_key, (), 0, SEQS)
    leading = jax.random.randint(lead_key, (SEQS, 1), 1, BLOCK)
    trailing = jax.random.randint(tail_key, (SEQS, 1), 1, BLOCK)
    doc_lengths = jax.random.randint(length_key, (SEQS, doc_count), DOC_MIN, DOC_MAX + 1).astype(jnp.int32)
    doc_ends = jnp.cumsum(doc_lengths, axis=1).astype(jnp.int32)
    doc_starts = doc_ends - doc_lengths
    places = jnp.arange(LENGTH, dtype=jnp.int32)[None, :]
    packed = jnp.any(doc_starts[:, None, :] == places[:, :, None], axis=2)
    spans = (places == leading) | (places == LENGTH - trailing)
    starts = jnp.where(sequence_ids == spanning, spans, packed)
    starts = starts | (places == 0) | (places == LENGTH - 1)
    firsts = lax.cummax(jnp.where(starts, places, 0), axis=1).astype(jnp.int32)
    offsets = jax.random.randint(offset_key, (SEQS, LENGTH), 0, 1024)
    offsets = jnp.where(places == 0, 0, offsets)
    offsets = jnp.where(places == LENGTH - 1, LENGTH + 1022, offsets)
    shifted = jnp.take_along_axis(offsets, firsts, axis=1)
    return (firsts, (shifted + places - firsts).astype(jnp.int32))


def draw_segments(key, part):
    shared = document_layout(key)
    return shared[0]


def draw_positions(key, part):
    shared = document_layout(key)
    return shared[1]


def draw_matrices(key, part):
    key = jax.random.fold_in(key, 3)
    per_group = MATS // N_TP
    head_count = H // N_TP
    unit_blocks = FF // HD // N_TP
    slots = jnp.arange(MATS) % per_group
    wide = MODEL_DIM ** (-0.5)
    output_scale = (H * HD // 64) ** (-0.5)
    down_scale = FF ** (-0.5)
    scales = jnp.where(slots < 3 * head_count, wide, jnp.where(slots < 4 * head_count, output_scale, jnp.where(slots < 4 * head_count + unit_blocks, wide, down_scale)))
    values = jax.random.normal(key, (MATS, MODEL_DIM, HD), jnp.float32) * scales[:, None, None]
    return values.reshape(MATS, MODEL_DIM * HD)


def draw_small(key, part):
    key = jax.random.fold_in(key, 4)
    gain_key, bias_key = jax.random.split(key)
    places = jnp.arange(SMALL)
    gains = jax.random.uniform(gain_key, (SMALL,), jnp.float32, 0.5, 1.5)
    biases = 0.3 * jax.random.normal(bias_key, (SMALL,), jnp.float32)
    is_gain = (places < MODEL_DIM) | (places >= 2 * MODEL_DIM) & (places < 3 * MODEL_DIM)
    return jnp.where(is_gain, gains, biases)


def steps_of(stream_key, shape, cuts, low, top_value):
    loudness, own = 1.0, jax.random.fold_in(stream_key, 6)
    for axis_at, blocks in cuts:
        heights = jnp.exp(jax.random.uniform(jax.random.fold_in(own, axis_at), (blocks,), jnp.float32, low / len(cuts), top_value / len(cuts)))
        loudness = loudness * jnp.repeat(heights, shape[axis_at] // blocks).reshape([-1 if axis == axis_at else 1 for axis in range(len(shape))])
    return loudness


def bell_draw(key, dims, scale, limit, cuts=(), kind=jnp.bfloat16):
    level = steps_of(key, dims, cuts, -0.22, 0.18) if cuts else 1.0
    result = jax.random.normal(key, dims, jnp.float32) * scale * level
    return jnp.minimum(jnp.maximum(result, -limit), limit).astype(kind)


def setup_inputs(seed: int = 0) -> dict:
    streams_of = jax.random.split(jax.random.key(seed), 10)
    inputs = bell_draw(streams_of[0], (SEQS, LENGTH, MODEL_DIM), 1.0, 6.0, ((1, 8),))
    cotangent = bell_draw(streams_of[1], (SEQS, LENGTH, MODEL_DIM), 1.0, 6.0, ((1, 8),))
    matrices = draw_matrices(jax.random.fold_in(streams_of[9], 71), 0)
    momenta = bell_draw(streams_of[3], (MATS, MODEL_DIM * HD), (0.3 * TOKENS ** 0.5), 80.0, ((0, 4), (1, 2)), jnp.float32)
    small = draw_small(jax.random.fold_in(streams_of[9], 71), 0)
    small_first = bell_draw(streams_of[5], (SMALL,), (0.1 * TOKENS ** 0.5), 28.0, (), jnp.float32)
    small_second = jnp.clip(jnp.exp(jax.random.uniform(streams_of[6], (SMALL,), jnp.float32, math.log(20.48), math.log(409.6))), 20.48, 409.6)
    segments = draw_segments(jax.random.fold_in(streams_of[9], 71), 0)
    positions = draw_positions(jax.random.fold_in(streams_of[9], 71), 0)
    return dict(inputs=inputs, cotangent=cotangent, matrices=matrices, momenta=momenta, small=small, small_first=small_first, small_second=small_second, segments=segments, positions=positions)


norm_epsilon = 1e-05
rope_base = 10000.0
masked_score = -1e+30
momentum_decay = 0.95
muon_rate = 0.2
weight_decay = 0.01
muon_epsilon = 1e-07
quintic = (3.4445, -4.775, 2.0315)
adam_first = 0.9
adam_second = 0.95
adam_epsilon = 1e-08
small_rate = 0.2

@jax.custom_vjp
def low(v):
    return lax.optimization_barrier(v.astype(jnp.bfloat16)).astype(jnp.float32)

@jax.custom_vjp
def reduced_backward(v):
    return v

def low_keep(v):
    return (low(v), None)

def low_pass(kept, grad):
    return (grad,)

def back_keep(v):
    return (v, None)

def back_low(kept, grad):
    return (low(grad),)
low.defvjp(low_keep, low_pass)
reduced_backward.defvjp(back_keep, back_low)

def layer_norm(values, scaling, offset):
    centre = lax.optimization_barrier(jnp.mean(values, axis=-1, keepdims=True))
    centred = values - centre
    spread = lax.optimization_barrier(jnp.mean(centred * centred, axis=-1, keepdims=True))
    return centred * lax.rsqrt(spread + norm_epsilon) * scaling + offset

def rope_tables(positions):
    halfway = ROTARY // 2
    frequency = rope_base ** (-2.0 * jnp.arange(halfway, dtype=jnp.float32) / ROTARY)
    angles = positions.astype(jnp.float32)[..., None] * frequency
    return (jnp.cos(angles)[:, :, None, :], jnp.sin(angles)[:, :, None, :])

def rotate(values, cosine, sine):
    halfway = ROTARY // 2
    former = values[..., :halfway]
    latter = values[..., halfway:ROTARY]
    return jnp.concatenate([former * cosine - latter * sine, latter * cosine + former * sine, values[..., ROTARY:]], axis=-1)

def attention(queries, keys, values, segments):
    sequences = queries.shape[0]
    length = queries.shape[1]
    block_rows = math.gcd(length, 512)
    score_scale = queries.shape[-1] ** (-0.5)
    key_place = jnp.arange(length, dtype=jnp.int32)

    @jax.checkpoint
    def block_attend(start):
        query_block = lax.dynamic_slice_in_dim(queries, start, block_rows, 1)
        query_place = start + jnp.arange(block_rows, dtype=jnp.int32)
        query_doc = lax.dynamic_slice_in_dim(segments, start, block_rows, 1)
        causal = key_place[None, :] <= query_place[:, None]
        allowed = (causal[None] & (query_doc[:, :, None] == segments[:, None, :]))[:, None]
        scores = reduced_backward(jnp.einsum('sqhe,skhe->shqk', query_block, keys, precision=lax.Precision.HIGHEST) * score_scale)
        masked = jnp.where(allowed, scores, masked_score)
        row_max = lax.optimization_barrier(jnp.max(masked, axis=-1, keepdims=True))
        row_total = lax.optimization_barrier(jnp.sum(jnp.where(allowed, jnp.exp(masked - row_max), 0.0), axis=-1, keepdims=True))
        log_total = row_max + jnp.log(row_total)
        probabilities = jnp.where(allowed, jnp.exp(masked - log_total), 0.0)
        return jnp.einsum('shqk,skhe->sqhe', low(probabilities), values, precision=lax.Precision.HIGHEST)
    starts = jnp.arange(length // block_rows, dtype=jnp.int32) * block_rows
    pieces = lax.map(block_attend, starts)
    return jnp.moveaxis(pieces, 0, 1).reshape(sequences, length, queries.shape[2], queries.shape[3])

def forward(inputs, matrices, small, segments, positions):
    per_group = MATS // N_TP
    head_count = H // N_TP
    unit_blocks = FF // HD // N_TP
    blocks = low(matrices).reshape(N_TP, per_group, MODEL_DIM, HD)
    query_weight = blocks[:, :head_count].reshape(H, MODEL_DIM, HD)
    key_weight = blocks[:, head_count:2 * head_count].reshape(H, MODEL_DIM, HD)
    value_weight = blocks[:, 2 * head_count:3 * head_count].reshape(H, MODEL_DIM, HD)
    final_output_weight = blocks[:, 3 * head_count:4 * head_count].reshape(H, MODEL_DIM, HD)
    input_weight = blocks[:, 4 * head_count:4 * head_count + unit_blocks].reshape(FF // HD, MODEL_DIM, HD)
    down_projection_weight = blocks[:, 4 * head_count + unit_blocks:].reshape(FF // HD, MODEL_DIM, HD)
    query_key_value_bias = small[6 * MODEL_DIM:6 * MODEL_DIM + 3 * H * HD].reshape(H, 3, HD)
    hidden_unit_bias = small[6 * MODEL_DIM + 3 * H * HD:].reshape(FF // HD, HD)
    first_input = low(layer_norm(inputs, small[0:MODEL_DIM], small[MODEL_DIM:2 * MODEL_DIM]))
    second_input = low(layer_norm(inputs, small[2 * MODEL_DIM:3 * MODEL_DIM], small[3 * MODEL_DIM:4 * MODEL_DIM]))

    def project(weight_matrix, layer_index):
        return jnp.einsum('pgk,jka->pgja', first_input, weight_matrix, precision=lax.Precision.HIGHEST) + query_key_value_bias[:, layer_index]
    cosine, sine = rope_tables(positions)
    queries = low(reduced_backward(rotate(reduced_backward(project(query_weight, 0)), cosine, sine)))
    keys = low(reduced_backward(rotate(reduced_backward(project(key_weight, 1)), cosine, sine)))
    values = low(reduced_backward(project(value_weight, 2)))
    attended_rows = low(reduced_backward(attention(queries, keys, values, segments)))
    attention_branch = jnp.einsum('roxu,xcu->roc', attended_rows, final_output_weight, precision=lax.Precision.HIGHEST) + small[4 * MODEL_DIM:5 * MODEL_DIM]
    hidden_preactivation = reduced_backward(jnp.einsum('ptr,kra->ptka', second_input, input_weight, precision=lax.Precision.HIGHEST) + hidden_unit_bias)
    activated_hidden = low(jax.nn.gelu(hidden_preactivation, approximate=False))
    perceptron_branch = jnp.einsum('xkzp,zop->xko', activated_hidden, down_projection_weight, precision=lax.Precision.HIGHEST) + small[5 * MODEL_DIM:6 * MODEL_DIM]
    return inputs + attention_branch + perceptron_branch

def newton_schulz(blocks):
    frobenius = jnp.sqrt(lax.optimization_barrier(jnp.sum(blocks * blocks, axis=(1, 2), keepdims=True)))
    current = blocks / (frobenius + muon_epsilon)
    linear_term, square_term, cubic_term = quintic
    for iteration in range(NEWTON):
        gram_matrix = jnp.einsum('mde,mdf->mef', current, current, precision=lax.Precision.HIGHEST)
        polynomial = square_term * gram_matrix + cubic_term * jnp.einsum('mef,mfg->meg', gram_matrix, gram_matrix, precision=lax.Precision.HIGHEST)
        current = linear_term * current + jnp.einsum('mde,mef->mdf', current, polynomial, precision=lax.Precision.HIGHEST)
    return current

def reference(inputs, cotangent, matrices, momenta, small, small_first, small_second, segments, positions):

    def whole_block(values, weights, params):
        return forward(values, weights, params, segments, positions)
    block_output, pullback = jax.vjp(whole_block, inputs.astype(jnp.float32), matrices, small)
    input_grad, matrix_grads, small_grads = pullback(cotangent.astype(jnp.float32))
    new_momenta = momentum_decay * momenta + matrix_grads
    update = matrix_grads + momentum_decay * new_momenta
    orthogonal = newton_schulz(update.reshape(MATS, MODEL_DIM, HD)).reshape(MATS, MODEL_DIM * HD)
    muon_scale = max(1.0, MODEL_DIM / HD) ** 0.5
    new_matrices = matrices - muon_rate * (muon_scale * orthogonal + weight_decay * matrices)
    new_first = adam_first * small_first + (1.0 - adam_first) * small_grads
    new_second = adam_second * small_second + (1.0 - adam_second) * small_grads * small_grads
    corrected = new_first / (1.0 - adam_first ** STEP)
    spread = jnp.sqrt(new_second / (1.0 - adam_second ** STEP))
    new_small = small - small_rate * corrected / (spread + adam_epsilon)
    return (block_output, input_grad, matrix_grads, new_matrices, new_momenta, small_grads, new_first, new_second, new_small)
```

```python
import functools

import jax
import jax.numpy as jnp
from jax import lax
from jax.experimental import pallas as pl
from jax.experimental.pallas import tpu as pltpu
from jax.sharding import PartitionSpec as P

MODEL_DIM = 1024
H = 16
HD = 64
FF = 4096
ROTARY = 16
NEWTON = 5
STEP = 10
SEQS = 2


norm_epsilon = 1e-05
rope_base = 10000.0
masked_score = -1e30
momentum_decay = 0.95
muon_rate = 0.2
weight_decay = 0.01
muon_epsilon = 1e-07
quintic = (3.4445, -4.775, 2.0315)
adam_first = 0.9
adam_second = 0.95
adam_epsilon = 1e-08
small_rate = 0.2


def passed_along(x, axis, by):
    devices = lax.axis_size(axis)
    pairs = [(i, i + by) for i in range(devices) if 0 <= i + by < devices]
    return lax.ppermute(x, axis, pairs)


def shifted(x, axis, by):
    devices = lax.axis_size(axis)
    return lax.ppermute(x, axis, [(i, (i + by) % devices) for i in range(devices)])


def as_sent(x):

    def short(part):
        return part.astype(jnp.bfloat16) if part.dtype == jnp.float32 else part

    return jax.tree.map(short, x)


def layer_norm(values, scaling, offset):
    centre = jnp.mean(values, axis=-1, keepdims=True)
    centred = values - centre
    spread = jnp.mean(centred * centred, axis=-1, keepdims=True)
    return centred * lax.rsqrt(spread + norm_epsilon) * scaling + offset


def rope_tables(positions):
    halfway = ROTARY // 2
    frequency = rope_base ** (-2.0 * jnp.arange(halfway, dtype=jnp.float32) / ROTARY)
    angles = positions.astype(jnp.float32)[..., None] * frequency
    return (jnp.cos(angles)[:, :, None, :], jnp.sin(angles)[:, :, None, :])


def rotate(values, cosine, sine):
    halfway = ROTARY // 2
    former = values[..., :halfway]
    latter = values[..., halfway:ROTARY]
    return jnp.concatenate(
        [former * cosine - latter * sine, latter * cosine + former * sine, values[..., ROTARY:]],
        axis=-1,
    )


def exact_gelu(values):
    return jax.nn.gelu(values, approximate=False)


def newton_schulz(blocks):
    frobenius = jnp.sqrt(jnp.sum(blocks * blocks, axis=(1, 2), keepdims=True))
    current = blocks / (frobenius + muon_epsilon)
    linear_term, square_term, cubic_term = quintic
    for iteration in range(NEWTON):
        gram_matrix = jnp.einsum("mde,mdf->mef", current, current, precision=lax.Precision.HIGHEST)
        polynomial = square_term * gram_matrix + cubic_term * jnp.einsum(
            "mef,mfg->meg", gram_matrix, gram_matrix, precision=lax.Precision.HIGHEST
        )
        current = linear_term * current + jnp.einsum(
            "mde,mef->mdf", current, polynomial, precision=lax.Precision.HIGHEST
        )
    return current


def to_heads(values):
    return lax.all_to_all(values, "ctx", split_axis=3, concat_axis=1, tiled=True)


def to_positions(values):
    return lax.all_to_all(values, "ctx", split_axis=1, concat_axis=3, tiled=True)


def pass_keys(pair):
    return passed_along(pair, "blk", 1)


def pass_grads(pair_grad):
    return shifted(pair_grad.astype(jnp.bfloat16), "blk", 1).astype(pair_grad.dtype)


def allowed_pairs(segments, query_block, key_block, block_rows):
    query_place = query_block * block_rows + jnp.arange(block_rows, dtype=jnp.int32)
    key_place = key_block * block_rows + jnp.arange(block_rows, dtype=jnp.int32)
    query_doc = lax.dynamic_slice_in_dim(segments, query_block * block_rows, block_rows, 1)
    key_doc = lax.dynamic_slice_in_dim(segments, key_block * block_rows, block_rows, 1)
    causal = key_place[None, :] <= query_place[:, None]
    return (causal[None] & (query_doc[:, :, None] == key_doc[:, None, :]))[:, None]


def masked_scores(queries, keys, allowed):
    score_scale = HD ** (-0.5)
    scores = (
        jnp.einsum("sqhe,skhe->shqk", queries, keys, preferred_element_type=jnp.float32)
        * score_scale
    )
    return jnp.where(allowed, scores, masked_score)


def on_device(
    inputs, cotangent, matrices, momenta, small, small_first, small_second, segments, positions
):
    tensor_size = lax.axis_size("tp")
    cycle_size = lax.axis_size("blk")
    context_size = lax.axis_size("ctx")
    tensor_index = lax.axis_index("tp")
    cycle_index = lax.axis_index("blk")
    sequences, local_rows, model_width = inputs.shape
    per_group = matrices.shape[0]
    head_count = H // tensor_size
    unit_blocks = FF // HD // tensor_size
    block_rows = local_rows * context_size
    gathered = lax.all_gather(matrices.astype(jnp.bfloat16), "blk", axis=1, tiled=True).reshape(
        per_group, model_width, HD
    )
    query_key_value_weight = gathered[: 3 * head_count]
    projection_out_weight = gathered[3 * head_count : 4 * head_count]
    input_weight = gathered[4 * head_count : 4 * head_count + unit_blocks]
    down_projection_weight = gathered[4 * head_count + unit_blocks :]
    qkv_start = 6 * model_width + tensor_index * head_count * 3 * HD
    query_key_value_bias = lax.dynamic_slice_in_dim(small, qkv_start, head_count * 3 * HD).reshape(
        head_count, 3, HD
    )
    unit_start = 6 * model_width + H * 3 * HD + tensor_index * unit_blocks * HD
    hidden_unit_bias = lax.dynamic_slice_in_dim(small, unit_start, unit_blocks * HD).reshape(
        unit_blocks, HD
    )
    residual = inputs.astype(jnp.float32)

    def both_norms(values, gain_one, offset_one, gain_two, offset_two):
        return (layer_norm(values, gain_one, offset_one), layer_norm(values, gain_two, offset_two))

    (normed_one, normed_two), norm_back = jax.vjp(
        both_norms,
        residual,
        small[0:model_width],
        small[model_width : 2 * model_width],
        small[2 * model_width : 3 * model_width],
        small[3 * model_width : 4 * model_width],
    )
    first_input = normed_one.astype(jnp.bfloat16)
    second_input = normed_two.astype(jnp.bfloat16)
    projected = jnp.einsum(
        "pgk,jka->pgja", first_input, query_key_value_weight, preferred_element_type=jnp.float32
    )
    projected = projected.reshape(sequences, local_rows, 3, head_count, HD) + jnp.transpose(
        query_key_value_bias, (1, 0, 2)
    )
    cosine, sine = rope_tables(positions)

    def turn_pair(query_pre, key_pre):
        return (rotate(query_pre, cosine, sine), rotate(key_pre, cosine, sine))

    (query_turned, key_turned), turn_back = jax.vjp(
        turn_pair, projected[:, :, 0], projected[:, :, 1]
    )
    stacked = jnp.stack([query_turned, key_turned, projected[:, :, 2]], axis=2).astype(jnp.bfloat16)
    by_heads = to_heads(stacked)
    queries = by_heads[:, :, 0]
    head_local = queries.shape[2]

    def forward_visit(state, pair, source):
        row_max, row_total, weighted = state
        allowed = allowed_pairs(segments, cycle_index, source, block_rows)
        scores = masked_scores(queries, pair[:, :, 0], allowed)
        new_max = jnp.maximum(row_max, jnp.max(scores, axis=-1))
        weights = jnp.where(allowed, jnp.exp(scores - new_max[..., None]), 0.0)
        rescale = jnp.exp(row_max - new_max)
        row_total = row_total * rescale + jnp.sum(weights, axis=-1)
        weighted = weighted * rescale[..., None] + jnp.einsum(
            "shqk,skhe->shqe",
            weights.astype(jnp.bfloat16),
            pair[:, :, 1],
            preferred_element_type=jnp.float32,
        )
        return (new_max, row_total, weighted)

    def forward_hop(hop_index, carry):
        pair, state = carry
        source = (cycle_index - hop_index) % cycle_size
        state = forward_visit(state, pair, source)
        return (pass_keys(pair), state)

    start_state = (
        jnp.full((sequences, head_local, block_rows), masked_score, jnp.float32),
        jnp.zeros((sequences, head_local, block_rows), jnp.float32),
        jnp.zeros((sequences, head_local, block_rows, HD), jnp.float32),
    )
    pair, state = lax.fori_loop(0, cycle_size - 1, forward_hop, (by_heads[:, :, 1:], start_state))
    row_max, row_total, weighted = forward_visit(state, pair, (cycle_index + 1) % cycle_size)
    log_total = row_max + jnp.log(row_total)
    attended_rows = jnp.transpose(weighted / row_total[..., None], (0, 2, 1, 3))
    attention_result = to_positions(attended_rows.astype(jnp.bfloat16)[:, :, None])[:, :, 0]
    attention_branch = jnp.einsum(
        "roxu,xcu->roc", attention_result, projection_out_weight, preferred_element_type=jnp.float32
    )
    hidden_preactivation = (
        jnp.einsum("ptr,kra->ptka", second_input, input_weight, preferred_element_type=jnp.float32)
        + hidden_unit_bias
    )
    activated_hidden, gelu_back = jax.vjp(exact_gelu, hidden_preactivation)
    activated_reduced = activated_hidden.astype(jnp.bfloat16)
    perceptron_branch = jnp.einsum(
        "xkzp,zop->xko",
        activated_reduced,
        down_projection_weight,
        preferred_element_type=jnp.float32,
    )
    branches = lax.psum((attention_branch + perceptron_branch).astype(jnp.bfloat16), "tp").astype(
        jnp.float32
    )
    block_output = (
        residual
        + branches
        + small[4 * model_width : 5 * model_width]
        + small[5 * model_width : 6 * model_width]
    )
    act_grad = jnp.einsum(
        "ptr,kra->ptka", cotangent, down_projection_weight, preferred_element_type=jnp.float32
    )
    hidden_gradient = gelu_back(act_grad)[0].astype(jnp.bfloat16)
    down_grad = jnp.einsum(
        "gup,guzb->zpb", cotangent, activated_reduced, preferred_element_type=jnp.float32
    )
    in_grad = jnp.einsum(
        "gup,guzb->zpb", second_input, hidden_gradient, preferred_element_type=jnp.float32
    )
    second_grad = jnp.einsum(
        "xkzp,zop->xko", hidden_gradient, input_weight, preferred_element_type=jnp.float32
    )
    attended_grad = jnp.einsum(
        "pgk,jka->pgja", cotangent, projection_out_weight, preferred_element_type=jnp.float32
    ).astype(jnp.bfloat16)
    outproj_grad = jnp.einsum(
        "ztu,ztqi->qui", cotangent, attention_result, preferred_element_type=jnp.float32
    )
    grad_heads = to_heads(attended_grad[:, :, None])[:, :, 0]
    row_delta = jnp.transpose(
        jnp.sum(grad_heads.astype(jnp.float32) * attended_rows, axis=-1), (0, 2, 1)
    )

    def backward_visit(query_grad, pair, source):
        allowed = allowed_pairs(segments, cycle_index, source, block_rows)
        scores = masked_scores(queries, pair[:, :, 0], allowed)
        probabilities = jnp.where(allowed, jnp.exp(scores - log_total[..., None]), 0.0)
        value_grad = jnp.einsum(
            "shqk,sqhe->skhe",
            probabilities.astype(jnp.bfloat16),
            grad_heads,
            preferred_element_type=jnp.float32,
        )
        prob_grad = jnp.einsum(
            "sqhe,skhe->shqk", grad_heads, pair[:, :, 1], preferred_element_type=jnp.float32
        )
        score_grad = (probabilities * (prob_grad - row_delta[..., None])).astype(jnp.bfloat16)
        score_scale = HD ** (-0.5)
        query_grad = (
            query_grad
            + jnp.einsum(
                "shqk,skhe->sqhe", score_grad, pair[:, :, 0], preferred_element_type=jnp.float32
            )
            * score_scale
        )
        key_grad = (
            jnp.einsum("shqk,sqhe->skhe", score_grad, queries, preferred_element_type=jnp.float32)
            * score_scale
        )
        return (query_grad, jnp.stack([key_grad, value_grad], axis=2))

    def backward_hop(hop_index, carry):
        pair, pair_grad, query_grad = carry
        source = (cycle_index - hop_index) % cycle_size
        query_grad, visit_grad = backward_visit(query_grad, pair, source)
        return (pass_keys(pair), pass_grads(pair_grad + visit_grad), query_grad)

    zero_pair = jnp.zeros(by_heads[:, :, 1:].shape, jnp.float32)
    pair, pair_grad, query_grad = lax.fori_loop(
        0,
        cycle_size - 1,
        backward_hop,
        (by_heads[:, :, 1:], zero_pair, jnp.zeros(queries.shape, jnp.float32)),
    )
    query_grad, visit_grad = backward_visit(query_grad, pair, (cycle_index + 1) % cycle_size)
    pair_grad = pass_grads(pair_grad + visit_grad)
    head_grads = jnp.concatenate([query_grad[:, :, None], pair_grad], axis=2).astype(jnp.bfloat16)
    position_grads = to_positions(head_grads).astype(jnp.float32)
    query_pre_grad, key_pre_grad = turn_back((position_grads[:, :, 0], position_grads[:, :, 1]))
    projected_grad = jnp.stack(
        [query_pre_grad, key_pre_grad, position_grads[:, :, 2]], axis=2
    ).astype(jnp.bfloat16)
    flattened_gradient = projected_grad.reshape(sequences, local_rows, 3 * head_count, HD)
    query_key_value_gradient = jnp.einsum(
        "ztu,ztqi->qui", first_input, flattened_gradient, preferred_element_type=jnp.float32
    )
    first_grad = jnp.einsum(
        "roxu,xcu->roc",
        flattened_gradient,
        query_key_value_weight,
        preferred_element_type=jnp.float32,
    )
    input_part, gain_one_grad, offset_one_grad, gain_two_grad, offset_two_grad = norm_back(
        (first_grad, second_grad)
    )
    input_grad = cotangent.astype(jnp.float32) + lax.psum(
        input_part.astype(jnp.bfloat16), "tp"
    ).astype(jnp.float32)
    owner_share = jnp.where(tensor_index == 0, 1.0, 0.0).astype(jnp.float32)
    bias_grad = jnp.sum(cotangent.astype(jnp.float32), axis=(0, 1)) * owner_share
    qkv_bias_grad = jnp.transpose(
        jnp.sum(projected_grad.astype(jnp.float32), axis=(0, 1)), (1, 0, 2)
    ).reshape(-1)
    unit_bias_grad = jnp.sum(hidden_gradient.astype(jnp.float32), axis=(0, 1)).reshape(-1)
    local_small = jnp.concatenate(
        [
            gain_one_grad,
            offset_one_grad,
            gain_two_grad,
            offset_two_grad,
            bias_grad,
            bias_grad,
            jnp.zeros((small.shape[0] - 6 * model_width,), jnp.float32),
        ]
    )
    local_small = lax.dynamic_update_slice_in_dim(local_small, qkv_bias_grad, qkv_start, 0)
    local_small = lax.dynamic_update_slice_in_dim(local_small, unit_bias_grad, unit_start, 0)
    small_grads = lax.psum(local_small, ("blk", "ctx", "tp"))
    local_grad = jnp.concatenate(
        [query_key_value_gradient, outproj_grad, in_grad, down_grad], axis=0
    ).reshape(per_group, -1)
    shares = lax.psum_scatter(
        local_grad.astype(jnp.bfloat16), "blk", scatter_dimension=1, tiled=True
    )
    matrix_grads = lax.psum(shares, "ctx").astype(jnp.float32)
    new_momenta = momentum_decay * momenta + matrix_grads
    update = matrix_grads + momentum_decay * new_momenta
    per_owner = per_group // cycle_size
    sectioned = update.reshape(cycle_size, per_owner, update.shape[1])
    pieces = lax.all_to_all(
        sectioned.astype(jnp.bfloat16), "blk", split_axis=0, concat_axis=2, tiled=True
    ).astype(sectioned.dtype)
    piece_count = pieces.shape[1]
    settled_blocks = newton_schulz(pieces.reshape(piece_count, MODEL_DIM, HD)).reshape(
        1, piece_count, MODEL_DIM * HD
    )
    settled = lax.all_to_all(
        as_sent(settled_blocks), "blk", split_axis=2, concat_axis=0, tiled=True
    ).astype(settled_blocks.dtype)
    orthogonal_all = settled.reshape(per_group, -1)
    muon_scale = max(1.0, MODEL_DIM / HD) ** 0.5
    new_matrices = matrices - muon_rate * (muon_scale * orthogonal_all + weight_decay * matrices)
    new_first = adam_first * small_first + (1.0 - adam_first) * small_grads
    new_second = adam_second * small_second + (1.0 - adam_second) * small_grads * small_grads
    corrected = new_first / (1.0 - adam_first**STEP)
    spread = jnp.sqrt(new_second / (1.0 - adam_second**STEP))
    new_small = small - small_rate * corrected / (spread + adam_epsilon)
    return (
        block_output,
        input_grad,
        matrix_grads,
        new_matrices,
        new_momenta,
        small_grads,
        new_first,
        new_second,
        new_small,
    )


def native_view(array):
    rows, columns = array.shape
    tiled = array.reshape(rows // 8, 8, columns // 128, 128).transpose(0, 2, 1, 3)
    return tiled.reshape(rows // 8, columns // 16, 128)


def native_back(array):
    groups, rows, _ = array.shape
    return array.reshape(groups, rows // 8, 8, 128).transpose(0, 2, 1, 3).reshape(groups * 8, rows * 16)


def piece_members(piece):
    chunk, place = divmod(piece, 4)
    if chunk == 0:
        return [place, 4 + place, 8 + place, 12 + place]
    return [16 * chunk + 4 * place + j for j in range(4)]


def mem(kind=pltpu.VMEM):
    return pl.BlockSpec(memory_space=kind)


def limits(mebibytes):
    return pltpu.CompilerParams(vmem_limit_bytes=mebibytes << 20)


def low_lanes(rows):
    return lax.broadcasted_iota(jnp.int32, (rows, 128), 1) < HD


def dot(a, b, dims=((1,), (0,)), precision=None):
    return lax.dot_general(
        a, b, (dims, ((), ())), precision=precision, preferred_element_type=jnp.float32
    )


NT = ((1,), (1,))
TN = ((0,), (0,))


def relayout_kernel(n, src, out, scratch):
    low = low_lanes(n)
    for piece in range(12):
        members = piece_members(piece)
        for half in range(2):
            k = 2 * piece + half
            first, second = members[2 * half : 2 * half + 2]
            a = src[first // 8, pl.ds(first % 8, n, stride=8), :]
            b = src[second // 8, pl.ds(second % 8, n, stride=8), :]
            scratch[k, pl.ds(0, n, stride=2), :] = jnp.where(low, a, pltpu.roll(b, 64, 1))
            scratch[k, pl.ds(1, n, stride=2), :] = jnp.where(low, pltpu.roll(a, 64, 1), b)
            out[piece, :, half * 128 : (half + 1) * 128] = scratch[k].astype(out.dtype)


def relayout(array, dtype, n=32):
    return pl.pallas_call(
        functools.partial(relayout_kernel, n),
        grid=(256 // n,),
        in_specs=[pl.BlockSpec((6, 8 * n, 128), lambda i: (0, i, 0))],
        out_specs=pl.BlockSpec((12, 2 * n, 256), lambda i: (0, i, 0)),
        out_shape=jax.ShapeDtypeStruct((12, 512, 256), dtype),
        scratch_shapes=[pltpu.VMEM((24, 2 * n, 128), jnp.float32)],
        compiler_params=limits(40),
        name="relayout",
    )(native_view(array))


def normalized(x):
    centred = x - jnp.mean(x, axis=-1, keepdims=True)
    spread = jnp.mean(centred * centred, axis=-1, keepdims=True)
    root = lax.rsqrt(spread + norm_epsilon)
    return centred * root, root


def halves(values, first):
    left, right = values[:, :512], values[:, 512:]
    return jnp.where(first, left, right), jnp.where(first, right, left)


def whole(own, other, first):
    return jnp.concatenate([jnp.where(first, own, other), jnp.where(first, other, own)], axis=1)


def norm_back(grad, hat, root, gain):
    scaled = grad * gain
    along = jnp.mean(scaled * hat, axis=-1, keepdims=True)
    return root * (scaled - jnp.mean(scaled, axis=-1, keepdims=True) - hat * along)


def turned(values, cosine, sine):
    lane = lax.broadcasted_iota(jnp.int32, values.shape, 1) % HD
    other = jnp.where(lane < 8, pltpu.roll(values, 120, 1), pltpu.roll(values, 8, 1))
    return values * cosine + other * sine


def project_kernel(scal, x, cot, norms, bias, cosine, sine, own, r0, r1, r2, r3, send, h1):
    first = scal[0] == 0
    hat, _ = normalized(x[...].astype(jnp.float32))
    h = (hat * norms[0:1] + norms[1:2]).astype(jnp.bfloat16)
    h1[...] = h
    h_own, h_other = halves(h, first)
    c_own, c_other = halves(cot[...], first)
    tokens = h.shape[0]
    low = low_lanes(tokens)
    for r, other in enumerate((r0, r1, r2, r3)):
        head = scal[1] ^ r
        mine = own[head]
        theirs = other[...]
        pre = dot(h_own, mine) + dot(h_other, theirs) + bias[pl.ds(head, 1), :]
        back = dot(c_own, mine[:, 128:]) + dot(c_other, theirs[:, 128:])
        left = turned(pre[:, :128], cosine[...], sine[...]).astype(jnp.bfloat16)
        right = jnp.where(low, pre[:, 128:], back).astype(jnp.bfloat16)
        for s in range(2):
            rows = slice(128 * s, 128 * s + 128)
            send[4 * s + head, :, :128] = left[rows]
            send[4 * s + head, :, 128:] = right[rows]


def attention_kernel(rows_ref, seg, out, key_total, value_total):
    key_total[...] = jnp.zeros_like(key_total)
    value_total[...] = jnp.zeros_like(value_total)
    step = 256
    for block in range(rows_ref.shape[0] // step):
        rows = slice(block * step, (block + 1) * step)
        n = (block + 1) * step
        query = rows_ref[rows, 0:HD] * jnp.bfloat16(0.125)
        grad = rows_ref[rows, 3 * HD : 4 * HD]
        keys = rows_ref[0:n, HD : 2 * HD]
        values = rows_ref[0:n, 2 * HD : 3 * HD]
        scores = dot(query, keys, NT)
        query_place = block * step + lax.broadcasted_iota(jnp.int32, (step, n), 0)
        key_place = lax.broadcasted_iota(jnp.int32, (step, n), 1)
        allowed = (key_place <= query_place) & (key_place >= seg[rows, :])
        scores = jnp.where(allowed, scores, masked_score)
        weights = jnp.exp(scores - jnp.max(scores, axis=-1, keepdims=True))
        weights = jnp.where(allowed, weights, 0.0)
        weights = weights * (1.0 / jnp.sum(weights, axis=-1, keepdims=True))
        short = weights.astype(jnp.bfloat16)
        attended = dot(short, values)
        weight_grad = dot(grad, values, NT)
        delta = jnp.sum(weights * weight_grad, axis=-1, keepdims=True)
        score_grad = (weights * (weight_grad - delta)).astype(jnp.bfloat16)
        query_grad = dot(score_grad, keys) * 0.125
        key_total[0:n, :] += dot(score_grad, query, TN)
        value_total[0:n, :] += dot(short, grad, TN)
        out[rows, 0:HD] = query_grad.astype(jnp.bfloat16)
        out[rows, 3 * HD : 4 * HD] = attended.astype(jnp.bfloat16)
    out[:, HD : 2 * HD] = key_total[...].astype(jnp.bfloat16)
    out[:, 2 * HD : 3 * HD] = value_total[...].astype(jnp.bfloat16)


def feed_forward_kernel(
    scal, x, cot, norms, bias, own_in, own_down, r0, r1, r2, r3,
    branch, input_part, keep, send, hidden_sums, norm_grads, cot_sums,
):
    first = scal[0] == 0
    hat, root = normalized(x[...].astype(jnp.float32))
    h = (hat * norms[2:3] + norms[3:4]).astype(jnp.bfloat16)
    h_own, h_other = halves(h, first)
    c_own, c_other = halves(cot[...], first)
    cot_sums[...] = jnp.sum(cot[...].astype(jnp.float32), axis=0, keepdims=True)
    outs = [0.0] * 4
    for r, other in enumerate((r0, r1, r2, r3)):
        piece = scal[1] ^ r
        in_own, in_other = own_in[piece], other[0]
        down_own, down_other = own_down[piece], other[1]
        pre = dot(h_own, in_own) + dot(h_other, in_other) + bias[pl.ds(piece, 1), :]
        cumulative = 0.5 * (1.0 + lax.erf(pre * 0.7071067811865476))
        slope = cumulative + pre * (0.3989422804014327 * jnp.exp(-0.5 * pre * pre))
        act = (pre * cumulative).astype(jnp.bfloat16)
        act_grad = dot(c_own, down_own) + dot(c_other, down_other)
        grad = (act_grad * slope).astype(jnp.bfloat16)
        hidden_sums[pl.ds(piece, 1), :] = jnp.sum(
            grad.astype(jnp.float32), axis=0, keepdims=True
        )
        outs[0] += dot(act, down_own, NT)
        outs[1] += dot(act, down_other, NT)
        outs[2] += dot(grad, in_own, NT)
        outs[3] += dot(grad, in_other, NT)
        target = send if r % 2 else keep
        for side, (h_side, c_side) in enumerate(((h_own, c_own), (h_other, c_other))):
            target[side, r // 2, 0] = dot(h_side, grad, TN).astype(jnp.bfloat16)
            target[side, r // 2, 1] = dot(c_side, act, TN).astype(jnp.bfloat16)
    branch[...] = whole(outs[0], outs[1], first)
    second = whole(outs[2], outs[3], first)
    norm_grads[0:1] = jnp.sum(second * hat, axis=0, keepdims=True)
    norm_grads[1:2] = jnp.sum(second, axis=0, keepdims=True)
    input_part[...] = norm_back(second, hat, root, norms[2:3])


def gather_kernel(
    scal, x, cot, norms, cosine, sine, back, h1, own, r0, r1, r2, r3, ff_branch, ff_part,
    near, far, keep, send, sums, norm_grads, parts,
):
    first = scal[0] == 0
    hat, root = normalized(x[...].astype(jnp.float32))
    h_own, h_other = halves(h1[...], first)
    c_own, c_other = halves(cot[...], first)
    tokens = h_own.shape[0]
    low = low_lanes(tokens)
    outs = [0.0] * 4
    for r, other in enumerate((r0, r1, r2, r3)):
        head = scal[1] ^ r
        mine, theirs = own[head], other[...]
        grads = jnp.concatenate([back[head], back[4 + head]], axis=0)
        left = turned(grads[:, :128].astype(jnp.float32), cosine[...], -sine[...])
        right = grads[:, 128:].astype(jnp.float32)
        value_grad = jnp.where(low, right, 0.0).astype(jnp.bfloat16)
        attended = jnp.where(low, 0.0, right).astype(jnp.bfloat16)
        pre_grad = jnp.concatenate([left.astype(jnp.bfloat16), value_grad], axis=1)
        sums[pl.ds(head, 1), :] = jnp.sum(pre_grad.astype(jnp.float32), axis=0, keepdims=True)
        outs[0] += dot(attended, mine[:, 128:], NT)
        outs[1] += dot(attended, theirs[:, 128:], NT)
        outs[2] += dot(pre_grad, mine, NT)
        outs[3] += dot(pre_grad, theirs, NT)
        target = send if r % 2 else keep
        for side, (h_side, c_side) in enumerate(((h_own, c_own), (h_other, c_other))):
            grad = dot(h_side, pre_grad, TN)
            out_grad = dot(c_side, attended, TN)
            target[side, r // 2, 0, :, :128] = grad[:, :128].astype(jnp.bfloat16)
            target[side, r // 2, 0, :, 128:] = (grad[:, 128:] + out_grad).astype(jnp.bfloat16)
    branch = ff_branch[...] + whole(outs[0], outs[1], first)
    grad = whole(outs[2], outs[3], first)
    norm_grads[0:1] = jnp.sum(grad * hat, axis=0, keepdims=True)
    norm_grads[1:2] = jnp.sum(grad, axis=0, keepdims=True)
    input_part = ff_part[...] + norm_back(grad, hat, root, norms[0:1])
    for q in range(4):
        parts[q, 0] = branch[64 * q : 64 * q + 64].astype(jnp.bfloat16)
        parts[q, 1] = input_part[64 * q : 64 * q + 64].astype(jnp.bfloat16)
    for r in range(4):
        (far if r % 2 else near)[r // 2] = parts[scal[2] ^ r]


def finish_rows_kernel(scal, x, cot, bias, r0, r1, r2, r3, block_output, input_grad):
    for r, piece in enumerate((r0, r1, r2, r3)):
        q = scal[2] ^ r
        block_output[q] = x[q].astype(jnp.float32) + piece[0].astype(jnp.float32) + bias[...]
        input_grad[q] = cot[q].astype(jnp.float32) + piece[1].astype(jnp.float32)


def gram_kernel(place, own, a, b, c, momenta, grads, grams):
    total = own[...].astype(jnp.float32) + a[...].astype(jnp.float32)
    total = total + b[...].astype(jnp.float32) + c[...].astype(jnp.float32)
    short = total.astype(jnp.bfloat16)
    grads[...] = short
    update = 1.95 * short[0].astype(jnp.float32) + 0.9025 * momenta[0]
    gram = dot(update, update, TN, lax.Precision.HIGHEST)
    for j in range(4):
        cut = slice(j * HD, (j + 1) * HD)
        grams[0, j] = gram[cut, cut]


def gram_of(own, a, b, c, momenta, first_chunk, place):
    chunks = own.shape[0]
    piece = pl.BlockSpec((1, 512, 256), lambda i, s: (i, 0, 0))
    return pl.pallas_call(
        gram_kernel,
        grid_spec=pltpu.PrefetchScalarGridSpec(
            num_scalar_prefetch=1,
            grid=(chunks,),
            in_specs=[piece] * 4
            + [pl.BlockSpec((1, 512, 256), lambda i, s: (4 * (first_chunk + i) + s[1], 0, 0))],
            out_specs=[piece, pl.BlockSpec((1, 4, HD, HD), lambda i, s: (i, 0, 0, 0))],
        ),
        out_shape=[
            jax.ShapeDtypeStruct((chunks, 512, 256), jnp.bfloat16),
            jax.ShapeDtypeStruct((chunks, 4, HD, HD), jnp.float32),
        ],
        compiler_params=limits(32),
        name="gram",
    )(place, own, a, b, c, momenta)


def newton_kernel(mine, theirs, out):
    linear, square, cubic = quintic
    shape = (HD, HD)
    eye = lax.broadcasted_iota(jnp.int32, shape, 0) == lax.broadcasted_iota(jnp.int32, shape, 1)
    high = lax.Precision.HIGHEST
    chunks = mine.shape[0]
    places = [(i, j) for i in range(chunks) for j in range(4)]
    states = []
    for i, j in places:
        gram = mine[i, j] + theirs[i, j]
        trace = jnp.sum(jnp.where(eye, gram, 0.0), axis=(0, 1), keepdims=True)
        scale = 1.0 / (jnp.sqrt(trace) + muon_epsilon)
        states.append([gram * scale * scale, None, scale])
    for iteration in range(NEWTON):
        squares = [dot(s[0], s[0], precision=high) for s in states]
        steps = [
            jnp.where(eye, linear, 0.0) + square * s[0] + cubic * sq
            for s, sq in zip(states, squares)
        ]
        if iteration == 0:
            halfway = [dot(s[0], m, precision=high) for s, m in zip(states, steps)]
            for s, m in zip(states, steps):
                s[1] = m
        elif iteration < NEWTON - 1:
            both = [
                dot(jnp.concatenate([s[0], s[1]], axis=0), m, precision=high)
                for s, m in zip(states, steps)
            ]
            halfway = [x[:HD] for x in both]
            for s, x in zip(states, both):
                s[1] = x[HD:]
        else:
            for s, m in zip(states, steps):
                s[1] = dot(s[1], m, precision=high)
        if iteration < NEWTON - 1:
            for s, x, m in zip(states, halfway, steps):
                s[0] = dot(x, m, precision=high)
    for (i, j), s in zip(places, states):
        out[i, j] = s[1] * s[2]


def newton(mine, theirs):
    return pl.pallas_call(
        newton_kernel,
        in_specs=[mem()] * 2,
        out_specs=mem(),
        out_shape=jax.ShapeDtypeStruct(mine.shape, jnp.float32),
        compiler_params=limits(32),
        name="newton",
    )(mine, theirs)


def update_kernel(
    n, chunk_start, scal, g0, g1, g2, g3, q0, q1, q2, q3, momenta, native_momenta, native,
    grads_in, weights_in, momenta_in, grads, weights, moved, mixing, first, second,
):
    if chunk_start == 0:
        place_of = lambda p, j: (j // 2, 4 * (j % 2) + p)
    else:
        place_of = lambda p, j: (p // 2, 4 * (p % 2) + j)

    @pl.when((pl.program_id(0) == 0) & (pl.program_id(1) == 0))
    def _():
        mixing[...] = jnp.zeros_like(mixing)

    @pl.when(pl.program_id(1) == 0)
    def _():
        for r, q in enumerate((q0, q1, q2, q3)):
            for j in range(4):
                mixing[r, j * HD : (j + 1) * HD, j * HD : (j + 1) * HD] = q[0, j]

    low = low_lanes(n)
    for r, piece in enumerate((g0, g1, g2, g3)):
        place = scal[1] ^ r
        grad = piece[0].astype(jnp.float32)
        update = 1.95 * grad + 0.9025 * momenta[place]
        settled = dot(update, mixing[r], precision=lax.Precision.HIGHEST)
        for half in range(2):
            k = 2 * r + half
            first[k] = grad[:, half * 128 : (half + 1) * 128]
            second[k] = settled[:, half * 128 : (half + 1) * 128]
            pairs = []
            for s in (first, second):
                even = s[k, pl.ds(0, n, stride=2), :]
                odd = s[k, pl.ds(1, n, stride=2), :]
                pairs.append(
                    (
                        jnp.where(low, even, pltpu.roll(odd, 64, 1)),
                        jnp.where(low, pltpu.roll(even, 64, 1), odd),
                    )
                )
            for w in range(2):
                group, line = place_of(place, 2 * half + w)
                rows = pl.ds(line, n, stride=8)
                value, step = pairs[0][w], pairs[1][w]
                grads[group, rows, :] = value
                moved[group, rows, :] = momentum_decay * native_momenta[group, rows, :] + value
                weight = native[group, rows, :]
                weights[group, rows, :] = weight - muon_rate * (4.0 * step + weight_decay * weight)


def update(chunk_start, chunks, scal, grads, mixes, momenta, native_momenta, native, before, n=32):
    block = pl.BlockSpec((2, 8 * n, 128), lambda k, i: (chunk_start + k, i, 0))
    piece = pl.BlockSpec((1, 2 * n, 256), lambda k, i: (k, i, 0))
    mix = pl.BlockSpec((1, 4, HD, HD), lambda k, i: (k, 0, 0, 0))
    full = jax.ShapeDtypeStruct((6, 2048, 128), jnp.float32)
    kernel = functools.partial(update_kernel, n, chunk_start)
    if before is None:
        body = kernel
        kernel = lambda *refs: body(*refs[:12], None, None, None, *refs[12:])
        before = ()
    return pl.pallas_call(
        kernel,
        grid=(chunks, 256 // n),
        in_specs=[mem(pltpu.SMEM)]
        + [piece] * 4
        + [mix] * 4
        + [pl.BlockSpec((4, 2 * n, 256), lambda k, i: (chunk_start + k, i, 0)), block, block]
        + [mem(pl.ANY)] * len(before),
        out_specs=[block] * 3,
        out_shape=[full] * 3,
        scratch_shapes=[
            pltpu.VMEM((4, 256, 256), jnp.float32),
            pltpu.VMEM((8, 2 * n, 128), jnp.float32),
            pltpu.VMEM((8, 2 * n, 128), jnp.float32),
        ],
        input_output_aliases={12 + i: i for i in range(len(before))},
        compiler_params=limits(40),
        name="update",
    )(scal, *grads, *mixes, momenta, native_momenta, native, *before)


def whole_device(
    inputs, cotangent, matrices, momenta, small, small_first, small_second, segments, positions
):
    blk_at = lax.axis_index("blk")
    ctx_at = lax.axis_index("ctx")
    tp_at = lax.axis_index("tp")
    scal = jnp.stack([blk_at, ctx_at, tp_at]).astype(jnp.int32)
    sequences, local_rows, width = inputs.shape
    tokens = sequences * local_rows
    both = ("blk", "ctx")
    f32, bf16 = jnp.float32, jnp.bfloat16
    shaped = jax.ShapeDtypeStruct

    def hop(values, by):
        return lax.ppermute(values, both, [(i, i ^ by) for i in range(8)])

    def hop_tp(values, by):
        return lax.ppermute(values, "tp", [(i, i ^ by) for i in range(4)])

    x = inputs.reshape(tokens, width)
    cot = cotangent.reshape(tokens, width)
    norms = small[: 4 * width].reshape(4, width)
    qkv_start = 6 * width + tp_at * 4 * 3 * HD
    qkv_bias = lax.dynamic_slice_in_dim(small, qkv_start, 4 * 3 * HD).reshape(4, 3 * HD)
    qkv_bias = jnp.pad(qkv_bias, ((0, 0), (0, HD)))
    unit_start = 6 * width + H * 3 * HD + tp_at * 1024
    unit_bias = lax.dynamic_slice_in_dim(small, unit_start, 1024).reshape(4, 256)
    frequency = rope_base ** (-2.0 * jnp.arange(ROTARY // 2, dtype=f32) / ROTARY)
    angles = positions.astype(f32).reshape(tokens, 1) * frequency
    cos, sin = jnp.cos(angles), jnp.sin(angles)
    rest = jnp.ones((tokens, HD - ROTARY), f32)
    cosine = jnp.concatenate([cos, cos, rest, cos, cos, rest], axis=1)
    sine = jnp.concatenate([-sin, sin, 0.0 * rest, -sin, sin, 0.0 * rest], axis=1)

    weights = relayout(matrices, bf16)

    def gathered(piece):
        a = hop(piece, 4)
        c = hop(a, 2)
        return [a, hop(a, 1), c, hop(c, 1)]

    by_chunk = weights.reshape(3, 4, 512, 256)
    mine = lax.dynamic_index_in_dim(by_chunk, ctx_at, 1, keepdims=False)
    others_head = gathered(mine[0])
    others_unit = gathered(mine[1:])
    piled = relayout(momenta, f32)

    own_chunk = lambda k: pl.BlockSpec((4, 512, 256), lambda *_: (k, 0, 0))
    send, h1 = pl.pallas_call(
        project_kernel,
        grid=(1,),
        in_specs=[mem(pltpu.SMEM)] + [mem()] * 6 + [own_chunk(0)] + [mem()] * 4,
        out_specs=[mem()] * 2,
        out_shape=[shaped((8, local_rows, 256), bf16), shaped((tokens, width), bf16)],
        compiler_params=limits(40),
        name="project",
    )(scal, x, cot, norms, qkv_bias, cosine, sine, weights, *others_head)

    arrived = lax.all_to_all(send, both, split_axis=0, concat_axis=0, tiled=True)
    documents = lax.dynamic_index_in_dim(segments, blk_at, 0, keepdims=False)
    length = documents.shape[0]
    attended = pl.pallas_call(
        attention_kernel,
        in_specs=[mem()] * 2,
        out_specs=mem(),
        out_shape=shaped((length, 256), bf16),
        scratch_shapes=[pltpu.VMEM((length, HD), f32)] * 2,
        compiler_params=limits(48),
        name="attention",
    )(arrived.reshape(length, 256), documents.reshape(length, 1))
    back = lax.all_to_all(
        attended.reshape(8, local_rows, 256), both, split_axis=0, concat_axis=0, tiled=True
    )

    ff_branch, ff_part, ff_keep, ff_send, unit_sums, norm_two, cot_sums = pl.pallas_call(
        feed_forward_kernel,
        grid=(1,),
        in_specs=[mem(pltpu.SMEM)] + [mem()] * 4 + [own_chunk(1), own_chunk(2)] + [mem()] * 4,
        out_specs=[mem()] * 7,
        out_shape=[
            shaped((tokens, width), f32),
            shaped((tokens, width), f32),
            shaped((2, 2, 2, 512, 256), bf16),
            shaped((2, 2, 2, 512, 256), bf16),
            shaped((4, 256), f32),
            shaped((2, width), f32),
            shaped((1, width), f32),
        ],
        compiler_params=limits(48),
        name="feed_forward",
    )(scal, x, cot, norms, unit_bias, weights, weights, *others_unit)

    def reduced(keep, send):
        came = hop(send, 1)
        summed = (keep.astype(f32) + came.astype(f32)).astype(bf16)
        return summed[0, 0], hop(summed[1, 0], 4), hop(summed[0, 1], 2), hop(summed[1, 1], 6)

    def spread(piece):
        c = hop(piece, 2)
        return [piece, hop(piece, 1), c, hop(c, 1)]

    def muon(keep, send, first_chunk, before):
        grads, grams = gram_of(*reduced(keep, send), piled, first_chunk, scal)
        pieces = spread(grads)
        mixes = spread(newton(grams, hop(grams, 4)))
        return update(
            first_chunk, grads.shape[0], scal, pieces, mixes, piled, native_view(momenta),
            native_view(matrices), before,
        )

    before = muon(ff_keep, ff_send, 1, None)

    near, far, keep, send_back, qkv_sums, norm_one = pl.pallas_call(
        gather_kernel,
        grid=(1,),
        in_specs=[mem(pltpu.SMEM)] + [mem()] * 7 + [own_chunk(0)] + [mem()] * 6,
        out_specs=[mem()] * 6,
        out_shape=[
            shaped((2, 2, 64, width), bf16),
            shaped((2, 2, 64, width), bf16),
            shaped((2, 2, 1, 512, 256), bf16),
            shaped((2, 2, 1, 512, 256), bf16),
            shaped((4, 256), f32),
            shaped((2, width), f32),
        ],
        scratch_shapes=[pltpu.VMEM((4, 2, 64, width), bf16)],
        compiler_params=limits(48),
        name="gather",
    )(scal, x, cot, norms, cosine, sine, back, h1, weights, *others_head, ff_branch, ff_part)

    outs = muon(keep, send_back, 0, before)

    summed = (near.astype(f32) + hop_tp(far, 1).astype(f32)).astype(bf16)
    total = (summed[0].astype(f32) + hop_tp(summed[1], 2).astype(f32)).astype(bf16)
    beside = hop_tp(total, 2)
    block_output, input_grad = pl.pallas_call(
        finish_rows_kernel,
        in_specs=[mem(pltpu.SMEM)] + [mem()] * 7,
        out_specs=[mem()] * 2,
        out_shape=[shaped((4, 64, width), f32)] * 2,
        compiler_params=limits(32),
        name="finish_rows",
    )(
        scal,
        x.reshape(4, 64, width),
        cot.reshape(4, 64, width),
        (small[4 * width : 5 * width] + small[5 * width : 6 * width]).reshape(1, width),
        total,
        hop_tp(total, 1),
        beside,
        hop_tp(beside, 1),
    )

    share = jnp.where(tp_at == 0, 1.0, 0.0).astype(f32)
    cot_total = cot_sums[0] * share
    local = jnp.concatenate(
        [
            norm_one.reshape(-1),
            norm_two.reshape(-1),
            cot_total,
            cot_total,
            jnp.zeros((small.shape[0] - 6 * width,), f32),
        ]
    )
    local = lax.dynamic_update_slice_in_dim(
        local, qkv_sums[:, : 3 * HD].reshape(-1), qkv_start, 0
    )
    small_grads = lax.dynamic_update_slice_in_dim(local, unit_sums.reshape(-1), unit_start, 0)
    for by in (1, 2, 4):
        small_grads = small_grads + hop(small_grads, by)
    for by in (1, 2):
        small_grads = small_grads + hop_tp(small_grads, by)
    new_matrices_at = native_back(outs[1])
    return (
        block_output.reshape(inputs.shape),
        input_grad.reshape(inputs.shape),
        native_back(outs[0]),
        new_matrices_at,
        native_back(outs[2]),
        small_grads,
        *small_step(small, small_first, small_second, small_grads),
    )


def small_step(small, small_first, small_second, small_grads):
    new_first = adam_first * small_first + (1.0 - adam_first) * small_grads
    new_second = adam_second * small_second + (1.0 - adam_second) * small_grads * small_grads
    corrected = new_first / (1.0 - adam_first**STEP)
    spread = jnp.sqrt(new_second / (1.0 - adam_second**STEP))
    new_small = small - small_rate * corrected / (spread + adam_epsilon)
    return new_first, new_second, new_small


def solution(mesh):
    in_specs = (
        P(None, ("blk", "ctx"), None),
        P(None, ("blk", "ctx"), None),
        P("tp", "blk"),
        P("tp", "blk"),
        P(),
        P(),
        P(),
        P(),
        P(None, ("blk", "ctx")),
    )
    out_specs = (
        P(None, ("blk", "ctx"), None),
        P(None, ("blk", "ctx"), None),
        P("tp", "blk"),
        P("tp", "blk"),
        P("tp", "blk"),
        P(),
        P(),
        P(),
        P(),
    )
    one_each = mesh.shape["blk"] == SEQS and mesh.shape["ctx"] * mesh.shape["tp"] == H
    one_each = one_each and mesh.shape["tp"] == 4
    return jax.shard_map(
        whole_device if one_each else on_device, mesh=mesh, in_specs=in_specs, out_specs=out_specs, check_vma=False
    )
```

```python
import functools

import jax
import jax.numpy as jnp
from jax import lax
from jax.experimental import pallas as pl
from jax.experimental.pallas import tpu as pltpu
from jax.sharding import PartitionSpec as P

MODEL_DIM = 1024
H = 16
HD = 64
FF = 4096
ROTARY = 16
NEWTON = 5
STEP = 10
SEQS = 2


norm_epsilon = 1e-05
rope_base = 10000.0
masked_score = -1e30
momentum_decay = 0.95
muon_rate = 0.2
weight_decay = 0.01
muon_epsilon = 1e-07
quintic = (3.4445, -4.775, 2.0315)
adam_first = 0.9
adam_second = 0.95
adam_epsilon = 1e-08
small_rate = 0.2


def passed_along(x, axis, by):
    devices = lax.axis_size(axis)
    pairs = [(i, i + by) for i in range(devices) if 0 <= i + by < devices]
    return lax.ppermute(x, axis, pairs)


def shifted(x, axis, by):
    devices = lax.axis_size(axis)
    return lax.ppermute(x, axis, [(i, (i + by) % devices) for i in range(devices)])


def as_sent(x):

    def short(part):
        return part.astype(jnp.bfloat16) if part.dtype == jnp.float32 else part

    return jax.tree.map(short, x)


def layer_norm(values, scaling, offset):
    centre = jnp.mean(values, axis=-1, keepdims=True)
    centred = values - centre
    spread = jnp.mean(centred * centred, axis=-1, keepdims=True)
    return centred * lax.rsqrt(spread + norm_epsilon) * scaling + offset


def rope_tables(positions):
    halfway = ROTARY // 2
    frequency = rope_base ** (-2.0 * jnp.arange(halfway, dtype=jnp.float32) / ROTARY)
    angles = positions.astype(jnp.float32)[..., None] * frequency
    return (jnp.cos(angles)[:, :, None, :], jnp.sin(angles)[:, :, None, :])


def rotate(values, cosine, sine):
    halfway = ROTARY // 2
    former = values[..., :halfway]
    latter = values[..., halfway:ROTARY]
    return jnp.concatenate(
        [former * cosine - latter * sine, latter * cosine + former * sine, values[..., ROTARY:]],
        axis=-1,
    )


def exact_gelu(values):
    return jax.nn.gelu(values, approximate=False)


def newton_schulz(blocks):
    frobenius = jnp.sqrt(jnp.sum(blocks * blocks, axis=(1, 2), keepdims=True))
    current = blocks / (frobenius + muon_epsilon)
    linear_term, square_term, cubic_term = quintic
    for iteration in range(NEWTON):
        gram_matrix = jnp.einsum("mde,mdf->mef", current, current, precision=lax.Precision.HIGHEST)
        polynomial = square_term * gram_matrix + cubic_term * jnp.einsum(
            "mef,mfg->meg", gram_matrix, gram_matrix, precision=lax.Precision.HIGHEST
        )
        current = linear_term * current + jnp.einsum(
            "mde,mef->mdf", current, polynomial, precision=lax.Precision.HIGHEST
        )
    return current


def to_heads(values):
    return lax.all_to_all(values, "ctx", split_axis=3, concat_axis=1, tiled=True)


def to_positions(values):
    return lax.all_to_all(values, "ctx", split_axis=1, concat_axis=3, tiled=True)


def pass_keys(pair):
    return passed_along(pair, "blk", 1)


def pass_grads(pair_grad):
    return shifted(pair_grad.astype(jnp.bfloat16), "blk", 1).astype(pair_grad.dtype)


def allowed_pairs(segments, query_block, key_block, block_rows):
    query_place = query_block * block_rows + jnp.arange(block_rows, dtype=jnp.int32)
    key_place = key_block * block_rows + jnp.arange(block_rows, dtype=jnp.int32)
    query_doc = lax.dynamic_slice_in_dim(segments, query_block * block_rows, block_rows, 1)
    key_doc = lax.dynamic_slice_in_dim(segments, key_block * block_rows, block_rows, 1)
    causal = key_place[None, :] <= query_place[:, None]
    return (causal[None] & (query_doc[:, :, None] == key_doc[:, None, :]))[:, None]


def masked_scores(queries, keys, allowed):
    score_scale = HD ** (-0.5)
    scores = (
        jnp.einsum("sqhe,skhe->shqk", queries, keys, preferred_element_type=jnp.float32)
        * score_scale
    )
    return jnp.where(allowed, scores, masked_score)


def on_device(
    inputs, cotangent, matrices, momenta, small, small_first, small_second, segments, positions
):
    tensor_size = lax.axis_size("tp")
    cycle_size = lax.axis_size("blk")
    context_size = lax.axis_size("ctx")
    tensor_index = lax.axis_index("tp")
    cycle_index = lax.axis_index("blk")
    sequences, local_rows, model_width = inputs.shape
    per_group = matrices.shape[0]
    head_count = H // tensor_size
    unit_blocks = FF // HD // tensor_size
    block_rows = local_rows * context_size
    gathered = lax.all_gather(matrices.astype(jnp.bfloat16), "blk", axis=1, tiled=True).reshape(
        per_group, model_width, HD
    )
    query_key_value_weight = gathered[: 3 * head_count]
    projection_out_weight = gathered[3 * head_count : 4 * head_count]
    input_weight = gathered[4 * head_count : 4 * head_count + unit_blocks]
    down_projection_weight = gathered[4 * head_count + unit_blocks :]
    qkv_start = 6 * model_width + tensor_index * head_count * 3 * HD
    query_key_value_bias = lax.dynamic_slice_in_dim(small, qkv_start, head_count * 3 * HD).reshape(
        head_count, 3, HD
    )
    unit_start = 6 * model_width + H * 3 * HD + tensor_index * unit_blocks * HD
    hidden_unit_bias = lax.dynamic_slice_in_dim(small, unit_start, unit_blocks * HD).reshape(
        unit_blocks, HD
    )
    residual = inputs.astype(jnp.float32)

    def both_norms(values, gain_one, offset_one, gain_two, offset_two):
        return (layer_norm(values, gain_one, offset_one), layer_norm(values, gain_two, offset_two))

    (normed_one, normed_two), norm_back = jax.vjp(
        both_norms,
        residual,
        small[0:model_width],
        small[model_width : 2 * model_width],
        small[2 * model_width : 3 * model_width],
        small[3 * model_width : 4 * model_width],
    )
    first_input = normed_one.astype(jnp.bfloat16)
    second_input = normed_two.astype(jnp.bfloat16)
    projected = jnp.einsum(
        "pgk,jka->pgja", first_input, query_key_value_weight, preferred_element_type=jnp.float32
    )
    projected = projected.reshape(sequences, local_rows, 3, head_count, HD) + jnp.transpose(
        query_key_value_bias, (1, 0, 2)
    )
    cosine, sine = rope_tables(positions)

    def turn_pair(query_pre, key_pre):
        return (rotate(query_pre, cosine, sine), rotate(key_pre, cosine, sine))

    (query_turned, key_turned), turn_back = jax.vjp(
        turn_pair, projected[:, :, 0], projected[:, :, 1]
    )
    stacked = jnp.stack([query_turned, key_turned, projected[:, :, 2]], axis=2).astype(jnp.bfloat16)
    by_heads = to_heads(stacked)
    queries = by_heads[:, :, 0]
    head_local = queries.shape[2]

    def forward_visit(state, pair, source):
        row_max, row_total, weighted = state
        allowed = allowed_pairs(segments, cycle_index, source, block_rows)
        scores = masked_scores(queries, pair[:, :, 0], allowed)
        new_max = jnp.maximum(row_max, jnp.max(scores, axis=-1))
        weights = jnp.where(allowed, jnp.exp(scores - new_max[..., None]), 0.0)
        rescale = jnp.exp(row_max - new_max)
        row_total = row_total * rescale + jnp.sum(weights, axis=-1)
        weighted = weighted * rescale[..., None] + jnp.einsum(
            "shqk,skhe->shqe",
            weights.astype(jnp.bfloat16),
            pair[:, :, 1],
            preferred_element_type=jnp.float32,
        )
        return (new_max, row_total, weighted)

    def forward_hop(hop_index, carry):
        pair, state = carry
        source = (cycle_index - hop_index) % cycle_size
        state = forward_visit(state, pair, source)
        return (pass_keys(pair), state)

    start_state = (
        jnp.full((sequences, head_local, block_rows), masked_score, jnp.float32),
        jnp.zeros((sequences, head_local, block_rows), jnp.float32),
        jnp.zeros((sequences, head_local, block_rows, HD), jnp.float32),
    )
    pair, state = lax.fori_loop(0, cycle_size - 1, forward_hop, (by_heads[:, :, 1:], start_state))
    row_max, row_total, weighted = forward_visit(state, pair, (cycle_index + 1) % cycle_size)
    log_total = row_max + jnp.log(row_total)
    attended_rows = jnp.transpose(weighted / row_total[..., None], (0, 2, 1, 3))
    attention_result = to_positions(attended_rows.astype(jnp.bfloat16)[:, :, None])[:, :, 0]
    attention_branch = jnp.einsum(
        "roxu,xcu->roc", attention_result, projection_out_weight, preferred_element_type=jnp.float32
    )
    hidden_preactivation = (
        jnp.einsum("ptr,kra->ptka", second_input, input_weight, preferred_element_type=jnp.float32)
        + hidden_unit_bias
    )
    activated_hidden, gelu_back = jax.vjp(exact_gelu, hidden_preactivation)
    activated_reduced = activated_hidden.astype(jnp.bfloat16)
    perceptron_branch = jnp.einsum(
        "xkzp,zop->xko",
        activated_reduced,
        down_projection_weight,
        preferred_element_type=jnp.float32,
    )
    branches = lax.psum((attention_branch + perceptron_branch).astype(jnp.bfloat16), "tp").astype(
        jnp.float32
    )
    block_output = (
        residual
        + branches
        + small[4 * model_width : 5 * model_width]
        + small[5 * model_width : 6 * model_width]
    )
    act_grad = jnp.einsum(
        "ptr,kra->ptka", cotangent, down_projection_weight, preferred_element_type=jnp.float32
    )
    hidden_gradient = gelu_back(act_grad)[0].astype(jnp.bfloat16)
    down_grad = jnp.einsum(
        "gup,guzb->zpb", cotangent, activated_reduced, preferred_element_type=jnp.float32
    )
    in_grad = jnp.einsum(
        "gup,guzb->zpb", second_input, hidden_gradient, preferred_element_type=jnp.float32
    )
    second_grad = jnp.einsum(
        "xkzp,zop->xko", hidden_gradient, input_weight, preferred_element_type=jnp.float32
    )
    attended_grad = jnp.einsum(
        "pgk,jka->pgja", cotangent, projection_out_weight, preferred_element_type=jnp.float32
    ).astype(jnp.bfloat16)
    outproj_grad = jnp.einsum(
        "ztu,ztqi->qui", cotangent, attention_result, preferred_element_type=jnp.float32
    )
    grad_heads = to_heads(attended_grad[:, :, None])[:, :, 0]
    row_delta = jnp.transpose(
        jnp.sum(grad_heads.astype(jnp.float32) * attended_rows, axis=-1), (0, 2, 1)
    )

    def backward_visit(query_grad, pair, source):
        allowed = allowed_pairs(segments, cycle_index, source, block_rows)
        scores = masked_scores(queries, pair[:, :, 0], allowed)
        probabilities = jnp.where(allowed, jnp.exp(scores - log_total[..., None]), 0.0)
        value_grad = jnp.einsum(
            "shqk,sqhe->skhe",
            probabilities.astype(jnp.bfloat16),
            grad_heads,
            preferred_element_type=jnp.float32,
        )
        prob_grad = jnp.einsum(
            "sqhe,skhe->shqk", grad_heads, pair[:, :, 1], preferred_element_type=jnp.float32
        )
        score_grad = (probabilities * (prob_grad - row_delta[..., None])).astype(jnp.bfloat16)
        score_scale = HD ** (-0.5)
        query_grad = (
            query_grad
            + jnp.einsum(
                "shqk,skhe->sqhe", score_grad, pair[:, :, 0], preferred_element_type=jnp.float32
            )
            * score_scale
        )
        key_grad = (
            jnp.einsum("shqk,sqhe->skhe", score_grad, queries, preferred_element_type=jnp.float32)
            * score_scale
        )
        return (query_grad, jnp.stack([key_grad, value_grad], axis=2))

    def backward_hop(hop_index, carry):
        pair, pair_grad, query_grad = carry
        source = (cycle_index - hop_index) % cycle_size
        query_grad, visit_grad = backward_visit(query_grad, pair, source)
        return (pass_keys(pair), pass_grads(pair_grad + visit_grad), query_grad)

    zero_pair = jnp.zeros(by_heads[:, :, 1:].shape, jnp.float32)
    pair, pair_grad, query_grad = lax.fori_loop(
        0,
        cycle_size - 1,
        backward_hop,
        (by_heads[:, :, 1:], zero_pair, jnp.zeros(queries.shape, jnp.float32)),
    )
    query_grad, visit_grad = backward_visit(query_grad, pair, (cycle_index + 1) % cycle_size)
    pair_grad = pass_grads(pair_grad + visit_grad)
    head_grads = jnp.concatenate([query_grad[:, :, None], pair_grad], axis=2).astype(jnp.bfloat16)
    position_grads = to_positions(head_grads).astype(jnp.float32)
    query_pre_grad, key_pre_grad = turn_back((position_grads[:, :, 0], position_grads[:, :, 1]))
    projected_grad = jnp.stack(
        [query_pre_grad, key_pre_grad, position_grads[:, :, 2]], axis=2
    ).astype(jnp.bfloat16)
    flattened_gradient = projected_grad.reshape(sequences, local_rows, 3 * head_count, HD)
    query_key_value_gradient = jnp.einsum(
        "ztu,ztqi->qui", first_input, flattened_gradient, preferred_element_type=jnp.float32
    )
    first_grad = jnp.einsum(
        "roxu,xcu->roc",
        flattened_gradient,
        query_key_value_weight,
        preferred_element_type=jnp.float32,
    )
    input_part, gain_one_grad, offset_one_grad, gain_two_grad, offset_two_grad = norm_back(
        (first_grad, second_grad)
    )
    input_grad = cotangent.astype(jnp.float32) + lax.psum(
        input_part.astype(jnp.bfloat16), "tp"
    ).astype(jnp.float32)
    owner_share = jnp.where(tensor_index == 0, 1.0, 0.0).astype(jnp.float32)
    bias_grad = jnp.sum(cotangent.astype(jnp.float32), axis=(0, 1)) * owner_share
    qkv_bias_grad = jnp.transpose(
        jnp.sum(projected_grad.astype(jnp.float32), axis=(0, 1)), (1, 0, 2)
    ).reshape(-1)
    unit_bias_grad = jnp.sum(hidden_gradient.astype(jnp.float32), axis=(0, 1)).reshape(-1)
    local_small = jnp.concatenate(
        [
            gain_one_grad,
            offset_one_grad,
            gain_two_grad,
            offset_two_grad,
            bias_grad,
            bias_grad,
            jnp.zeros((small.shape[0] - 6 * model_width,), jnp.float32),
        ]
    )
    local_small = lax.dynamic_update_slice_in_dim(local_small, qkv_bias_grad, qkv_start, 0)
    local_small = lax.dynamic_update_slice_in_dim(local_small, unit_bias_grad, unit_start, 0)
    small_grads = lax.psum(local_small, ("blk", "ctx", "tp"))
    local_grad = jnp.concatenate(
        [query_key_value_gradient, outproj_grad, in_grad, down_grad], axis=0
    ).reshape(per_group, -1)
    shares = lax.psum_scatter(
        local_grad.astype(jnp.bfloat16), "blk", scatter_dimension=1, tiled=True
    )
    matrix_grads = lax.psum(shares, "ctx").astype(jnp.float32)
    new_momenta = momentum_decay * momenta + matrix_grads
    update = matrix_grads + momentum_decay * new_momenta
    per_owner = per_group // cycle_size
    sectioned = update.reshape(cycle_size, per_owner, update.shape[1])
    pieces = lax.all_to_all(
        sectioned.astype(jnp.bfloat16), "blk", split_axis=0, concat_axis=2, tiled=True
    ).astype(sectioned.dtype)
    piece_count = pieces.shape[1]
    settled_blocks = newton_schulz(pieces.reshape(piece_count, MODEL_DIM, HD)).reshape(
        1, piece_count, MODEL_DIM * HD
    )
    settled = lax.all_to_all(
        as_sent(settled_blocks), "blk", split_axis=2, concat_axis=0, tiled=True
    ).astype(settled_blocks.dtype)
    orthogonal_all = settled.reshape(per_group, -1)
    muon_scale = max(1.0, MODEL_DIM / HD) ** 0.5
    new_matrices = matrices - muon_rate * (muon_scale * orthogonal_all + weight_decay * matrices)
    new_first = adam_first * small_first + (1.0 - adam_first) * small_grads
    new_second = adam_second * small_second + (1.0 - adam_second) * small_grads * small_grads
    corrected = new_first / (1.0 - adam_first**STEP)
    spread = jnp.sqrt(new_second / (1.0 - adam_second**STEP))
    new_small = small - small_rate * corrected / (spread + adam_epsilon)
    return (
        block_output,
        input_grad,
        matrix_grads,
        new_matrices,
        new_momenta,
        small_grads,
        new_first,
        new_second,
        new_small,
    )


def native_view(array):
    rows, columns = array.shape
    tiled = array.reshape(rows // 8, 8, columns // 128, 128).transpose(0, 2, 1, 3)
    return tiled.reshape(rows // 8, columns // 16, 128)


def native_back(array):
    groups, rows, _ = array.shape
    return array.reshape(groups, rows // 8, 8, 128).transpose(0, 2, 1, 3).reshape(groups * 8, rows * 16)


def members_of(head):
    if head:
        return lambda piece, j: (j // 2, 4 * (j % 2) + piece)
    return lambda piece, j: (piece // 2, 4 * (piece % 2) + j)


def mem(kind=pltpu.VMEM):
    return pl.BlockSpec(memory_space=kind)


def limits(mebibytes):
    return pltpu.CompilerParams(vmem_limit_bytes=mebibytes << 20)


def low_lanes(rows):
    return lax.broadcasted_iota(jnp.int32, (rows, 128), 1) < HD


def dot(a, b, dims=((1,), (0,)), precision=None):
    return lax.dot_general(
        a, b, (dims, ((), ())), precision=precision, preferred_element_type=jnp.float32
    )


NT = ((1,), (1,))
TN = ((0,), (0,))


def corner(array):
    block = (1,) * (array.ndim - 2) + (min(16, array.shape[-2]), 128)
    return pl.BlockSpec(block, lambda *_: (0,) * array.ndim)


def launch(kernel, operands, out_shapes, name, specs=None, after=(), vmem=20, **more):
    taken = len(operands)
    body = kernel
    if after:
        body = lambda *refs: kernel(*refs[:taken], *refs[taken + len(after) :])
    if specs is None:
        specs = [mem(pltpu.SMEM)] + [mem()] * (taken - 1)
    more.setdefault("grid", (1,))
    return pl.pallas_call(
        body,
        in_specs=list(specs) + [corner(a) for a in after],
        out_shape=out_shapes,
        compiler_params=limits(vmem),
        name=name,
        **more,
    )(*operands, *after)


def relayout_kernel(n, head, src, out, scratch):
    low = low_lanes(n)
    place_of = members_of(head)
    for piece in range(4):
        for half in range(2):
            k = 2 * piece + half
            pair = []
            for j in (2 * half, 2 * half + 1):
                group, line = place_of(piece, j)
                pair.append(src[group, pl.ds(line, n, stride=8), :])
            a, b = pair
            scratch[k, pl.ds(0, n, stride=2), :] = jnp.where(low, a, pltpu.roll(b, 64, 1))
            scratch[k, pl.ds(1, n, stride=2), :] = jnp.where(low, pltpu.roll(a, 64, 1), b)
            out[piece, :, half * 128 : (half + 1) * 128] = scratch[k].astype(out.dtype)


def relayout(array, dtype, first, count, n=64, after=()):
    return launch(
        functools.partial(relayout_kernel, n, first == 0),
        [native_view(array)],
        jax.ShapeDtypeStruct((4 * count, 512, 256), dtype),
        "relayout",
        specs=[pl.BlockSpec((2, 8 * n, 128), lambda k, i: (first + k, i, 0))],
        after=after,
        grid=(count, 256 // n),
        out_specs=pl.BlockSpec((4, 2 * n, 256), lambda k, i: (k, i, 0)),
        scratch_shapes=[pltpu.VMEM((8, 2 * n, 128), jnp.float32)],
    )


def pick_kernel(place, piece, *refs):
    refs[-1][...] = piece[...]


def picked(weights, place, after=()):
    count = weights.shape[0] // 4
    return pl.pallas_call(
        pick_kernel,
        grid_spec=pltpu.PrefetchScalarGridSpec(
            num_scalar_prefetch=1,
            grid=(count,),
            in_specs=[pl.BlockSpec((1, 512, 256), lambda i, s: (4 * i + s[1], 0, 0))]
            + [corner(a) for a in after],
            out_specs=pl.BlockSpec((1, 512, 256), lambda i, s: (i, 0, 0)),
        ),
        out_shape=jax.ShapeDtypeStruct((count, 512, 256), weights.dtype),
        name="pick",
    )(place, weights, *after)


def normalized(x):
    centred = x - jnp.mean(x, axis=-1, keepdims=True)
    spread = jnp.mean(centred * centred, axis=-1, keepdims=True)
    root = lax.rsqrt(spread + norm_epsilon)
    return centred * root, root


def halves(values, first):
    left, right = values[:, :512], values[:, 512:]
    return jnp.where(first, left, right), jnp.where(first, right, left)


def whole(own, other, first):
    return jnp.concatenate([jnp.where(first, own, other), jnp.where(first, other, own)], axis=1)


def norm_back(grad, hat, root, gain):
    scaled = grad * gain
    along = jnp.mean(scaled * hat, axis=-1, keepdims=True)
    return root * (scaled - jnp.mean(scaled, axis=-1, keepdims=True) - hat * along)


def turned(values, cosine, sine):
    lane = lax.broadcasted_iota(jnp.int32, values.shape, 1) % HD
    other = jnp.where(lane < 8, pltpu.roll(values, 120, 1), pltpu.roll(values, 8, 1))
    return values * cosine + other * sine


def project_kernel(scal, x, cot, norms, bias, cosine, sine, own, r0, r1, r2, r3, send):
    first = scal[0] == 0
    hat, _ = normalized(x[...].astype(jnp.float32))
    h = (hat * norms[0:1] + norms[1:2]).astype(jnp.bfloat16)
    h_own, h_other = halves(h, first)
    c_own, c_other = halves(cot[...], first)
    tokens = h.shape[0]
    low = low_lanes(tokens)
    for r, other in enumerate((r0, r1, r2, r3)):
        head = scal[1] ^ r
        mine = own[head]
        theirs = other[...]
        pre = dot(h_own, mine) + dot(h_other, theirs) + bias[pl.ds(head, 1), :]
        back = dot(c_own, mine[:, 128:]) + dot(c_other, theirs[:, 128:])
        left = turned(pre[:, :128], cosine[...], sine[...]).astype(jnp.bfloat16)
        right = jnp.where(low, pre[:, 128:], back).astype(jnp.bfloat16)
        for s in range(2):
            rows = slice(128 * s, 128 * s + 128)
            send[4 * s + head, :, :128] = left[rows]
            send[4 * s + head, :, 128:] = right[rows]


def attention_kernel(rows_ref, seg, out, key_total, value_total):
    key_total[...] = jnp.zeros_like(key_total)
    value_total[...] = jnp.zeros_like(value_total)
    step = 256
    for block in range(rows_ref.shape[0] // step):
        rows = slice(block * step, (block + 1) * step)
        n = (block + 1) * step
        query = rows_ref[rows, 0:HD] * jnp.bfloat16(0.125)
        grad = rows_ref[rows, 3 * HD : 4 * HD]
        keys = rows_ref[0:n, HD : 2 * HD]
        values = rows_ref[0:n, 2 * HD : 3 * HD]
        scores = dot(query, keys, NT)
        query_place = block * step + lax.broadcasted_iota(jnp.int32, (step, n), 0)
        key_place = lax.broadcasted_iota(jnp.int32, (step, n), 1)
        allowed = (key_place <= query_place) & (key_place >= seg[rows, :])
        scores = jnp.where(allowed, scores, masked_score)
        weights = jnp.exp(scores - jnp.max(scores, axis=-1, keepdims=True))
        weights = jnp.where(allowed, weights, 0.0)
        weights = weights * (1.0 / jnp.sum(weights, axis=-1, keepdims=True))
        short = weights.astype(jnp.bfloat16)
        attended = dot(short, values)
        weight_grad = dot(grad, values, NT)
        delta = jnp.sum(weights * weight_grad, axis=-1, keepdims=True)
        score_grad = (weights * (weight_grad - delta)).astype(jnp.bfloat16)
        query_grad = dot(score_grad, keys) * 0.125
        key_total[0:n, :] += dot(score_grad, query, TN)
        value_total[0:n, :] += dot(short, grad, TN)
        out[rows, 0:HD] = query_grad.astype(jnp.bfloat16)
        out[rows, 3 * HD : 4 * HD] = attended.astype(jnp.bfloat16)
    out[:, HD : 2 * HD] = key_total[...].astype(jnp.bfloat16)
    out[:, 2 * HD : 3 * HD] = value_total[...].astype(jnp.bfloat16)


def feed_forward_kernel(
    scal, x, cot, norms, bias, weights, r0, r1, r2, r3,
    branch, input_part, keep, send, hidden_sums, norm_grads, cot_sums,
):
    first = scal[0] == 0
    hat, root = normalized(x[...].astype(jnp.float32))
    h = (hat * norms[2:3] + norms[3:4]).astype(jnp.bfloat16)
    h_own, h_other = halves(h, first)
    c_own, c_other = halves(cot[...], first)
    cot_sums[...] = jnp.sum(cot[...].astype(jnp.float32), axis=0, keepdims=True)
    outs = [0.0] * 4
    for r, other in enumerate((r0, r1, r2, r3)):
        piece = scal[1] ^ r
        in_own, in_other = weights[piece], other[0]
        down_own, down_other = weights[4 + piece], other[1]
        pre = dot(h_own, in_own) + dot(h_other, in_other) + bias[pl.ds(piece, 1), :]
        cumulative = 0.5 * (1.0 + lax.erf(pre * 0.7071067811865476))
        slope = cumulative + pre * (0.3989422804014327 * jnp.exp(-0.5 * pre * pre))
        act = (pre * cumulative).astype(jnp.bfloat16)
        act_grad = dot(c_own, down_own) + dot(c_other, down_other)
        grad = (act_grad * slope).astype(jnp.bfloat16)
        hidden_sums[pl.ds(piece, 1), :] = jnp.sum(
            grad.astype(jnp.float32), axis=0, keepdims=True
        )
        outs[0] += dot(act, down_own, NT)
        outs[1] += dot(act, down_other, NT)
        outs[2] += dot(grad, in_own, NT)
        outs[3] += dot(grad, in_other, NT)
        target = send if r % 2 else keep
        target[r // 2, 0] = grad
        target[r // 2, 1] = act
    branch[...] = whole(outs[0], outs[1], first)
    second = whole(outs[2], outs[3], first)
    norm_grads[0:1] = jnp.sum(second * hat, axis=0, keepdims=True)
    norm_grads[1:2] = jnp.sum(second, axis=0, keepdims=True)
    input_part[...] = norm_back(second, hat, root, norms[2:3])


def both_cores(scal, x, x_beside, cot, cot_beside, norms, at):
    first = scal[0] == 0
    tokens = jnp.concatenate([x[...], x_beside[...]], axis=0).astype(jnp.float32)
    hat, _ = normalized(tokens)
    h = (hat * norms[at : at + 1] + norms[at + 1 : at + 2]).astype(jnp.bfloat16)
    c = jnp.concatenate([cot[...], cot_beside[...]], axis=0)
    return list(zip(halves(h, first), halves(c, first)))


def unit_grads_kernel(scal, x, x_beside, cot, cot_beside, norms, keep, came, *outs):
    for side, (h, c) in enumerate(both_cores(scal, x, x_beside, cot, cot_beside, norms, 2)):
        for far in range(2):
            grad = jnp.concatenate([keep[far, 0], came[far, 0]], axis=0)
            act = jnp.concatenate([keep[far, 1], came[far, 1]], axis=0)
            outs[2 * far + side][0] = dot(h, grad, TN).astype(jnp.bfloat16)
            outs[2 * far + side][1] = dot(c, act, TN).astype(jnp.bfloat16)


def turn_kernel(scal, cosine, sine, back, keep, send, sums):
    low = low_lanes(keep.shape[1])
    for r in range(4):
        head = scal[1] ^ r
        grads = jnp.concatenate([back[head], back[4 + head]], axis=0)
        left = turned(grads[:, :128].astype(jnp.float32), cosine[...], -sine[...])
        left = left.astype(jnp.bfloat16)
        right = grads[:, 128:]
        target = send if r % 2 else keep
        target[r // 2, :, :128] = left
        target[r // 2, :, 128:] = right
        right = jnp.where(low, right.astype(jnp.float32), 0.0)
        wide = jnp.concatenate([left.astype(jnp.float32), right], axis=1)
        sums[pl.ds(head, 1), :] = jnp.sum(wide, axis=0, keepdims=True)


def split_last(piece):
    wide = piece.astype(jnp.float32)
    lane = lax.broadcasted_iota(jnp.int32, (1, wide.shape[1]), 1)
    share = (lane < 3 * HD).astype(jnp.float32)
    pre_grad = (wide * share).astype(jnp.bfloat16)
    attended = (wide * (1.0 - share)).astype(jnp.bfloat16)
    return pre_grad, attended


def head_grads_kernel(scal, x, x_beside, cot, cot_beside, norms, keep, came, *outs):
    sides = both_cores(scal, x, x_beside, cot, cot_beside, norms, 0)
    for far in range(2):
        piece = jnp.concatenate([keep[far], came[far]], axis=0)
        pre_grad, attended = split_last(piece)
        for side, (h, c) in enumerate(sides):
            grad = dot(h, pre_grad, TN) + dot(c, attended, TN)
            outs[2 * far + side][0] = grad.astype(jnp.bfloat16)


def gather_kernel(
    scal, x, norms, keep, send, weights, r0, r1, r2, r3, ff_branch, ff_part,
    near, far, norm_grads, parts,
):
    first = scal[0] == 0
    hat, root = normalized(x[...].astype(jnp.float32))
    outs = [0.0] * 4
    for r, other in enumerate((r0, r1, r2, r3)):
        mine, theirs = weights[scal[1] ^ r], other[0]
        pre_grad, attended = split_last((send if r % 2 else keep)[r // 2])
        outs[0] += dot(attended, mine, NT)
        outs[1] += dot(attended, theirs, NT)
        outs[2] += dot(pre_grad, mine, NT)
        outs[3] += dot(pre_grad, theirs, NT)
    branch = ff_branch[...] + whole(outs[0], outs[1], first)
    grad = whole(outs[2], outs[3], first)
    norm_grads[0:1] = jnp.sum(grad * hat, axis=0, keepdims=True)
    norm_grads[1:2] = jnp.sum(grad, axis=0, keepdims=True)
    input_part = ff_part[...] + norm_back(grad, hat, root, norms[0:1])
    for q in range(4):
        parts[q, 0] = branch[64 * q : 64 * q + 64].astype(jnp.bfloat16)
        parts[q, 1] = input_part[64 * q : 64 * q + 64].astype(jnp.bfloat16)
    for r in range(4):
        (far if r % 2 else near)[r // 2] = parts[scal[2] ^ r]


def finish_rows_kernel(scal, x, cot, bias, r0, r1, r2, r3, block_output, input_grad):
    for r, piece in enumerate((r0, r1, r2, r3)):
        q = scal[2] ^ r
        block_output[q] = x[q].astype(jnp.float32) + piece[0].astype(jnp.float32) + bias[...]
        input_grad[q] = cot[q].astype(jnp.float32) + piece[1].astype(jnp.float32)


def gram_kernel(place, own, a, b, c, momenta, *refs):
    grads, grams = refs[-2:]
    total = own[...].astype(jnp.float32) + a[...].astype(jnp.float32)
    total = total + b[...].astype(jnp.float32) + c[...].astype(jnp.float32)
    short = total.astype(jnp.bfloat16)
    grads[...] = short
    update = 1.95 * short[0].astype(jnp.float32) + 0.9025 * momenta[0]
    gram = dot(update, update, TN, lax.Precision.HIGHEST)
    for j in range(4):
        cut = slice(j * HD, (j + 1) * HD)
        grams[0, j] = gram[cut, cut]


def gram_of(own, a, b, c, momenta, place, after=()):
    chunks = own.shape[0]
    piece = pl.BlockSpec((1, 512, 256), lambda i, s: (i, 0, 0))
    return pl.pallas_call(
        gram_kernel,
        grid_spec=pltpu.PrefetchScalarGridSpec(
            num_scalar_prefetch=1,
            grid=(chunks,),
            in_specs=[piece] * 4
            + [pl.BlockSpec((1, 512, 256), lambda i, s: (4 * i + s[1], 0, 0))]
            + [corner(a) for a in after],
            out_specs=[piece, pl.BlockSpec((1, 4, HD, HD), lambda i, s: (i, 0, 0, 0))],
        ),
        out_shape=[
            jax.ShapeDtypeStruct((chunks, 512, 256), jnp.bfloat16),
            jax.ShapeDtypeStruct((chunks, 4, HD, HD), jnp.float32),
        ],
        compiler_params=limits(20),
        name="gram",
    )(place, own, a, b, c, momenta, *after)


def newton_kernel(mine, theirs, out):
    linear, square, cubic = quintic
    shape = (HD, HD)
    eye = lax.broadcasted_iota(jnp.int32, shape, 0) == lax.broadcasted_iota(jnp.int32, shape, 1)
    full = lax.Precision.HIGHEST
    chunks = mine.shape[0]
    places = [(i, j) for i in range(chunks) for j in range(4)]
    states = []
    for i, j in places:
        gram = mine[i, j] + theirs[i, j]
        trace = jnp.sum(jnp.where(eye, gram, 0.0), axis=(0, 1), keepdims=True)
        scale = 1.0 / (jnp.sqrt(trace) + muon_epsilon)
        states.append([gram * scale * scale, None, scale])
    for iteration in range(NEWTON):
        squares = [dot(s[0], s[0], precision=full) for s in states]
        steps = [
            jnp.where(eye, linear, 0.0) + square * s[0] + cubic * sq
            for s, sq in zip(states, squares)
        ]
        if iteration == 0:
            halfway = [dot(s[0], m, precision=full) for s, m in zip(states, steps)]
            for s, m in zip(states, steps):
                s[1] = m
        elif iteration < NEWTON - 1:
            both = [
                dot(jnp.concatenate([s[0], s[1]], axis=0), m, precision=full)
                for s, m in zip(states, steps)
            ]
            halfway = [x[:HD] for x in both]
            for s, x in zip(states, both):
                s[1] = x[HD:]
        else:
            for s, m in zip(states, steps):
                s[1] = dot(s[1], m, precision=full)
        if iteration < NEWTON - 1:
            for s, x, m in zip(states, halfway, steps):
                s[0] = dot(x, m, precision=full)
    for (i, j), s in zip(places, states):
        mix = s[1] * s[2]
        coarse = mix.astype(jnp.bfloat16)
        fine = (mix - coarse.astype(jnp.float32)).astype(jnp.bfloat16)
        out[i, j] = jnp.concatenate([coarse, fine], axis=1)


def newton(mine, theirs, after=()):
    return launch(
        newton_kernel,
        [mine, theirs],
        jax.ShapeDtypeStruct((*mine.shape[:-1], 2 * HD), jnp.bfloat16),
        "newton",
        specs=[mem()] * 2,
        after=after,
        out_specs=mem(),
    )


def update_kernel(
    n, head, scal, g0, g1, g2, g3, q0, q1, q2, q3, momenta, native_momenta, native, *refs
):
    grads, weights, moved, mixing, first, second, steps = refs[-7:]
    place_of = members_of(head)

    @pl.when((pl.program_id(0) == 0) & (pl.program_id(1) == 0))
    def _():
        mixing[...] = jnp.zeros_like(mixing)

    @pl.when(pl.program_id(1) == 0)
    def _():
        for r, q in enumerate((q0, q1, q2, q3)):
            for j in range(4):
                wide = q[0, j].astype(jnp.float32)
                other = pltpu.roll(wide, HD, 1)
                below = low_lanes(HD) == (j % 2 == 0)
                rows = slice(j * HD, (j + 1) * HD)
                lanes = slice(128 * (j // 2), 128 * (j // 2) + 128)
                pair = (wide, other) if j % 2 == 0 else (other, wide)
                for level in range(2):
                    part = jnp.where(below, pair[level], 0.0)
                    mixing[r, level, rows, lanes] = part.astype(jnp.bfloat16)

    low = low_lanes(n)
    for r, piece in enumerate((g0, g1, g2, g3)):
        place = scal[1] ^ r
        grad = piece[0].astype(jnp.float32)
        update = 1.95 * grad + 0.9025 * momenta[place]
        coarse = update.astype(jnp.bfloat16)
        fine = (update - coarse.astype(jnp.float32)).astype(jnp.bfloat16)
        settled = dot(coarse, mixing[r, 0]) + dot(coarse, mixing[r, 1]) + dot(fine, mixing[r, 0])
        for half in range(2):
            k = 2 * r + half
            first[k] = grad[:, half * 128 : (half + 1) * 128]
            second[k] = settled[:, half * 128 : (half + 1) * 128]
            for source, target in ((first, grads), (second, steps)):
                even = source[k, pl.ds(0, n, stride=2), :]
                odd = source[k, pl.ds(1, n, stride=2), :]
                lines = (
                    jnp.where(low, even, pltpu.roll(odd, 64, 1)),
                    jnp.where(low, pltpu.roll(even, 64, 1), odd),
                )
                for w in range(2):
                    group, line = place_of(place, 2 * half + w)
                    target[group, pl.ds(line, n, stride=8), :] = lines[w]
    moved[...] = momentum_decay * native_momenta[...] + grads[...]
    weight = native[...]
    weights[...] = weight - muon_rate * (4.0 * steps[...] + weight_decay * weight)


def update(first, scal, grads, mixes, momenta, native_momenta, native, before=(), after=(), n=64):
    chunks = grads[0].shape[0]
    block = pl.BlockSpec((2, 8 * n, 128), lambda k, i: (first + k, i, 0))
    piece = pl.BlockSpec((1, 2 * n, 256), lambda k, i: (k, i, 0))
    mix = pl.BlockSpec((1, 4, HD, 2 * HD), lambda k, i: (k, 0, 0, 0))
    return launch(
        functools.partial(update_kernel, n, first == 0),
        [scal, *grads, *mixes, momenta, native_view(native_momenta), native_view(native), *before],
        [jax.ShapeDtypeStruct((6, 2048, 128), jnp.float32)] * 3,
        "update",
        specs=[mem(pltpu.SMEM)]
        + [piece] * 4
        + [mix] * 4
        + [pl.BlockSpec((4, 2 * n, 256), lambda k, i: (k, i, 0)), block, block]
        + [mem(pl.ANY)] * len(before),
        after=after,
        vmem=32,
        grid=(chunks, 256 // n),
        out_specs=[block] * 3,
        scratch_shapes=[
            pltpu.VMEM((4, 2, 256, 256), jnp.bfloat16),
            pltpu.VMEM((8, 2 * n, 128), jnp.float32),
            pltpu.VMEM((8, 2 * n, 128), jnp.float32),
            pltpu.VMEM((2, 8 * n, 128), jnp.float32),
        ],
        input_output_aliases={12 + i: i for i in range(len(before))},
    )


def whole_device(
    inputs, cotangent, matrices, momenta, small, small_first, small_second, segments, positions
):
    blk_at = lax.axis_index("blk")
    ctx_at = lax.axis_index("ctx")
    tp_at = lax.axis_index("tp")
    scal = jnp.stack([blk_at, ctx_at, tp_at]).astype(jnp.int32)
    sequences, local_rows, width = inputs.shape
    tokens = sequences * local_rows
    both = ("blk", "ctx")
    f32, bf16 = jnp.float32, jnp.bfloat16
    shaped = jax.ShapeDtypeStruct

    def hop(values, by):
        return lax.ppermute(values, both, [(i, i ^ by) for i in range(8)])

    def hop_tp(values, by):
        return lax.ppermute(values, "tp", [(i, i ^ by) for i in range(4)])

    def spread(piece):
        c = hop(piece, 2)
        return [piece, hop(piece, 1), c, hop(c, 1)]

    x = inputs.reshape(tokens, width)
    cot = cotangent.reshape(tokens, width)
    norms = small[: 4 * width].reshape(4, width)
    qkv_start = 6 * width + tp_at * 4 * 3 * HD
    qkv_bias = lax.dynamic_slice_in_dim(small, qkv_start, 4 * 3 * HD).reshape(4, 3 * HD)
    qkv_bias = jnp.pad(qkv_bias, ((0, 0), (0, HD)))
    unit_start = 6 * width + H * 3 * HD + tp_at * 1024
    unit_bias = lax.dynamic_slice_in_dim(small, unit_start, 1024).reshape(4, 256)
    lane = jnp.arange(128) % HD
    frequency = rope_base ** (-2.0 * (lane % 8).astype(f32) / ROTARY)
    angles = positions.astype(f32).reshape(tokens, 1) * frequency
    cosine = jnp.where(lane < ROTARY, jnp.cos(angles), 1.0)
    sign = jnp.where(lane < 8, -1.0, jnp.where(lane < ROTARY, 1.0, 0.0))
    sine = jnp.sin(angles) * sign

    head_weights = relayout(matrices, bf16, 0, 1)
    first_hop = hop(picked(head_weights, scal), 4)
    other_heads = spread(first_hop)
    unit_weights = relayout(matrices, bf16, 1, 2)
    other_units = spread(hop(picked(unit_weights, scal, after=(first_hop, cosine, sine)), 4))
    x_beside = hop(x, 1)
    cot_beside = hop(cot, 1)

    send = launch(
        project_kernel,
        [scal, x, cot, norms, qkv_bias, cosine, sine, head_weights]
        + [piece[0] for piece in other_heads],
        shaped((8, local_rows, 256), bf16),
        "project",
        out_specs=mem(),
    )
    arrived = lax.all_to_all(send, both, split_axis=0, concat_axis=0, tiled=True)
    piled_heads = relayout(momenta, f32, 0, 1, after=(send,))
    piled_units = relayout(momenta, f32, 1, 2, after=(send,))
    documents = lax.dynamic_index_in_dim(segments, blk_at, 0, keepdims=False)
    length = documents.shape[0]
    attended = launch(
        attention_kernel,
        [arrived.reshape(length, 256), documents.reshape(length, 1)],
        shaped((length, 256), bf16),
        "attention",
        specs=[mem()] * 2,
        after=(piled_units,),
        vmem=32,
        out_specs=mem(),
        scratch_shapes=[pltpu.VMEM((length, HD), f32)] * 2,
    )
    back = lax.all_to_all(
        attended.reshape(8, local_rows, 256), both, split_axis=0, concat_axis=0, tiled=True
    )

    ff_branch, ff_part, unit_keep, unit_send, unit_sums, norm_two, cot_sums = launch(
        feed_forward_kernel,
        [scal, x, cot, norms, unit_bias, unit_weights, *other_units],
        [
            shaped((tokens, width), f32),
            shaped((tokens, width), f32),
            shaped((2, 2, tokens, 256), bf16),
            shaped((2, 2, tokens, 256), bf16),
            shaped((4, 256), f32),
            shaped((2, width), f32),
            shaped((1, width), f32),
        ],
        "feed_forward",
        after=(attended,),
        out_specs=[mem()] * 7,
    )
    unit_grads = launch(
        unit_grads_kernel,
        [scal, x, x_beside, cot, cot_beside, norms, unit_keep, hop(unit_send, 1)],
        [shaped((2, 512, 256), bf16)] * 4,
        "unit_grads",
        out_specs=[mem()] * 4,
    )
    head_keep, head_send, qkv_sums = launch(
        turn_kernel,
        [scal, cosine, sine, back],
        [shaped((2, tokens, 256), bf16)] * 2 + [shaped((4, 256), f32)],
        "turn",
        after=(unit_grads[0],),
        out_specs=[mem()] * 3,
    )
    near, far, norm_one = launch(
        gather_kernel,
        [scal, x, norms, head_keep, head_send, head_weights, *other_heads, ff_branch, ff_part],
        [
            shaped((2, 2, 64, width), bf16),
            shaped((2, 2, 64, width), bf16),
            shaped((2, width), f32),
        ],
        "gather",
        out_specs=[mem()] * 3,
        scratch_shapes=[pltpu.VMEM((4, 2, 64, width), bf16)],
    )
    head_grads = launch(
        head_grads_kernel,
        [scal, x, x_beside, cot, cot_beside, norms, head_keep, hop(head_send, 1)],
        [shaped((1, 512, 256), bf16)] * 4,
        "head_grads",
        after=(norm_one,),
        out_specs=[mem()] * 4,
    )

    def reduced(grads):
        return grads[0], hop(grads[1], 4), hop(grads[2], 2), hop(grads[3], 6)

    unit_sum, unit_grams = gram_of(*reduced(unit_grads), piled_units, scal, after=(head_grads[0],))
    unit_pieces = spread(unit_sum)
    unit_mixes = spread(newton(unit_grams, hop(unit_grams, 4)))
    before = update(1, scal, unit_pieces, unit_mixes, piled_units, momenta, matrices)
    head_sum, head_grams = gram_of(*reduced(head_grads), piled_heads, scal)
    head_pieces = spread(head_sum)
    head_mixes = spread(newton(head_grams, hop(head_grams, 4), after=(before[0],)))
    outs = update(0, scal, head_pieces, head_mixes, piled_heads, momenta, matrices, before)

    summed = (near.astype(f32) + hop_tp(far, 1).astype(f32)).astype(bf16)
    total = (summed[0].astype(f32) + hop_tp(summed[1], 2).astype(f32)).astype(bf16)
    beside = hop_tp(total, 2)
    block_output, input_grad = launch(
        finish_rows_kernel,
        [
            scal,
            x.reshape(4, 64, width),
            cot.reshape(4, 64, width),
            (small[4 * width : 5 * width] + small[5 * width : 6 * width]).reshape(1, width),
            total,
            hop_tp(total, 1),
            beside,
            hop_tp(beside, 1),
        ],
        [shaped((4, 64, width), f32)] * 2,
        "finish_rows",
        out_specs=[mem()] * 2,
    )

    local = jnp.concatenate(
        [
            norm_one.reshape(-1),
            norm_two.reshape(-1),
            cot_sums[0],
            qkv_sums[:, : 3 * HD].reshape(-1),
            unit_sums.reshape(-1),
        ]
    )
    parts = lax.all_gather(local, ("tp", "blk", "ctx")).reshape(4, 8, -1).sum(axis=1)
    shared = parts[:, : 4 * width].sum(axis=0)
    cot_total = parts[0, 4 * width : 5 * width]
    small_grads = jnp.concatenate(
        [
            shared,
            cot_total,
            cot_total,
            parts[:, 5 * width : 5 * width + 12 * HD].reshape(-1),
            parts[:, 5 * width + 12 * HD :].reshape(-1),
        ]
    )
    return (
        block_output.reshape(inputs.shape),
        input_grad.reshape(inputs.shape),
        native_back(outs[0]),
        native_back(outs[1]),
        native_back(outs[2]),
        small_grads,
        *small_step(small, small_first, small_second, small_grads),
    )


def small_step(small, small_first, small_second, small_grads):
    new_first = adam_first * small_first + (1.0 - adam_first) * small_grads
    new_second = adam_second * small_second + (1.0 - adam_second) * small_grads * small_grads
    corrected = new_first / (1.0 - adam_first**STEP)
    spread = jnp.sqrt(new_second / (1.0 - adam_second**STEP))
    new_small = small - small_rate * corrected / (spread + adam_epsilon)
    return new_first, new_second, new_small


def solution(mesh):
    in_specs = (
        P(None, ("blk", "ctx"), None),
        P(None, ("blk", "ctx"), None),
        P("tp", "blk"),
        P("tp", "blk"),
        P(),
        P(),
        P(),
        P(),
        P(None, ("blk", "ctx")),
    )
    out_specs = (
        P(None, ("blk", "ctx"), None),
        P(None, ("blk", "ctx"), None),
        P("tp", "blk"),
        P("tp", "blk"),
        P("tp", "blk"),
        P(),
        P(),
        P(),
        P(),
    )
    one_each = mesh.shape["blk"] == SEQS and mesh.shape["ctx"] * mesh.shape["tp"] == H
    one_each = one_each and mesh.shape["tp"] == 4
    return jax.shard_map(
        whole_device if one_each else on_device, mesh=mesh, in_specs=in_specs, out_specs=out_specs, check_vma=False
    )
```

```python
import functools

import jax
import jax.numpy as jnp
from jax import lax
from jax.experimental import pallas as pl
from jax.experimental.pallas import tpu as pltpu
from jax.sharding import PartitionSpec as P

MODEL_DIM = 1024
H = 16
HD = 64
FF = 4096
ROTARY = 16
NEWTON = 5
STEP = 10
SEQS = 2


norm_epsilon = 1e-05
rope_base = 10000.0
masked_score = -1e30
momentum_decay = 0.95
muon_rate = 0.2
weight_decay = 0.01
muon_epsilon = 1e-07
quintic = (3.4445, -4.775, 2.0315)
adam_first = 0.9
adam_second = 0.95
adam_epsilon = 1e-08
small_rate = 0.2


def passed_along(x, axis, by):
    devices = lax.axis_size(axis)
    pairs = [(i, i + by) for i in range(devices) if 0 <= i + by < devices]
    return lax.ppermute(x, axis, pairs)


def shifted(x, axis, by):
    devices = lax.axis_size(axis)
    return lax.ppermute(x, axis, [(i, (i + by) % devices) for i in range(devices)])


def as_sent(x):

    def short(part):
        return part.astype(jnp.bfloat16) if part.dtype == jnp.float32 else part

    return jax.tree.map(short, x)


def layer_norm(values, scaling, offset):
    centre = jnp.mean(values, axis=-1, keepdims=True)
    centred = values - centre
    spread = jnp.mean(centred * centred, axis=-1, keepdims=True)
    return centred * lax.rsqrt(spread + norm_epsilon) * scaling + offset


def rope_tables(positions):
    halfway = ROTARY // 2
    frequency = rope_base ** (-2.0 * jnp.arange(halfway, dtype=jnp.float32) / ROTARY)
    angles = positions.astype(jnp.float32)[..., None] * frequency
    return (jnp.cos(angles)[:, :, None, :], jnp.sin(angles)[:, :, None, :])


def rotate(values, cosine, sine):
    halfway = ROTARY // 2
    former = values[..., :halfway]
    latter = values[..., halfway:ROTARY]
    return jnp.concatenate(
        [former * cosine - latter * sine, latter * cosine + former * sine, values[..., ROTARY:]],
        axis=-1,
    )


def exact_gelu(values):
    return jax.nn.gelu(values, approximate=False)


def newton_schulz(blocks):
    frobenius = jnp.sqrt(jnp.sum(blocks * blocks, axis=(1, 2), keepdims=True))
    current = blocks / (frobenius + muon_epsilon)
    linear_term, square_term, cubic_term = quintic
    for iteration in range(NEWTON):
        gram_matrix = jnp.einsum("mde,mdf->mef", current, current, precision=lax.Precision.HIGHEST)
        polynomial = square_term * gram_matrix + cubic_term * jnp.einsum(
            "mef,mfg->meg", gram_matrix, gram_matrix, precision=lax.Precision.HIGHEST
        )
        current = linear_term * current + jnp.einsum(
            "mde,mef->mdf", current, polynomial, precision=lax.Precision.HIGHEST
        )
    return current


def to_heads(values):
    return lax.all_to_all(values, "ctx", split_axis=3, concat_axis=1, tiled=True)


def to_positions(values):
    return lax.all_to_all(values, "ctx", split_axis=1, concat_axis=3, tiled=True)


def pass_keys(pair):
    return passed_along(pair, "blk", 1)


def pass_grads(pair_grad):
    return shifted(pair_grad.astype(jnp.bfloat16), "blk", 1).astype(pair_grad.dtype)


def allowed_pairs(segments, query_block, key_block, block_rows):
    query_place = query_block * block_rows + jnp.arange(block_rows, dtype=jnp.int32)
    key_place = key_block * block_rows + jnp.arange(block_rows, dtype=jnp.int32)
    query_doc = lax.dynamic_slice_in_dim(segments, query_block * block_rows, block_rows, 1)
    key_doc = lax.dynamic_slice_in_dim(segments, key_block * block_rows, block_rows, 1)
    causal = key_place[None, :] <= query_place[:, None]
    return (causal[None] & (query_doc[:, :, None] == key_doc[:, None, :]))[:, None]


def masked_scores(queries, keys, allowed):
    score_scale = HD ** (-0.5)
    scores = (
        jnp.einsum("sqhe,skhe->shqk", queries, keys, preferred_element_type=jnp.float32)
        * score_scale
    )
    return jnp.where(allowed, scores, masked_score)


def on_device(
    inputs, cotangent, matrices, momenta, small, small_first, small_second, segments, positions
):
    tensor_size = lax.axis_size("tp")
    cycle_size = lax.axis_size("blk")
    context_size = lax.axis_size("ctx")
    tensor_index = lax.axis_index("tp")
    cycle_index = lax.axis_index("blk")
    sequences, local_rows, model_width = inputs.shape
    per_group = matrices.shape[0]
    head_count = H // tensor_size
    unit_blocks = FF // HD // tensor_size
    block_rows = local_rows * context_size
    gathered = lax.all_gather(matrices.astype(jnp.bfloat16), "blk", axis=1, tiled=True).reshape(
        per_group, model_width, HD
    )
    query_key_value_weight = gathered[: 3 * head_count]
    projection_out_weight = gathered[3 * head_count : 4 * head_count]
    input_weight = gathered[4 * head_count : 4 * head_count + unit_blocks]
    down_projection_weight = gathered[4 * head_count + unit_blocks :]
    qkv_start = 6 * model_width + tensor_index * head_count * 3 * HD
    query_key_value_bias = lax.dynamic_slice_in_dim(small, qkv_start, head_count * 3 * HD).reshape(
        head_count, 3, HD
    )
    unit_start = 6 * model_width + H * 3 * HD + tensor_index * unit_blocks * HD
    hidden_unit_bias = lax.dynamic_slice_in_dim(small, unit_start, unit_blocks * HD).reshape(
        unit_blocks, HD
    )
    residual = inputs.astype(jnp.float32)

    def both_norms(values, gain_one, offset_one, gain_two, offset_two):
        return (layer_norm(values, gain_one, offset_one), layer_norm(values, gain_two, offset_two))

    (normed_one, normed_two), norm_back = jax.vjp(
        both_norms,
        residual,
        small[0:model_width],
        small[model_width : 2 * model_width],
        small[2 * model_width : 3 * model_width],
        small[3 * model_width : 4 * model_width],
    )
    first_input = normed_one.astype(jnp.bfloat16)
    second_input = normed_two.astype(jnp.bfloat16)
    projected = jnp.einsum(
        "pgk,jka->pgja", first_input, query_key_value_weight, preferred_element_type=jnp.float32
    )
    projected = projected.reshape(sequences, local_rows, 3, head_count, HD) + jnp.transpose(
        query_key_value_bias, (1, 0, 2)
    )
    cosine, sine = rope_tables(positions)

    def turn_pair(query_pre, key_pre):
        return (rotate(query_pre, cosine, sine), rotate(key_pre, cosine, sine))

    (query_turned, key_turned), turn_back = jax.vjp(
        turn_pair, projected[:, :, 0], projected[:, :, 1]
    )
    stacked = jnp.stack([query_turned, key_turned, projected[:, :, 2]], axis=2).astype(jnp.bfloat16)
    by_heads = to_heads(stacked)
    queries = by_heads[:, :, 0]
    head_local = queries.shape[2]

    def forward_visit(state, pair, source):
        row_max, row_total, weighted = state
        allowed = allowed_pairs(segments, cycle_index, source, block_rows)
        scores = masked_scores(queries, pair[:, :, 0], allowed)
        new_max = jnp.maximum(row_max, jnp.max(scores, axis=-1))
        weights = jnp.where(allowed, jnp.exp(scores - new_max[..., None]), 0.0)
        rescale = jnp.exp(row_max - new_max)
        row_total = row_total * rescale + jnp.sum(weights, axis=-1)
        weighted = weighted * rescale[..., None] + jnp.einsum(
            "shqk,skhe->shqe",
            weights.astype(jnp.bfloat16),
            pair[:, :, 1],
            preferred_element_type=jnp.float32,
        )
        return (new_max, row_total, weighted)

    def forward_hop(hop_index, carry):
        pair, state = carry
        source = (cycle_index - hop_index) % cycle_size
        state = forward_visit(state, pair, source)
        return (pass_keys(pair), state)

    start_state = (
        jnp.full((sequences, head_local, block_rows), masked_score, jnp.float32),
        jnp.zeros((sequences, head_local, block_rows), jnp.float32),
        jnp.zeros((sequences, head_local, block_rows, HD), jnp.float32),
    )
    pair, state = lax.fori_loop(0, cycle_size - 1, forward_hop, (by_heads[:, :, 1:], start_state))
    row_max, row_total, weighted = forward_visit(state, pair, (cycle_index + 1) % cycle_size)
    log_total = row_max + jnp.log(row_total)
    attended_rows = jnp.transpose(weighted / row_total[..., None], (0, 2, 1, 3))
    attention_result = to_positions(attended_rows.astype(jnp.bfloat16)[:, :, None])[:, :, 0]
    attention_branch = jnp.einsum(
        "roxu,xcu->roc", attention_result, projection_out_weight, preferred_element_type=jnp.float32
    )
    hidden_preactivation = (
        jnp.einsum("ptr,kra->ptka", second_input, input_weight, preferred_element_type=jnp.float32)
        + hidden_unit_bias
    )
    activated_hidden, gelu_back = jax.vjp(exact_gelu, hidden_preactivation)
    activated_reduced = activated_hidden.astype(jnp.bfloat16)
    perceptron_branch = jnp.einsum(
        "xkzp,zop->xko",
        activated_reduced,
        down_projection_weight,
        preferred_element_type=jnp.float32,
    )
    branches = lax.psum((attention_branch + perceptron_branch).astype(jnp.bfloat16), "tp").astype(
        jnp.float32
    )
    block_output = (
        residual
        + branches
        + small[4 * model_width : 5 * model_width]
        + small[5 * model_width : 6 * model_width]
    )
    act_grad = jnp.einsum(
        "ptr,kra->ptka", cotangent, down_projection_weight, preferred_element_type=jnp.float32
    )
    hidden_gradient = gelu_back(act_grad)[0].astype(jnp.bfloat16)
    down_grad = jnp.einsum(
        "gup,guzb->zpb", cotangent, activated_reduced, preferred_element_type=jnp.float32
    )
    in_grad = jnp.einsum(
        "gup,guzb->zpb", second_input, hidden_gradient, preferred_element_type=jnp.float32
    )
    second_grad = jnp.einsum(
        "xkzp,zop->xko", hidden_gradient, input_weight, preferred_element_type=jnp.float32
    )
    attended_grad = jnp.einsum(
        "pgk,jka->pgja", cotangent, projection_out_weight, preferred_element_type=jnp.float32
    ).astype(jnp.bfloat16)
    outproj_grad = jnp.einsum(
        "ztu,ztqi->qui", cotangent, attention_result, preferred_element_type=jnp.float32
    )
    grad_heads = to_heads(attended_grad[:, :, None])[:, :, 0]
    row_delta = jnp.transpose(
        jnp.sum(grad_heads.astype(jnp.float32) * attended_rows, axis=-1), (0, 2, 1)
    )

    def backward_visit(query_grad, pair, source):
        allowed = allowed_pairs(segments, cycle_index, source, block_rows)
        scores = masked_scores(queries, pair[:, :, 0], allowed)
        probabilities = jnp.where(allowed, jnp.exp(scores - log_total[..., None]), 0.0)
        value_grad = jnp.einsum(
            "shqk,sqhe->skhe",
            probabilities.astype(jnp.bfloat16),
            grad_heads,
            preferred_element_type=jnp.float32,
        )
        prob_grad = jnp.einsum(
            "sqhe,skhe->shqk", grad_heads, pair[:, :, 1], preferred_element_type=jnp.float32
        )
        score_grad = (probabilities * (prob_grad - row_delta[..., None])).astype(jnp.bfloat16)
        score_scale = HD ** (-0.5)
        query_grad = (
            query_grad
            + jnp.einsum(
                "shqk,skhe->sqhe", score_grad, pair[:, :, 0], preferred_element_type=jnp.float32
            )
            * score_scale
        )
        key_grad = (
            jnp.einsum("shqk,sqhe->skhe", score_grad, queries, preferred_element_type=jnp.float32)
            * score_scale
        )
        return (query_grad, jnp.stack([key_grad, value_grad], axis=2))

    def backward_hop(hop_index, carry):
        pair, pair_grad, query_grad = carry
        source = (cycle_index - hop_index) % cycle_size
        query_grad, visit_grad = backward_visit(query_grad, pair, source)
        return (pass_keys(pair), pass_grads(pair_grad + visit_grad), query_grad)

    zero_pair = jnp.zeros(by_heads[:, :, 1:].shape, jnp.float32)
    pair, pair_grad, query_grad = lax.fori_loop(
        0,
        cycle_size - 1,
        backward_hop,
        (by_heads[:, :, 1:], zero_pair, jnp.zeros(queries.shape, jnp.float32)),
    )
    query_grad, visit_grad = backward_visit(query_grad, pair, (cycle_index + 1) % cycle_size)
    pair_grad = pass_grads(pair_grad + visit_grad)
    head_grads = jnp.concatenate([query_grad[:, :, None], pair_grad], axis=2).astype(jnp.bfloat16)
    position_grads = to_positions(head_grads).astype(jnp.float32)
    query_pre_grad, key_pre_grad = turn_back((position_grads[:, :, 0], position_grads[:, :, 1]))
    projected_grad = jnp.stack(
        [query_pre_grad, key_pre_grad, position_grads[:, :, 2]], axis=2
    ).astype(jnp.bfloat16)
    flattened_gradient = projected_grad.reshape(sequences, local_rows, 3 * head_count, HD)
    query_key_value_gradient = jnp.einsum(
        "ztu,ztqi->qui", first_input, flattened_gradient, preferred_element_type=jnp.float32
    )
    first_grad = jnp.einsum(
        "roxu,xcu->roc",
        flattened_gradient,
        query_key_value_weight,
        preferred_element_type=jnp.float32,
    )
    input_part, gain_one_grad, offset_one_grad, gain_two_grad, offset_two_grad = norm_back(
        (first_grad, second_grad)
    )
    input_grad = cotangent.astype(jnp.float32) + lax.psum(
        input_part.astype(jnp.bfloat16), "tp"
    ).astype(jnp.float32)
    owner_share = jnp.where(tensor_index == 0, 1.0, 0.0).astype(jnp.float32)
    bias_grad = jnp.sum(cotangent.astype(jnp.float32), axis=(0, 1)) * owner_share
    qkv_bias_grad = jnp.transpose(
        jnp.sum(projected_grad.astype(jnp.float32), axis=(0, 1)), (1, 0, 2)
    ).reshape(-1)
    unit_bias_grad = jnp.sum(hidden_gradient.astype(jnp.float32), axis=(0, 1)).reshape(-1)
    local_small = jnp.concatenate(
        [
            gain_one_grad,
            offset_one_grad,
            gain_two_grad,
            offset_two_grad,
            bias_grad,
            bias_grad,
            jnp.zeros((small.shape[0] - 6 * model_width,), jnp.float32),
        ]
    )
    local_small = lax.dynamic_update_slice_in_dim(local_small, qkv_bias_grad, qkv_start, 0)
    local_small = lax.dynamic_update_slice_in_dim(local_small, unit_bias_grad, unit_start, 0)
    small_grads = lax.psum(local_small, ("blk", "ctx", "tp"))
    local_grad = jnp.concatenate(
        [query_key_value_gradient, outproj_grad, in_grad, down_grad], axis=0
    ).reshape(per_group, -1)
    shares = lax.psum_scatter(
        local_grad.astype(jnp.bfloat16), "blk", scatter_dimension=1, tiled=True
    )
    matrix_grads = lax.psum(shares, "ctx").astype(jnp.float32)
    new_momenta = momentum_decay * momenta + matrix_grads
    update = matrix_grads + momentum_decay * new_momenta
    per_owner = per_group // cycle_size
    sectioned = update.reshape(cycle_size, per_owner, update.shape[1])
    pieces = lax.all_to_all(
        sectioned.astype(jnp.bfloat16), "blk", split_axis=0, concat_axis=2, tiled=True
    ).astype(sectioned.dtype)
    piece_count = pieces.shape[1]
    settled_blocks = newton_schulz(pieces.reshape(piece_count, MODEL_DIM, HD)).reshape(
        1, piece_count, MODEL_DIM * HD
    )
    settled = lax.all_to_all(
        as_sent(settled_blocks), "blk", split_axis=2, concat_axis=0, tiled=True
    ).astype(settled_blocks.dtype)
    orthogonal_all = settled.reshape(per_group, -1)
    muon_scale = max(1.0, MODEL_DIM / HD) ** 0.5
    new_matrices = matrices - muon_rate * (muon_scale * orthogonal_all + weight_decay * matrices)
    new_first = adam_first * small_first + (1.0 - adam_first) * small_grads
    new_second = adam_second * small_second + (1.0 - adam_second) * small_grads * small_grads
    corrected = new_first / (1.0 - adam_first**STEP)
    spread = jnp.sqrt(new_second / (1.0 - adam_second**STEP))
    new_small = small - small_rate * corrected / (spread + adam_epsilon)
    return (
        block_output,
        input_grad,
        matrix_grads,
        new_matrices,
        new_momenta,
        small_grads,
        new_first,
        new_second,
        new_small,
    )


def native_view(array):
    rows, columns = array.shape
    tiled = array.reshape(rows // 8, 8, columns // 128, 128).transpose(0, 2, 1, 3)
    return tiled.reshape(rows // 8, columns // 16, 128)


def native_back(array):
    groups, rows, _ = array.shape
    return array.reshape(groups, rows // 8, 8, 128).transpose(0, 2, 1, 3).reshape(groups * 8, rows * 16)


def members_of(head):
    if head:
        return lambda piece, j: (j // 2, 4 * (j % 2) + piece)
    return lambda piece, j: (piece // 2, 4 * (piece % 2) + j)


def mem(kind=pltpu.VMEM):
    return pl.BlockSpec(memory_space=kind)


def limits(mebibytes):
    return pltpu.CompilerParams(vmem_limit_bytes=mebibytes << 20)


def low_lanes(rows):
    return lax.broadcasted_iota(jnp.int32, (rows, 128), 1) < HD


def dot(a, b, dims=((1,), (0,)), precision=None):
    return lax.dot_general(
        a, b, (dims, ((), ())), precision=precision, preferred_element_type=jnp.float32
    )


NT = ((1,), (1,))
TN = ((0,), (0,))


def corner(array):
    block = (1,) * (array.ndim - 2) + (min(16, array.shape[-2]), 128)
    return pl.BlockSpec(block, lambda *_: (0,) * array.ndim)


def takes(microseconds):
    return pl.CostEstimate(
        flops=int(microseconds * 1.15e9), transcendentals=0, bytes_accessed=int(1e6)
    )


def full(array):
    return pl.BlockSpec(array.shape, lambda *_: (0,) * array.ndim)


def launch(kernel, operands, out_shapes, name, specs=None, after=(), vmem=20, cost=3, **more):
    taken = len(operands)
    body = kernel
    if after:
        body = lambda *refs: kernel(*refs[:taken], *refs[taken + len(after) :])
    if specs is None:
        specs = [mem(pltpu.SMEM)] + [full(a) for a in operands[1:]]
    if "out_specs" not in more:
        more["out_specs"] = jax.tree.map(full, out_shapes)
    more.setdefault("grid", (1,))
    return pl.pallas_call(
        body,
        in_specs=list(specs) + [corner(a) for a in after],
        out_shape=out_shapes,
        compiler_params=limits(vmem),
        cost_estimate=takes(cost),
        name=name,
        **more,
    )(*operands, *after)


def relayout_kernel(n, head, scal, src, out, *refs):
    scratch = refs[-1]
    low = low_lanes(n)
    place_of = members_of(head)
    for piece in range(4):
        for half in range(2):
            k = 2 * piece + half
            pair = []
            for j in (2 * half, 2 * half + 1):
                group, line = place_of(piece, j)
                pair.append(src[group, pl.ds(line, n, stride=8), :])
            a, b = pair
            scratch[k, pl.ds(0, n, stride=2), :] = jnp.where(low, a, pltpu.roll(b, 64, 1))
            scratch[k, pl.ds(1, n, stride=2), :] = jnp.where(low, pltpu.roll(a, 64, 1), b)
            out[piece, :, half * 128 : (half + 1) * 128] = scratch[k].astype(out.dtype)
    if len(refs) == 2:
        refs[0][0] = out[scal[1]]


def relayout(scal, array, dtype, first, count, mine=False, n=64, after=()):
    shapes = [jax.ShapeDtypeStruct((4 * count, 512, 256), dtype)]
    specs = [pl.BlockSpec((4, 2 * n, 256), lambda k, i: (k, i, 0))]
    if mine:
        shapes.append(jax.ShapeDtypeStruct((count, 512, 256), dtype))
        specs.append(pl.BlockSpec((1, 2 * n, 256), lambda k, i: (k, i, 0)))
    return launch(
        functools.partial(relayout_kernel, n, first == 0),
        [scal, native_view(array)],
        shapes,
        "relayout",
        specs=[
            mem(pltpu.SMEM),
            pl.BlockSpec((2, 8 * n, 128), lambda k, i: (first + k, i, 0)),
        ],
        after=after,
        cost=1.3 * count,
        grid=(count, 256 // n),
        out_specs=specs,
        scratch_shapes=[pltpu.VMEM((8, 2 * n, 128), jnp.float32)],
    )


def add_up(groups):
    for parts, target in groups:
        values = [part[...].astype(jnp.float32) for part in parts]
        while len(values) > 1:
            values = [sum(values[i : i + 2]) for i in range(0, len(values), 2)]
        target[...] = values[0].astype(target.dtype)


def grouped(refs, counts, targets):
    refs = iter(refs)
    return [([next(refs) for _ in range(n)], target) for n, target in zip(counts, targets)]


def normalized(x):
    centred = x - jnp.mean(x, axis=-1, keepdims=True)
    spread = jnp.mean(centred * centred, axis=-1, keepdims=True)
    root = lax.rsqrt(spread + norm_epsilon)
    return centred * root, root


def halves(values, first):
    left, right = values[:, :512], values[:, 512:]
    return jnp.where(first, left, right), jnp.where(first, right, left)


def whole(own, other, first):
    return jnp.concatenate([jnp.where(first, own, other), jnp.where(first, other, own)], axis=1)


def norm_back(grad, hat, root, gain):
    scaled = grad * gain
    along = jnp.mean(scaled * hat, axis=-1, keepdims=True)
    return root * (scaled - jnp.mean(scaled, axis=-1, keepdims=True) - hat * along)


def turned(values, cosine, sine):
    lane = lax.broadcasted_iota(jnp.int32, values.shape, 1) % HD
    other = jnp.where(lane < 8, pltpu.roll(values, 120, 1), pltpu.roll(values, 8, 1))
    return values * cosine + other * sine


def project_kernel(scal, x, cot, norms, bias, cosine, sine, own, r0, r1, r2, r3, send):
    first = scal[0] == 0
    hat, _ = normalized(x[...].astype(jnp.float32))
    h = (hat * norms[0:1] + norms[1:2]).astype(jnp.bfloat16)
    h_own, h_other = halves(h, first)
    c_own, c_other = halves(cot[...], first)
    tokens = h.shape[0]
    low = low_lanes(tokens)
    for r, other in enumerate((r0, r1, r2, r3)):
        head = scal[1] ^ r
        mine = own[head]
        theirs = other[...]
        pre = dot(h_own, mine) + dot(h_other, theirs) + bias[pl.ds(head, 1), :]
        back = dot(c_own, mine[:, 128:]) + dot(c_other, theirs[:, 128:])
        left = turned(pre[:, :128], cosine[...], sine[...]).astype(jnp.bfloat16)
        right = jnp.where(low, pre[:, 128:], back).astype(jnp.bfloat16)
        for s in range(2):
            rows = slice(128 * s, 128 * s + 128)
            send[4 * s + head, :, :128] = left[rows]
            send[4 * s + head, :, 128:] = right[rows]


def attention_kernel(rows_ref, seg, out, key_total, value_total):
    key_total[...] = jnp.zeros_like(key_total)
    value_total[...] = jnp.zeros_like(value_total)
    step = 256
    for block in range(rows_ref.shape[0] // step):
        rows = slice(block * step, (block + 1) * step)
        n = (block + 1) * step
        query = rows_ref[rows, 0:HD] * jnp.bfloat16(0.125)
        grad = rows_ref[rows, 3 * HD : 4 * HD]
        keys = rows_ref[0:n, HD : 2 * HD]
        values = rows_ref[0:n, 2 * HD : 3 * HD]
        scores = dot(query, keys, NT)
        query_place = block * step + lax.broadcasted_iota(jnp.int32, (step, n), 0)
        key_place = lax.broadcasted_iota(jnp.int32, (step, n), 1)
        allowed = (key_place <= query_place) & (key_place >= seg[rows, :])
        scores = jnp.where(allowed, scores, masked_score)
        weights = jnp.exp(scores - jnp.max(scores, axis=-1, keepdims=True))
        weights = jnp.where(allowed, weights, 0.0)
        weights = weights * (1.0 / jnp.sum(weights, axis=-1, keepdims=True))
        short = weights.astype(jnp.bfloat16)
        attended = dot(short, values)
        weight_grad = dot(grad, values, NT)
        delta = jnp.sum(weights * weight_grad, axis=-1, keepdims=True)
        score_grad = (weights * (weight_grad - delta)).astype(jnp.bfloat16)
        query_grad = dot(score_grad, keys) * 0.125
        key_total[0:n, :] += dot(score_grad, query, TN)
        value_total[0:n, :] += dot(short, grad, TN)
        out[rows, 0:HD] = query_grad.astype(jnp.bfloat16)
        out[rows, 3 * HD : 4 * HD] = attended.astype(jnp.bfloat16)
    out[:, HD : 2 * HD] = key_total[...].astype(jnp.bfloat16)
    out[:, 2 * HD : 3 * HD] = value_total[...].astype(jnp.bfloat16)


def feed_forward_kernel(
    scal, x, cot, norms, bias, weights, r0, r1, r2, r3,
    branch, input_part, keep, send, hidden_sums, norm_grads, cot_sums,
):
    first = scal[0] == 0
    hat, root = normalized(x[...].astype(jnp.float32))
    h = (hat * norms[2:3] + norms[3:4]).astype(jnp.bfloat16)
    h_own, h_other = halves(h, first)
    c_own, c_other = halves(cot[...], first)
    cot_sums[...] = jnp.sum(cot[...].astype(jnp.float32), axis=0, keepdims=True)
    outs = [0.0] * 4
    for r, other in enumerate((r0, r1, r2, r3)):
        piece = scal[1] ^ r
        in_own, in_other = weights[piece], other[0]
        down_own, down_other = weights[4 + piece], other[1]
        pre = dot(h_own, in_own) + dot(h_other, in_other) + bias[pl.ds(piece, 1), :]
        cumulative = 0.5 * (1.0 + lax.erf(pre * 0.7071067811865476))
        slope = cumulative + pre * (0.3989422804014327 * jnp.exp(-0.5 * pre * pre))
        act = (pre * cumulative).astype(jnp.bfloat16)
        act_grad = dot(c_own, down_own) + dot(c_other, down_other)
        grad = (act_grad * slope).astype(jnp.bfloat16)
        hidden_sums[pl.ds(piece, 1), :] = jnp.sum(
            grad.astype(jnp.float32), axis=0, keepdims=True
        )
        outs[0] += dot(act, down_own, NT)
        outs[1] += dot(act, down_other, NT)
        outs[2] += dot(grad, in_own, NT)
        outs[3] += dot(grad, in_other, NT)
        target = send if r % 2 else keep
        target[r // 2, 0] = grad
        target[r // 2, 1] = act
    branch[...] = whole(outs[0], outs[1], first)
    second = whole(outs[2], outs[3], first)
    norm_grads[0:1] = jnp.sum(second * hat, axis=0, keepdims=True)
    norm_grads[1:2] = jnp.sum(second, axis=0, keepdims=True)
    input_part[...] = norm_back(second, hat, root, norms[2:3])


def both_cores(scal, x, x_beside, cot, cot_beside, norms, at):
    first = scal[0] == 0
    tokens = jnp.concatenate([x[...], x_beside[...]], axis=0).astype(jnp.float32)
    hat, _ = normalized(tokens)
    h = (hat * norms[at : at + 1] + norms[at + 1 : at + 2]).astype(jnp.bfloat16)
    c = jnp.concatenate([cot[...], cot_beside[...]], axis=0)
    return list(zip(halves(h, first), halves(c, first)))


def unit_grads_kernel(scal, x, x_beside, cot, cot_beside, norms, keep, came, *outs):
    for side, (h, c) in enumerate(both_cores(scal, x, x_beside, cot, cot_beside, norms, 2)):
        for far in range(2):
            grad = jnp.concatenate([keep[far, 0], came[far, 0]], axis=0)
            act = jnp.concatenate([keep[far, 1], came[far, 1]], axis=0)
            outs[2 * far + side][0] = dot(h, grad, TN).astype(jnp.bfloat16)
            outs[2 * far + side][1] = dot(c, act, TN).astype(jnp.bfloat16)


def turn_kernel(scal, cosine, sine, back, keep, send, sums):
    low = low_lanes(keep.shape[1])
    for r in range(4):
        head = scal[1] ^ r
        grads = jnp.concatenate([back[head], back[4 + head]], axis=0)
        left = turned(grads[:, :128].astype(jnp.float32), cosine[...], -sine[...])
        left = left.astype(jnp.bfloat16)
        right = grads[:, 128:]
        target = send if r % 2 else keep
        target[r // 2, :, :128] = left
        target[r // 2, :, 128:] = right
        right = jnp.where(low, right.astype(jnp.float32), 0.0)
        wide = jnp.concatenate([left.astype(jnp.float32), right], axis=1)
        sums[pl.ds(head, 1), :] = jnp.sum(wide, axis=0, keepdims=True)


def split_last(piece):
    wide = piece.astype(jnp.float32)
    lane = lax.broadcasted_iota(jnp.int32, (1, wide.shape[1]), 1)
    share = (lane < 3 * HD).astype(jnp.float32)
    pre_grad = (wide * share).astype(jnp.bfloat16)
    attended = (wide * (1.0 - share)).astype(jnp.bfloat16)
    return pre_grad, attended


def head_grads_kernel(
    scal, x, x_beside, cot, cot_beside, norms, keep, came, totals, totals_came, *outs
):
    add_up([((totals, totals_came), outs[4])])
    sides = both_cores(scal, x, x_beside, cot, cot_beside, norms, 0)
    for far in range(2):
        piece = jnp.concatenate([keep[far], came[far]], axis=0)
        pre_grad, attended = split_last(piece)
        for side, (h, c) in enumerate(sides):
            grad = dot(h, pre_grad, TN) + dot(c, attended, TN)
            outs[2 * far + side][0] = grad.astype(jnp.bfloat16)


def gather_kernel(
    scal, x, norms, keep, send, weights, r0, r1, r2, r3, ff_branch, ff_part,
    norm_two, cot_sums, unit_sums, qkv_sums, z0, z1, z2, z3, totals, parts,
):
    first = scal[0] == 0
    hat, root = normalized(x[...].astype(jnp.float32))
    outs = [0.0] * 4
    for r, other in enumerate((r0, r1, r2, r3)):
        mine, theirs = weights[scal[1] ^ r], other[0]
        pre_grad, attended = split_last((send if r % 2 else keep)[r // 2])
        outs[0] += dot(attended, mine, NT)
        outs[1] += dot(attended, theirs, NT)
        outs[2] += dot(pre_grad, mine, NT)
        outs[3] += dot(pre_grad, theirs, NT)
    branch = ff_branch[...] + whole(outs[0], outs[1], first)
    grad = whole(outs[2], outs[3], first)
    totals[...] = jnp.zeros_like(totals)
    rows = [jnp.sum(grad * hat, axis=0, keepdims=True), jnp.sum(grad, axis=0, keepdims=True)]
    rows += [norm_two[0:1], norm_two[1:2], cot_sums[...]]
    for i, row in enumerate(rows):
        for q in range(4):
            at = 4 * (i % 2) + q
            totals[i // 2, at : at + 1, :] = row[:, 256 * q : 256 * q + 256]
    totals[3 + scal[2], 0:4, :] = qkv_sums[...]
    totals[3 + scal[2], 4:8, :] = unit_sums[...]
    input_part = ff_part[...] + norm_back(grad, hat, root, norms[0:1])
    for q in range(4):
        parts[q, 0] = branch[64 * q : 64 * q + 64].astype(jnp.bfloat16)
        parts[q, 1] = input_part[64 * q : 64 * q + 64].astype(jnp.bfloat16)
    for r in range(4):
        (z0, z1, z2, z3)[r][...] = parts[scal[2] ^ r]


def finish_rows_kernel(scal, x, cot, bias, r0, r1, r2, r3, block_output, input_grad):
    for r, piece in enumerate((r0, r1, r2, r3)):
        q = scal[2] ^ r
        block_output[q] = x[q].astype(jnp.float32) + piece[0].astype(jnp.float32) + bias[...]
        input_grad[q] = cot[q].astype(jnp.float32) + piece[1].astype(jnp.float32)


def gram_kernel(counts, place, own, a, b, c, momenta, *refs):
    sums = len(counts)
    grads, grams = refs[-2 - sums], refs[-1 - sums]

    @pl.when(pl.program_id(0) == 0)
    def _():
        add_up(grouped(refs, counts, refs[len(refs) - sums :]))

    total = own[...].astype(jnp.float32) + a[...].astype(jnp.float32)
    total = total + b[...].astype(jnp.float32) + c[...].astype(jnp.float32)
    short = total.astype(jnp.bfloat16)
    grads[...] = short
    update = 1.95 * short[0].astype(jnp.float32) + 0.9025 * momenta[0]
    gram = dot(update, update, TN, lax.Precision.HIGHEST)
    for j in range(4):
        cut = slice(j * HD, (j + 1) * HD)
        grams[0, j] = gram[cut, cut]


def gram_of(own, a, b, c, momenta, place, sums, after=()):
    chunks = own.shape[0]
    piece = pl.BlockSpec((1, 512, 256), lambda i, s: (i, 0, 0))
    flat = [part for group in sums for part in group]
    targets = [jax.ShapeDtypeStruct(group[0].shape, group[0].dtype) for group in sums]
    return pl.pallas_call(
        functools.partial(gram_kernel, [len(group) for group in sums]),
        grid_spec=pltpu.PrefetchScalarGridSpec(
            num_scalar_prefetch=1,
            grid=(chunks,),
            in_specs=[piece] * 4
            + [pl.BlockSpec((1, 512, 256), lambda i, s: (4 * i + s[1], 0, 0))]
            + [full(part) for part in flat]
            + [corner(a) for a in after],
            out_specs=[piece, pl.BlockSpec((1, 4, HD, HD), lambda i, s: (i, 0, 0, 0))]
            + [full(target) for target in targets],
        ),
        out_shape=[
            jax.ShapeDtypeStruct((chunks, 512, 256), jnp.bfloat16),
            jax.ShapeDtypeStruct((chunks, 4, HD, HD), jnp.float32),
            *targets,
        ],
        compiler_params=limits(20),
        cost_estimate=takes(2.5),
        name="gram",
    )(place, own, a, b, c, momenta, *flat, *after)


def newton_kernel(counts, mine, theirs, *refs):
    taken = sum(counts)
    out = refs[taken]
    add_up(grouped(refs, counts, refs[taken + 1 :]))
    linear, square, cubic = quintic
    shape = (HD, HD)
    eye = lax.broadcasted_iota(jnp.int32, shape, 0) == lax.broadcasted_iota(jnp.int32, shape, 1)
    full = lax.Precision.HIGHEST
    chunks = mine.shape[0]
    places = [(i, j) for i in range(chunks) for j in range(4)]
    states = []
    for i, j in places:
        gram = mine[i, j] + theirs[i, j]
        trace = jnp.sum(jnp.where(eye, gram, 0.0), axis=(0, 1), keepdims=True)
        scale = 1.0 / (jnp.sqrt(trace) + muon_epsilon)
        states.append([gram * scale * scale, None, scale])
    for iteration in range(NEWTON):
        squares = [dot(s[0], s[0], precision=full) for s in states]
        steps = [
            jnp.where(eye, linear, 0.0) + square * s[0] + cubic * sq
            for s, sq in zip(states, squares)
        ]
        if iteration == 0:
            halfway = [dot(s[0], m, precision=full) for s, m in zip(states, steps)]
            for s, m in zip(states, steps):
                s[1] = m
        elif iteration < NEWTON - 1:
            both = [
                dot(jnp.concatenate([s[0], s[1]], axis=0), m, precision=full)
                for s, m in zip(states, steps)
            ]
            halfway = [x[:HD] for x in both]
            for s, x in zip(states, both):
                s[1] = x[HD:]
        else:
            for s, m in zip(states, steps):
                s[1] = dot(s[1], m, precision=full)
        if iteration < NEWTON - 1:
            for s, x, m in zip(states, halfway, steps):
                s[0] = dot(x, m, precision=full)
    for (i, j), s in zip(places, states):
        mix = s[1] * s[2]
        coarse = mix.astype(jnp.bfloat16)
        fine = (mix - coarse.astype(jnp.float32)).astype(jnp.bfloat16)
        out[i, j] = jnp.concatenate([coarse, fine], axis=1)


def newton(mine, theirs, sums, after=()):
    flat = [part for group in sums for part in group]
    operands = [mine, theirs, *flat]
    return launch(
        functools.partial(newton_kernel, [len(group) for group in sums]),
        operands,
        [jax.ShapeDtypeStruct((*mine.shape[:-1], 2 * HD), jnp.bfloat16)]
        + [jax.ShapeDtypeStruct(group[0].shape, group[0].dtype) for group in sums],
        "newton",
        cost=3.5,
        specs=[full(a) for a in operands],
        after=after,
    )


def update_kernel(
    n, head, scal, g0, g1, g2, g3, q0, q1, q2, q3, momenta, native_momenta, native, *refs
):
    grads, weights, moved, mixing, first, second, steps = refs[-7:]
    place_of = members_of(head)

    @pl.when((pl.program_id(0) == 0) & (pl.program_id(1) == 0))
    def _():
        mixing[...] = jnp.zeros_like(mixing)

    @pl.when(pl.program_id(1) == 0)
    def _():
        for r, q in enumerate((q0, q1, q2, q3)):
            for j in range(4):
                wide = q[0, j].astype(jnp.float32)
                other = pltpu.roll(wide, HD, 1)
                below = low_lanes(HD) == (j % 2 == 0)
                rows = slice(j * HD, (j + 1) * HD)
                lanes = slice(128 * (j // 2), 128 * (j // 2) + 128)
                pair = (wide, other) if j % 2 == 0 else (other, wide)
                for level in range(2):
                    part = jnp.where(below, pair[level], 0.0)
                    mixing[r, level, rows, lanes] = part.astype(jnp.bfloat16)

    low = low_lanes(n)
    for r, piece in enumerate((g0, g1, g2, g3)):
        place = scal[1] ^ r
        grad = piece[0].astype(jnp.float32)
        update = 1.95 * grad + 0.9025 * momenta[place]
        coarse = update.astype(jnp.bfloat16)
        fine = (update - coarse.astype(jnp.float32)).astype(jnp.bfloat16)
        settled = dot(coarse, mixing[r, 0]) + dot(coarse, mixing[r, 1]) + dot(fine, mixing[r, 0])
        for half in range(2):
            k = 2 * r + half
            first[k] = grad[:, half * 128 : (half + 1) * 128]
            second[k] = settled[:, half * 128 : (half + 1) * 128]
            for source, target in ((first, grads), (second, steps)):
                even = source[k, pl.ds(0, n, stride=2), :]
                odd = source[k, pl.ds(1, n, stride=2), :]
                lines = (
                    jnp.where(low, even, pltpu.roll(odd, 64, 1)),
                    jnp.where(low, pltpu.roll(even, 64, 1), odd),
                )
                for w in range(2):
                    group, line = place_of(place, 2 * half + w)
                    target[group, pl.ds(line, n, stride=8), :] = lines[w]
    moved[...] = momentum_decay * native_momenta[...] + grads[...]
    weight = native[...]
    weights[...] = weight - muon_rate * (4.0 * steps[...] + weight_decay * weight)


def update(first, scal, grads, mixes, momenta, native_momenta, native, before=(), after=(), n=64):
    chunks = grads[0].shape[0]
    block = pl.BlockSpec((2, 8 * n, 128), lambda k, i: (first + k, i, 0))
    piece = pl.BlockSpec((1, 2 * n, 256), lambda k, i: (k, i, 0))
    mix = pl.BlockSpec((1, 4, HD, 2 * HD), lambda k, i: (k, 0, 0, 0))
    return launch(
        functools.partial(update_kernel, n, first == 0),
        [scal, *grads, *mixes, momenta, native_view(native_momenta), native_view(native), *before],
        [jax.ShapeDtypeStruct((6, 2048, 128), jnp.float32)] * 3,
        "update",
        specs=[mem(pltpu.SMEM)]
        + [piece] * 4
        + [mix] * 4
        + [pl.BlockSpec((4, 2 * n, 256), lambda k, i: (k, i, 0)), block, block]
        + [mem(pl.ANY)] * len(before),
        after=after,
        cost=5.5 * chunks,
        grid=(chunks, 256 // n),
        out_specs=[block] * 3,
        scratch_shapes=[
            pltpu.VMEM((4, 2, 256, 256), jnp.bfloat16),
            pltpu.VMEM((8, 2 * n, 128), jnp.float32),
            pltpu.VMEM((8, 2 * n, 128), jnp.float32),
            pltpu.VMEM((2, 8 * n, 128), jnp.float32),
        ],
        input_output_aliases={12 + i: i for i in range(len(before))},
    )


def whole_device(
    inputs, cotangent, matrices, momenta, small, small_first, small_second, segments, positions
):
    blk_at = lax.axis_index("blk")
    ctx_at = lax.axis_index("ctx")
    tp_at = lax.axis_index("tp")
    scal = jnp.stack([blk_at, ctx_at, tp_at]).astype(jnp.int32)
    sequences, local_rows, width = inputs.shape
    tokens = sequences * local_rows
    both = ("blk", "ctx")
    f32, bf16 = jnp.float32, jnp.bfloat16
    shaped = jax.ShapeDtypeStruct

    def hop(values, by):
        return lax.ppermute(values, both, [(i, i ^ by) for i in range(8)])

    def hop_tp(values, by):
        return lax.ppermute(values, "tp", [(i, i ^ by) for i in range(4)])

    def spread(piece):
        c = hop(piece, 2)
        return [piece, hop(piece, 1), c, hop(c, 1)]

    x = inputs.reshape(tokens, width)
    cot = cotangent.reshape(tokens, width)
    norms = small[: 4 * width].reshape(4, width)
    qkv_start = 6 * width + tp_at * 4 * 3 * HD
    qkv_bias = lax.dynamic_slice_in_dim(small, qkv_start, 4 * 3 * HD).reshape(4, 3 * HD)
    qkv_bias = jnp.pad(qkv_bias, ((0, 0), (0, HD)))
    unit_start = 6 * width + H * 3 * HD + tp_at * 1024
    unit_bias = lax.dynamic_slice_in_dim(small, unit_start, 1024).reshape(4, 256)
    lane = jnp.arange(128) % HD
    frequency = rope_base ** (-2.0 * (lane % 8).astype(f32) / ROTARY)
    angles = positions.astype(f32).reshape(tokens, 1) * frequency
    cosine = jnp.where(lane < ROTARY, jnp.cos(angles), 1.0)
    sign = jnp.where(lane < 8, -1.0, jnp.where(lane < ROTARY, 1.0, 0.0))
    sine = jnp.sin(angles) * sign

    head_weights, mine = relayout(scal, matrices, bf16, 0, 1, mine=True)
    first_hop = hop(mine, 4)
    other_heads = spread(first_hop)
    (piled_heads,) = relayout(scal, momenta, f32, 0, 1, after=(mine,))
    (piled_units,) = relayout(scal, momenta, f32, 1, 2, after=(mine,))
    unit_weights, mine = relayout(
        scal, matrices, bf16, 1, 2, mine=True, after=(first_hop, piled_heads, piled_units, cosine, sine)
    )
    other_units = spread(hop(mine, 4))
    x_beside = hop(x, 1)
    cot_beside = hop(cot, 1)

    send = launch(
        project_kernel,
        [scal, x, cot, norms, qkv_bias, cosine, sine, head_weights]
        + [piece[0] for piece in other_heads],
        shaped((8, local_rows, 256), bf16),
        "project",
    )
    arrived = lax.all_to_all(send, both, split_axis=0, concat_axis=0, tiled=True)
    documents = lax.dynamic_index_in_dim(segments, blk_at, 0, keepdims=False)
    length = documents.shape[0]
    attended = launch(
        attention_kernel,
        [arrived.reshape(length, 256), documents.reshape(length, 1)],
        shaped((length, 256), bf16),
        "attention",
        cost=6,
        specs=[full(arrived.reshape(length, 256)), pl.BlockSpec((length, 1), lambda *_: (0, 0))],
        scratch_shapes=[pltpu.VMEM((length, HD), f32)] * 2,
    )
    back = lax.all_to_all(
        attended.reshape(8, local_rows, 256), both, split_axis=0, concat_axis=0, tiled=True
    )

    ff_branch, ff_part, unit_keep, unit_send, unit_sums, norm_two, cot_sums = launch(
        feed_forward_kernel,
        [scal, x, cot, norms, unit_bias, unit_weights, *other_units],
        [
            shaped((tokens, width), f32),
            shaped((tokens, width), f32),
            shaped((2, 2, tokens, 256), bf16),
            shaped((2, 2, tokens, 256), bf16),
            shaped((4, 256), f32),
            shaped((2, width), f32),
            shaped((1, width), f32),
        ],
        "feed_forward",
        cost=5.5,
        after=(attended,),
    )
    head_keep, head_send, qkv_sums = launch(
        turn_kernel,
        [scal, cosine, sine, back],
        [shaped((2, tokens, 256), bf16)] * 2 + [shaped((4, 256), f32)],
        "turn",
        cost=2,
        after=(unit_sums,),
    )
    unit_grads = launch(
        unit_grads_kernel,
        [scal, x, x_beside, cot, cot_beside, norms, unit_keep, hop(unit_send, 1)],
        [shaped((2, 512, 256), bf16)] * 4,
        "unit_grads",
        cost=3.5,
        after=(qkv_sums,),
    )
    sums = [norm_two, cot_sums, unit_sums, qkv_sums]
    *quarters, totals = launch(
        gather_kernel,
        [scal, x, norms, head_keep, head_send, head_weights, *other_heads, ff_branch, ff_part, *sums],
        [shaped((2, 64, width), bf16)] * 4 + [shaped((7, 8, 256), f32)],
        "gather",
        after=(unit_grads[0],),
        scratch_shapes=[pltpu.VMEM((4, 2, 64, width), bf16)],
    )
    *head_grads, totals = launch(
        head_grads_kernel,
        [scal, x, x_beside, cot, cot_beside, norms, head_keep, hop(head_send, 1), totals, hop(totals, 1)],
        [shaped((1, 512, 256), bf16)] * 4 + [shaped((7, 8, 256), f32)],
        "head_grads",
        cost=4,
    )

    def reduced(grads):
        return grads[0], hop(grads[1], 4), hop(grads[2], 2), hop(grads[3], 6)

    unit_reduced = reduced(unit_grads)
    head_reduced = reduced(head_grads)
    spread_totals = [totals, hop(totals, 4), hop(totals, 2), hop(totals, 6)]
    unit_sum, unit_grams, near, far = gram_of(
        *unit_reduced,
        piled_units,
        scal,
        [(quarters[0], hop_tp(quarters[1], 1)), (quarters[2], hop_tp(quarters[3], 1))],
        after=(head_grads[0],),
    )
    unit_pieces = spread(unit_sum)
    unit_mix, total, totals = newton(
        unit_grams, hop(unit_grams, 4), [(near, hop_tp(far, 2)), spread_totals]
    )
    head_sum, head_grams, totals = gram_of(
        *head_reduced, piled_heads, scal, [(totals, hop_tp(totals, 1))], after=(unit_mix,)
    )
    head_pieces = spread(head_sum)
    before = update(1, scal, unit_pieces, spread(unit_mix), piled_units, momenta, matrices)
    head_mix, totals = newton(
        head_grams, hop(head_grams, 4), [(totals, hop_tp(totals, 2))], after=(before[0],)
    )
    outs = update(0, scal, head_pieces, spread(head_mix), piled_heads, momenta, matrices, before)

    beside = hop_tp(total, 2)
    block_output, input_grad = launch(
        finish_rows_kernel,
        [
            scal,
            x.reshape(4, 64, width),
            cot.reshape(4, 64, width),
            (small[4 * width : 5 * width] + small[5 * width : 6 * width]).reshape(1, width),
            total,
            hop_tp(total, 1),
            beside,
            hop_tp(beside, 1),
        ],
        [shaped((4, 64, width), f32)] * 2,
        "finish_rows",
        cost=2,
    )

    cot_total = totals[2, :4].reshape(-1) * 0.25
    small_grads = jnp.concatenate(
        [
            totals[:2].reshape(-1),
            cot_total,
            cot_total,
            totals[3:, :4, : 3 * HD].reshape(-1),
            totals[3:, 4:].reshape(-1),
        ]
    )
    return (
        block_output.reshape(inputs.shape),
        input_grad.reshape(inputs.shape),
        native_back(outs[0]),
        native_back(outs[1]),
        native_back(outs[2]),
        small_grads,
        *small_step(small, small_first, small_second, small_grads),
    )


def small_step(small, small_first, small_second, small_grads):
    new_first = adam_first * small_first + (1.0 - adam_first) * small_grads
    new_second = adam_second * small_second + (1.0 - adam_second) * small_grads * small_grads
    corrected = new_first / (1.0 - adam_first**STEP)
    spread = jnp.sqrt(new_second / (1.0 - adam_second**STEP))
    new_small = small - small_rate * corrected / (spread + adam_epsilon)
    return new_first, new_second, new_small


def solution(mesh):
    in_specs = (
        P(None, ("blk", "ctx"), None),
        P(None, ("blk", "ctx"), None),
        P("tp", "blk"),
        P("tp", "blk"),
        P(),
        P(),
        P(),
        P(),
        P(None, ("blk", "ctx")),
    )
    out_specs = (
        P(None, ("blk", "ctx"), None),
        P(None, ("blk", "ctx"), None),
        P("tp", "blk"),
        P("tp", "blk"),
        P("tp", "blk"),
        P(),
        P(),
        P(),
        P(),
    )
    one_each = mesh.shape["blk"] == SEQS and mesh.shape["ctx"] * mesh.shape["tp"] == H
    one_each = one_each and mesh.shape["tp"] == 4
    return jax.shard_map(
        whole_device if one_each else on_device, mesh=mesh, in_specs=in_specs, out_specs=out_specs, check_vma=False
    )
```

```python
import functools

import jax
import jax.numpy as jnp
from jax import lax
from jax.experimental import pallas as pl
from jax.experimental.pallas import tpu as pltpu
from jax.sharding import PartitionSpec as P

MODEL_DIM = 1024
H = 16
HD = 64
FF = 4096
ROTARY = 16
NEWTON = 5
STEP = 10
SEQS = 2


norm_epsilon = 1e-05
rope_base = 10000.0
masked_score = -1e30
momentum_decay = 0.95
muon_rate = 0.2
weight_decay = 0.01
muon_epsilon = 1e-07
quintic = (3.4445, -4.775, 2.0315)
adam_first = 0.9
adam_second = 0.95
adam_epsilon = 1e-08
small_rate = 0.2


def passed_along(x, axis, by):
    devices = lax.axis_size(axis)
    pairs = [(i, i + by) for i in range(devices) if 0 <= i + by < devices]
    return lax.ppermute(x, axis, pairs)


def shifted(x, axis, by):
    devices = lax.axis_size(axis)
    return lax.ppermute(x, axis, [(i, (i + by) % devices) for i in range(devices)])


def as_sent(x):

    def short(part):
        return part.astype(jnp.bfloat16) if part.dtype == jnp.float32 else part

    return jax.tree.map(short, x)


def layer_norm(values, scaling, offset):
    centre = jnp.mean(values, axis=-1, keepdims=True)
    centred = values - centre
    spread = jnp.mean(centred * centred, axis=-1, keepdims=True)
    return centred * lax.rsqrt(spread + norm_epsilon) * scaling + offset


def rope_tables(positions):
    halfway = ROTARY // 2
    frequency = rope_base ** (-2.0 * jnp.arange(halfway, dtype=jnp.float32) / ROTARY)
    angles = positions.astype(jnp.float32)[..., None] * frequency
    return (jnp.cos(angles)[:, :, None, :], jnp.sin(angles)[:, :, None, :])


def rotate(values, cosine, sine):
    halfway = ROTARY // 2
    former = values[..., :halfway]
    latter = values[..., halfway:ROTARY]
    return jnp.concatenate(
        [former * cosine - latter * sine, latter * cosine + former * sine, values[..., ROTARY:]],
        axis=-1,
    )


def exact_gelu(values):
    return jax.nn.gelu(values, approximate=False)


def newton_schulz(blocks):
    frobenius = jnp.sqrt(jnp.sum(blocks * blocks, axis=(1, 2), keepdims=True))
    current = blocks / (frobenius + muon_epsilon)
    linear_term, square_term, cubic_term = quintic
    for iteration in range(NEWTON):
        gram_matrix = jnp.einsum("mde,mdf->mef", current, current, precision=lax.Precision.HIGHEST)
        polynomial = square_term * gram_matrix + cubic_term * jnp.einsum(
            "mef,mfg->meg", gram_matrix, gram_matrix, precision=lax.Precision.HIGHEST
        )
        current = linear_term * current + jnp.einsum(
            "mde,mef->mdf", current, polynomial, precision=lax.Precision.HIGHEST
        )
    return current


def to_heads(values):
    return lax.all_to_all(values, "ctx", split_axis=3, concat_axis=1, tiled=True)


def to_positions(values):
    return lax.all_to_all(values, "ctx", split_axis=1, concat_axis=3, tiled=True)


def pass_keys(pair):
    return passed_along(pair, "blk", 1)


def pass_grads(pair_grad):
    return shifted(pair_grad.astype(jnp.bfloat16), "blk", 1).astype(pair_grad.dtype)


def allowed_pairs(segments, query_block, key_block, block_rows):
    query_place = query_block * block_rows + jnp.arange(block_rows, dtype=jnp.int32)
    key_place = key_block * block_rows + jnp.arange(block_rows, dtype=jnp.int32)
    query_doc = lax.dynamic_slice_in_dim(segments, query_block * block_rows, block_rows, 1)
    key_doc = lax.dynamic_slice_in_dim(segments, key_block * block_rows, block_rows, 1)
    causal = key_place[None, :] <= query_place[:, None]
    return (causal[None] & (query_doc[:, :, None] == key_doc[:, None, :]))[:, None]


def masked_scores(queries, keys, allowed):
    score_scale = HD ** (-0.5)
    scores = (
        jnp.einsum("sqhe,skhe->shqk", queries, keys, preferred_element_type=jnp.float32)
        * score_scale
    )
    return jnp.where(allowed, scores, masked_score)


def on_device(
    inputs, cotangent, matrices, momenta, small, small_first, small_second, segments, positions
):
    tensor_size = lax.axis_size("tp")
    cycle_size = lax.axis_size("blk")
    context_size = lax.axis_size("ctx")
    tensor_index = lax.axis_index("tp")
    cycle_index = lax.axis_index("blk")
    sequences, local_rows, model_width = inputs.shape
    per_group = matrices.shape[0]
    head_count = H // tensor_size
    unit_blocks = FF // HD // tensor_size
    block_rows = local_rows * context_size
    gathered = lax.all_gather(matrices.astype(jnp.bfloat16), "blk", axis=1, tiled=True).reshape(
        per_group, model_width, HD
    )
    query_key_value_weight = gathered[: 3 * head_count]
    projection_out_weight = gathered[3 * head_count : 4 * head_count]
    input_weight = gathered[4 * head_count : 4 * head_count + unit_blocks]
    down_projection_weight = gathered[4 * head_count + unit_blocks :]
    qkv_start = 6 * model_width + tensor_index * head_count * 3 * HD
    query_key_value_bias = lax.dynamic_slice_in_dim(small, qkv_start, head_count * 3 * HD).reshape(
        head_count, 3, HD
    )
    unit_start = 6 * model_width + H * 3 * HD + tensor_index * unit_blocks * HD
    hidden_unit_bias = lax.dynamic_slice_in_dim(small, unit_start, unit_blocks * HD).reshape(
        unit_blocks, HD
    )
    residual = inputs.astype(jnp.float32)

    def both_norms(values, gain_one, offset_one, gain_two, offset_two):
        return (layer_norm(values, gain_one, offset_one), layer_norm(values, gain_two, offset_two))

    (normed_one, normed_two), norm_back = jax.vjp(
        both_norms,
        residual,
        small[0:model_width],
        small[model_width : 2 * model_width],
        small[2 * model_width : 3 * model_width],
        small[3 * model_width : 4 * model_width],
    )
    first_input = normed_one.astype(jnp.bfloat16)
    second_input = normed_two.astype(jnp.bfloat16)
    projected = jnp.einsum(
        "pgk,jka->pgja", first_input, query_key_value_weight, preferred_element_type=jnp.float32
    )
    projected = projected.reshape(sequences, local_rows, 3, head_count, HD) + jnp.transpose(
        query_key_value_bias, (1, 0, 2)
    )
    cosine, sine = rope_tables(positions)

    def turn_pair(query_pre, key_pre):
        return (rotate(query_pre, cosine, sine), rotate(key_pre, cosine, sine))

    (query_turned, key_turned), turn_back = jax.vjp(
        turn_pair, projected[:, :, 0], projected[:, :, 1]
    )
    stacked = jnp.stack([query_turned, key_turned, projected[:, :, 2]], axis=2).astype(jnp.bfloat16)
    by_heads = to_heads(stacked)
    queries = by_heads[:, :, 0]
    head_local = queries.shape[2]

    def forward_visit(state, pair, source):
        row_max, row_total, weighted = state
        allowed = allowed_pairs(segments, cycle_index, source, block_rows)
        scores = masked_scores(queries, pair[:, :, 0], allowed)
        new_max = jnp.maximum(row_max, jnp.max(scores, axis=-1))
        weights = jnp.where(allowed, jnp.exp(scores - new_max[..., None]), 0.0)
        rescale = jnp.exp(row_max - new_max)
        row_total = row_total * rescale + jnp.sum(weights, axis=-1)
        weighted = weighted * rescale[..., None] + jnp.einsum(
            "shqk,skhe->shqe",
            weights.astype(jnp.bfloat16),
            pair[:, :, 1],
            preferred_element_type=jnp.float32,
        )
        return (new_max, row_total, weighted)

    def forward_hop(hop_index, carry):
        pair, state = carry
        source = (cycle_index - hop_index) % cycle_size
        state = forward_visit(state, pair, source)
        return (pass_keys(pair), state)

    start_state = (
        jnp.full((sequences, head_local, block_rows), masked_score, jnp.float32),
        jnp.zeros((sequences, head_local, block_rows), jnp.float32),
        jnp.zeros((sequences, head_local, block_rows, HD), jnp.float32),
    )
    pair, state = lax.fori_loop(0, cycle_size - 1, forward_hop, (by_heads[:, :, 1:], start_state))
    row_max, row_total, weighted = forward_visit(state, pair, (cycle_index + 1) % cycle_size)
    log_total = row_max + jnp.log(row_total)
    attended_rows = jnp.transpose(weighted / row_total[..., None], (0, 2, 1, 3))
    attention_result = to_positions(attended_rows.astype(jnp.bfloat16)[:, :, None])[:, :, 0]
    attention_branch = jnp.einsum(
        "roxu,xcu->roc", attention_result, projection_out_weight, preferred_element_type=jnp.float32
    )
    hidden_preactivation = (
        jnp.einsum("ptr,kra->ptka", second_input, input_weight, preferred_element_type=jnp.float32)
        + hidden_unit_bias
    )
    activated_hidden, gelu_back = jax.vjp(exact_gelu, hidden_preactivation)
    activated_reduced = activated_hidden.astype(jnp.bfloat16)
    perceptron_branch = jnp.einsum(
        "xkzp,zop->xko",
        activated_reduced,
        down_projection_weight,
        preferred_element_type=jnp.float32,
    )
    branches = lax.psum((attention_branch + perceptron_branch).astype(jnp.bfloat16), "tp").astype(
        jnp.float32
    )
    block_output = (
        residual
        + branches
        + small[4 * model_width : 5 * model_width]
        + small[5 * model_width : 6 * model_width]
    )
    act_grad = jnp.einsum(
        "ptr,kra->ptka", cotangent, down_projection_weight, preferred_element_type=jnp.float32
    )
    hidden_gradient = gelu_back(act_grad)[0].astype(jnp.bfloat16)
    down_grad = jnp.einsum(
        "gup,guzb->zpb", cotangent, activated_reduced, preferred_element_type=jnp.float32
    )
    in_grad = jnp.einsum(
        "gup,guzb->zpb", second_input, hidden_gradient, preferred_element_type=jnp.float32
    )
    second_grad = jnp.einsum(
        "xkzp,zop->xko", hidden_gradient, input_weight, preferred_element_type=jnp.float32
    )
    attended_grad = jnp.einsum(
        "pgk,jka->pgja", cotangent, projection_out_weight, preferred_element_type=jnp.float32
    ).astype(jnp.bfloat16)
    outproj_grad = jnp.einsum(
        "ztu,ztqi->qui", cotangent, attention_result, preferred_element_type=jnp.float32
    )
    grad_heads = to_heads(attended_grad[:, :, None])[:, :, 0]
    row_delta = jnp.transpose(
        jnp.sum(grad_heads.astype(jnp.float32) * attended_rows, axis=-1), (0, 2, 1)
    )

    def backward_visit(query_grad, pair, source):
        allowed = allowed_pairs(segments, cycle_index, source, block_rows)
        scores = masked_scores(queries, pair[:, :, 0], allowed)
        probabilities = jnp.where(allowed, jnp.exp(scores - log_total[..., None]), 0.0)
        value_grad = jnp.einsum(
            "shqk,sqhe->skhe",
            probabilities.astype(jnp.bfloat16),
            grad_heads,
            preferred_element_type=jnp.float32,
        )
        prob_grad = jnp.einsum(
            "sqhe,skhe->shqk", grad_heads, pair[:, :, 1], preferred_element_type=jnp.float32
        )
        score_grad = (probabilities * (prob_grad - row_delta[..., None])).astype(jnp.bfloat16)
        score_scale = HD ** (-0.5)
        query_grad = (
            query_grad
            + jnp.einsum(
                "shqk,skhe->sqhe", score_grad, pair[:, :, 0], preferred_element_type=jnp.float32
            )
            * score_scale
        )
        key_grad = (
            jnp.einsum("shqk,sqhe->skhe", score_grad, queries, preferred_element_type=jnp.float32)
            * score_scale
        )
        return (query_grad, jnp.stack([key_grad, value_grad], axis=2))

    def backward_hop(hop_index, carry):
        pair, pair_grad, query_grad = carry
        source = (cycle_index - hop_index) % cycle_size
        query_grad, visit_grad = backward_visit(query_grad, pair, source)
        return (pass_keys(pair), pass_grads(pair_grad + visit_grad), query_grad)

    zero_pair = jnp.zeros(by_heads[:, :, 1:].shape, jnp.float32)
    pair, pair_grad, query_grad = lax.fori_loop(
        0,
        cycle_size - 1,
        backward_hop,
        (by_heads[:, :, 1:], zero_pair, jnp.zeros(queries.shape, jnp.float32)),
    )
    query_grad, visit_grad = backward_visit(query_grad, pair, (cycle_index + 1) % cycle_size)
    pair_grad = pass_grads(pair_grad + visit_grad)
    head_grads = jnp.concatenate([query_grad[:, :, None], pair_grad], axis=2).astype(jnp.bfloat16)
    position_grads = to_positions(head_grads).astype(jnp.float32)
    query_pre_grad, key_pre_grad = turn_back((position_grads[:, :, 0], position_grads[:, :, 1]))
    projected_grad = jnp.stack(
        [query_pre_grad, key_pre_grad, position_grads[:, :, 2]], axis=2
    ).astype(jnp.bfloat16)
    flattened_gradient = projected_grad.reshape(sequences, local_rows, 3 * head_count, HD)
    query_key_value_gradient = jnp.einsum(
        "ztu,ztqi->qui", first_input, flattened_gradient, preferred_element_type=jnp.float32
    )
    first_grad = jnp.einsum(
        "roxu,xcu->roc",
        flattened_gradient,
        query_key_value_weight,
        preferred_element_type=jnp.float32,
    )
    input_part, gain_one_grad, offset_one_grad, gain_two_grad, offset_two_grad = norm_back(
        (first_grad, second_grad)
    )
    input_grad = cotangent.astype(jnp.float32) + lax.psum(
        input_part.astype(jnp.bfloat16), "tp"
    ).astype(jnp.float32)
    owner_share = jnp.where(tensor_index == 0, 1.0, 0.0).astype(jnp.float32)
    bias_grad = jnp.sum(cotangent.astype(jnp.float32), axis=(0, 1)) * owner_share
    qkv_bias_grad = jnp.transpose(
        jnp.sum(projected_grad.astype(jnp.float32), axis=(0, 1)), (1, 0, 2)
    ).reshape(-1)
    unit_bias_grad = jnp.sum(hidden_gradient.astype(jnp.float32), axis=(0, 1)).reshape(-1)
    local_small = jnp.concatenate(
        [
            gain_one_grad,
            offset_one_grad,
            gain_two_grad,
            offset_two_grad,
            bias_grad,
            bias_grad,
            jnp.zeros((small.shape[0] - 6 * model_width,), jnp.float32),
        ]
    )
    local_small = lax.dynamic_update_slice_in_dim(local_small, qkv_bias_grad, qkv_start, 0)
    local_small = lax.dynamic_update_slice_in_dim(local_small, unit_bias_grad, unit_start, 0)
    small_grads = lax.psum(local_small, ("blk", "ctx", "tp"))
    local_grad = jnp.concatenate(
        [query_key_value_gradient, outproj_grad, in_grad, down_grad], axis=0
    ).reshape(per_group, -1)
    shares = lax.psum_scatter(
        local_grad.astype(jnp.bfloat16), "blk", scatter_dimension=1, tiled=True
    )
    matrix_grads = lax.psum(shares, "ctx").astype(jnp.float32)
    new_momenta = momentum_decay * momenta + matrix_grads
    update = matrix_grads + momentum_decay * new_momenta
    per_owner = per_group // cycle_size
    sectioned = update.reshape(cycle_size, per_owner, update.shape[1])
    pieces = lax.all_to_all(
        sectioned.astype(jnp.bfloat16), "blk", split_axis=0, concat_axis=2, tiled=True
    ).astype(sectioned.dtype)
    piece_count = pieces.shape[1]
    settled_blocks = newton_schulz(pieces.reshape(piece_count, MODEL_DIM, HD)).reshape(
        1, piece_count, MODEL_DIM * HD
    )
    settled = lax.all_to_all(
        as_sent(settled_blocks), "blk", split_axis=2, concat_axis=0, tiled=True
    ).astype(settled_blocks.dtype)
    orthogonal_all = settled.reshape(per_group, -1)
    muon_scale = max(1.0, MODEL_DIM / HD) ** 0.5
    new_matrices = matrices - muon_rate * (muon_scale * orthogonal_all + weight_decay * matrices)
    new_first = adam_first * small_first + (1.0 - adam_first) * small_grads
    new_second = adam_second * small_second + (1.0 - adam_second) * small_grads * small_grads
    corrected = new_first / (1.0 - adam_first**STEP)
    spread = jnp.sqrt(new_second / (1.0 - adam_second**STEP))
    new_small = small - small_rate * corrected / (spread + adam_epsilon)
    return (
        block_output,
        input_grad,
        matrix_grads,
        new_matrices,
        new_momenta,
        small_grads,
        new_first,
        new_second,
        new_small,
    )


def native_view(array):
    rows, columns = array.shape
    tiled = array.reshape(rows // 8, 8, columns // 128, 128).transpose(0, 2, 1, 3)
    return tiled.reshape(rows // 8, columns // 16, 128)


def native_back(array):
    groups, rows, _ = array.shape
    return array.reshape(groups, rows // 8, 8, 128).transpose(0, 2, 1, 3).reshape(groups * 8, rows * 16)


def members_of(head):
    if head:
        return lambda piece, j: (j // 2, 4 * (j % 2) + piece)
    return lambda piece, j: (piece // 2, 4 * (piece % 2) + j)


def mem(kind=pltpu.VMEM):
    return pl.BlockSpec(memory_space=kind)


def limits(mebibytes):
    return pltpu.CompilerParams(vmem_limit_bytes=mebibytes << 20)


def low_lanes(rows):
    return lax.broadcasted_iota(jnp.int32, (rows, 128), 1) < HD


def dot(a, b, dims=((1,), (0,)), precision=None):
    return lax.dot_general(
        a, b, (dims, ((), ())), precision=precision, preferred_element_type=jnp.float32
    )


NT = ((1,), (1,))
TN = ((0,), (0,))


def corner(array):
    block = (1,) * (array.ndim - 2) + (min(16, array.shape[-2]), 128)
    return pl.BlockSpec(block, lambda *_: (0,) * array.ndim)


def takes(microseconds):
    return pl.CostEstimate(
        flops=int(microseconds * 1.15e9), transcendentals=0, bytes_accessed=int(1e6)
    )


def in_hbm(array):
    if array.size * array.dtype.itemsize < 1 << 20:
        return array
    return pltpu.with_memory_space_constraint(array, pltpu.HBM)


def out_hbm(shape):
    if shape.size * shape.dtype.itemsize < 1 << 20:
        return shape
    return pltpu.HBM(shape.shape, shape.dtype)


def full(array):
    return pl.BlockSpec(array.shape, lambda *_: (0,) * array.ndim)


def launch(kernel, operands, out_shapes, name, specs=None, after=(), vmem=20, cost=3, **more):
    taken = len(operands)
    body = kernel
    if after:
        body = lambda *refs: kernel(*refs[:taken], *refs[taken + len(after) :])
    if specs is None:
        specs = [mem(pltpu.SMEM)] + [full(a) for a in operands[1:]]
    if "out_specs" not in more:
        more["out_specs"] = jax.tree.map(full, out_shapes)
    more.setdefault("grid", (1,))
    return pl.pallas_call(
        body,
        in_specs=list(specs) + [corner(a) for a in after],
        out_shape=jax.tree.map(out_hbm, out_shapes),
        compiler_params=limits(vmem),
        cost_estimate=takes(cost),
        name=name,
        **more,
    )(*map(in_hbm, operands), *map(in_hbm, after))


def relayout_kernel(n, head, scal, src, out, *refs):
    scratch = refs[-1]
    low = low_lanes(n)
    place_of = members_of(head)
    for piece in range(4):
        for half in range(2):
            k = 2 * piece + half
            pair = []
            for j in (2 * half, 2 * half + 1):
                group, line = place_of(piece, j)
                pair.append(src[group, pl.ds(line, n, stride=8), :])
            a, b = pair
            scratch[k, pl.ds(0, n, stride=2), :] = jnp.where(low, a, pltpu.roll(b, 64, 1))
            scratch[k, pl.ds(1, n, stride=2), :] = jnp.where(low, pltpu.roll(a, 64, 1), b)
            out[piece, :, half * 128 : (half + 1) * 128] = scratch[k].astype(out.dtype)
    if len(refs) == 2:
        refs[0][0] = out[scal[1]]


def relayout(scal, array, dtype, first, count, mine=False, n=64, after=()):
    shapes = [jax.ShapeDtypeStruct((4 * count, 512, 256), dtype)]
    specs = [pl.BlockSpec((4, 2 * n, 256), lambda k, i: (k, i, 0))]
    if mine:
        shapes.append(jax.ShapeDtypeStruct((count, 512, 256), dtype))
        specs.append(pl.BlockSpec((1, 2 * n, 256), lambda k, i: (k, i, 0)))
    return launch(
        functools.partial(relayout_kernel, n, first == 0),
        [scal, native_view(array)],
        shapes,
        "relayout",
        specs=[
            mem(pltpu.SMEM),
            pl.BlockSpec((2, 8 * n, 128), lambda k, i: (first + k, i, 0)),
        ],
        after=after,
        cost=1.3 * count,
        grid=(count, 256 // n),
        out_specs=specs,
        scratch_shapes=[pltpu.VMEM((8, 2 * n, 128), jnp.float32)],
    )


def add_up(groups):
    for parts, target in groups:
        values = [part[...].astype(jnp.float32) for part in parts]
        while len(values) > 1:
            values = [sum(values[i : i + 2]) for i in range(0, len(values), 2)]
        if isinstance(target, list):
            for i, part in enumerate(target):
                part[...] = values[0][i].astype(part.dtype)
        else:
            target[...] = values[0].astype(target.dtype)


def grouped(refs, counts, targets):
    refs = iter(refs)
    return [([next(refs) for _ in range(n)], target) for n, target in zip(counts, targets)]


def normalized(x):
    centred = x - jnp.mean(x, axis=-1, keepdims=True)
    spread = jnp.mean(centred * centred, axis=-1, keepdims=True)
    root = lax.rsqrt(spread + norm_epsilon)
    return centred * root, root


def halves(values, first):
    left, right = values[:, :512], values[:, 512:]
    return jnp.where(first, left, right), jnp.where(first, right, left)


def whole(own, other, first):
    return jnp.concatenate([jnp.where(first, own, other), jnp.where(first, other, own)], axis=1)


def norm_back(grad, hat, root, gain):
    scaled = grad * gain
    along = jnp.mean(scaled * hat, axis=-1, keepdims=True)
    return root * (scaled - jnp.mean(scaled, axis=-1, keepdims=True) - hat * along)


def turned(values, cosine, sine):
    lane = lax.broadcasted_iota(jnp.int32, values.shape, 1) % HD
    other = jnp.where(lane < 8, pltpu.roll(values, 120, 1), pltpu.roll(values, 8, 1))
    return values * cosine + other * sine


def project_kernel(scal, x, cot, norms, bias, cosine, sine, own, r0, r1, r2, r3, send):
    first = scal[0] == 0
    hat, _ = normalized(x[...].astype(jnp.float32))
    h = (hat * norms[0:1] + norms[1:2]).astype(jnp.bfloat16)
    h_own, h_other = halves(h, first)
    c_own, c_other = halves(cot[...], first)
    tokens = h.shape[0]
    low = low_lanes(tokens)
    for r, other in enumerate((r0, r1, r2, r3)):
        head = scal[1] ^ r
        mine = own[head]
        theirs = other[...]
        pre = dot(h_own, mine) + dot(h_other, theirs) + bias[pl.ds(head, 1), :]
        back = dot(c_own, mine[:, 128:]) + dot(c_other, theirs[:, 128:])
        left = turned(pre[:, :128], cosine[...], sine[...]).astype(jnp.bfloat16)
        right = jnp.where(low, pre[:, 128:], back).astype(jnp.bfloat16)
        for s in range(2):
            rows = slice(128 * s, 128 * s + 128)
            send[4 * s + head, :, :128] = left[rows]
            send[4 * s + head, :, 128:] = right[rows]


def attention_kernel(rows_ref, seg, out, key_total, value_total):
    key_total[...] = jnp.zeros_like(key_total)
    value_total[...] = jnp.zeros_like(value_total)
    step = 256
    for block in range(rows_ref.shape[0] // step):
        rows = slice(block * step, (block + 1) * step)
        n = (block + 1) * step
        query = rows_ref[rows, 0:HD] * jnp.bfloat16(0.125)
        grad = rows_ref[rows, 3 * HD : 4 * HD]
        keys = rows_ref[0:n, HD : 2 * HD]
        values = rows_ref[0:n, 2 * HD : 3 * HD]
        scores = dot(query, keys, NT)
        query_place = block * step + lax.broadcasted_iota(jnp.int32, (step, n), 0)
        key_place = lax.broadcasted_iota(jnp.int32, (step, n), 1)
        allowed = (key_place <= query_place) & (key_place >= seg[rows, :])
        scores = jnp.where(allowed, scores, masked_score)
        weights = jnp.exp(scores - jnp.max(scores, axis=-1, keepdims=True))
        weights = jnp.where(allowed, weights, 0.0)
        weights = weights * (1.0 / jnp.sum(weights, axis=-1, keepdims=True))
        short = weights.astype(jnp.bfloat16)
        attended = dot(short, values)
        weight_grad = dot(grad, values, NT)
        delta = jnp.sum(weights * weight_grad, axis=-1, keepdims=True)
        score_grad = (weights * (weight_grad - delta)).astype(jnp.bfloat16)
        query_grad = dot(score_grad, keys) * 0.125
        key_total[0:n, :] += dot(score_grad, query, TN)
        value_total[0:n, :] += dot(short, grad, TN)
        out[rows, 0:HD] = query_grad.astype(jnp.bfloat16)
        out[rows, 3 * HD : 4 * HD] = attended.astype(jnp.bfloat16)
    out[:, HD : 2 * HD] = key_total[...].astype(jnp.bfloat16)
    out[:, 2 * HD : 3 * HD] = value_total[...].astype(jnp.bfloat16)


def feed_forward_kernel(
    scal, x, cot, norms, bias, weights, r0, r1, r2, r3,
    branch, input_part, keep, send, hidden_sums, norm_grads, cot_sums,
):
    first = scal[0] == 0
    hat, root = normalized(x[...].astype(jnp.float32))
    h = (hat * norms[2:3] + norms[3:4]).astype(jnp.bfloat16)
    h_own, h_other = halves(h, first)
    c_own, c_other = halves(cot[...], first)
    cot_sums[...] = jnp.sum(cot[...].astype(jnp.float32), axis=0, keepdims=True)
    outs = [0.0] * 4
    for r, other in enumerate((r0, r1, r2, r3)):
        piece = scal[1] ^ r
        in_own, in_other = weights[piece], other[0]
        down_own, down_other = weights[4 + piece], other[1]
        pre = dot(h_own, in_own) + dot(h_other, in_other) + bias[pl.ds(piece, 1), :]
        cumulative = 0.5 * (1.0 + lax.erf(pre * 0.7071067811865476))
        slope = cumulative + pre * (0.3989422804014327 * jnp.exp(-0.5 * pre * pre))
        act = (pre * cumulative).astype(jnp.bfloat16)
        act_grad = dot(c_own, down_own) + dot(c_other, down_other)
        grad = (act_grad * slope).astype(jnp.bfloat16)
        hidden_sums[pl.ds(piece, 1), :] = jnp.sum(
            grad.astype(jnp.float32), axis=0, keepdims=True
        )
        outs[0] += dot(act, down_own, NT)
        outs[1] += dot(act, down_other, NT)
        outs[2] += dot(grad, in_own, NT)
        outs[3] += dot(grad, in_other, NT)
        target = send if r % 2 else keep
        target[r // 2, 0] = grad
        target[r // 2, 1] = act
    branch[...] = whole(outs[0], outs[1], first)
    second = whole(outs[2], outs[3], first)
    norm_grads[0:1] = jnp.sum(second * hat, axis=0, keepdims=True)
    norm_grads[1:2] = jnp.sum(second, axis=0, keepdims=True)
    input_part[...] = norm_back(second, hat, root, norms[2:3])


def both_cores(scal, x, x_beside, cot, cot_beside, norms, at):
    first = scal[0] == 0
    tokens = jnp.concatenate([x[...], x_beside[...]], axis=0).astype(jnp.float32)
    hat, _ = normalized(tokens)
    h = (hat * norms[at : at + 1] + norms[at + 1 : at + 2]).astype(jnp.bfloat16)
    c = jnp.concatenate([cot[...], cot_beside[...]], axis=0)
    return list(zip(halves(h, first), halves(c, first)))


def unit_grads_kernel(
    scal, x, x_beside, cot, cot_beside, norms, keep, came, in_keep, in_send, down_keep, down_send
):
    for side, (h, c) in enumerate(both_cores(scal, x, x_beside, cot, cot_beside, norms, 2)):
        for far in range(2):
            grad = jnp.concatenate([keep[far, 0], came[far, 0]], axis=0)
            act = jnp.concatenate([keep[far, 1], came[far, 1]], axis=0)
            (in_send if side else in_keep)[far] = dot(h, grad, TN).astype(jnp.bfloat16)
            (down_send if far else down_keep)[side] = dot(c, act, TN).astype(jnp.bfloat16)


def combine_kernel(in_keep, in_came, down_keep, down_came, own, in_send, down_send):
    pairs = ((in_keep, in_came, in_send), (down_keep, down_came, down_send))
    for k, (keep, came, send) in enumerate(pairs):
        total = keep[...].astype(jnp.float32) + came[...].astype(jnp.float32)
        own[k] = total[0].astype(jnp.bfloat16)
        send[0] = total[1].astype(jnp.bfloat16)


def turn_kernel(scal, cosine, sine, back, keep, send, sums):
    low = low_lanes(keep.shape[1])
    for r in range(4):
        head = scal[1] ^ r
        grads = jnp.concatenate([back[head], back[4 + head]], axis=0)
        left = turned(grads[:, :128].astype(jnp.float32), cosine[...], -sine[...])
        left = left.astype(jnp.bfloat16)
        right = grads[:, 128:]
        target = send if r % 2 else keep
        target[r // 2, :, :128] = left
        target[r // 2, :, 128:] = right
        right = jnp.where(low, right.astype(jnp.float32), 0.0)
        wide = jnp.concatenate([left.astype(jnp.float32), right], axis=1)
        sums[pl.ds(head, 1), :] = jnp.sum(wide, axis=0, keepdims=True)


def split_last(piece):
    wide = piece.astype(jnp.float32)
    lane = lax.broadcasted_iota(jnp.int32, (1, wide.shape[1]), 1)
    share = (lane < 3 * HD).astype(jnp.float32)
    pre_grad = (wide * share).astype(jnp.bfloat16)
    attended = (wide * (1.0 - share)).astype(jnp.bfloat16)
    return pre_grad, attended


def head_grads_kernel(
    scal, x, x_beside, cot, cot_beside, norms, keep, came, totals, totals_came, *outs
):
    both = (totals[...] + totals_came[...]).reshape(64, 256)
    coarse = both.astype(jnp.bfloat16)
    fine = (both - coarse.astype(jnp.float32)).astype(jnp.bfloat16)
    sides = both_cores(scal, x, x_beside, cot, cot_beside, norms, 0)
    for far in range(2):
        piece = jnp.concatenate([keep[far], came[far]], axis=0)
        pre_grad, attended = split_last(piece)
        for side, (h, c) in enumerate(sides):
            grad = dot(h, pre_grad, TN) + dot(c, attended, TN)
            target = outs[2 * far + side]
            target[0:512] = grad.astype(jnp.bfloat16)
            target[512:576] = coarse
            target[576:640] = fine


def gather_kernel(
    scal, x, norms, keep, send, weights, r0, r1, r2, r3, ff_branch, ff_part,
    norm_two, cot_sums, unit_sums, qkv_sums, near, far, totals, parts,
):
    first = scal[0] == 0
    hat, root = normalized(x[...].astype(jnp.float32))
    outs = [0.0] * 4
    for r, other in enumerate((r0, r1, r2, r3)):
        mine, theirs = weights[scal[1] ^ r], other[0]
        pre_grad, attended = split_last((send if r % 2 else keep)[r // 2])
        outs[0] += dot(attended, mine, NT)
        outs[1] += dot(attended, theirs, NT)
        outs[2] += dot(pre_grad, mine, NT)
        outs[3] += dot(pre_grad, theirs, NT)
    branch = ff_branch[...] + whole(outs[0], outs[1], first)
    grad = whole(outs[2], outs[3], first)
    totals[...] = jnp.zeros_like(totals)
    rows = [jnp.sum(grad * hat, axis=0, keepdims=True), jnp.sum(grad, axis=0, keepdims=True)]
    rows += [norm_two[0:1], norm_two[1:2], cot_sums[...]]
    for i, row in enumerate(rows):
        for q in range(4):
            at = 4 * (i % 2) + q
            totals[i // 2, at : at + 1, :] = row[:, 256 * q : 256 * q + 256]
    totals[3 + scal[2], 0:4, :] = qkv_sums[...]
    totals[3 + scal[2], 4:8, :] = unit_sums[...]
    input_part = ff_part[...] + norm_back(grad, hat, root, norms[0:1])
    for q in range(4):
        parts[q, 0] = branch[64 * q : 64 * q + 64].astype(jnp.bfloat16)
        parts[q, 1] = input_part[64 * q : 64 * q + 64].astype(jnp.bfloat16)
    for r in range(4):
        (far if r % 2 else near)[r // 2] = parts[scal[2] ^ r]


def finish_rows_kernel(scal, x, cot, bias, r0, r1, r2, r3, block_output, input_grad):
    for r, piece in enumerate((r0, r1, r2, r3)):
        q = scal[2] ^ r
        block_output[q] = x[q].astype(jnp.float32) + piece[0].astype(jnp.float32) + bias[...]
        input_grad[q] = cot[q].astype(jnp.float32) + piece[1].astype(jnp.float32)


def gram_of_piece(total, momenta, grads, grams):
    short = total.astype(jnp.bfloat16)
    grads[0] = short
    update = 1.95 * short.astype(jnp.float32) + 0.9025 * momenta[0]
    gram = dot(update, update, TN, lax.Precision.HIGHEST)
    for j in range(4):
        cut = slice(j * HD, (j + 1) * HD)
        grams[0, j] = gram[cut, cut]


def unit_gram_kernel(place, own, in_came, down_came, momenta, near, came, *refs):
    grads, grams, first, second = refs[-4:]

    @pl.when(pl.program_id(0) == 0)
    def _():
        add_up([((near, came), [first, second])])

    a = in_came[0].astype(jnp.float32)
    b = down_came[0].astype(jnp.float32)
    other = jnp.where(pl.program_id(0) == 0, a, b)
    gram_of_piece(own[0].astype(jnp.float32) + other, momenta, grads, grams)


def head_gram_kernel(place, own, a, b, c, momenta, *refs):
    grads, grams, totals = refs[-3:]
    values = [part[...].astype(jnp.float32) for part in (own, a, b, c)]
    total = (values[0] + values[1]) + (values[2] + values[3])
    gram_of_piece(total[0:512], momenta, grads, grams)
    sums = [v[512:576] + v[576:640] for v in values]
    totals[...] = ((sums[0] + sums[1]) + (sums[2] + sums[3])).reshape(8, 8, 256)


def gram_of(kernel, first, others, momenta, place, more, shapes, after=()):
    chunks = momenta.shape[0] // 4
    piece = pl.BlockSpec((1, 512, 256), lambda i, s: (i, 0, 0))
    block = pl.BlockSpec((1, 512, 256), lambda i, s: (4 * i + s[1], 0, 0))
    return pl.pallas_call(
        kernel,
        grid_spec=pltpu.PrefetchScalarGridSpec(
            num_scalar_prefetch=1,
            grid=(chunks,),
            in_specs=[piece if first.ndim == 3 else full(first)]
            + [full(other) for other in others]
            + [block]
            + [full(part) for part in more]
            + [corner(a) for a in after],
            out_specs=[piece, pl.BlockSpec((1, 4, HD, HD), lambda i, s: (i, 0, 0, 0))]
            + [full(shape) for shape in shapes],
        ),
        out_shape=[
            jax.ShapeDtypeStruct((chunks, 512, 256), jnp.bfloat16),
            jax.ShapeDtypeStruct((chunks, 4, HD, HD), jnp.float32),
            *map(out_hbm, shapes),
        ],
        compiler_params=limits(20),
        cost_estimate=takes(2.5),
        name="gram",
    )(place, *map(in_hbm, [first, *others, momenta, *more, *after]))


def newton_kernel(counts, mine, theirs, *refs):
    taken = sum(counts)
    out = refs[taken]
    add_up(grouped(refs, counts, refs[taken + 1 :]))
    linear, square, cubic = quintic
    shape = (HD, HD)
    eye = lax.broadcasted_iota(jnp.int32, shape, 0) == lax.broadcasted_iota(jnp.int32, shape, 1)
    full = lax.Precision.HIGHEST
    chunks = mine.shape[0]
    places = [(i, j) for i in range(chunks) for j in range(4)]
    states = []
    for i, j in places:
        gram = mine[i, j] + theirs[i, j]
        trace = jnp.sum(jnp.where(eye, gram, 0.0), axis=(0, 1), keepdims=True)
        scale = 1.0 / (jnp.sqrt(trace) + muon_epsilon)
        states.append([gram * scale * scale, None, scale])
    for iteration in range(NEWTON):
        squares = [dot(s[0], s[0], precision=full) for s in states]
        steps = [
            jnp.where(eye, linear, 0.0) + square * s[0] + cubic * sq
            for s, sq in zip(states, squares)
        ]
        if iteration == 0:
            halfway = [dot(s[0], m, precision=full) for s, m in zip(states, steps)]
            for s, m in zip(states, steps):
                s[1] = m
        elif iteration < NEWTON - 1:
            both = [
                dot(jnp.concatenate([s[0], s[1]], axis=0), m, precision=full)
                for s, m in zip(states, steps)
            ]
            halfway = [x[:HD] for x in both]
            for s, x in zip(states, both):
                s[1] = x[HD:]
        else:
            for s, m in zip(states, steps):
                s[1] = dot(s[1], m, precision=full)
        if iteration < NEWTON - 1:
            for s, x, m in zip(states, halfway, steps):
                s[0] = dot(x, m, precision=full)
    for (i, j), s in zip(places, states):
        mix = s[1] * s[2]
        coarse = mix.astype(jnp.bfloat16)
        fine = (mix - coarse.astype(jnp.float32)).astype(jnp.bfloat16)
        out[i, j] = jnp.concatenate([coarse, fine], axis=1)


def newton(mine, theirs, sums, after=()):
    flat = [part for group in sums for part in group]
    operands = [mine, theirs, *flat]
    return launch(
        functools.partial(newton_kernel, [len(group) for group in sums]),
        operands,
        [jax.ShapeDtypeStruct((*mine.shape[:-1], 2 * HD), jnp.bfloat16)]
        + [jax.ShapeDtypeStruct(group[0].shape, group[0].dtype) for group in sums],
        "newton",
        cost=3.5,
        specs=[full(a) for a in operands],
        after=after,
    )


def update_kernel(
    n, head, scal, g0, g1, g2, g3, q0, q1, q2, q3, momenta, native_momenta, native, *refs
):
    grads, weights, moved, mixing, first, second, steps = refs[-7:]
    place_of = members_of(head)

    @pl.when((pl.program_id(0) == 0) & (pl.program_id(1) == 0))
    def _():
        mixing[...] = jnp.zeros_like(mixing)

    @pl.when(pl.program_id(1) == 0)
    def _():
        for r, q in enumerate((q0, q1, q2, q3)):
            for j in range(4):
                wide = q[0, j].astype(jnp.float32)
                other = pltpu.roll(wide, HD, 1)
                below = low_lanes(HD) == (j % 2 == 0)
                rows = slice(j * HD, (j + 1) * HD)
                lanes = slice(128 * (j // 2), 128 * (j // 2) + 128)
                pair = (wide, other) if j % 2 == 0 else (other, wide)
                for level in range(2):
                    part = jnp.where(below, pair[level], 0.0)
                    mixing[r, level, rows, lanes] = part.astype(jnp.bfloat16)

    low = low_lanes(n)
    for r, piece in enumerate((g0, g1, g2, g3)):
        place = scal[1] ^ r
        grad = piece[0].astype(jnp.float32)
        update = 1.95 * grad + 0.9025 * momenta[place]
        coarse = update.astype(jnp.bfloat16)
        fine = (update - coarse.astype(jnp.float32)).astype(jnp.bfloat16)
        settled = dot(coarse, mixing[r, 0]) + dot(coarse, mixing[r, 1]) + dot(fine, mixing[r, 0])
        for half in range(2):
            k = 2 * r + half
            first[k] = grad[:, half * 128 : (half + 1) * 128]
            second[k] = settled[:, half * 128 : (half + 1) * 128]
            for source, target in ((first, grads), (second, steps)):
                even = source[k, pl.ds(0, n, stride=2), :]
                odd = source[k, pl.ds(1, n, stride=2), :]
                lines = (
                    jnp.where(low, even, pltpu.roll(odd, 64, 1)),
                    jnp.where(low, pltpu.roll(even, 64, 1), odd),
                )
                for w in range(2):
                    group, line = place_of(place, 2 * half + w)
                    target[group, pl.ds(line, n, stride=8), :] = lines[w]
    moved[...] = momentum_decay * native_momenta[...] + grads[...]
    weight = native[...]
    weights[...] = weight - muon_rate * (4.0 * steps[...] + weight_decay * weight)


def update(first, scal, grads, mixes, momenta, native_momenta, native, before=(), after=(), n=64):
    chunks = grads[0].shape[0]
    block = pl.BlockSpec((2, 8 * n, 128), lambda k, i: (first + k, i, 0))
    piece = pl.BlockSpec((1, 2 * n, 256), lambda k, i: (k, i, 0))
    mix = pl.BlockSpec((1, 4, HD, 2 * HD), lambda k, i: (k, 0, 0, 0))
    return launch(
        functools.partial(update_kernel, n, first == 0),
        [scal, *grads, *mixes, momenta, native_view(native_momenta), native_view(native), *before],
        [jax.ShapeDtypeStruct((6, 2048, 128), jnp.float32)] * 3,
        "update",
        specs=[mem(pltpu.SMEM)]
        + [piece] * 4
        + [mix] * 4
        + [pl.BlockSpec((4, 2 * n, 256), lambda k, i: (k, i, 0)), block, block]
        + [mem(pl.ANY)] * len(before),
        after=after,
        cost=5.5 * chunks,
        grid=(chunks, 256 // n),
        out_specs=[block] * 3,
        scratch_shapes=[
            pltpu.VMEM((4, 2, 256, 256), jnp.bfloat16),
            pltpu.VMEM((8, 2 * n, 128), jnp.float32),
            pltpu.VMEM((8, 2 * n, 128), jnp.float32),
            pltpu.VMEM((2, 8 * n, 128), jnp.float32),
        ],
        input_output_aliases={12 + i: i for i in range(len(before))},
    )


def whole_device(
    inputs, cotangent, matrices, momenta, small, small_first, small_second, segments, positions
):
    blk_at = lax.axis_index("blk")
    ctx_at = lax.axis_index("ctx")
    tp_at = lax.axis_index("tp")
    scal = jnp.stack([blk_at, ctx_at, tp_at]).astype(jnp.int32)
    sequences, local_rows, width = inputs.shape
    tokens = sequences * local_rows
    both = ("blk", "ctx")
    f32, bf16 = jnp.float32, jnp.bfloat16
    shaped = jax.ShapeDtypeStruct

    def hop(values, by):
        return lax.ppermute(values, both, [(i, i ^ by) for i in range(8)])

    def hop_tp(values, by):
        return lax.ppermute(values, "tp", [(i, i ^ by) for i in range(4)])

    def spread(piece):
        c = hop(piece, 2)
        return [piece, hop(piece, 1), c, hop(c, 1)]

    x = inputs.reshape(tokens, width)
    cot = cotangent.reshape(tokens, width)
    norms = small[: 4 * width].reshape(4, width)
    qkv_start = 6 * width + tp_at * 4 * 3 * HD
    qkv_bias = lax.dynamic_slice_in_dim(small, qkv_start, 4 * 3 * HD).reshape(4, 3 * HD)
    qkv_bias = jnp.pad(qkv_bias, ((0, 0), (0, HD)))
    unit_start = 6 * width + H * 3 * HD + tp_at * 1024
    unit_bias = lax.dynamic_slice_in_dim(small, unit_start, 1024).reshape(4, 256)
    lane = jnp.arange(128) % HD
    frequency = rope_base ** (-2.0 * (lane % 8).astype(f32) / ROTARY)
    angles = positions.astype(f32).reshape(tokens, 1) * frequency
    cosine = jnp.where(lane < ROTARY, jnp.cos(angles), 1.0)
    sign = jnp.where(lane < 8, -1.0, jnp.where(lane < ROTARY, 1.0, 0.0))
    sine = jnp.sin(angles) * sign

    head_weights, mine = relayout(scal, matrices, bf16, 0, 1, mine=True)
    first_hop = hop(mine, 4)
    other_heads = spread(first_hop)
    unit_weights, mine_units = relayout(scal, matrices, bf16, 1, 2, mine=True, after=(mine,))
    (piled_heads,) = relayout(scal, momenta, f32, 0, 1, after=(mine_units,))
    first_hop, mine_units, cosine, sine, _ = lax.optimization_barrier(
        (first_hop, mine_units, cosine, sine, piled_heads)
    )
    other_units = spread(hop(mine_units, 4))
    x_beside = hop(x, 1)
    cot_beside = hop(cot, 1)

    send = launch(
        project_kernel,
        [scal, x, cot, norms, qkv_bias, cosine, sine, head_weights]
        + [piece[0] for piece in other_heads],
        shaped((8, local_rows, 256), bf16),
        "project",
    )
    arrived = lax.all_to_all(send, both, split_axis=0, concat_axis=0, tiled=True)
    (piled_units,) = relayout(scal, momenta, f32, 1, 2, after=(send,))
    documents = lax.dynamic_index_in_dim(segments, blk_at, 0, keepdims=False)
    length = documents.shape[0]
    attended = launch(
        attention_kernel,
        [arrived.reshape(length, 256), documents.reshape(length, 1)],
        shaped((length, 256), bf16),
        "attention",
        cost=6,
        specs=[full(arrived.reshape(length, 256)), pl.BlockSpec((length, 1), lambda *_: (0, 0))],
        scratch_shapes=[pltpu.VMEM((length, HD), f32)] * 2,
    )
    back = lax.all_to_all(
        attended.reshape(8, local_rows, 256), both, split_axis=0, concat_axis=0, tiled=True
    )

    ff_branch, ff_part, unit_keep, unit_send, unit_sums, norm_two, cot_sums = launch(
        feed_forward_kernel,
        [scal, x, cot, norms, unit_bias, unit_weights, *other_units],
        [
            shaped((tokens, width), f32),
            shaped((tokens, width), f32),
            shaped((2, 2, tokens, 256), bf16),
            shaped((2, 2, tokens, 256), bf16),
            shaped((4, 256), f32),
            shaped((2, width), f32),
            shaped((1, width), f32),
        ],
        "feed_forward",
        cost=5.5,
        after=(attended,),
    )
    head_keep, head_send, qkv_sums = launch(
        turn_kernel,
        [scal, cosine, sine, back],
        [shaped((2, tokens, 256), bf16)] * 2 + [shaped((4, 256), f32)],
        "turn",
        cost=2,
        after=(unit_sums,),
    )
    in_keep, in_send, down_keep, down_send = launch(
        unit_grads_kernel,
        [scal, x, x_beside, cot, cot_beside, norms, unit_keep, hop(unit_send, 1)],
        [shaped((2, 512, 256), bf16)] * 4,
        "unit_grads",
        cost=3.5,
        after=(qkv_sums,),
    )
    sums = [norm_two, cot_sums, unit_sums, qkv_sums]
    near, far, totals = launch(
        gather_kernel,
        [scal, x, norms, head_keep, head_send, head_weights, *other_heads, ff_branch, ff_part, *sums],
        [shaped((2, 2, 64, width), bf16)] * 2 + [shaped((8, 8, 256), f32)],
        "gather",
        after=(in_keep,),
        scratch_shapes=[pltpu.VMEM((4, 2, 64, width), bf16)],
    )
    head_grads = launch(
        head_grads_kernel,
        [scal, x, x_beside, cot, cot_beside, norms, head_keep, hop(head_send, 1), totals, hop(totals, 1)],
        [shaped((640, 256), bf16)] * 4,
        "head_grads",
        cost=4,
    )
    operands = [in_keep, hop(in_send, 4), down_keep, hop(down_send, 2)]
    own, in_send, down_send = launch(
        combine_kernel,
        operands,
        [shaped((2, 512, 256), bf16)] + [shaped((1, 512, 256), bf16)] * 2,
        "combine",
        specs=[full(a) for a in operands],
        cost=2,
        after=(head_grads[0],),
    )
    unit_sum, unit_grams, kept, passed = gram_of(
        unit_gram_kernel,
        own,
        [hop(in_send, 2), hop(down_send, 4)],
        piled_units,
        scal,
        [near, hop_tp(far, 1)],
        [shaped((2, 64, width), bf16)] * 2,
    )
    unit_pieces = spread(unit_sum)
    unit_mix, total = newton(unit_grams, hop(unit_grams, 4), [(kept, hop_tp(passed, 2))])
    head_sum, head_grams, totals = gram_of(
        head_gram_kernel,
        head_grads[0],
        [hop(head_grads[1], 4), hop(head_grads[2], 2), hop(head_grads[3], 6)],
        piled_heads,
        scal,
        [],
        [shaped((8, 8, 256), f32)],
    )
    head_pieces = spread(head_sum)
    head_mix, totals = newton(
        head_grams, hop(head_grams, 4), [(totals, hop_tp(totals, 1))], after=(unit_mix,)
    )
    before = update(1, scal, unit_pieces, spread(unit_mix), piled_units, momenta, matrices)
    outs = update(0, scal, head_pieces, spread(head_mix), piled_heads, momenta, matrices, before)
    totals = totals + hop_tp(totals, 2)

    beside = hop_tp(total, 2)
    block_output, input_grad = launch(
        finish_rows_kernel,
        [
            scal,
            x.reshape(4, 64, width),
            cot.reshape(4, 64, width),
            (small[4 * width : 5 * width] + small[5 * width : 6 * width]).reshape(1, width),
            total,
            hop_tp(total, 1),
            beside,
            hop_tp(beside, 1),
        ],
        [shaped((4, 64, width), f32)] * 2,
        "finish_rows",
        cost=2,
    )

    cot_total = totals[2, :4].reshape(-1) * 0.25
    small_grads = jnp.concatenate(
        [
            totals[:2].reshape(-1),
            cot_total,
            cot_total,
            totals[3:7, :4, : 3 * HD].reshape(-1),
            totals[3:7, 4:].reshape(-1),
        ]
    )
    return (
        block_output.reshape(inputs.shape),
        input_grad.reshape(inputs.shape),
        native_back(outs[0]),
        native_back(outs[1]),
        native_back(outs[2]),
        small_grads,
        *small_step(small, small_first, small_second, small_grads),
    )


def small_step(small, small_first, small_second, small_grads):
    new_first = adam_first * small_first + (1.0 - adam_first) * small_grads
    new_second = adam_second * small_second + (1.0 - adam_second) * small_grads * small_grads
    corrected = new_first / (1.0 - adam_first**STEP)
    spread = jnp.sqrt(new_second / (1.0 - adam_second**STEP))
    new_small = small - small_rate * corrected / (spread + adam_epsilon)
    return new_first, new_second, new_small


def solution(mesh):
    in_specs = (
        P(None, ("blk", "ctx"), None),
        P(None, ("blk", "ctx"), None),
        P("tp", "blk"),
        P("tp", "blk"),
        P(),
        P(),
        P(),
        P(),
        P(None, ("blk", "ctx")),
    )
    out_specs = (
        P(None, ("blk", "ctx"), None),
        P(None, ("blk", "ctx"), None),
        P("tp", "blk"),
        P("tp", "blk"),
        P("tp", "blk"),
        P(),
        P(),
        P(),
        P(),
    )
    one_each = mesh.shape["blk"] == SEQS and mesh.shape["ctx"] * mesh.shape["tp"] == H
    one_each = one_each and mesh.shape["tp"] == 4
    return jax.shard_map(
        whole_device if one_each else on_device, mesh=mesh, in_specs=in_specs, out_specs=out_specs, check_vma=False
    )
```

```python
import functools

import jax
import jax.numpy as jnp
from jax import lax
from jax.experimental import pallas as pl
from jax.experimental.pallas import tpu as pltpu
from jax.sharding import PartitionSpec as P

MODEL_DIM = 1024
H = 16
HD = 64
FF = 4096
ROTARY = 16
NEWTON = 5
STEP = 10
SEQS = 2


norm_epsilon = 1e-05
rope_base = 10000.0
masked_score = -1e30
momentum_decay = 0.95
muon_rate = 0.2
weight_decay = 0.01
muon_epsilon = 1e-07
quintic = (3.4445, -4.775, 2.0315)
adam_first = 0.9
adam_second = 0.95
adam_epsilon = 1e-08
small_rate = 0.2


def passed_along(x, axis, by):
    devices = lax.axis_size(axis)
    pairs = [(i, i + by) for i in range(devices) if 0 <= i + by < devices]
    return lax.ppermute(x, axis, pairs)


def shifted(x, axis, by):
    devices = lax.axis_size(axis)
    return lax.ppermute(x, axis, [(i, (i + by) % devices) for i in range(devices)])


def as_sent(x):

    def short(part):
        return part.astype(jnp.bfloat16) if part.dtype == jnp.float32 else part

    return jax.tree.map(short, x)


def layer_norm(values, scaling, offset):
    centre = jnp.mean(values, axis=-1, keepdims=True)
    centred = values - centre
    spread = jnp.mean(centred * centred, axis=-1, keepdims=True)
    return centred * lax.rsqrt(spread + norm_epsilon) * scaling + offset


def rope_tables(positions):
    halfway = ROTARY // 2
    frequency = rope_base ** (-2.0 * jnp.arange(halfway, dtype=jnp.float32) / ROTARY)
    angles = positions.astype(jnp.float32)[..., None] * frequency
    return (jnp.cos(angles)[:, :, None, :], jnp.sin(angles)[:, :, None, :])


def rotate(values, cosine, sine):
    halfway = ROTARY // 2
    former = values[..., :halfway]
    latter = values[..., halfway:ROTARY]
    return jnp.concatenate(
        [former * cosine - latter * sine, latter * cosine + former * sine, values[..., ROTARY:]],
        axis=-1,
    )


def exact_gelu(values):
    return jax.nn.gelu(values, approximate=False)


def newton_schulz(blocks):
    frobenius = jnp.sqrt(jnp.sum(blocks * blocks, axis=(1, 2), keepdims=True))
    current = blocks / (frobenius + muon_epsilon)
    linear_term, square_term, cubic_term = quintic
    for iteration in range(NEWTON):
        gram_matrix = jnp.einsum("mde,mdf->mef", current, current, precision=lax.Precision.HIGHEST)
        polynomial = square_term * gram_matrix + cubic_term * jnp.einsum(
            "mef,mfg->meg", gram_matrix, gram_matrix, precision=lax.Precision.HIGHEST
        )
        current = linear_term * current + jnp.einsum(
            "mde,mef->mdf", current, polynomial, precision=lax.Precision.HIGHEST
        )
    return current


def to_heads(values):
    return lax.all_to_all(values, "ctx", split_axis=3, concat_axis=1, tiled=True)


def to_positions(values):
    return lax.all_to_all(values, "ctx", split_axis=1, concat_axis=3, tiled=True)


def pass_keys(pair):
    return passed_along(pair, "blk", 1)


def pass_grads(pair_grad):
    return shifted(pair_grad.astype(jnp.bfloat16), "blk", 1).astype(pair_grad.dtype)


def allowed_pairs(segments, query_block, key_block, block_rows):
    query_place = query_block * block_rows + jnp.arange(block_rows, dtype=jnp.int32)
    key_place = key_block * block_rows + jnp.arange(block_rows, dtype=jnp.int32)
    query_doc = lax.dynamic_slice_in_dim(segments, query_block * block_rows, block_rows, 1)
    key_doc = lax.dynamic_slice_in_dim(segments, key_block * block_rows, block_rows, 1)
    causal = key_place[None, :] <= query_place[:, None]
    return (causal[None] & (query_doc[:, :, None] == key_doc[:, None, :]))[:, None]


def masked_scores(queries, keys, allowed):
    score_scale = HD ** (-0.5)
    scores = (
        jnp.einsum("sqhe,skhe->shqk", queries, keys, preferred_element_type=jnp.float32)
        * score_scale
    )
    return jnp.where(allowed, scores, masked_score)


def on_device(
    inputs, cotangent, matrices, momenta, small, small_first, small_second, segments, positions
):
    tensor_size = lax.axis_size("tp")
    cycle_size = lax.axis_size("blk")
    context_size = lax.axis_size("ctx")
    tensor_index = lax.axis_index("tp")
    cycle_index = lax.axis_index("blk")
    sequences, local_rows, model_width = inputs.shape
    per_group = matrices.shape[0]
    head_count = H // tensor_size
    unit_blocks = FF // HD // tensor_size
    block_rows = local_rows * context_size
    gathered = lax.all_gather(matrices.astype(jnp.bfloat16), "blk", axis=1, tiled=True).reshape(
        per_group, model_width, HD
    )
    query_key_value_weight = gathered[: 3 * head_count]
    projection_out_weight = gathered[3 * head_count : 4 * head_count]
    input_weight = gathered[4 * head_count : 4 * head_count + unit_blocks]
    down_projection_weight = gathered[4 * head_count + unit_blocks :]
    qkv_start = 6 * model_width + tensor_index * head_count * 3 * HD
    query_key_value_bias = lax.dynamic_slice_in_dim(small, qkv_start, head_count * 3 * HD).reshape(
        head_count, 3, HD
    )
    unit_start = 6 * model_width + H * 3 * HD + tensor_index * unit_blocks * HD
    hidden_unit_bias = lax.dynamic_slice_in_dim(small, unit_start, unit_blocks * HD).reshape(
        unit_blocks, HD
    )
    residual = inputs.astype(jnp.float32)

    def both_norms(values, gain_one, offset_one, gain_two, offset_two):
        return (layer_norm(values, gain_one, offset_one), layer_norm(values, gain_two, offset_two))

    (normed_one, normed_two), norm_back = jax.vjp(
        both_norms,
        residual,
        small[0:model_width],
        small[model_width : 2 * model_width],
        small[2 * model_width : 3 * model_width],
        small[3 * model_width : 4 * model_width],
    )
    first_input = normed_one.astype(jnp.bfloat16)
    second_input = normed_two.astype(jnp.bfloat16)
    projected = jnp.einsum(
        "pgk,jka->pgja", first_input, query_key_value_weight, preferred_element_type=jnp.float32
    )
    projected = projected.reshape(sequences, local_rows, 3, head_count, HD) + jnp.transpose(
        query_key_value_bias, (1, 0, 2)
    )
    cosine, sine = rope_tables(positions)

    def turn_pair(query_pre, key_pre):
        return (rotate(query_pre, cosine, sine), rotate(key_pre, cosine, sine))

    (query_turned, key_turned), turn_back = jax.vjp(
        turn_pair, projected[:, :, 0], projected[:, :, 1]
    )
    stacked = jnp.stack([query_turned, key_turned, projected[:, :, 2]], axis=2).astype(jnp.bfloat16)
    by_heads = to_heads(stacked)
    queries = by_heads[:, :, 0]
    head_local = queries.shape[2]

    def forward_visit(state, pair, source):
        row_max, row_total, weighted = state
        allowed = allowed_pairs(segments, cycle_index, source, block_rows)
        scores = masked_scores(queries, pair[:, :, 0], allowed)
        new_max = jnp.maximum(row_max, jnp.max(scores, axis=-1))
        weights = jnp.where(allowed, jnp.exp(scores - new_max[..., None]), 0.0)
        rescale = jnp.exp(row_max - new_max)
        row_total = row_total * rescale + jnp.sum(weights, axis=-1)
        weighted = weighted * rescale[..., None] + jnp.einsum(
            "shqk,skhe->shqe",
            weights.astype(jnp.bfloat16),
            pair[:, :, 1],
            preferred_element_type=jnp.float32,
        )
        return (new_max, row_total, weighted)

    def forward_hop(hop_index, carry):
        pair, state = carry
        source = (cycle_index - hop_index) % cycle_size
        state = forward_visit(state, pair, source)
        return (pass_keys(pair), state)

    start_state = (
        jnp.full((sequences, head_local, block_rows), masked_score, jnp.float32),
        jnp.zeros((sequences, head_local, block_rows), jnp.float32),
        jnp.zeros((sequences, head_local, block_rows, HD), jnp.float32),
    )
    pair, state = lax.fori_loop(0, cycle_size - 1, forward_hop, (by_heads[:, :, 1:], start_state))
    row_max, row_total, weighted = forward_visit(state, pair, (cycle_index + 1) % cycle_size)
    log_total = row_max + jnp.log(row_total)
    attended_rows = jnp.transpose(weighted / row_total[..., None], (0, 2, 1, 3))
    attention_result = to_positions(attended_rows.astype(jnp.bfloat16)[:, :, None])[:, :, 0]
    attention_branch = jnp.einsum(
        "roxu,xcu->roc", attention_result, projection_out_weight, preferred_element_type=jnp.float32
    )
    hidden_preactivation = (
        jnp.einsum("ptr,kra->ptka", second_input, input_weight, preferred_element_type=jnp.float32)
        + hidden_unit_bias
    )
    activated_hidden, gelu_back = jax.vjp(exact_gelu, hidden_preactivation)
    activated_reduced = activated_hidden.astype(jnp.bfloat16)
    perceptron_branch = jnp.einsum(
        "xkzp,zop->xko",
        activated_reduced,
        down_projection_weight,
        preferred_element_type=jnp.float32,
    )
    branches = lax.psum((attention_branch + perceptron_branch).astype(jnp.bfloat16), "tp").astype(
        jnp.float32
    )
    block_output = (
        residual
        + branches
        + small[4 * model_width : 5 * model_width]
        + small[5 * model_width : 6 * model_width]
    )
    act_grad = jnp.einsum(
        "ptr,kra->ptka", cotangent, down_projection_weight, preferred_element_type=jnp.float32
    )
    hidden_gradient = gelu_back(act_grad)[0].astype(jnp.bfloat16)
    down_grad = jnp.einsum(
        "gup,guzb->zpb", cotangent, activated_reduced, preferred_element_type=jnp.float32
    )
    in_grad = jnp.einsum(
        "gup,guzb->zpb", second_input, hidden_gradient, preferred_element_type=jnp.float32
    )
    second_grad = jnp.einsum(
        "xkzp,zop->xko", hidden_gradient, input_weight, preferred_element_type=jnp.float32
    )
    attended_grad = jnp.einsum(
        "pgk,jka->pgja", cotangent, projection_out_weight, preferred_element_type=jnp.float32
    ).astype(jnp.bfloat16)
    outproj_grad = jnp.einsum(
        "ztu,ztqi->qui", cotangent, attention_result, preferred_element_type=jnp.float32
    )
    grad_heads = to_heads(attended_grad[:, :, None])[:, :, 0]
    row_delta = jnp.transpose(
        jnp.sum(grad_heads.astype(jnp.float32) * attended_rows, axis=-1), (0, 2, 1)
    )

    def backward_visit(query_grad, pair, source):
        allowed = allowed_pairs(segments, cycle_index, source, block_rows)
        scores = masked_scores(queries, pair[:, :, 0], allowed)
        probabilities = jnp.where(allowed, jnp.exp(scores - log_total[..., None]), 0.0)
        value_grad = jnp.einsum(
            "shqk,sqhe->skhe",
            probabilities.astype(jnp.bfloat16),
            grad_heads,
            preferred_element_type=jnp.float32,
        )
        prob_grad = jnp.einsum(
            "sqhe,skhe->shqk", grad_heads, pair[:, :, 1], preferred_element_type=jnp.float32
        )
        score_grad = (probabilities * (prob_grad - row_delta[..., None])).astype(jnp.bfloat16)
        score_scale = HD ** (-0.5)
        query_grad = (
            query_grad
            + jnp.einsum(
                "shqk,skhe->sqhe", score_grad, pair[:, :, 0], preferred_element_type=jnp.float32
            )
            * score_scale
        )
        key_grad = (
            jnp.einsum("shqk,sqhe->skhe", score_grad, queries, preferred_element_type=jnp.float32)
            * score_scale
        )
        return (query_grad, jnp.stack([key_grad, value_grad], axis=2))

    def backward_hop(hop_index, carry):
        pair, pair_grad, query_grad = carry
        source = (cycle_index - hop_index) % cycle_size
        query_grad, visit_grad = backward_visit(query_grad, pair, source)
        return (pass_keys(pair), pass_grads(pair_grad + visit_grad), query_grad)

    zero_pair = jnp.zeros(by_heads[:, :, 1:].shape, jnp.float32)
    pair, pair_grad, query_grad = lax.fori_loop(
        0,
        cycle_size - 1,
        backward_hop,
        (by_heads[:, :, 1:], zero_pair, jnp.zeros(queries.shape, jnp.float32)),
    )
    query_grad, visit_grad = backward_visit(query_grad, pair, (cycle_index + 1) % cycle_size)
    pair_grad = pass_grads(pair_grad + visit_grad)
    head_grads = jnp.concatenate([query_grad[:, :, None], pair_grad], axis=2).astype(jnp.bfloat16)
    position_grads = to_positions(head_grads).astype(jnp.float32)
    query_pre_grad, key_pre_grad = turn_back((position_grads[:, :, 0], position_grads[:, :, 1]))
    projected_grad = jnp.stack(
        [query_pre_grad, key_pre_grad, position_grads[:, :, 2]], axis=2
    ).astype(jnp.bfloat16)
    flattened_gradient = projected_grad.reshape(sequences, local_rows, 3 * head_count, HD)
    query_key_value_gradient = jnp.einsum(
        "ztu,ztqi->qui", first_input, flattened_gradient, preferred_element_type=jnp.float32
    )
    first_grad = jnp.einsum(
        "roxu,xcu->roc",
        flattened_gradient,
        query_key_value_weight,
        preferred_element_type=jnp.float32,
    )
    input_part, gain_one_grad, offset_one_grad, gain_two_grad, offset_two_grad = norm_back(
        (first_grad, second_grad)
    )
    input_grad = cotangent.astype(jnp.float32) + lax.psum(
        input_part.astype(jnp.bfloat16), "tp"
    ).astype(jnp.float32)
    owner_share = jnp.where(tensor_index == 0, 1.0, 0.0).astype(jnp.float32)
    bias_grad = jnp.sum(cotangent.astype(jnp.float32), axis=(0, 1)) * owner_share
    qkv_bias_grad = jnp.transpose(
        jnp.sum(projected_grad.astype(jnp.float32), axis=(0, 1)), (1, 0, 2)
    ).reshape(-1)
    unit_bias_grad = jnp.sum(hidden_gradient.astype(jnp.float32), axis=(0, 1)).reshape(-1)
    local_small = jnp.concatenate(
        [
            gain_one_grad,
            offset_one_grad,
            gain_two_grad,
            offset_two_grad,
            bias_grad,
            bias_grad,
            jnp.zeros((small.shape[0] - 6 * model_width,), jnp.float32),
        ]
    )
    local_small = lax.dynamic_update_slice_in_dim(local_small, qkv_bias_grad, qkv_start, 0)
    local_small = lax.dynamic_update_slice_in_dim(local_small, unit_bias_grad, unit_start, 0)
    small_grads = lax.psum(local_small, ("blk", "ctx", "tp"))
    local_grad = jnp.concatenate(
        [query_key_value_gradient, outproj_grad, in_grad, down_grad], axis=0
    ).reshape(per_group, -1)
    shares = lax.psum_scatter(
        local_grad.astype(jnp.bfloat16), "blk", scatter_dimension=1, tiled=True
    )
    matrix_grads = lax.psum(shares, "ctx").astype(jnp.float32)
    new_momenta = momentum_decay * momenta + matrix_grads
    update = matrix_grads + momentum_decay * new_momenta
    per_owner = per_group // cycle_size
    sectioned = update.reshape(cycle_size, per_owner, update.shape[1])
    pieces = lax.all_to_all(
        sectioned.astype(jnp.bfloat16), "blk", split_axis=0, concat_axis=2, tiled=True
    ).astype(sectioned.dtype)
    piece_count = pieces.shape[1]
    settled_blocks = newton_schulz(pieces.reshape(piece_count, MODEL_DIM, HD)).reshape(
        1, piece_count, MODEL_DIM * HD
    )
    settled = lax.all_to_all(
        as_sent(settled_blocks), "blk", split_axis=2, concat_axis=0, tiled=True
    ).astype(settled_blocks.dtype)
    orthogonal_all = settled.reshape(per_group, -1)
    muon_scale = max(1.0, MODEL_DIM / HD) ** 0.5
    new_matrices = matrices - muon_rate * (muon_scale * orthogonal_all + weight_decay * matrices)
    new_first = adam_first * small_first + (1.0 - adam_first) * small_grads
    new_second = adam_second * small_second + (1.0 - adam_second) * small_grads * small_grads
    corrected = new_first / (1.0 - adam_first**STEP)
    spread = jnp.sqrt(new_second / (1.0 - adam_second**STEP))
    new_small = small - small_rate * corrected / (spread + adam_epsilon)
    return (
        block_output,
        input_grad,
        matrix_grads,
        new_matrices,
        new_momenta,
        small_grads,
        new_first,
        new_second,
        new_small,
    )


def native_view(array):
    rows, columns = array.shape
    tiled = array.reshape(rows // 8, 8, columns // 128, 128).transpose(0, 2, 1, 3)
    return tiled.reshape(rows // 8, columns // 16, 128)


def native_back(array):
    groups, rows, _ = array.shape
    return array.reshape(groups, rows // 8, 8, 128).transpose(0, 2, 1, 3).reshape(groups * 8, rows * 16)


def members_of(head):
    if head:
        return lambda piece, j: (j // 2, 4 * (j % 2) + piece)
    return lambda piece, j: (piece // 2, 4 * (piece % 2) + j)


def mem(kind=pltpu.VMEM):
    return pl.BlockSpec(memory_space=kind)


def limits(mebibytes):
    return pltpu.CompilerParams(vmem_limit_bytes=mebibytes << 20)


def low_lanes(rows):
    return lax.broadcasted_iota(jnp.int32, (rows, 128), 1) < HD


def dot(a, b, dims=((1,), (0,)), precision=None):
    return lax.dot_general(
        a, b, (dims, ((), ())), precision=precision, preferred_element_type=jnp.float32
    )


NT = ((1,), (1,))
TN = ((0,), (0,))


def corner(array):
    block = (1,) * (array.ndim - 2) + (min(16, array.shape[-2]), 128)
    return pl.BlockSpec(block, lambda *_: (0,) * array.ndim)


def takes(microseconds):
    return pl.CostEstimate(
        flops=int(microseconds * 1.15e9), transcendentals=0, bytes_accessed=int(1e6)
    )


def in_hbm(array):
    if array.size * array.dtype.itemsize < 1 << 21:
        return array
    return pltpu.with_memory_space_constraint(array, pltpu.HBM)


def out_hbm(shape):
    if shape.size * shape.dtype.itemsize < 1 << 21:
        return shape
    return pltpu.HBM(shape.shape, shape.dtype)


def full(array):
    return pl.BlockSpec(array.shape, lambda *_: (0,) * array.ndim)


def launch(kernel, operands, out_shapes, name, specs=None, after=(), vmem=20, cost=3, **more):
    taken = len(operands)
    body = kernel
    if after:
        body = lambda *refs: kernel(*refs[:taken], *refs[taken + len(after) :])
    if specs is None:
        specs = [mem(pltpu.SMEM)] + [full(a) for a in operands[1:]]
    if "out_specs" not in more:
        more["out_specs"] = jax.tree.map(full, out_shapes)
    more.setdefault("grid", (1,))
    return pl.pallas_call(
        body,
        in_specs=list(specs) + [corner(a) for a in after],
        out_shape=jax.tree.map(out_hbm, out_shapes),
        compiler_params=limits(vmem),
        cost_estimate=takes(cost),
        name=name,
        **more,
    )(*map(in_hbm, operands), *map(in_hbm, after))


def relayout_kernel(n, head, scal, lower, upper, out, *refs):
    scratch = refs[-1]
    low = low_lanes(n)
    place_of = members_of(head)
    for piece in range(4):
        for half in range(2):
            k = 2 * piece + half
            pair = []
            for j in (2 * half, 2 * half + 1):
                group, line = place_of(piece, j)
                pair.append((lower, upper)[group][0, pl.ds(line, n, stride=8), :])
            a, b = pair
            scratch[k, pl.ds(0, n, stride=2), :] = jnp.where(low, a, pltpu.roll(b, 64, 1))
            scratch[k, pl.ds(1, n, stride=2), :] = jnp.where(low, pltpu.roll(a, 64, 1), b)
            out[piece, :, half * 128 : (half + 1) * 128] = scratch[k].astype(out.dtype)
    if len(refs) == 2:
        refs[0][0] = out[scal[1]]


def relayout(scal, array, dtype, first, count, mine=False, n=64, after=()):
    shapes = [jax.ShapeDtypeStruct((4 * count, 512, 256), dtype)]
    specs = [pl.BlockSpec((4, 2 * n, 256), lambda k, i: (k, i, 0))]
    if mine:
        shapes.append(jax.ShapeDtypeStruct((count, 512, 256), dtype))
        specs.append(pl.BlockSpec((1, 2 * n, 256), lambda k, i: (k, i, 0)))
    return launch(
        functools.partial(relayout_kernel, n, first == 0),
        [scal, native_view(array), native_view(array)],
        shapes,
        "relayout",
        specs=[
            mem(pltpu.SMEM),
            pl.BlockSpec((1, 8 * n, 128), lambda k, i: (2 * first + 2 * k, i, 0)),
            pl.BlockSpec((1, 8 * n, 128), lambda k, i: (2 * first + 2 * k + 1, i, 0)),
        ],
        after=after,
        cost=1.3 * count,
        grid=(count, 256 // n),
        out_specs=specs,
        scratch_shapes=[pltpu.VMEM((8, 2 * n, 128), jnp.float32)],
    )


def add_up(groups):
    for parts, target in groups:
        values = [part[...].astype(jnp.float32) for part in parts]
        while len(values) > 1:
            values = [sum(values[i : i + 2]) for i in range(0, len(values), 2)]
        if isinstance(target, list):
            for i, part in enumerate(target):
                part[...] = values[0][i].astype(part.dtype)
        else:
            target[...] = values[0].astype(target.dtype)


def grouped(refs, counts, targets):
    refs = iter(refs)
    return [([next(refs) for _ in range(n)], target) for n, target in zip(counts, targets)]


def normalized(x):
    centred = x - jnp.mean(x, axis=-1, keepdims=True)
    spread = jnp.mean(centred * centred, axis=-1, keepdims=True)
    root = lax.rsqrt(spread + norm_epsilon)
    return centred * root, root


def halves(values, first):
    left, right = values[:, :512], values[:, 512:]
    return jnp.where(first, left, right), jnp.where(first, right, left)


def whole(own, other, first):
    return jnp.concatenate([jnp.where(first, own, other), jnp.where(first, other, own)], axis=1)


def norm_back(grad, hat, root, gain):
    scaled = grad * gain
    along = jnp.mean(scaled * hat, axis=-1, keepdims=True)
    return root * (scaled - jnp.mean(scaled, axis=-1, keepdims=True) - hat * along)


def turned(values, cosine, sine):
    lane = lax.broadcasted_iota(jnp.int32, values.shape, 1) % HD
    other = jnp.where(lane < 8, pltpu.roll(values, 120, 1), pltpu.roll(values, 8, 1))
    return values * cosine + other * sine


def project_kernel(scal, x, cot, norms, bias, cosine, sine, own, r0, r1, r2, r3, send):
    first = scal[0] == 0
    hat, _ = normalized(x[...].astype(jnp.float32))
    h = (hat * norms[0:1] + norms[1:2]).astype(jnp.bfloat16)
    h_own, h_other = halves(h, first)
    c_own, c_other = halves(cot[...], first)
    tokens = h.shape[0]
    low = low_lanes(tokens)
    for r, other in enumerate((r0, r1, r2, r3)):
        head = scal[1] ^ r
        mine = own[head]
        theirs = other[...]
        pre = dot(h_own, mine) + dot(h_other, theirs) + bias[pl.ds(head, 1), :]
        back = dot(c_own, mine[:, 128:]) + dot(c_other, theirs[:, 128:])
        left = turned(pre[:, :128], cosine[...], sine[...]).astype(jnp.bfloat16)
        right = jnp.where(low, pre[:, 128:], back).astype(jnp.bfloat16)
        for s in range(2):
            rows = slice(128 * s, 128 * s + 128)
            send[4 * s + head, :, :128] = left[rows]
            send[4 * s + head, :, 128:] = right[rows]


def attention_kernel(rows_ref, seg, out, key_total, value_total):
    key_total[...] = jnp.zeros_like(key_total)
    value_total[...] = jnp.zeros_like(value_total)
    step = 256
    for block in range(rows_ref.shape[0] // step):
        rows = slice(block * step, (block + 1) * step)
        n = (block + 1) * step
        query = rows_ref[rows, 0:HD] * jnp.bfloat16(0.125)
        grad = rows_ref[rows, 3 * HD : 4 * HD]
        keys = rows_ref[0:n, HD : 2 * HD]
        values = rows_ref[0:n, 2 * HD : 3 * HD]
        scores = dot(query, keys, NT)
        query_place = block * step + lax.broadcasted_iota(jnp.int32, (step, n), 0)
        key_place = lax.broadcasted_iota(jnp.int32, (step, n), 1)
        allowed = (key_place <= query_place) & (key_place >= seg[rows, :])
        scores = jnp.where(allowed, scores, masked_score)
        weights = jnp.exp(scores - jnp.max(scores, axis=-1, keepdims=True))
        weights = jnp.where(allowed, weights, 0.0)
        weights = weights * (1.0 / jnp.sum(weights, axis=-1, keepdims=True))
        short = weights.astype(jnp.bfloat16)
        attended = dot(short, values)
        weight_grad = dot(grad, values, NT)
        delta = jnp.sum(weights * weight_grad, axis=-1, keepdims=True)
        score_grad = (weights * (weight_grad - delta)).astype(jnp.bfloat16)
        query_grad = dot(score_grad, keys) * 0.125
        key_total[0:n, :] += dot(score_grad, query, TN)
        value_total[0:n, :] += dot(short, grad, TN)
        out[rows, 0:HD] = query_grad.astype(jnp.bfloat16)
        out[rows, 3 * HD : 4 * HD] = attended.astype(jnp.bfloat16)
    out[:, HD : 2 * HD] = key_total[...].astype(jnp.bfloat16)
    out[:, 2 * HD : 3 * HD] = value_total[...].astype(jnp.bfloat16)


def feed_forward_kernel(
    scal, x, cot, norms, bias, weights, r0, r1, r2, r3,
    branch, input_part, keep, send, hidden_sums, norm_grads, cot_sums,
):
    first = scal[0] == 0
    hat, root = normalized(x[...].astype(jnp.float32))
    h = (hat * norms[2:3] + norms[3:4]).astype(jnp.bfloat16)
    h_own, h_other = halves(h, first)
    c_own, c_other = halves(cot[...], first)
    cot_sums[...] = jnp.sum(cot[...].astype(jnp.float32), axis=0, keepdims=True)
    outs = [0.0] * 4
    for r, other in enumerate((r0, r1, r2, r3)):
        piece = scal[1] ^ r
        in_own, in_other = weights[piece], other[0]
        down_own, down_other = weights[4 + piece], other[1]
        pre = dot(h_own, in_own) + dot(h_other, in_other) + bias[pl.ds(piece, 1), :]
        cumulative = 0.5 * (1.0 + lax.erf(pre * 0.7071067811865476))
        slope = cumulative + pre * (0.3989422804014327 * jnp.exp(-0.5 * pre * pre))
        act = (pre * cumulative).astype(jnp.bfloat16)
        act_grad = dot(c_own, down_own) + dot(c_other, down_other)
        grad = (act_grad * slope).astype(jnp.bfloat16)
        hidden_sums[pl.ds(piece, 1), :] = jnp.sum(
            grad.astype(jnp.float32), axis=0, keepdims=True
        )
        outs[0] += dot(act, down_own, NT)
        outs[1] += dot(act, down_other, NT)
        outs[2] += dot(grad, in_own, NT)
        outs[3] += dot(grad, in_other, NT)
        target = send if r % 2 else keep
        target[r // 2, 0] = grad
        target[r // 2, 1] = act
    branch[...] = whole(outs[0], outs[1], first)
    second = whole(outs[2], outs[3], first)
    norm_grads[0:1] = jnp.sum(second * hat, axis=0, keepdims=True)
    norm_grads[1:2] = jnp.sum(second, axis=0, keepdims=True)
    input_part[...] = norm_back(second, hat, root, norms[2:3])


def both_cores(scal, x, x_beside, cot, cot_beside, norms, at):
    first = scal[0] == 0
    tokens = jnp.concatenate([x[...], x_beside[...]], axis=0).astype(jnp.float32)
    hat, _ = normalized(tokens)
    h = (hat * norms[at : at + 1] + norms[at + 1 : at + 2]).astype(jnp.bfloat16)
    c = jnp.concatenate([cot[...], cot_beside[...]], axis=0)
    return list(zip(halves(h, first), halves(c, first)))


def unit_grads_kernel(
    scal, x, x_beside, cot, cot_beside, norms, keep, came, in_keep, in_send, down_keep, down_send
):
    for side, (h, c) in enumerate(both_cores(scal, x, x_beside, cot, cot_beside, norms, 2)):
        for far in range(2):
            grad = jnp.concatenate([keep[far, 0], came[far, 0]], axis=0)
            act = jnp.concatenate([keep[far, 1], came[far, 1]], axis=0)
            (in_send if side else in_keep)[far] = dot(h, grad, TN).astype(jnp.bfloat16)
            (down_send if far else down_keep)[side] = dot(c, act, TN).astype(jnp.bfloat16)


def combine_kernel(in_keep, in_came, down_keep, down_came, own, in_send, down_send):
    pairs = ((in_keep, in_came, in_send), (down_keep, down_came, down_send))
    for k, (keep, came, send) in enumerate(pairs):
        total = keep[...].astype(jnp.float32) + came[...].astype(jnp.float32)
        own[k] = total[0].astype(jnp.bfloat16)
        send[0] = total[1].astype(jnp.bfloat16)


def turn_kernel(scal, cosine, sine, back, keep, send, sums):
    low = low_lanes(keep.shape[1])
    for r in range(4):
        head = scal[1] ^ r
        grads = jnp.concatenate([back[head], back[4 + head]], axis=0)
        left = turned(grads[:, :128].astype(jnp.float32), cosine[...], -sine[...])
        left = left.astype(jnp.bfloat16)
        right = grads[:, 128:]
        target = send if r % 2 else keep
        target[r // 2, :, :128] = left
        target[r // 2, :, 128:] = right
        right = jnp.where(low, right.astype(jnp.float32), 0.0)
        wide = jnp.concatenate([left.astype(jnp.float32), right], axis=1)
        sums[pl.ds(head, 1), :] = jnp.sum(wide, axis=0, keepdims=True)


def split_last(piece):
    wide = piece.astype(jnp.float32)
    lane = lax.broadcasted_iota(jnp.int32, (1, wide.shape[1]), 1)
    share = (lane < 3 * HD).astype(jnp.float32)
    pre_grad = (wide * share).astype(jnp.bfloat16)
    attended = (wide * (1.0 - share)).astype(jnp.bfloat16)
    return pre_grad, attended


def head_grads_kernel(
    scal, x, x_beside, cot, cot_beside, norms, keep, came, totals, *outs
):
    both = totals[...].reshape(64, 256)
    coarse = both.astype(jnp.bfloat16)
    fine = (both - coarse.astype(jnp.float32)).astype(jnp.bfloat16)
    sides = both_cores(scal, x, x_beside, cot, cot_beside, norms, 0)
    for far in range(2):
        piece = jnp.concatenate([keep[far], came[far]], axis=0)
        pre_grad, attended = split_last(piece)
        for side, (h, c) in enumerate(sides):
            grad = dot(h, pre_grad, TN) + dot(c, attended, TN)
            outs[side][far, 0:512] = grad.astype(jnp.bfloat16)
            outs[side][far, 512:576] = coarse
            outs[side][far, 576:640] = fine


def combine_heads_kernel(keep, came, own, send):
    for target, at in ((own, 0), (send, 1)):
        total = keep[at].astype(jnp.float32) + came[at].astype(jnp.float32)
        target[0:512] = total[0:512].astype(jnp.bfloat16)
        tail = total[512:576] + total[576:640]
        coarse = tail.astype(jnp.bfloat16)
        target[512:576] = coarse
        target[576:640] = (tail - coarse.astype(jnp.float32)).astype(jnp.bfloat16)


def add_kernel(near, came, kept, passed):
    add_up([((near, came), [kept, passed])])


def gather_kernel(
    scal, x, norms, keep, send, weights, r0, r1, r2, r3, ff_branch, ff_part,
    norm_two, cot_sums, unit_sums, qkv_sums, near, far, totals, parts,
):
    first = scal[0] == 0
    hat, root = normalized(x[...].astype(jnp.float32))
    outs = [0.0] * 4
    for r, other in enumerate((r0, r1, r2, r3)):
        mine, theirs = weights[scal[1] ^ r], other[0]
        pre_grad, attended = split_last((send if r % 2 else keep)[r // 2])
        outs[0] += dot(attended, mine, NT)
        outs[1] += dot(attended, theirs, NT)
        outs[2] += dot(pre_grad, mine, NT)
        outs[3] += dot(pre_grad, theirs, NT)
    branch = ff_branch[...] + whole(outs[0], outs[1], first)
    grad = whole(outs[2], outs[3], first)
    totals[...] = jnp.zeros_like(totals)
    rows = [jnp.sum(grad * hat, axis=0, keepdims=True), jnp.sum(grad, axis=0, keepdims=True)]
    rows += [norm_two[0:1], norm_two[1:2], cot_sums[...]]
    for i, row in enumerate(rows):
        for q in range(4):
            at = 4 * (i % 2) + q
            totals[i // 2, at : at + 1, :] = row[:, 256 * q : 256 * q + 256]
    totals[3 + scal[2], 0:4, :] = qkv_sums[...]
    totals[3 + scal[2], 4:8, :] = unit_sums[...]
    input_part = ff_part[...] + norm_back(grad, hat, root, norms[0:1])
    for q in range(4):
        parts[q, 0] = branch[64 * q : 64 * q + 64].astype(jnp.bfloat16)
        parts[q, 1] = input_part[64 * q : 64 * q + 64].astype(jnp.bfloat16)
    for r in range(4):
        (far if r % 2 else near)[r // 2] = parts[scal[2] ^ r]


def finish_rows_kernel(scal, x, cot, bias, r0, r1, r2, r3, block_output, input_grad):
    for r, piece in enumerate((r0, r1, r2, r3)):
        q = scal[2] ^ r
        block_output[q] = x[q].astype(jnp.float32) + piece[0].astype(jnp.float32) + bias[...]
        input_grad[q] = cot[q].astype(jnp.float32) + piece[1].astype(jnp.float32)


def gram_of_piece(total, momenta, grads, grams):
    short = total.astype(jnp.bfloat16)
    grads[0] = short
    update = 1.95 * short.astype(jnp.float32) + 0.9025 * momenta[0]
    gram = dot(update, update, TN, lax.Precision.HIGHEST)
    for j in range(4):
        cut = slice(j * HD, (j + 1) * HD)
        grams[0, j] = gram[cut, cut]


def unit_gram_kernel(place, own, in_came, down_came, momenta, kept, came, *refs):
    grads, grams, total = refs[-3:]

    @pl.when(pl.program_id(0) == 0)
    def _():
        add_up([((kept, came), total)])

    a = in_came[0].astype(jnp.float32)
    b = down_came[0].astype(jnp.float32)
    other = jnp.where(pl.program_id(0) == 0, a, b)
    gram_of_piece(own[0].astype(jnp.float32) + other, momenta, grads, grams)


def head_gram_kernel(place, own, came, momenta, *refs):
    grads, grams, totals = refs[-3:]
    total = own[...].astype(jnp.float32) + came[...].astype(jnp.float32)
    gram_of_piece(total[0:512], momenta, grads, grams)
    totals[...] = (total[512:576] + total[576:640]).reshape(8, 8, 256)


def gram_of(kernel, first, others, momenta, place, more, shapes, after=()):
    chunks = momenta.shape[0] // 4
    piece = pl.BlockSpec((1, 512, 256), lambda i, s: (i, 0, 0))
    block = pl.BlockSpec((1, 512, 256), lambda i, s: (4 * i + s[1], 0, 0))
    return pl.pallas_call(
        kernel,
        grid_spec=pltpu.PrefetchScalarGridSpec(
            num_scalar_prefetch=1,
            grid=(chunks,),
            in_specs=[piece if first.ndim == 3 else full(first)]
            + [full(other) for other in others]
            + [block]
            + [full(part) for part in more]
            + [corner(a) for a in after],
            out_specs=[piece, pl.BlockSpec((1, 4, HD, HD), lambda i, s: (i, 0, 0, 0))]
            + [full(shape) for shape in shapes],
        ),
        out_shape=[
            jax.ShapeDtypeStruct((chunks, 512, 256), jnp.bfloat16),
            jax.ShapeDtypeStruct((chunks, 4, HD, HD), jnp.float32),
            *map(out_hbm, shapes),
        ],
        compiler_params=limits(20),
        cost_estimate=takes(2.5),
        name="gram",
    )(place, *map(in_hbm, [first, *others, momenta, *more, *after]))


def newton_kernel(counts, mine, theirs, *refs):
    taken = sum(counts)
    out = refs[taken]
    add_up(grouped(refs, counts, refs[taken + 1 :]))
    linear, square, cubic = quintic
    shape = (HD, HD)
    eye = lax.broadcasted_iota(jnp.int32, shape, 0) == lax.broadcasted_iota(jnp.int32, shape, 1)
    full = lax.Precision.HIGHEST
    chunks = mine.shape[0]
    places = [(i, j) for i in range(chunks) for j in range(4)]
    states = []
    for i, j in places:
        gram = mine[i, j] + theirs[i, j]
        trace = jnp.sum(jnp.where(eye, gram, 0.0), axis=(0, 1), keepdims=True)
        scale = 1.0 / (jnp.sqrt(trace) + muon_epsilon)
        states.append([gram * scale * scale, None, scale])
    for iteration in range(NEWTON):
        squares = [dot(s[0], s[0], precision=full) for s in states]
        steps = [
            jnp.where(eye, linear, 0.0) + square * s[0] + cubic * sq
            for s, sq in zip(states, squares)
        ]
        if iteration == 0:
            halfway = [dot(s[0], m, precision=full) for s, m in zip(states, steps)]
            for s, m in zip(states, steps):
                s[1] = m
        elif iteration < NEWTON - 1:
            both = [
                dot(jnp.concatenate([s[0], s[1]], axis=0), m, precision=full)
                for s, m in zip(states, steps)
            ]
            halfway = [x[:HD] for x in both]
            for s, x in zip(states, both):
                s[1] = x[HD:]
        else:
            for s, m in zip(states, steps):
                s[1] = dot(s[1], m, precision=full)
        if iteration < NEWTON - 1:
            for s, x, m in zip(states, halfway, steps):
                s[0] = dot(x, m, precision=full)
    for (i, j), s in zip(places, states):
        mix = s[1] * s[2]
        coarse = mix.astype(jnp.bfloat16)
        fine = (mix - coarse.astype(jnp.float32)).astype(jnp.bfloat16)
        rows, lanes = slice(64 * (j // 2), 64 * (j // 2) + 64), slice(128 * (j % 2), 128 * (j % 2) + 128)
        out[i, rows, lanes] = jnp.concatenate([coarse, fine], axis=1)


def newton(mine, theirs, sums, after=()):
    flat = [part for group in sums for part in group]
    operands = [mine, theirs, *flat]
    return launch(
        functools.partial(newton_kernel, [len(group) for group in sums]),
        operands,
        [jax.ShapeDtypeStruct((mine.shape[0], 2 * HD, 256), jnp.bfloat16)]
        + [jax.ShapeDtypeStruct(group[0].shape, group[0].dtype) for group in sums],
        "newton",
        cost=3.5,
        specs=[full(a) for a in operands],
        after=after,
    )


def update_kernel(
    n, head, scal, g0, g1, g2, g3, q0, q1, q2, q3, momenta, native_momenta, native, *refs
):
    grads, weights, moved, mixing, first, second, steps = refs[-7:]
    place_of = members_of(head)

    @pl.when((pl.program_id(0) == 0) & (pl.program_id(1) == 0))
    def _():
        mixing[...] = jnp.zeros_like(mixing)

    @pl.when(pl.program_id(1) == 0)
    def _():
        for r, q in enumerate((q0, q1, q2, q3)):
            for j in range(4):
                at = slice(HD * (j // 2), HD * (j // 2) + HD), slice(128 * (j % 2), 128 * (j % 2) + 128)
                wide = q[(0,) * (len(q.shape) - 2) + at].astype(jnp.float32)
                other = pltpu.roll(wide, HD, 1)
                below = low_lanes(HD) == (j % 2 == 0)
                rows = slice(j * HD, (j + 1) * HD)
                lanes = slice(128 * (j // 2), 128 * (j // 2) + 128)
                pair = (wide, other) if j % 2 == 0 else (other, wide)
                for level in range(2):
                    part = jnp.where(below, pair[level], 0.0)
                    mixing[r, level, rows, lanes] = part.astype(jnp.bfloat16)

    low = low_lanes(n)
    for r, piece in enumerate((g0, g1, g2, g3)):
        place = scal[1] ^ r
        grad = piece[(0,) * (len(piece.shape) - 2)].astype(jnp.float32)
        update = 1.95 * grad + 0.9025 * momenta[place]
        coarse = update.astype(jnp.bfloat16)
        fine = (update - coarse.astype(jnp.float32)).astype(jnp.bfloat16)
        settled = dot(coarse, mixing[r, 0]) + dot(coarse, mixing[r, 1]) + dot(fine, mixing[r, 0])
        for half in range(2):
            k = 2 * r + half
            first[k] = grad[:, half * 128 : (half + 1) * 128]
            second[k] = settled[:, half * 128 : (half + 1) * 128]
            for source, target in ((first, grads), (second, steps)):
                even = source[k, pl.ds(0, n, stride=2), :]
                odd = source[k, pl.ds(1, n, stride=2), :]
                lines = (
                    jnp.where(low, even, pltpu.roll(odd, 64, 1)),
                    jnp.where(low, pltpu.roll(even, 64, 1), odd),
                )
                for w in range(2):
                    group, line = place_of(place, 2 * half + w)
                    target[group, pl.ds(line, n, stride=8), :] = lines[w]
    moved[...] = momentum_decay * native_momenta[...] + grads[...]
    weight = native[...]
    weights[...] = weight - muon_rate * (4.0 * steps[...] + weight_decay * weight)


def update(
    first, scal, own, far, mix, mix_far, beside, momenta, native_momenta, native, before=(), after=(), n=64
):
    chunks = own.shape[0]
    block = pl.BlockSpec((2, 8 * n, 128), lambda k, i: (first + k, i, 0))
    piece = pl.BlockSpec((1, 2 * n, 256), lambda k, i: (k, i, 0))
    factor = pl.BlockSpec((1, 2 * HD, 256), lambda k, i: (k, 0, 0))
    pieces, factors = [piece, None, piece, None], [factor, None, factor, None]
    for r in (0, 1):
        pieces[2 * r + 1] = pl.BlockSpec((1, 1, 2 * n, 256), lambda k, i, r=r: (r, k, i, 0))
        factors[2 * r + 1] = pl.BlockSpec((1, 1, 2 * HD, 256), lambda k, i, r=r: (r, k, 4, 0))
    grads, mixes = [own, beside, far, beside], [mix, beside, mix_far, beside]
    return launch(
        functools.partial(update_kernel, n, first == 0),
        [scal, *grads, *mixes, momenta, native_view(native_momenta), native_view(native), *before],
        [jax.ShapeDtypeStruct((6, 2048, 128), jnp.float32)] * 3,
        "update",
        specs=[mem(pltpu.SMEM)]
        + pieces
        + factors
        + [pl.BlockSpec((4, 2 * n, 256), lambda k, i: (k, i, 0)), block, block]
        + [mem(pl.ANY)] * len(before),
        after=after,
        cost=5.5 * chunks,
        grid=(chunks, 256 // n),
        out_specs=[block] * 3,
        scratch_shapes=[
            pltpu.VMEM((4, 2, 256, 256), jnp.bfloat16),
            pltpu.VMEM((8, 2 * n, 128), jnp.float32),
            pltpu.VMEM((8, 2 * n, 128), jnp.float32),
            pltpu.VMEM((2, 8 * n, 128), jnp.float32),
        ],
        input_output_aliases={12 + i: i for i in range(len(before))},
    )


def whole_device(
    inputs, cotangent, matrices, momenta, small, small_first, small_second, segments, positions
):
    blk_at = lax.axis_index("blk")
    ctx_at = lax.axis_index("ctx")
    tp_at = lax.axis_index("tp")
    scal = jnp.stack([blk_at, ctx_at, tp_at]).astype(jnp.int32)
    sequences, local_rows, width = inputs.shape
    tokens = sequences * local_rows
    both = ("blk", "ctx")
    f32, bf16 = jnp.float32, jnp.bfloat16
    shaped = jax.ShapeDtypeStruct

    def hop(values, by):
        return lax.ppermute(values, both, [(i, i ^ by) for i in range(8)])

    def hop_tp(values, by):
        return lax.ppermute(values, "tp", [(i, i ^ by) for i in range(4)])

    def tied(values, *results):
        return lax.optimization_barrier((values, *results))[0]

    def spread(piece):
        c = hop(piece, 2)
        return [piece, hop(piece, 1), c, hop(c, 1)]

    x = inputs.reshape(tokens, width)
    cot = cotangent.reshape(tokens, width)
    norms = small[: 4 * width].reshape(4, width)
    qkv_start = 6 * width + tp_at * 4 * 3 * HD
    qkv_bias = lax.dynamic_slice_in_dim(small, qkv_start, 4 * 3 * HD).reshape(4, 3 * HD)
    qkv_bias = jnp.pad(qkv_bias, ((0, 0), (0, HD)))
    unit_start = 6 * width + H * 3 * HD + tp_at * 1024
    unit_bias = lax.dynamic_slice_in_dim(small, unit_start, 1024).reshape(4, 256)
    lane = jnp.arange(128) % HD
    frequency = rope_base ** (-2.0 * (lane % 8).astype(f32) / ROTARY)
    angles = positions.astype(f32).reshape(tokens, 1) * frequency
    cosine = jnp.where(lane < ROTARY, jnp.cos(angles), 1.0)
    sign = jnp.where(lane < 8, -1.0, jnp.where(lane < ROTARY, 1.0, 0.0))
    sine = jnp.sin(angles) * sign

    head_weights, mine = relayout(scal, matrices, bf16, 0, 1, mine=True)
    first_hop = hop(mine, 4)
    other_heads = spread(first_hop)
    unit_weights, mine_units = relayout(scal, matrices, bf16, 1, 2, mine=True, after=(mine,))
    (piled_heads,) = relayout(scal, momenta, f32, 0, 1, after=(mine_units, first_hop))
    units_near = hop(tied(mine_units, first_hop), 4)
    x_beside = hop(x, 1)
    cot_beside = hop(cot, 1)

    send = launch(
        project_kernel,
        [scal, x, cot, norms, qkv_bias, cosine, sine, head_weights]
        + [piece[0] for piece in other_heads],
        shaped((8, local_rows, 256), bf16),
        "project",
    )
    arrived = lax.all_to_all(send, both, split_axis=0, concat_axis=0, tiled=True)
    (piled_units,) = relayout(scal, momenta, f32, 1, 2, after=(send,))
    units_near = tied(units_near, send)
    units_far = hop(units_near, 2)
    units_beside = hop(units_near, 1)
    documents = lax.dynamic_index_in_dim(segments, blk_at, 0, keepdims=False)
    length = documents.shape[0]
    attended = launch(
        attention_kernel,
        [arrived.reshape(length, 256), documents.reshape(length, 1)],
        shaped((length, 256), bf16),
        "attention",
        cost=6,
        specs=[full(arrived.reshape(length, 256)), pl.BlockSpec((length, 1), lambda *_: (0, 0))],
        scratch_shapes=[pltpu.VMEM((length, HD), f32)] * 2,
    )
    back = lax.all_to_all(
        attended.reshape(8, local_rows, 256), both, split_axis=0, concat_axis=0, tiled=True
    )

    units_far = tied(units_far, attended)
    other_units = [units_near, units_beside, units_far, hop(units_far, 1)]
    ff_branch, ff_part, unit_keep, unit_send, unit_sums, norm_two, cot_sums = launch(
        feed_forward_kernel,
        [scal, x, cot, norms, unit_bias, unit_weights, *other_units],
        [
            shaped((tokens, width), f32),
            shaped((tokens, width), f32),
            shaped((2, 2, tokens, 256), bf16),
            shaped((2, 2, tokens, 256), bf16),
            shaped((4, 256), f32),
            shaped((2, width), f32),
            shaped((1, width), f32),
        ],
        "feed_forward",
        cost=5.5,
        after=(attended,),
    )
    head_keep, head_send, qkv_sums = launch(
        turn_kernel,
        [scal, cosine, sine, back],
        [shaped((2, tokens, 256), bf16)] * 2 + [shaped((4, 256), f32)],
        "turn",
        cost=2,
        after=(unit_sums,),
    )
    in_keep, in_send, down_keep, down_send = launch(
        unit_grads_kernel,
        [scal, x, x_beside, cot, cot_beside, norms, unit_keep, hop(unit_send, 1)],
        [shaped((2, 512, 256), bf16)] * 4,
        "unit_grads",
        cost=3.5,
        after=(qkv_sums,),
    )
    sums = [norm_two, cot_sums, unit_sums, qkv_sums]
    near, far, totals = launch(
        gather_kernel,
        [scal, x, norms, head_keep, head_send, head_weights, *other_heads, ff_branch, ff_part, *sums],
        [shaped((2, 2, 64, width), bf16)] * 2 + [shaped((8, 8, 256), f32)],
        "gather",
        after=(in_keep,),
        scratch_shapes=[pltpu.VMEM((4, 2, 64, width), bf16)],
    )
    heads_keep, heads_send = launch(
        head_grads_kernel,
        [scal, x, x_beside, cot, cot_beside, norms, head_keep, hop(head_send, 1), totals],
        [shaped((2, 640, 256), bf16)] * 2,
        "head_grads",
        cost=4,
    )
    came = hop_tp(far, 1)
    heads_came = hop(heads_send, 4)
    operands = [in_keep, hop(in_send, 4), down_keep, hop(down_send, 2)]
    own, in_send, down_send = launch(
        combine_kernel,
        operands,
        [shaped((2, 512, 256), bf16)] + [shaped((1, 512, 256), bf16)] * 2,
        "combine",
        specs=[full(a) for a in operands],
        cost=2,
        after=(heads_keep,),
    )
    in_came, down_came = hop(in_send, 2), hop(down_send, 4)
    kept, passed = launch(
        add_kernel,
        [near, came],
        [shaped((2, 64, width), bf16)] * 2,
        "add",
        specs=[full(near)] * 2,
        after=(in_send,),
    )
    passed = hop_tp(passed, 2)
    heads_own, heads_send = launch(
        combine_heads_kernel,
        [heads_keep, heads_came],
        [shaped((640, 256), bf16)] * 2,
        "combine_heads",
        specs=[full(heads_keep)] * 2,
        after=(kept,),
    )
    heads_came = hop(heads_send, 2)
    unit_sum, unit_grams, total = gram_of(
        unit_gram_kernel,
        own,
        [in_came, down_came],
        piled_units,
        scal,
        [kept, passed],
        [shaped((2, 64, width), bf16)],
        after=(heads_own,),
    )
    unit_theirs = hop(unit_grams, 4)
    unit_far = hop(unit_sum, 2)
    total_far = hop_tp(total, 2)
    head_sum, head_grams, totals = gram_of(
        head_gram_kernel,
        heads_own,
        [heads_came],
        piled_heads,
        scal,
        [],
        [shaped((8, 8, 256), f32)],
        after=(unit_sum,),
    )
    head_theirs = hop(head_grams, 4)
    head_far = hop(head_sum, 2)
    (unit_mix,) = newton(unit_grams, unit_theirs, [], after=(head_sum,))
    unit_mix_far = hop(unit_mix, 2)
    head_mix, totals = newton(
        head_grams,
        head_theirs,
        [(totals, hop(totals, 1))],
        after=(unit_mix, unit_far, total_far),
    )
    head_mix_far = hop(head_mix, 2)

    def to_beside(*pieces):
        return hop(jnp.stack([jnp.concatenate(pair, axis=1) for pair in pieces]), 1)

    beside = to_beside((unit_sum, unit_mix), (unit_far, tied(unit_mix_far, head_mix)))
    totals_came = hop_tp(totals, 1)
    before = update(
        1, scal, unit_sum, unit_far, unit_mix, unit_mix_far, beside, piled_units, momenta, matrices,
        after=(head_mix,),
    )
    beside = to_beside((head_sum, head_mix), (head_far, head_mix_far))
    outs = update(
        0, scal, head_sum, head_far, head_mix, head_mix_far, beside, piled_heads, momenta, matrices,
        before,
    )
    total_beside = hop_tp(tied(jnp.stack([total, total_far]), head_mix), 1)
    totals = tied(totals + totals_came, before[0])
    totals = totals + hop_tp(totals, 2)

    block_output, input_grad = launch(
        finish_rows_kernel,
        [
            scal,
            x.reshape(4, 64, width),
            cot.reshape(4, 64, width),
            (small[4 * width : 5 * width] + small[5 * width : 6 * width]).reshape(1, width),
            total,
            total_beside[0],
            total_far,
            total_beside[1],
        ],
        [shaped((4, 64, width), f32)] * 2,
        "finish_rows",
        cost=2,
        after=(before[0],),
    )

    cot_total = totals[2, :4].reshape(-1) * 0.25
    small_grads = jnp.concatenate(
        [
            totals[:2].reshape(-1),
            cot_total,
            cot_total,
            totals[3:7, :4, : 3 * HD].reshape(-1),
            totals[3:7, 4:].reshape(-1),
        ]
    )
    return (
        block_output.reshape(inputs.shape),
        input_grad.reshape(inputs.shape),
        native_back(outs[0]),
        native_back(outs[1]),
        native_back(outs[2]),
        small_grads,
        *small_step(small, small_first, small_second, small_grads),
    )


def small_step(small, small_first, small_second, small_grads):
    new_first = adam_first * small_first + (1.0 - adam_first) * small_grads
    new_second = adam_second * small_second + (1.0 - adam_second) * small_grads * small_grads
    corrected = new_first / (1.0 - adam_first**STEP)
    spread = jnp.sqrt(new_second / (1.0 - adam_second**STEP))
    new_small = small - small_rate * corrected / (spread + adam_epsilon)
    return new_first, new_second, new_small


def solution(mesh):
    in_specs = (
        P(None, ("blk", "ctx"), None),
        P(None, ("blk", "ctx"), None),
        P("tp", "blk"),
        P("tp", "blk"),
        P(),
        P(),
        P(),
        P(),
        P(None, ("blk", "ctx")),
    )
    out_specs = (
        P(None, ("blk", "ctx"), None),
        P(None, ("blk", "ctx"), None),
        P("tp", "blk"),
        P("tp", "blk"),
        P("tp", "blk"),
        P(),
        P(),
        P(),
        P(),
    )
    one_each = mesh.shape["blk"] == SEQS and mesh.shape["ctx"] * mesh.shape["tp"] == H
    one_each = one_each and mesh.shape["tp"] == 4
    return jax.shard_map(
        whole_device if one_each else on_device, mesh=mesh, in_specs=in_specs, out_specs=out_specs, check_vma=False
    )
```

```python
import functools

import jax
import jax.numpy as jnp
from jax import lax
from jax.experimental import pallas as pl
from jax.experimental.pallas import tpu as pltpu
from jax.sharding import PartitionSpec as P

MODEL_DIM = 1024
H = 16
HD = 64
FF = 4096
ROTARY = 16
NEWTON = 5
STEP = 10
SEQS = 2


norm_epsilon = 1e-05
rope_base = 10000.0
masked_score = -1e30
momentum_decay = 0.95
muon_rate = 0.2
weight_decay = 0.01
muon_epsilon = 1e-07
quintic = (3.4445, -4.775, 2.0315)
adam_first = 0.9
adam_second = 0.95
adam_epsilon = 1e-08
small_rate = 0.2


def passed_along(x, axis, by):
    devices = lax.axis_size(axis)
    pairs = [(i, i + by) for i in range(devices) if 0 <= i + by < devices]
    return lax.ppermute(x, axis, pairs)


def shifted(x, axis, by):
    devices = lax.axis_size(axis)
    return lax.ppermute(x, axis, [(i, (i + by) % devices) for i in range(devices)])


def as_sent(x):

    def short(part):
        return part.astype(jnp.bfloat16) if part.dtype == jnp.float32 else part

    return jax.tree.map(short, x)


def layer_norm(values, scaling, offset):
    centre = jnp.mean(values, axis=-1, keepdims=True)
    centred = values - centre
    spread = jnp.mean(centred * centred, axis=-1, keepdims=True)
    return centred * lax.rsqrt(spread + norm_epsilon) * scaling + offset


def rope_tables(positions):
    halfway = ROTARY // 2
    frequency = rope_base ** (-2.0 * jnp.arange(halfway, dtype=jnp.float32) / ROTARY)
    angles = positions.astype(jnp.float32)[..., None] * frequency
    return (jnp.cos(angles)[:, :, None, :], jnp.sin(angles)[:, :, None, :])


def rotate(values, cosine, sine):
    halfway = ROTARY // 2
    former = values[..., :halfway]
    latter = values[..., halfway:ROTARY]
    return jnp.concatenate(
        [former * cosine - latter * sine, latter * cosine + former * sine, values[..., ROTARY:]],
        axis=-1,
    )


def exact_gelu(values):
    return jax.nn.gelu(values, approximate=False)


def newton_schulz(blocks):
    frobenius = jnp.sqrt(jnp.sum(blocks * blocks, axis=(1, 2), keepdims=True))
    current = blocks / (frobenius + muon_epsilon)
    linear_term, square_term, cubic_term = quintic
    for iteration in range(NEWTON):
        gram_matrix = jnp.einsum("mde,mdf->mef", current, current, precision=lax.Precision.HIGHEST)
        polynomial = square_term * gram_matrix + cubic_term * jnp.einsum(
            "mef,mfg->meg", gram_matrix, gram_matrix, precision=lax.Precision.HIGHEST
        )
        current = linear_term * current + jnp.einsum(
            "mde,mef->mdf", current, polynomial, precision=lax.Precision.HIGHEST
        )
    return current


def to_heads(values):
    return lax.all_to_all(values, "ctx", split_axis=3, concat_axis=1, tiled=True)


def to_positions(values):
    return lax.all_to_all(values, "ctx", split_axis=1, concat_axis=3, tiled=True)


def pass_keys(pair):
    return passed_along(pair, "blk", 1)


def pass_grads(pair_grad):
    return shifted(pair_grad.astype(jnp.bfloat16), "blk", 1).astype(pair_grad.dtype)


def allowed_pairs(segments, query_block, key_block, block_rows):
    query_place = query_block * block_rows + jnp.arange(block_rows, dtype=jnp.int32)
    key_place = key_block * block_rows + jnp.arange(block_rows, dtype=jnp.int32)
    query_doc = lax.dynamic_slice_in_dim(segments, query_block * block_rows, block_rows, 1)
    key_doc = lax.dynamic_slice_in_dim(segments, key_block * block_rows, block_rows, 1)
    causal = key_place[None, :] <= query_place[:, None]
    return (causal[None] & (query_doc[:, :, None] == key_doc[:, None, :]))[:, None]


def masked_scores(queries, keys, allowed):
    score_scale = HD ** (-0.5)
    scores = (
        jnp.einsum("sqhe,skhe->shqk", queries, keys, preferred_element_type=jnp.float32)
        * score_scale
    )
    return jnp.where(allowed, scores, masked_score)


def on_device(
    inputs, cotangent, matrices, momenta, small, small_first, small_second, segments, positions
):
    tensor_size = lax.axis_size("tp")
    cycle_size = lax.axis_size("blk")
    context_size = lax.axis_size("ctx")
    tensor_index = lax.axis_index("tp")
    cycle_index = lax.axis_index("blk")
    sequences, local_rows, model_width = inputs.shape
    per_group = matrices.shape[0]
    head_count = H // tensor_size
    unit_blocks = FF // HD // tensor_size
    block_rows = local_rows * context_size
    gathered = lax.all_gather(matrices.astype(jnp.bfloat16), "blk", axis=1, tiled=True).reshape(
        per_group, model_width, HD
    )
    query_key_value_weight = gathered[: 3 * head_count]
    projection_out_weight = gathered[3 * head_count : 4 * head_count]
    input_weight = gathered[4 * head_count : 4 * head_count + unit_blocks]
    down_projection_weight = gathered[4 * head_count + unit_blocks :]
    qkv_start = 6 * model_width + tensor_index * head_count * 3 * HD
    query_key_value_bias = lax.dynamic_slice_in_dim(small, qkv_start, head_count * 3 * HD).reshape(
        head_count, 3, HD
    )
    unit_start = 6 * model_width + H * 3 * HD + tensor_index * unit_blocks * HD
    hidden_unit_bias = lax.dynamic_slice_in_dim(small, unit_start, unit_blocks * HD).reshape(
        unit_blocks, HD
    )
    residual = inputs.astype(jnp.float32)

    def both_norms(values, gain_one, offset_one, gain_two, offset_two):
        return (layer_norm(values, gain_one, offset_one), layer_norm(values, gain_two, offset_two))

    (normed_one, normed_two), norm_back = jax.vjp(
        both_norms,
        residual,
        small[0:model_width],
        small[model_width : 2 * model_width],
        small[2 * model_width : 3 * model_width],
        small[3 * model_width : 4 * model_width],
    )
    first_input = normed_one.astype(jnp.bfloat16)
    second_input = normed_two.astype(jnp.bfloat16)
    projected = jnp.einsum(
        "pgk,jka->pgja", first_input, query_key_value_weight, preferred_element_type=jnp.float32
    )
    projected = projected.reshape(sequences, local_rows, 3, head_count, HD) + jnp.transpose(
        query_key_value_bias, (1, 0, 2)
    )
    cosine, sine = rope_tables(positions)

    def turn_pair(query_pre, key_pre):
        return (rotate(query_pre, cosine, sine), rotate(key_pre, cosine, sine))

    (query_turned, key_turned), turn_back = jax.vjp(
        turn_pair, projected[:, :, 0], projected[:, :, 1]
    )
    stacked = jnp.stack([query_turned, key_turned, projected[:, :, 2]], axis=2).astype(jnp.bfloat16)
    by_heads = to_heads(stacked)
    queries = by_heads[:, :, 0]
    head_local = queries.shape[2]

    def forward_visit(state, pair, source):
        row_max, row_total, weighted = state
        allowed = allowed_pairs(segments, cycle_index, source, block_rows)
        scores = masked_scores(queries, pair[:, :, 0], allowed)
        new_max = jnp.maximum(row_max, jnp.max(scores, axis=-1))
        weights = jnp.where(allowed, jnp.exp(scores - new_max[..., None]), 0.0)
        rescale = jnp.exp(row_max - new_max)
        row_total = row_total * rescale + jnp.sum(weights, axis=-1)
        weighted = weighted * rescale[..., None] + jnp.einsum(
            "shqk,skhe->shqe",
            weights.astype(jnp.bfloat16),
            pair[:, :, 1],
            preferred_element_type=jnp.float32,
        )
        return (new_max, row_total, weighted)

    def forward_hop(hop_index, carry):
        pair, state = carry
        source = (cycle_index - hop_index) % cycle_size
        state = forward_visit(state, pair, source)
        return (pass_keys(pair), state)

    start_state = (
        jnp.full((sequences, head_local, block_rows), masked_score, jnp.float32),
        jnp.zeros((sequences, head_local, block_rows), jnp.float32),
        jnp.zeros((sequences, head_local, block_rows, HD), jnp.float32),
    )
    pair, state = lax.fori_loop(0, cycle_size - 1, forward_hop, (by_heads[:, :, 1:], start_state))
    row_max, row_total, weighted = forward_visit(state, pair, (cycle_index + 1) % cycle_size)
    log_total = row_max + jnp.log(row_total)
    attended_rows = jnp.transpose(weighted / row_total[..., None], (0, 2, 1, 3))
    attention_result = to_positions(attended_rows.astype(jnp.bfloat16)[:, :, None])[:, :, 0]
    attention_branch = jnp.einsum(
        "roxu,xcu->roc", attention_result, projection_out_weight, preferred_element_type=jnp.float32
    )
    hidden_preactivation = (
        jnp.einsum("ptr,kra->ptka", second_input, input_weight, preferred_element_type=jnp.float32)
        + hidden_unit_bias
    )
    activated_hidden, gelu_back = jax.vjp(exact_gelu, hidden_preactivation)
    activated_reduced = activated_hidden.astype(jnp.bfloat16)
    perceptron_branch = jnp.einsum(
        "xkzp,zop->xko",
        activated_reduced,
        down_projection_weight,
        preferred_element_type=jnp.float32,
    )
    branches = lax.psum((attention_branch + perceptron_branch).astype(jnp.bfloat16), "tp").astype(
        jnp.float32
    )
    block_output = (
        residual
        + branches
        + small[4 * model_width : 5 * model_width]
        + small[5 * model_width : 6 * model_width]
    )
    act_grad = jnp.einsum(
        "ptr,kra->ptka", cotangent, down_projection_weight, preferred_element_type=jnp.float32
    )
    hidden_gradient = gelu_back(act_grad)[0].astype(jnp.bfloat16)
    down_grad = jnp.einsum(
        "gup,guzb->zpb", cotangent, activated_reduced, preferred_element_type=jnp.float32
    )
    in_grad = jnp.einsum(
        "gup,guzb->zpb", second_input, hidden_gradient, preferred_element_type=jnp.float32
    )
    second_grad = jnp.einsum(
        "xkzp,zop->xko", hidden_gradient, input_weight, preferred_element_type=jnp.float32
    )
    attended_grad = jnp.einsum(
        "pgk,jka->pgja", cotangent, projection_out_weight, preferred_element_type=jnp.float32
    ).astype(jnp.bfloat16)
    outproj_grad = jnp.einsum(
        "ztu,ztqi->qui", cotangent, attention_result, preferred_element_type=jnp.float32
    )
    grad_heads = to_heads(attended_grad[:, :, None])[:, :, 0]
    row_delta = jnp.transpose(
        jnp.sum(grad_heads.astype(jnp.float32) * attended_rows, axis=-1), (0, 2, 1)
    )

    def backward_visit(query_grad, pair, source):
        allowed = allowed_pairs(segments, cycle_index, source, block_rows)
        scores = masked_scores(queries, pair[:, :, 0], allowed)
        probabilities = jnp.where(allowed, jnp.exp(scores - log_total[..., None]), 0.0)
        value_grad = jnp.einsum(
            "shqk,sqhe->skhe",
            probabilities.astype(jnp.bfloat16),
            grad_heads,
            preferred_element_type=jnp.float32,
        )
        prob_grad = jnp.einsum(
            "sqhe,skhe->shqk", grad_heads, pair[:, :, 1], preferred_element_type=jnp.float32
        )
        score_grad = (probabilities * (prob_grad - row_delta[..., None])).astype(jnp.bfloat16)
        score_scale = HD ** (-0.5)
        query_grad = (
            query_grad
            + jnp.einsum(
                "shqk,skhe->sqhe", score_grad, pair[:, :, 0], preferred_element_type=jnp.float32
            )
            * score_scale
        )
        key_grad = (
            jnp.einsum("shqk,sqhe->skhe", score_grad, queries, preferred_element_type=jnp.float32)
            * score_scale
        )
        return (query_grad, jnp.stack([key_grad, value_grad], axis=2))

    def backward_hop(hop_index, carry):
        pair, pair_grad, query_grad = carry
        source = (cycle_index - hop_index) % cycle_size
        query_grad, visit_grad = backward_visit(query_grad, pair, source)
        return (pass_keys(pair), pass_grads(pair_grad + visit_grad), query_grad)

    zero_pair = jnp.zeros(by_heads[:, :, 1:].shape, jnp.float32)
    pair, pair_grad, query_grad = lax.fori_loop(
        0,
        cycle_size - 1,
        backward_hop,
        (by_heads[:, :, 1:], zero_pair, jnp.zeros(queries.shape, jnp.float32)),
    )
    query_grad, visit_grad = backward_visit(query_grad, pair, (cycle_index + 1) % cycle_size)
    pair_grad = pass_grads(pair_grad + visit_grad)
    head_grads = jnp.concatenate([query_grad[:, :, None], pair_grad], axis=2).astype(jnp.bfloat16)
    position_grads = to_positions(head_grads).astype(jnp.float32)
    query_pre_grad, key_pre_grad = turn_back((position_grads[:, :, 0], position_grads[:, :, 1]))
    projected_grad = jnp.stack(
        [query_pre_grad, key_pre_grad, position_grads[:, :, 2]], axis=2
    ).astype(jnp.bfloat16)
    flattened_gradient = projected_grad.reshape(sequences, local_rows, 3 * head_count, HD)
    query_key_value_gradient = jnp.einsum(
        "ztu,ztqi->qui", first_input, flattened_gradient, preferred_element_type=jnp.float32
    )
    first_grad = jnp.einsum(
        "roxu,xcu->roc",
        flattened_gradient,
        query_key_value_weight,
        preferred_element_type=jnp.float32,
    )
    input_part, gain_one_grad, offset_one_grad, gain_two_grad, offset_two_grad = norm_back(
        (first_grad, second_grad)
    )
    input_grad = cotangent.astype(jnp.float32) + lax.psum(
        input_part.astype(jnp.bfloat16), "tp"
    ).astype(jnp.float32)
    owner_share = jnp.where(tensor_index == 0, 1.0, 0.0).astype(jnp.float32)
    bias_grad = jnp.sum(cotangent.astype(jnp.float32), axis=(0, 1)) * owner_share
    qkv_bias_grad = jnp.transpose(
        jnp.sum(projected_grad.astype(jnp.float32), axis=(0, 1)), (1, 0, 2)
    ).reshape(-1)
    unit_bias_grad = jnp.sum(hidden_gradient.astype(jnp.float32), axis=(0, 1)).reshape(-1)
    local_small = jnp.concatenate(
        [
            gain_one_grad,
            offset_one_grad,
            gain_two_grad,
            offset_two_grad,
            bias_grad,
            bias_grad,
            jnp.zeros((small.shape[0] - 6 * model_width,), jnp.float32),
        ]
    )
    local_small = lax.dynamic_update_slice_in_dim(local_small, qkv_bias_grad, qkv_start, 0)
    local_small = lax.dynamic_update_slice_in_dim(local_small, unit_bias_grad, unit_start, 0)
    small_grads = lax.psum(local_small, ("blk", "ctx", "tp"))
    local_grad = jnp.concatenate(
        [query_key_value_gradient, outproj_grad, in_grad, down_grad], axis=0
    ).reshape(per_group, -1)
    shares = lax.psum_scatter(
        local_grad.astype(jnp.bfloat16), "blk", scatter_dimension=1, tiled=True
    )
    matrix_grads = lax.psum(shares, "ctx").astype(jnp.float32)
    new_momenta = momentum_decay * momenta + matrix_grads
    update = matrix_grads + momentum_decay * new_momenta
    per_owner = per_group // cycle_size
    sectioned = update.reshape(cycle_size, per_owner, update.shape[1])
    pieces = lax.all_to_all(
        sectioned.astype(jnp.bfloat16), "blk", split_axis=0, concat_axis=2, tiled=True
    ).astype(sectioned.dtype)
    piece_count = pieces.shape[1]
    settled_blocks = newton_schulz(pieces.reshape(piece_count, MODEL_DIM, HD)).reshape(
        1, piece_count, MODEL_DIM * HD
    )
    settled = lax.all_to_all(
        as_sent(settled_blocks), "blk", split_axis=2, concat_axis=0, tiled=True
    ).astype(settled_blocks.dtype)
    orthogonal_all = settled.reshape(per_group, -1)
    muon_scale = max(1.0, MODEL_DIM / HD) ** 0.5
    new_matrices = matrices - muon_rate * (muon_scale * orthogonal_all + weight_decay * matrices)
    new_first = adam_first * small_first + (1.0 - adam_first) * small_grads
    new_second = adam_second * small_second + (1.0 - adam_second) * small_grads * small_grads
    corrected = new_first / (1.0 - adam_first**STEP)
    spread = jnp.sqrt(new_second / (1.0 - adam_second**STEP))
    new_small = small - small_rate * corrected / (spread + adam_epsilon)
    return (
        block_output,
        input_grad,
        matrix_grads,
        new_matrices,
        new_momenta,
        small_grads,
        new_first,
        new_second,
        new_small,
    )


def native_view(array):
    rows, columns = array.shape
    tiled = array.reshape(rows // 8, 8, columns // 128, 128).transpose(0, 2, 1, 3)
    return tiled.reshape(rows // 8, columns // 16, 128)


def native_back(array):
    groups, rows, _ = array.shape
    return array.reshape(groups, rows // 8, 8, 128).transpose(0, 2, 1, 3).reshape(groups * 8, rows * 16)


def members_of(head):
    if head:
        return lambda piece, j: (j // 2, 4 * (j % 2) + piece)
    return lambda piece, j: (piece // 2, 4 * (piece % 2) + j)


def mem(kind=pltpu.VMEM):
    return pl.BlockSpec(memory_space=kind)


def limits(mebibytes):
    return pltpu.CompilerParams(vmem_limit_bytes=mebibytes << 20)


def low_lanes(rows):
    return lax.broadcasted_iota(jnp.int32, (rows, 128), 1) < HD


def dot(a, b, dims=((1,), (0,)), precision=None):
    return lax.dot_general(
        a, b, (dims, ((), ())), precision=precision, preferred_element_type=jnp.float32
    )


NT = ((1,), (1,))
TN = ((0,), (0,))


def corner(array):
    block = (1,) * (array.ndim - 2) + (min(16, array.shape[-2]), 128)
    return pl.BlockSpec(block, lambda *_: (0,) * array.ndim)


def takes(microseconds):
    return pl.CostEstimate(
        flops=int(microseconds * 1.15e9), transcendentals=0, bytes_accessed=int(1e6)
    )


def in_hbm(array):
    if array.size * array.dtype.itemsize < 1 << 21:
        return array
    return pltpu.with_memory_space_constraint(array, pltpu.HBM)


def out_hbm(shape):
    if shape.size * shape.dtype.itemsize < 1 << 20:
        return shape
    return pltpu.HBM(shape.shape, shape.dtype)


def full(array):
    return pl.BlockSpec(array.shape, lambda *_: (0,) * array.ndim)


def launch(kernel, operands, out_shapes, name, specs=None, after=(), vmem=20, cost=3, **more):
    taken = len(operands)
    body = kernel
    if after:
        body = lambda *refs: kernel(*refs[:taken], *refs[taken + len(after) :])
    if specs is None:
        specs = [mem(pltpu.SMEM)] + [full(a) for a in operands[1:]]
    if "out_specs" not in more:
        more["out_specs"] = jax.tree.map(full, out_shapes)
    more.setdefault("grid", (1,))
    return pl.pallas_call(
        body,
        in_specs=list(specs) + [corner(a) for a in after],
        out_shape=jax.tree.map(out_hbm, out_shapes),
        compiler_params=limits(vmem),
        cost_estimate=takes(cost),
        name=name,
        **more,
    )(*map(in_hbm, operands), *map(in_hbm, after))


def relayout_kernel(n, first, count, scal, src, out, *refs):
    fetched, paired, packed, arrivals, departures = refs[-5:]
    low = low_lanes(n)
    place_of = members_of(first == 0)
    steps = [(k, i) for k in range(count) for i in range(256 // n)]

    def fetch(k, i, group):
        rows = pl.ds(i * 8 * n, 8 * n)
        return pltpu.make_async_copy(
            src.at[2 * first + 2 * k + group, rows],
            fetched.at[2 * k + group, rows],
            arrivals.at[2 * k + group, i],
        )

    def leave(k, i):
        rows = pl.ds(i * 2 * n, 2 * n)
        return pltpu.make_async_copy(
            packed.at[pl.ds(4 * k, 4), rows], out.at[pl.ds(4 * k, 4), rows], departures.at[k, i]
        )

    for k, i in steps:
        for group in range(2):
            fetch(k, i, group).start()
    for k, i in steps:
        for group in range(2):
            fetch(k, i, group).wait()
        for piece in range(4):
            for half in range(2):
                pair = []
                for j in (2 * half, 2 * half + 1):
                    group, line = place_of(piece, j)
                    rows = pl.ds(i * 8 * n + line, n, stride=8)
                    pair.append(fetched[2 * k + group, rows, :])
                a, b = pair
                at = 2 * piece + half
                paired[at, pl.ds(0, n, stride=2), :] = jnp.where(low, a, pltpu.roll(b, 64, 1))
                paired[at, pl.ds(1, n, stride=2), :] = jnp.where(low, pltpu.roll(a, 64, 1), b)
                lanes = slice(half * 128, (half + 1) * 128)
                rows = slice(i * 2 * n, (i + 1) * 2 * n)
                packed[4 * k + piece, rows, lanes] = paired[at].astype(packed.dtype)
        leave(k, i).start()
    if len(refs) == 6:
        for k in range(count):
            refs[0][k] = packed[4 * k + scal[1]]
    for k, i in steps:
        leave(k, i).wait()


def relayout(scal, array, dtype, first, count, mine=False, n=128, after=()):
    shapes = [jax.ShapeDtypeStruct((4 * count, 512, 256), dtype)]
    specs = [mem(pl.ANY)]
    if mine:
        shapes.append(jax.ShapeDtypeStruct((count, 512, 256), dtype))
        specs.append(full(shapes[1]))
    return launch(
        functools.partial(relayout_kernel, n, first, count),
        [scal, native_view(array)],
        shapes,
        "relayout",
        specs=[mem(pltpu.SMEM), mem(pl.ANY)],
        after=after,
        cost=2 * count,
        vmem=24,
        out_specs=specs,
        scratch_shapes=[
            pltpu.VMEM((2 * count, 2048, 128), jnp.float32),
            pltpu.VMEM((8, 2 * n, 128), jnp.float32),
            pltpu.VMEM((4 * count, 512, 256), dtype),
            pltpu.SemaphoreType.DMA((2 * count, 256 // n)),
            pltpu.SemaphoreType.DMA((count, 256 // n)),
        ],
    )


def add_up(groups):
    for parts, target in groups:
        values = [part[...].astype(jnp.float32) for part in parts]
        while len(values) > 1:
            values = [sum(values[i : i + 2]) for i in range(0, len(values), 2)]
        if isinstance(target, list):
            for i, part in enumerate(target):
                part[...] = values[0][i].astype(part.dtype)
        else:
            target[...] = values[0].astype(target.dtype)


def grouped(refs, counts, targets):
    refs = iter(refs)
    return [([next(refs) for _ in range(n)], target) for n, target in zip(counts, targets)]


def normalized(x):
    centred = x - jnp.mean(x, axis=-1, keepdims=True)
    spread = jnp.mean(centred * centred, axis=-1, keepdims=True)
    root = lax.rsqrt(spread + norm_epsilon)
    return centred * root, root


def halves(values, first):
    left, right = values[:, :512], values[:, 512:]
    return jnp.where(first, left, right), jnp.where(first, right, left)


def whole(own, other, first):
    return jnp.concatenate([jnp.where(first, own, other), jnp.where(first, other, own)], axis=1)


def norm_back(grad, hat, root, gain):
    scaled = grad * gain
    along = jnp.mean(scaled * hat, axis=-1, keepdims=True)
    return root * (scaled - jnp.mean(scaled, axis=-1, keepdims=True) - hat * along)


def turned(values, cosine, sine):
    lane = lax.broadcasted_iota(jnp.int32, values.shape, 1) % HD
    other = jnp.where(lane < 8, pltpu.roll(values, 120, 1), pltpu.roll(values, 8, 1))
    return values * cosine + other * sine


def project_kernel(scal, x, cot, norms, bias, cosine, sine, own, r0, r1, r2, r3, send):
    first = scal[0] == 0
    hat, _ = normalized(x[...].astype(jnp.float32))
    h = (hat * norms[0:1] + norms[1:2]).astype(jnp.bfloat16)
    h_own, h_other = halves(h, first)
    c_own, c_other = halves(cot[...], first)
    tokens = h.shape[0]
    low = low_lanes(tokens)
    for r, other in enumerate((r0, r1, r2, r3)):
        head = scal[1] ^ r
        mine = own[head]
        theirs = other[...]
        pre = dot(h_own, mine) + dot(h_other, theirs) + bias[pl.ds(head, 1), :]
        back = dot(c_own, mine[:, 128:]) + dot(c_other, theirs[:, 128:])
        left = turned(pre[:, :128], cosine[...], sine[...]).astype(jnp.bfloat16)
        right = jnp.where(low, pre[:, 128:], back).astype(jnp.bfloat16)
        for s in range(2):
            rows = slice(128 * s, 128 * s + 128)
            send[4 * s + head, :, :128] = left[rows]
            send[4 * s + head, :, 128:] = right[rows]


def attention_kernel(rows_ref, seg, out, key_total, value_total):
    key_total[...] = jnp.zeros_like(key_total)
    value_total[...] = jnp.zeros_like(value_total)
    step = 256
    for block in range(rows_ref.shape[0] // step):
        rows = slice(block * step, (block + 1) * step)
        n = (block + 1) * step
        query = rows_ref[rows, 0:HD] * jnp.bfloat16(0.125)
        grad = rows_ref[rows, 3 * HD : 4 * HD]
        keys = rows_ref[0:n, HD : 2 * HD]
        values = rows_ref[0:n, 2 * HD : 3 * HD]
        scores = dot(query, keys, NT)
        query_place = block * step + lax.broadcasted_iota(jnp.int32, (step, n), 0)
        key_place = lax.broadcasted_iota(jnp.int32, (step, n), 1)
        allowed = (key_place <= query_place) & (key_place >= seg[rows, :])
        scores = jnp.where(allowed, scores, masked_score)
        weights = jnp.exp(scores - jnp.max(scores, axis=-1, keepdims=True))
        weights = jnp.where(allowed, weights, 0.0)
        weights = weights * (1.0 / jnp.sum(weights, axis=-1, keepdims=True))
        short = weights.astype(jnp.bfloat16)
        attended = dot(short, values)
        weight_grad = dot(grad, values, NT)
        delta = jnp.sum(weights * weight_grad, axis=-1, keepdims=True)
        score_grad = (weights * (weight_grad - delta)).astype(jnp.bfloat16)
        query_grad = dot(score_grad, keys) * 0.125
        key_total[0:n, :] += dot(score_grad, query, TN)
        value_total[0:n, :] += dot(short, grad, TN)
        out[rows, 0:HD] = query_grad.astype(jnp.bfloat16)
        out[rows, 3 * HD : 4 * HD] = attended.astype(jnp.bfloat16)
    out[:, HD : 2 * HD] = key_total[...].astype(jnp.bfloat16)
    out[:, 2 * HD : 3 * HD] = value_total[...].astype(jnp.bfloat16)


def feed_forward_kernel(
    scal, x, cot, norms, bias, weights, r0, r1, r2, r3,
    branch, input_part, keep, send, hidden_sums, norm_grads, cot_sums,
):
    first = scal[0] == 0
    hat, root = normalized(x[...].astype(jnp.float32))
    h = (hat * norms[2:3] + norms[3:4]).astype(jnp.bfloat16)
    h_own, h_other = halves(h, first)
    c_own, c_other = halves(cot[...], first)
    cot_sums[...] = jnp.sum(cot[...].astype(jnp.float32), axis=0, keepdims=True)
    outs = [0.0] * 4
    for r, other in enumerate((r0, r1, r2, r3)):
        piece = scal[1] ^ r
        in_own, in_other = weights[piece], other[0]
        down_own, down_other = weights[4 + piece], other[1]
        pre = dot(h_own, in_own) + dot(h_other, in_other) + bias[pl.ds(piece, 1), :]
        cumulative = 0.5 * (1.0 + lax.erf(pre * 0.7071067811865476))
        slope = cumulative + pre * (0.3989422804014327 * jnp.exp(-0.5 * pre * pre))
        act = (pre * cumulative).astype(jnp.bfloat16)
        act_grad = dot(c_own, down_own) + dot(c_other, down_other)
        grad = (act_grad * slope).astype(jnp.bfloat16)
        hidden_sums[pl.ds(piece, 1), :] = jnp.sum(
            grad.astype(jnp.float32), axis=0, keepdims=True
        )
        outs[0] += dot(act, down_own, NT)
        outs[1] += dot(act, down_other, NT)
        outs[2] += dot(grad, in_own, NT)
        outs[3] += dot(grad, in_other, NT)
        target = send if r % 2 else keep
        target[r // 2, 0] = grad
        target[r // 2, 1] = act
    branch[...] = whole(outs[0], outs[1], first)
    second = whole(outs[2], outs[3], first)
    norm_grads[0:1] = jnp.sum(second * hat, axis=0, keepdims=True)
    norm_grads[1:2] = jnp.sum(second, axis=0, keepdims=True)
    input_part[...] = norm_back(second, hat, root, norms[2:3])


def both_cores(scal, x, x_beside, cot, cot_beside, norms, at):
    first = scal[0] == 0
    tokens = jnp.concatenate([x[...], x_beside[...]], axis=0).astype(jnp.float32)
    hat, _ = normalized(tokens)
    h = (hat * norms[at : at + 1] + norms[at + 1 : at + 2]).astype(jnp.bfloat16)
    c = jnp.concatenate([cot[...], cot_beside[...]], axis=0)
    return list(zip(halves(h, first), halves(c, first)))


def unit_grads_kernel(
    scal, x, x_beside, cot, cot_beside, norms, keep, came, in_keep, in_send, down_keep, down_send
):
    for side, (h, c) in enumerate(both_cores(scal, x, x_beside, cot, cot_beside, norms, 2)):
        for far in range(2):
            grad = jnp.concatenate([keep[far, 0], came[far, 0]], axis=0)
            act = jnp.concatenate([keep[far, 1], came[far, 1]], axis=0)
            (in_send if side else in_keep)[far] = dot(h, grad, TN).astype(jnp.bfloat16)
            (down_send if far else down_keep)[side] = dot(c, act, TN).astype(jnp.bfloat16)


def combine_kernel(in_keep, in_came, down_keep, down_came, own, in_send, down_send):
    pairs = ((in_keep, in_came, in_send), (down_keep, down_came, down_send))
    for k, (keep, came, send) in enumerate(pairs):
        total = keep[...].astype(jnp.float32) + came[...].astype(jnp.float32)
        own[k] = total[0].astype(jnp.bfloat16)
        send[0] = total[1].astype(jnp.bfloat16)


def turn_kernel(scal, cosine, sine, back, keep, send, sums):
    low = low_lanes(keep.shape[1])
    for r in range(4):
        head = scal[1] ^ r
        grads = jnp.concatenate([back[head], back[4 + head]], axis=0)
        left = turned(grads[:, :128].astype(jnp.float32), cosine[...], -sine[...])
        left = left.astype(jnp.bfloat16)
        right = grads[:, 128:]
        target = send if r % 2 else keep
        target[r // 2, :, :128] = left
        target[r // 2, :, 128:] = right
        right = jnp.where(low, right.astype(jnp.float32), 0.0)
        wide = jnp.concatenate([left.astype(jnp.float32), right], axis=1)
        sums[pl.ds(head, 1), :] = jnp.sum(wide, axis=0, keepdims=True)


def split_last(piece):
    wide = piece.astype(jnp.float32)
    lane = lax.broadcasted_iota(jnp.int32, (1, wide.shape[1]), 1)
    share = (lane < 3 * HD).astype(jnp.float32)
    pre_grad = (wide * share).astype(jnp.bfloat16)
    attended = (wide * (1.0 - share)).astype(jnp.bfloat16)
    return pre_grad, attended


def head_grads_kernel(
    scal, x, x_beside, cot, cot_beside, norms, keep, came, totals, *outs
):
    both = totals[...].reshape(64, 256)
    coarse = both.astype(jnp.bfloat16)
    fine = (both - coarse.astype(jnp.float32)).astype(jnp.bfloat16)
    sides = both_cores(scal, x, x_beside, cot, cot_beside, norms, 0)
    a_keep, a_send, b_keep, b_send = outs
    for far in range(2):
        piece = jnp.concatenate([keep[far], came[far]], axis=0)
        pre_grad, attended = split_last(piece)
        for side, (h, c) in enumerate(sides):
            grad = (dot(h, pre_grad, TN) + dot(c, attended, TN)).astype(jnp.bfloat16)
            target = a_send if side else a_keep
            target[far, 0:256] = grad[0:256]
            target[far, 256:320] = coarse
            target[far, 320:384] = fine
            (b_send if far else b_keep)[side] = grad[256:512]


def combine_heads_kernel(a_keep, a_came, b_keep, b_came, a_own, a_send, b_own, b_send):
    for targets, at in (((a_own, b_own), 0), ((a_send, b_send), 1)):
        total = a_keep[at].astype(jnp.float32) + a_came[at].astype(jnp.float32)
        targets[0][0:256] = total[0:256].astype(jnp.bfloat16)
        tail = total[256:320] + total[320:384]
        coarse = tail.astype(jnp.bfloat16)
        targets[0][256:320] = coarse
        targets[0][320:384] = (tail - coarse.astype(jnp.float32)).astype(jnp.bfloat16)
        total = b_keep[at].astype(jnp.float32) + b_came[at].astype(jnp.float32)
        targets[1][...] = total.astype(jnp.bfloat16)


def add_kernel(near, came, kept, passed):
    add_up([((near, came), [kept, passed])])


def gather_kernel(
    scal, x, norms, keep, send, weights, r0, r1, r2, r3, ff_branch, ff_part,
    norm_two, cot_sums, unit_sums, qkv_sums, near, far, totals, parts,
):
    first = scal[0] == 0
    hat, root = normalized(x[...].astype(jnp.float32))
    outs = [0.0] * 4
    for r, other in enumerate((r0, r1, r2, r3)):
        mine, theirs = weights[scal[1] ^ r], other[0]
        pre_grad, attended = split_last((send if r % 2 else keep)[r // 2])
        outs[0] += dot(attended, mine, NT)
        outs[1] += dot(attended, theirs, NT)
        outs[2] += dot(pre_grad, mine, NT)
        outs[3] += dot(pre_grad, theirs, NT)
    branch = ff_branch[...] + whole(outs[0], outs[1], first)
    grad = whole(outs[2], outs[3], first)
    totals[...] = jnp.zeros_like(totals)
    rows = [jnp.sum(grad * hat, axis=0, keepdims=True), jnp.sum(grad, axis=0, keepdims=True)]
    rows += [norm_two[0:1], norm_two[1:2], cot_sums[...]]
    for i, row in enumerate(rows):
        for q in range(4):
            at = 4 * (i % 2) + q
            totals[i // 2, at : at + 1, :] = row[:, 256 * q : 256 * q + 256]
    totals[3 + scal[2], 0:4, :] = qkv_sums[...]
    totals[3 + scal[2], 4:8, :] = unit_sums[...]
    input_part = ff_part[...] + norm_back(grad, hat, root, norms[0:1])
    for q in range(4):
        parts[q, 0] = branch[64 * q : 64 * q + 64].astype(jnp.bfloat16)
        parts[q, 1] = input_part[64 * q : 64 * q + 64].astype(jnp.bfloat16)
    for r in range(4):
        (far if r % 2 else near)[r // 2] = parts[scal[2] ^ r]


def finish_rows_kernel(scal, x, cot, bias, r0, r1, r2, r3, block_output, input_grad):
    for r, piece in enumerate((r0, r1, r2, r3)):
        q = scal[2] ^ r
        block_output[q] = x[q].astype(jnp.float32) + piece[0].astype(jnp.float32) + bias[...]
        input_grad[q] = cot[q].astype(jnp.float32) + piece[1].astype(jnp.float32)


def gram_of_piece(total, momenta, grads, grams):
    short = total.astype(jnp.bfloat16)
    grads[0] = short
    update = 1.95 * short.astype(jnp.float32) + 0.9025 * momenta[0]
    gram = dot(update, update, TN, lax.Precision.HIGHEST)
    for j in range(4):
        cut = slice(j * HD, (j + 1) * HD)
        grams[0, j] = gram[cut, cut]


def unit_gram_kernel(place, own, in_came, down_came, momenta, kept, came, *refs):
    grads, grams, total = refs[-3:]

    @pl.when(pl.program_id(0) == 0)
    def _():
        add_up([((kept, came), total)])

    a = in_came[0].astype(jnp.float32)
    b = down_came[0].astype(jnp.float32)
    other = jnp.where(pl.program_id(0) == 0, a, b)
    gram_of_piece(own[0].astype(jnp.float32) + other, momenta, grads, grams)


def head_gram_kernel(place, a_own, a_came, b_own, b_came, momenta, *refs):
    grads, grams, totals = refs[-3:]
    a = a_own[...].astype(jnp.float32) + a_came[...].astype(jnp.float32)
    b = b_own[...].astype(jnp.float32) + b_came[...].astype(jnp.float32)
    gram_of_piece(jnp.concatenate([a[0:256], b], axis=0), momenta, grads, grams)
    totals[...] = (a[256:320] + a[320:384]).reshape(8, 8, 256)


def gram_of(kernel, first, others, momenta, place, more, shapes, after=()):
    chunks = momenta.shape[0] // 4
    piece = pl.BlockSpec((1, 512, 256), lambda i, s: (i, 0, 0))
    block = pl.BlockSpec((1, 512, 256), lambda i, s: (4 * i + s[1], 0, 0))
    return pl.pallas_call(
        kernel,
        grid_spec=pltpu.PrefetchScalarGridSpec(
            num_scalar_prefetch=1,
            grid=(chunks,),
            in_specs=[piece if first.ndim == 3 else full(first)]
            + [full(other) for other in others]
            + [block]
            + [full(part) for part in more]
            + [corner(a) for a in after],
            out_specs=[piece, pl.BlockSpec((1, 4, HD, HD), lambda i, s: (i, 0, 0, 0))]
            + [full(shape) for shape in shapes],
        ),
        out_shape=[
            jax.ShapeDtypeStruct((chunks, 512, 256), jnp.bfloat16),
            jax.ShapeDtypeStruct((chunks, 4, HD, HD), jnp.float32),
            *map(out_hbm, shapes),
        ],
        compiler_params=limits(20),
        cost_estimate=takes(2.5),
        name="gram",
    )(place, *map(in_hbm, [first, *others, momenta, *more, *after]))


def newton_kernel(counts, mine, theirs, *refs):
    taken = sum(counts)
    out = refs[taken]
    add_up(grouped(refs, counts, refs[taken + 1 :]))
    linear, square, cubic = quintic
    shape = (HD, HD)
    eye = lax.broadcasted_iota(jnp.int32, shape, 0) == lax.broadcasted_iota(jnp.int32, shape, 1)
    full = lax.Precision.HIGHEST
    chunks = mine.shape[0]
    places = [(i, j) for i in range(chunks) for j in range(4)]
    states = []
    for i, j in places:
        gram = mine[i, j] + theirs[i, j]
        trace = jnp.sum(jnp.where(eye, gram, 0.0), axis=(0, 1), keepdims=True)
        scale = 1.0 / (jnp.sqrt(trace) + muon_epsilon)
        states.append([gram * scale * scale, None, scale])
    for iteration in range(NEWTON):
        squares = [dot(s[0], s[0], precision=full) for s in states]
        steps = [
            jnp.where(eye, linear, 0.0) + square * s[0] + cubic * sq
            for s, sq in zip(states, squares)
        ]
        if iteration == 0:
            halfway = [dot(s[0], m, precision=full) for s, m in zip(states, steps)]
            for s, m in zip(states, steps):
                s[1] = m
        elif iteration < NEWTON - 1:
            both = [
                dot(jnp.concatenate([s[0], s[1]], axis=0), m, precision=full)
                for s, m in zip(states, steps)
            ]
            halfway = [x[:HD] for x in both]
            for s, x in zip(states, both):
                s[1] = x[HD:]
        else:
            for s, m in zip(states, steps):
                s[1] = dot(s[1], m, precision=full)
        if iteration < NEWTON - 1:
            for s, x, m in zip(states, halfway, steps):
                s[0] = dot(x, m, precision=full)
    for (i, j), s in zip(places, states):
        mix = s[1] * s[2]
        coarse = mix.astype(jnp.bfloat16)
        fine = (mix - coarse.astype(jnp.float32)).astype(jnp.bfloat16)
        rows, lanes = slice(64 * (j // 2), 64 * (j // 2) + 64), slice(128 * (j % 2), 128 * (j % 2) + 128)
        out[i, rows, lanes] = jnp.concatenate([coarse, fine], axis=1)


def newton(mine, theirs, sums, after=()):
    flat = [part for group in sums for part in group]
    operands = [mine, theirs, *flat]
    return launch(
        functools.partial(newton_kernel, [len(group) for group in sums]),
        operands,
        [jax.ShapeDtypeStruct((mine.shape[0], 2 * HD, 256), jnp.bfloat16)]
        + [jax.ShapeDtypeStruct(group[0].shape, group[0].dtype) for group in sums],
        "newton",
        cost=3.5,
        specs=[full(a) for a in operands],
        after=after,
    )


def update_kernel(
    n, head, scal, g0, g1, g2, g3, q0, q1, q2, q3, momenta, native_momenta, native, *refs
):
    grads, weights, moved, mixing, first, second, steps = refs[-7:]
    place_of = members_of(head)

    @pl.when((pl.program_id(0) == 0) & (pl.program_id(1) == 0))
    def _():
        mixing[...] = jnp.zeros_like(mixing)

    @pl.when(pl.program_id(1) == 0)
    def _():
        for r, q in enumerate((q0, q1, q2, q3)):
            for j in range(4):
                at = slice(HD * (j // 2), HD * (j // 2) + HD), slice(128 * (j % 2), 128 * (j % 2) + 128)
                wide = q[(0,) * (len(q.shape) - 2) + at].astype(jnp.float32)
                other = pltpu.roll(wide, HD, 1)
                below = low_lanes(HD) == (j % 2 == 0)
                rows = slice(j * HD, (j + 1) * HD)
                lanes = slice(128 * (j // 2), 128 * (j // 2) + 128)
                pair = (wide, other) if j % 2 == 0 else (other, wide)
                for level in range(2):
                    part = jnp.where(below, pair[level], 0.0)
                    mixing[r, level, rows, lanes] = part.astype(jnp.bfloat16)

    low = low_lanes(n)
    for r, piece in enumerate((g0, g1, g2, g3)):
        place = scal[1] ^ r
        grad = piece[(0,) * (len(piece.shape) - 2)].astype(jnp.float32)
        update = 1.95 * grad + 0.9025 * momenta[place]
        coarse = update.astype(jnp.bfloat16)
        fine = (update - coarse.astype(jnp.float32)).astype(jnp.bfloat16)
        settled = dot(coarse, mixing[r, 0]) + dot(coarse, mixing[r, 1]) + dot(fine, mixing[r, 0])
        for half in range(2):
            k = 2 * r + half
            first[k] = grad[:, half * 128 : (half + 1) * 128]
            second[k] = settled[:, half * 128 : (half + 1) * 128]
            for source, target in ((first, grads), (second, steps)):
                even = source[k, pl.ds(0, n, stride=2), :]
                odd = source[k, pl.ds(1, n, stride=2), :]
                lines = (
                    jnp.where(low, even, pltpu.roll(odd, 64, 1)),
                    jnp.where(low, pltpu.roll(even, 64, 1), odd),
                )
                for w in range(2):
                    group, line = place_of(place, 2 * half + w)
                    target[group, pl.ds(line, n, stride=8), :] = lines[w]
    moved[...] = momentum_decay * native_momenta[...] + grads[...]
    weight = native[...]
    weights[...] = weight - muon_rate * (4.0 * steps[...] + weight_decay * weight)


def update(
    first, scal, own, far, mix, mix_far, beside, momenta, native_momenta, native, before=(), after=(), n=128
):
    chunks = own.shape[0]
    block = pl.BlockSpec((2, 8 * n, 128), lambda k, i: (first + k, i, 0))
    piece = pl.BlockSpec((1, 2 * n, 256), lambda k, i: (k, i, 0))
    factor = pl.BlockSpec((1, 2 * HD, 256), lambda k, i: (k, 0, 0))
    pieces, factors = [piece, None, piece, None], [factor, None, factor, None]
    for r in (0, 1):
        pieces[2 * r + 1] = pl.BlockSpec((1, 1, 2 * n, 256), lambda k, i, r=r: (r, k, i, 0))
        factors[2 * r + 1] = pl.BlockSpec((1, 1, 2 * HD, 256), lambda k, i, r=r: (r, k, 4, 0))
    grads, mixes = [own, beside, far, beside], [mix, beside, mix_far, beside]
    return launch(
        functools.partial(update_kernel, n, first == 0),
        [scal, *grads, *mixes, momenta, native_view(native_momenta), native_view(native), *before],
        [jax.ShapeDtypeStruct((6, 2048, 128), jnp.float32)] * 3,
        "update",
        specs=[mem(pltpu.SMEM)]
        + pieces
        + factors
        + [pl.BlockSpec((4, 2 * n, 256), lambda k, i: (k, i, 0)), block, block]
        + [mem(pl.ANY)] * len(before),
        after=after,
        vmem=32,
        cost=5.5 * chunks,
        grid=(chunks, 256 // n),
        out_specs=[block] * 3,
        scratch_shapes=[
            pltpu.VMEM((4, 2, 256, 256), jnp.bfloat16),
            pltpu.VMEM((8, 2 * n, 128), jnp.float32),
            pltpu.VMEM((8, 2 * n, 128), jnp.float32),
            pltpu.VMEM((2, 8 * n, 128), jnp.float32),
        ],
        input_output_aliases={12 + i: i for i in range(len(before))},
    )


def whole_device(
    inputs, cotangent, matrices, momenta, small, small_first, small_second, segments, positions
):
    blk_at = lax.axis_index("blk")
    ctx_at = lax.axis_index("ctx")
    tp_at = lax.axis_index("tp")
    scal = jnp.stack([blk_at, ctx_at, tp_at]).astype(jnp.int32)
    sequences, local_rows, width = inputs.shape
    tokens = sequences * local_rows
    both = ("blk", "ctx")
    f32, bf16 = jnp.float32, jnp.bfloat16
    shaped = jax.ShapeDtypeStruct

    def hop(values, by):
        return lax.ppermute(values, both, [(i, i ^ by) for i in range(8)])

    def hop_tp(values, by):
        return lax.ppermute(values, "tp", [(i, i ^ by) for i in range(4)])

    def tied(values, *results):
        return lax.optimization_barrier((values, *results))[0]

    def spread(piece):
        c = hop(piece, 2)
        return [piece, hop(piece, 1), c, hop(c, 1)]

    x = inputs.reshape(tokens, width)
    cot = cotangent.reshape(tokens, width)
    norms = small[: 4 * width].reshape(4, width)
    qkv_start = 6 * width + tp_at * 4 * 3 * HD
    qkv_bias = lax.dynamic_slice_in_dim(small, qkv_start, 4 * 3 * HD).reshape(4, 3 * HD)
    qkv_bias = jnp.pad(qkv_bias, ((0, 0), (0, HD)))
    unit_start = 6 * width + H * 3 * HD + tp_at * 1024
    unit_bias = lax.dynamic_slice_in_dim(small, unit_start, 1024).reshape(4, 256)
    lane = jnp.arange(128) % HD
    frequency = rope_base ** (-2.0 * (lane % 8).astype(f32) / ROTARY)
    angles = positions.astype(f32).reshape(tokens, 1) * frequency
    cosine = jnp.where(lane < ROTARY, jnp.cos(angles), 1.0)
    sign = jnp.where(lane < 8, -1.0, jnp.where(lane < ROTARY, 1.0, 0.0))
    sine = jnp.sin(angles) * sign

    head_weights, mine = relayout(scal, matrices, bf16, 0, 1, mine=True)
    first_hop = hop(mine, 4)
    unit_weights, mine_units = relayout(scal, matrices, bf16, 1, 2, mine=True, after=(mine,))
    first_hop = tied(first_hop, mine_units)
    other_heads = spread(first_hop)
    (piled_heads,) = relayout(scal, momenta, f32, 0, 1, after=(first_hop,))
    units_near = hop(tied(mine_units, first_hop), 4)
    x_beside = hop(x, 1)
    cot_beside = hop(cot, 1)

    send = launch(
        project_kernel,
        [scal, x, cot, norms, qkv_bias, cosine, sine, head_weights]
        + [piece[0] for piece in other_heads],
        shaped((8, local_rows, 256), bf16),
        "project",
    )
    arrived = lax.all_to_all(send, both, split_axis=0, concat_axis=0, tiled=True)
    (piled_units,) = relayout(scal, momenta, f32, 1, 2, after=(send,))
    units_near = tied(units_near, send)
    units_far = hop(units_near, 2)
    units_beside = hop(units_near, 1)
    documents = lax.dynamic_index_in_dim(segments, blk_at, 0, keepdims=False)
    length = documents.shape[0]
    attended = launch(
        attention_kernel,
        [arrived.reshape(length, 256), documents.reshape(length, 1)],
        shaped((length, 256), bf16),
        "attention",
        cost=6,
        specs=[full(arrived.reshape(length, 256)), pl.BlockSpec((length, 1), lambda *_: (0, 0))],
        after=(piled_heads, piled_units),
        scratch_shapes=[pltpu.VMEM((length, HD), f32)] * 2,
    )
    back = lax.all_to_all(
        attended.reshape(8, local_rows, 256), both, split_axis=0, concat_axis=0, tiled=True
    )

    units_far = tied(units_far, attended)
    other_units = [units_near, units_beside, units_far, hop(units_far, 1)]
    ff_branch, ff_part, unit_keep, unit_send, unit_sums, norm_two, cot_sums = launch(
        feed_forward_kernel,
        [scal, x, cot, norms, unit_bias, unit_weights, *other_units],
        [
            shaped((tokens, width), f32),
            shaped((tokens, width), f32),
            shaped((2, 2, tokens, 256), bf16),
            shaped((2, 2, tokens, 256), bf16),
            shaped((4, 256), f32),
            shaped((2, width), f32),
            shaped((1, width), f32),
        ],
        "feed_forward",
        cost=5.5,
        after=(attended,),
    )
    head_keep, head_send, qkv_sums = launch(
        turn_kernel,
        [scal, cosine, sine, back],
        [shaped((2, tokens, 256), bf16)] * 2 + [shaped((4, 256), f32)],
        "turn",
        cost=2,
        after=(unit_sums,),
    )
    in_keep, in_send, down_keep, down_send = launch(
        unit_grads_kernel,
        [scal, x, x_beside, cot, cot_beside, norms, unit_keep, hop(unit_send, 1)],
        [shaped((2, 512, 256), bf16)] * 4,
        "unit_grads",
        cost=3.5,
        after=(qkv_sums,),
    )
    sums = [norm_two, cot_sums, unit_sums, qkv_sums]
    near, far, totals = launch(
        gather_kernel,
        [scal, x, norms, head_keep, head_send, head_weights, *other_heads, ff_branch, ff_part, *sums],
        [shaped((2, 2, 64, width), bf16)] * 2 + [shaped((8, 8, 256), f32)],
        "gather",
        after=(in_keep,),
        scratch_shapes=[pltpu.VMEM((4, 2, 64, width), bf16)],
    )
    a_keep, a_send, b_keep, b_send = launch(
        head_grads_kernel,
        [scal, x, x_beside, cot, cot_beside, norms, head_keep, hop(head_send, 1), totals],
        [shaped((2, 384, 256), bf16)] * 2 + [shaped((2, 256, 256), bf16)] * 2,
        "head_grads",
        cost=4,
    )
    came = hop_tp(far, 1)
    a_came, b_came = hop(a_send, 4), hop(b_send, 2)
    operands = [in_keep, hop(in_send, 4), down_keep, hop(down_send, 2)]
    own, in_send, down_send = launch(
        combine_kernel,
        operands,
        [shaped((2, 512, 256), bf16)] + [shaped((1, 512, 256), bf16)] * 2,
        "combine",
        specs=[full(a) for a in operands],
        cost=2,
        after=(a_keep,),
    )
    in_came, down_came = hop(in_send, 2), hop(down_send, 4)
    kept, passed = launch(
        add_kernel,
        [near, came],
        [shaped((2, 64, width), bf16)] * 2,
        "add",
        specs=[full(near)] * 2,
        after=(in_send,),
    )
    passed = hop_tp(passed, 2)
    operands = [a_keep, a_came, b_keep, b_came]
    a_own, a_send, b_own, b_send = launch(
        combine_heads_kernel,
        operands,
        [shaped((384, 256), bf16)] * 2 + [shaped((256, 256), bf16)] * 2,
        "combine_heads",
        specs=[full(a) for a in operands],
        after=(kept,),
    )
    a_came, b_came = hop(a_send, 2), hop(b_send, 4)
    unit_sum, unit_grams, total = gram_of(
        unit_gram_kernel,
        own,
        [in_came, down_came],
        piled_units,
        scal,
        [kept, passed],
        [shaped((2, 64, width), bf16)],
        after=(a_own,),
    )
    unit_theirs = hop(unit_grams, 4)
    unit_far = hop(unit_sum, 2)
    total_far = hop_tp(total, 2)
    head_sum, head_grams, totals = gram_of(
        head_gram_kernel,
        a_own,
        [a_came, b_own, b_came],
        piled_heads,
        scal,
        [],
        [shaped((8, 8, 256), f32)],
        after=(unit_sum,),
    )
    head_theirs = hop(head_grams, 4)
    head_far = hop(head_sum, 2)
    (unit_mix,) = newton(unit_grams, unit_theirs, [], after=(head_sum,))
    unit_mix_far = hop(unit_mix, 2)
    head_mix, totals = newton(
        head_grams,
        head_theirs,
        [(totals, hop(totals, 1))],
        after=(unit_mix, unit_far, total_far),
    )
    head_mix_far = hop(head_mix, 2)

    def to_beside(*pieces):
        return hop(jnp.stack([jnp.concatenate(pair, axis=1) for pair in pieces]), 1)

    beside = to_beside((unit_sum, unit_mix), (unit_far, tied(unit_mix_far, head_mix)))
    totals_came = hop_tp(totals, 1)
    before = update(
        1, scal, unit_sum, unit_far, unit_mix, unit_mix_far, beside, piled_units, momenta, matrices,
        after=(head_mix,),
    )
    head_far, head_mix_far = tied((head_far, head_mix_far), before[0])
    beside = to_beside((head_sum, head_mix), (head_far, head_mix_far))
    outs = update(
        0, scal, head_sum, head_far, head_mix, head_mix_far, beside, piled_heads, momenta, matrices,
        before,
    )
    total_beside = hop_tp(tied(jnp.stack([total, total_far]), head_mix), 1)
    totals = tied(totals + totals_came, before[0])
    totals = totals + hop_tp(totals, 2)

    block_output, input_grad = launch(
        finish_rows_kernel,
        [
            scal,
            x.reshape(4, 64, width),
            cot.reshape(4, 64, width),
            (small[4 * width : 5 * width] + small[5 * width : 6 * width]).reshape(1, width),
            total,
            total_beside[0],
            total_far,
            total_beside[1],
        ],
        [shaped((4, 64, width), f32)] * 2,
        "finish_rows",
        cost=2,
        after=(before[0],),
    )

    cot_total = totals[2, :4].reshape(-1) * 0.25
    small_grads = jnp.concatenate(
        [
            totals[:2].reshape(-1),
            cot_total,
            cot_total,
            totals[3:7, :4, : 3 * HD].reshape(-1),
            totals[3:7, 4:].reshape(-1),
        ]
    )
    return (
        block_output.reshape(inputs.shape),
        input_grad.reshape(inputs.shape),
        native_back(outs[0]),
        native_back(outs[1]),
        native_back(outs[2]),
        small_grads,
        *small_step(small, small_first, small_second, small_grads),
    )


def small_step(small, small_first, small_second, small_grads):
    new_first = adam_first * small_first + (1.0 - adam_first) * small_grads
    new_second = adam_second * small_second + (1.0 - adam_second) * small_grads * small_grads
    corrected = new_first / (1.0 - adam_first**STEP)
    spread = jnp.sqrt(new_second / (1.0 - adam_second**STEP))
    new_small = small - small_rate * corrected / (spread + adam_epsilon)
    return new_first, new_second, new_small


def solution(mesh):
    in_specs = (
        P(None, ("blk", "ctx"), None),
        P(None, ("blk", "ctx"), None),
        P("tp", "blk"),
        P("tp", "blk"),
        P(),
        P(),
        P(),
        P(),
        P(None, ("blk", "ctx")),
    )
    out_specs = (
        P(None, ("blk", "ctx"), None),
        P(None, ("blk", "ctx"), None),
        P("tp", "blk"),
        P("tp", "blk"),
        P("tp", "blk"),
        P(),
        P(),
        P(),
        P(),
    )
    one_each = mesh.shape["blk"] == SEQS and mesh.shape["ctx"] * mesh.shape["tp"] == H
    one_each = one_each and mesh.shape["tp"] == 4
    return jax.shard_map(
        whole_device if one_each else on_device, mesh=mesh, in_specs=in_specs, out_specs=out_specs, check_vma=False
    )
```

```python
import functools

import jax
import jax.numpy as jnp
from jax import lax
from jax.experimental import pallas as pl
from jax.experimental.pallas import tpu as pltpu
from jax.sharding import PartitionSpec as P

MODEL_DIM = 1024
H = 16
HD = 64
FF = 4096
ROTARY = 16
NEWTON = 5
STEP = 10
SEQS = 2


norm_epsilon = 1e-05
rope_base = 10000.0
masked_score = -1e30
momentum_decay = 0.95
muon_rate = 0.2
weight_decay = 0.01
muon_epsilon = 1e-07
quintic = (3.4445, -4.775, 2.0315)
adam_first = 0.9
adam_second = 0.95
adam_epsilon = 1e-08
small_rate = 0.2


def passed_along(x, axis, by):
    devices = lax.axis_size(axis)
    pairs = [(i, i + by) for i in range(devices) if 0 <= i + by < devices]
    return lax.ppermute(x, axis, pairs)


def shifted(x, axis, by):
    devices = lax.axis_size(axis)
    return lax.ppermute(x, axis, [(i, (i + by) % devices) for i in range(devices)])


def as_sent(x):

    def short(part):
        return part.astype(jnp.bfloat16) if part.dtype == jnp.float32 else part

    return jax.tree.map(short, x)


def layer_norm(values, scaling, offset):
    centre = jnp.mean(values, axis=-1, keepdims=True)
    centred = values - centre
    spread = jnp.mean(centred * centred, axis=-1, keepdims=True)
    return centred * lax.rsqrt(spread + norm_epsilon) * scaling + offset


def rope_tables(positions):
    halfway = ROTARY // 2
    frequency = rope_base ** (-2.0 * jnp.arange(halfway, dtype=jnp.float32) / ROTARY)
    angles = positions.astype(jnp.float32)[..., None] * frequency
    return (jnp.cos(angles)[:, :, None, :], jnp.sin(angles)[:, :, None, :])


def rotate(values, cosine, sine):
    halfway = ROTARY // 2
    former = values[..., :halfway]
    latter = values[..., halfway:ROTARY]
    return jnp.concatenate(
        [former * cosine - latter * sine, latter * cosine + former * sine, values[..., ROTARY:]],
        axis=-1,
    )


def exact_gelu(values):
    return jax.nn.gelu(values, approximate=False)


def newton_schulz(blocks):
    frobenius = jnp.sqrt(jnp.sum(blocks * blocks, axis=(1, 2), keepdims=True))
    current = blocks / (frobenius + muon_epsilon)
    linear_term, square_term, cubic_term = quintic
    for iteration in range(NEWTON):
        gram_matrix = jnp.einsum("mde,mdf->mef", current, current, precision=lax.Precision.HIGHEST)
        polynomial = square_term * gram_matrix + cubic_term * jnp.einsum(
            "mef,mfg->meg", gram_matrix, gram_matrix, precision=lax.Precision.HIGHEST
        )
        current = linear_term * current + jnp.einsum(
            "mde,mef->mdf", current, polynomial, precision=lax.Precision.HIGHEST
        )
    return current


def to_heads(values):
    return lax.all_to_all(values, "ctx", split_axis=3, concat_axis=1, tiled=True)


def to_positions(values):
    return lax.all_to_all(values, "ctx", split_axis=1, concat_axis=3, tiled=True)


def pass_keys(pair):
    return passed_along(pair, "blk", 1)


def pass_grads(pair_grad):
    return shifted(pair_grad.astype(jnp.bfloat16), "blk", 1).astype(pair_grad.dtype)


def allowed_pairs(segments, query_block, key_block, block_rows):
    query_place = query_block * block_rows + jnp.arange(block_rows, dtype=jnp.int32)
    key_place = key_block * block_rows + jnp.arange(block_rows, dtype=jnp.int32)
    query_doc = lax.dynamic_slice_in_dim(segments, query_block * block_rows, block_rows, 1)
    key_doc = lax.dynamic_slice_in_dim(segments, key_block * block_rows, block_rows, 1)
    causal = key_place[None, :] <= query_place[:, None]
    return (causal[None] & (query_doc[:, :, None] == key_doc[:, None, :]))[:, None]


def masked_scores(queries, keys, allowed):
    score_scale = HD ** (-0.5)
    scores = (
        jnp.einsum("sqhe,skhe->shqk", queries, keys, preferred_element_type=jnp.float32)
        * score_scale
    )
    return jnp.where(allowed, scores, masked_score)


def on_device(
    inputs, cotangent, matrices, momenta, small, small_first, small_second, segments, positions
):
    tensor_size = lax.axis_size("tp")
    cycle_size = lax.axis_size("blk")
    context_size = lax.axis_size("ctx")
    tensor_index = lax.axis_index("tp")
    cycle_index = lax.axis_index("blk")
    sequences, local_rows, model_width = inputs.shape
    per_group = matrices.shape[0]
    head_count = H // tensor_size
    unit_blocks = FF // HD // tensor_size
    block_rows = local_rows * context_size
    gathered = lax.all_gather(matrices.astype(jnp.bfloat16), "blk", axis=1, tiled=True).reshape(
        per_group, model_width, HD
    )
    query_key_value_weight = gathered[: 3 * head_count]
    projection_out_weight = gathered[3 * head_count : 4 * head_count]
    input_weight = gathered[4 * head_count : 4 * head_count + unit_blocks]
    down_projection_weight = gathered[4 * head_count + unit_blocks :]
    qkv_start = 6 * model_width + tensor_index * head_count * 3 * HD
    query_key_value_bias = lax.dynamic_slice_in_dim(small, qkv_start, head_count * 3 * HD).reshape(
        head_count, 3, HD
    )
    unit_start = 6 * model_width + H * 3 * HD + tensor_index * unit_blocks * HD
    hidden_unit_bias = lax.dynamic_slice_in_dim(small, unit_start, unit_blocks * HD).reshape(
        unit_blocks, HD
    )
    residual = inputs.astype(jnp.float32)

    def both_norms(values, gain_one, offset_one, gain_two, offset_two):
        return (layer_norm(values, gain_one, offset_one), layer_norm(values, gain_two, offset_two))

    (normed_one, normed_two), norm_back = jax.vjp(
        both_norms,
        residual,
        small[0:model_width],
        small[model_width : 2 * model_width],
        small[2 * model_width : 3 * model_width],
        small[3 * model_width : 4 * model_width],
    )
    first_input = normed_one.astype(jnp.bfloat16)
    second_input = normed_two.astype(jnp.bfloat16)
    projected = jnp.einsum(
        "pgk,jka->pgja", first_input, query_key_value_weight, preferred_element_type=jnp.float32
    )
    projected = projected.reshape(sequences, local_rows, 3, head_count, HD) + jnp.transpose(
        query_key_value_bias, (1, 0, 2)
    )
    cosine, sine = rope_tables(positions)

    def turn_pair(query_pre, key_pre):
        return (rotate(query_pre, cosine, sine), rotate(key_pre, cosine, sine))

    (query_turned, key_turned), turn_back = jax.vjp(
        turn_pair, projected[:, :, 0], projected[:, :, 1]
    )
    stacked = jnp.stack([query_turned, key_turned, projected[:, :, 2]], axis=2).astype(jnp.bfloat16)
    by_heads = to_heads(stacked)
    queries = by_heads[:, :, 0]
    head_local = queries.shape[2]

    def forward_visit(state, pair, source):
        row_max, row_total, weighted = state
        allowed = allowed_pairs(segments, cycle_index, source, block_rows)
        scores = masked_scores(queries, pair[:, :, 0], allowed)
        new_max = jnp.maximum(row_max, jnp.max(scores, axis=-1))
        weights = jnp.where(allowed, jnp.exp(scores - new_max[..., None]), 0.0)
        rescale = jnp.exp(row_max - new_max)
        row_total = row_total * rescale + jnp.sum(weights, axis=-1)
        weighted = weighted * rescale[..., None] + jnp.einsum(
            "shqk,skhe->shqe",
            weights.astype(jnp.bfloat16),
            pair[:, :, 1],
            preferred_element_type=jnp.float32,
        )
        return (new_max, row_total, weighted)

    def forward_hop(hop_index, carry):
        pair, state = carry
        source = (cycle_index - hop_index) % cycle_size
        state = forward_visit(state, pair, source)
        return (pass_keys(pair), state)

    start_state = (
        jnp.full((sequences, head_local, block_rows), masked_score, jnp.float32),
        jnp.zeros((sequences, head_local, block_rows), jnp.float32),
        jnp.zeros((sequences, head_local, block_rows, HD), jnp.float32),
    )
    pair, state = lax.fori_loop(0, cycle_size - 1, forward_hop, (by_heads[:, :, 1:], start_state))
    row_max, row_total, weighted = forward_visit(state, pair, (cycle_index + 1) % cycle_size)
    log_total = row_max + jnp.log(row_total)
    attended_rows = jnp.transpose(weighted / row_total[..., None], (0, 2, 1, 3))
    attention_result = to_positions(attended_rows.astype(jnp.bfloat16)[:, :, None])[:, :, 0]
    attention_branch = jnp.einsum(
        "roxu,xcu->roc", attention_result, projection_out_weight, preferred_element_type=jnp.float32
    )
    hidden_preactivation = (
        jnp.einsum("ptr,kra->ptka", second_input, input_weight, preferred_element_type=jnp.float32)
        + hidden_unit_bias
    )
    activated_hidden, gelu_back = jax.vjp(exact_gelu, hidden_preactivation)
    activated_reduced = activated_hidden.astype(jnp.bfloat16)
    perceptron_branch = jnp.einsum(
        "xkzp,zop->xko",
        activated_reduced,
        down_projection_weight,
        preferred_element_type=jnp.float32,
    )
    branches = lax.psum((attention_branch + perceptron_branch).astype(jnp.bfloat16), "tp").astype(
        jnp.float32
    )
    block_output = (
        residual
        + branches
        + small[4 * model_width : 5 * model_width]
        + small[5 * model_width : 6 * model_width]
    )
    act_grad = jnp.einsum(
        "ptr,kra->ptka", cotangent, down_projection_weight, preferred_element_type=jnp.float32
    )
    hidden_gradient = gelu_back(act_grad)[0].astype(jnp.bfloat16)
    down_grad = jnp.einsum(
        "gup,guzb->zpb", cotangent, activated_reduced, preferred_element_type=jnp.float32
    )
    in_grad = jnp.einsum(
        "gup,guzb->zpb", second_input, hidden_gradient, preferred_element_type=jnp.float32
    )
    second_grad = jnp.einsum(
        "xkzp,zop->xko", hidden_gradient, input_weight, preferred_element_type=jnp.float32
    )
    attended_grad = jnp.einsum(
        "pgk,jka->pgja", cotangent, projection_out_weight, preferred_element_type=jnp.float32
    ).astype(jnp.bfloat16)
    outproj_grad = jnp.einsum(
        "ztu,ztqi->qui", cotangent, attention_result, preferred_element_type=jnp.float32
    )
    grad_heads = to_heads(attended_grad[:, :, None])[:, :, 0]
    row_delta = jnp.transpose(
        jnp.sum(grad_heads.astype(jnp.float32) * attended_rows, axis=-1), (0, 2, 1)
    )

    def backward_visit(query_grad, pair, source):
        allowed = allowed_pairs(segments, cycle_index, source, block_rows)
        scores = masked_scores(queries, pair[:, :, 0], allowed)
        probabilities = jnp.where(allowed, jnp.exp(scores - log_total[..., None]), 0.0)
        value_grad = jnp.einsum(
            "shqk,sqhe->skhe",
            probabilities.astype(jnp.bfloat16),
            grad_heads,
            preferred_element_type=jnp.float32,
        )
        prob_grad = jnp.einsum(
            "sqhe,skhe->shqk", grad_heads, pair[:, :, 1], preferred_element_type=jnp.float32
        )
        score_grad = (probabilities * (prob_grad - row_delta[..., None])).astype(jnp.bfloat16)
        score_scale = HD ** (-0.5)
        query_grad = (
            query_grad
            + jnp.einsum(
                "shqk,skhe->sqhe", score_grad, pair[:, :, 0], preferred_element_type=jnp.float32
            )
            * score_scale
        )
        key_grad = (
            jnp.einsum("shqk,sqhe->skhe", score_grad, queries, preferred_element_type=jnp.float32)
            * score_scale
        )
        return (query_grad, jnp.stack([key_grad, value_grad], axis=2))

    def backward_hop(hop_index, carry):
        pair, pair_grad, query_grad = carry
        source = (cycle_index - hop_index) % cycle_size
        query_grad, visit_grad = backward_visit(query_grad, pair, source)
        return (pass_keys(pair), pass_grads(pair_grad + visit_grad), query_grad)

    zero_pair = jnp.zeros(by_heads[:, :, 1:].shape, jnp.float32)
    pair, pair_grad, query_grad = lax.fori_loop(
        0,
        cycle_size - 1,
        backward_hop,
        (by_heads[:, :, 1:], zero_pair, jnp.zeros(queries.shape, jnp.float32)),
    )
    query_grad, visit_grad = backward_visit(query_grad, pair, (cycle_index + 1) % cycle_size)
    pair_grad = pass_grads(pair_grad + visit_grad)
    head_grads = jnp.concatenate([query_grad[:, :, None], pair_grad], axis=2).astype(jnp.bfloat16)
    position_grads = to_positions(head_grads).astype(jnp.float32)
    query_pre_grad, key_pre_grad = turn_back((position_grads[:, :, 0], position_grads[:, :, 1]))
    projected_grad = jnp.stack(
        [query_pre_grad, key_pre_grad, position_grads[:, :, 2]], axis=2
    ).astype(jnp.bfloat16)
    flattened_gradient = projected_grad.reshape(sequences, local_rows, 3 * head_count, HD)
    query_key_value_gradient = jnp.einsum(
        "ztu,ztqi->qui", first_input, flattened_gradient, preferred_element_type=jnp.float32
    )
    first_grad = jnp.einsum(
        "roxu,xcu->roc",
        flattened_gradient,
        query_key_value_weight,
        preferred_element_type=jnp.float32,
    )
    input_part, gain_one_grad, offset_one_grad, gain_two_grad, offset_two_grad = norm_back(
        (first_grad, second_grad)
    )
    input_grad = cotangent.astype(jnp.float32) + lax.psum(
        input_part.astype(jnp.bfloat16), "tp"
    ).astype(jnp.float32)
    owner_share = jnp.where(tensor_index == 0, 1.0, 0.0).astype(jnp.float32)
    bias_grad = jnp.sum(cotangent.astype(jnp.float32), axis=(0, 1)) * owner_share
    qkv_bias_grad = jnp.transpose(
        jnp.sum(projected_grad.astype(jnp.float32), axis=(0, 1)), (1, 0, 2)
    ).reshape(-1)
    unit_bias_grad = jnp.sum(hidden_gradient.astype(jnp.float32), axis=(0, 1)).reshape(-1)
    local_small = jnp.concatenate(
        [
            gain_one_grad,
            offset_one_grad,
            gain_two_grad,
            offset_two_grad,
            bias_grad,
            bias_grad,
            jnp.zeros((small.shape[0] - 6 * model_width,), jnp.float32),
        ]
    )
    local_small = lax.dynamic_update_slice_in_dim(local_small, qkv_bias_grad, qkv_start, 0)
    local_small = lax.dynamic_update_slice_in_dim(local_small, unit_bias_grad, unit_start, 0)
    small_grads = lax.psum(local_small, ("blk", "ctx", "tp"))
    local_grad = jnp.concatenate(
        [query_key_value_gradient, outproj_grad, in_grad, down_grad], axis=0
    ).reshape(per_group, -1)
    shares = lax.psum_scatter(
        local_grad.astype(jnp.bfloat16), "blk", scatter_dimension=1, tiled=True
    )
    matrix_grads = lax.psum(shares, "ctx").astype(jnp.float32)
    new_momenta = momentum_decay * momenta + matrix_grads
    update = matrix_grads + momentum_decay * new_momenta
    per_owner = per_group // cycle_size
    sectioned = update.reshape(cycle_size, per_owner, update.shape[1])
    pieces = lax.all_to_all(
        sectioned.astype(jnp.bfloat16), "blk", split_axis=0, concat_axis=2, tiled=True
    ).astype(sectioned.dtype)
    piece_count = pieces.shape[1]
    settled_blocks = newton_schulz(pieces.reshape(piece_count, MODEL_DIM, HD)).reshape(
        1, piece_count, MODEL_DIM * HD
    )
    settled = lax.all_to_all(
        as_sent(settled_blocks), "blk", split_axis=2, concat_axis=0, tiled=True
    ).astype(settled_blocks.dtype)
    orthogonal_all = settled.reshape(per_group, -1)
    muon_scale = max(1.0, MODEL_DIM / HD) ** 0.5
    new_matrices = matrices - muon_rate * (muon_scale * orthogonal_all + weight_decay * matrices)
    new_first = adam_first * small_first + (1.0 - adam_first) * small_grads
    new_second = adam_second * small_second + (1.0 - adam_second) * small_grads * small_grads
    corrected = new_first / (1.0 - adam_first**STEP)
    spread = jnp.sqrt(new_second / (1.0 - adam_second**STEP))
    new_small = small - small_rate * corrected / (spread + adam_epsilon)
    return (
        block_output,
        input_grad,
        matrix_grads,
        new_matrices,
        new_momenta,
        small_grads,
        new_first,
        new_second,
        new_small,
    )


def native_view(array):
    rows, columns = array.shape
    tiled = array.reshape(rows // 8, 8, columns // 128, 128).transpose(0, 2, 1, 3)
    return tiled.reshape(rows // 8, columns // 16, 128)


def native_back(array):
    groups, rows, _ = array.shape
    return array.reshape(groups, rows // 8, 8, 128).transpose(0, 2, 1, 3).reshape(groups * 8, rows * 16)


def members_of(head):
    if head:
        return lambda piece, j: (j // 2, 4 * (j % 2) + piece)
    return lambda piece, j: (piece // 2, 4 * (piece % 2) + j)


def mem(kind=pltpu.VMEM):
    return pl.BlockSpec(memory_space=kind)


def limits(mebibytes):
    return pltpu.CompilerParams(vmem_limit_bytes=mebibytes << 20)


def low_lanes(rows):
    return lax.broadcasted_iota(jnp.int32, (rows, 128), 1) < HD


def dot(a, b, dims=((1,), (0,)), precision=None):
    return lax.dot_general(
        a, b, (dims, ((), ())), precision=precision, preferred_element_type=jnp.float32
    )


NT = ((1,), (1,))
TN = ((0,), (0,))


def corner(array):
    block = (1,) * (array.ndim - 2) + (min(16, array.shape[-2]), 128)
    return pl.BlockSpec(block, lambda *_: (0,) * array.ndim)


def takes(microseconds):
    return pl.CostEstimate(
        flops=int(microseconds * 1.15e9), transcendentals=0, bytes_accessed=int(1e6)
    )


def in_hbm(array):
    if array.size * array.dtype.itemsize < 1 << 21:
        return array
    return pltpu.with_memory_space_constraint(array, pltpu.HBM)


def out_hbm(shape):
    if shape.size * shape.dtype.itemsize < 1 << 20:
        return shape
    return pltpu.HBM(shape.shape, shape.dtype)


def full(array):
    return pl.BlockSpec(array.shape, lambda *_: (0,) * array.ndim)


def launch(kernel, operands, out_shapes, name, specs=None, after=(), vmem=20, cost=3, **more):
    taken = len(operands)
    body = kernel
    if after:
        body = lambda *refs: kernel(*refs[:taken], *refs[taken + len(after) :])
    if specs is None:
        specs = [mem(pltpu.SMEM)] + [full(a) for a in operands[1:]]
    if "out_specs" not in more:
        more["out_specs"] = jax.tree.map(full, out_shapes)
    more.setdefault("grid", (1,))
    return pl.pallas_call(
        body,
        in_specs=list(specs) + [corner(a) for a in after],
        out_shape=jax.tree.map(out_hbm, out_shapes),
        compiler_params=limits(vmem),
        cost_estimate=takes(cost),
        name=name,
        **more,
    )(*map(in_hbm, operands), *map(in_hbm, after))


def relayout_kernel(n, first, count, scal, src, out, *refs):
    fetched, paired, packed, arrivals, departures = refs[-5:]
    low = low_lanes(n)
    place_of = members_of(first == 0)
    steps = [(k, i) for k in range(count) for i in range(256 // n)]

    def fetch(k, i, group):
        rows = pl.ds(i * 8 * n, 8 * n)
        return pltpu.make_async_copy(
            src.at[2 * first + 2 * k + group, rows],
            fetched.at[2 * k + group, rows],
            arrivals.at[2 * k + group, i],
        )

    def leave(k, i):
        rows = pl.ds(i * 2 * n, 2 * n)
        return pltpu.make_async_copy(
            packed.at[pl.ds(4 * k, 4), rows], out.at[pl.ds(4 * k, 4), rows], departures.at[k, i]
        )

    for k, i in steps:
        for group in range(2):
            fetch(k, i, group).start()
    for k, i in steps:
        for group in range(2):
            fetch(k, i, group).wait()
        for piece in range(4):
            for half in range(2):
                pair = []
                for j in (2 * half, 2 * half + 1):
                    group, line = place_of(piece, j)
                    rows = pl.ds(i * 8 * n + line, n, stride=8)
                    pair.append(fetched[2 * k + group, rows, :])
                a, b = pair
                at = 2 * piece + half
                paired[at, pl.ds(0, n, stride=2), :] = jnp.where(low, a, pltpu.roll(b, 64, 1))
                paired[at, pl.ds(1, n, stride=2), :] = jnp.where(low, pltpu.roll(a, 64, 1), b)
                lanes = slice(half * 128, (half + 1) * 128)
                rows = slice(i * 2 * n, (i + 1) * 2 * n)
                packed[4 * k + piece, rows, lanes] = paired[at].astype(packed.dtype)
        leave(k, i).start()
    if len(refs) == 6:
        for k in range(count):
            refs[0][k] = packed[4 * k + scal[1]]
    for k, i in steps:
        leave(k, i).wait()


def relayout(scal, array, dtype, first, count, mine=False, n=128, after=()):
    shapes = [jax.ShapeDtypeStruct((4 * count, 512, 256), dtype)]
    specs = [mem(pl.ANY)]
    if mine:
        shapes.append(jax.ShapeDtypeStruct((count, 512, 256), dtype))
        specs.append(full(shapes[1]))
    return launch(
        functools.partial(relayout_kernel, n, first, count),
        [scal, native_view(array)],
        shapes,
        "relayout",
        specs=[mem(pltpu.SMEM), mem(pl.ANY)],
        after=after,
        cost=2 * count,
        vmem=24,
        out_specs=specs,
        scratch_shapes=[
            pltpu.VMEM((2 * count, 2048, 128), jnp.float32),
            pltpu.VMEM((8, 2 * n, 128), jnp.float32),
            pltpu.VMEM((4 * count, 512, 256), dtype),
            pltpu.SemaphoreType.DMA((2 * count, 256 // n)),
            pltpu.SemaphoreType.DMA((count, 256 // n)),
        ],
    )


def add_up(groups):
    for parts, target in groups:
        values = [part[...].astype(jnp.float32) for part in parts]
        while len(values) > 1:
            values = [sum(values[i : i + 2]) for i in range(0, len(values), 2)]
        if isinstance(target, list):
            for i, part in enumerate(target):
                part[...] = values[0][i].astype(part.dtype)
        else:
            target[...] = values[0].astype(target.dtype)


def grouped(refs, counts, targets):
    refs = iter(refs)
    return [([next(refs) for _ in range(n)], target) for n, target in zip(counts, targets)]


def normalized(x):
    centred = x - jnp.mean(x, axis=-1, keepdims=True)
    spread = jnp.mean(centred * centred, axis=-1, keepdims=True)
    root = lax.rsqrt(spread + norm_epsilon)
    return centred * root, root


def halves(values, first):
    left, right = values[:, :512], values[:, 512:]
    return jnp.where(first, left, right), jnp.where(first, right, left)


def whole(own, other, first):
    return jnp.concatenate([jnp.where(first, own, other), jnp.where(first, other, own)], axis=1)


def norm_back(grad, hat, root, gain):
    scaled = grad * gain
    along = jnp.mean(scaled * hat, axis=-1, keepdims=True)
    return root * (scaled - jnp.mean(scaled, axis=-1, keepdims=True) - hat * along)


def turned(values, cosine, sine):
    lane = lax.broadcasted_iota(jnp.int32, values.shape, 1) % HD
    other = jnp.where(lane < 8, pltpu.roll(values, 120, 1), pltpu.roll(values, 8, 1))
    return values * cosine + other * sine


def project_kernel(scal, x, cot, norms, bias, cosine, sine, own, r0, r1, r2, r3, send):
    first = scal[0] == 0
    hat, _ = normalized(x[...].astype(jnp.float32))
    h = (hat * norms[0:1] + norms[1:2]).astype(jnp.bfloat16)
    h_own, h_other = halves(h, first)
    c_own, c_other = halves(cot[...], first)
    tokens = h.shape[0]
    low = low_lanes(tokens)
    for r, other in enumerate((r0, r1, r2, r3)):
        head = scal[1] ^ r
        mine = own[head]
        theirs = other[...]
        pre = dot(h_own, mine) + dot(h_other, theirs) + bias[pl.ds(head, 1), :]
        back = dot(c_own, mine[:, 128:]) + dot(c_other, theirs[:, 128:])
        left = turned(pre[:, :128], cosine[...], sine[...]).astype(jnp.bfloat16)
        right = jnp.where(low, pre[:, 128:], back).astype(jnp.bfloat16)
        for s in range(2):
            rows = slice(128 * s, 128 * s + 128)
            send[4 * s + head, :, :128] = left[rows]
            send[4 * s + head, :, 128:] = right[rows]


def attention_kernel(rows_ref, seg, out, key_total, value_total):
    key_total[...] = jnp.zeros_like(key_total)
    value_total[...] = jnp.zeros_like(value_total)
    step = 256
    for block in range(rows_ref.shape[0] // step):
        rows = slice(block * step, (block + 1) * step)
        n = (block + 1) * step
        query = rows_ref[rows, 0:HD] * jnp.bfloat16(0.125)
        grad = rows_ref[rows, 3 * HD : 4 * HD]
        keys = rows_ref[0:n, HD : 2 * HD]
        values = rows_ref[0:n, 2 * HD : 3 * HD]
        scores = dot(query, keys, NT)
        query_place = block * step + lax.broadcasted_iota(jnp.int32, (step, n), 0)
        key_place = lax.broadcasted_iota(jnp.int32, (step, n), 1)
        allowed = (key_place <= query_place) & (key_place >= seg[rows, :])
        scores = jnp.where(allowed, scores, masked_score)
        weights = jnp.exp(scores - jnp.max(scores, axis=-1, keepdims=True))
        weights = jnp.where(allowed, weights, 0.0)
        weights = weights * (1.0 / jnp.sum(weights, axis=-1, keepdims=True))
        short = weights.astype(jnp.bfloat16)
        attended = dot(short, values)
        weight_grad = dot(grad, values, NT)
        delta = jnp.sum(weights * weight_grad, axis=-1, keepdims=True)
        score_grad = (weights * (weight_grad - delta)).astype(jnp.bfloat16)
        query_grad = dot(score_grad, keys) * 0.125
        key_total[0:n, :] += dot(score_grad, query, TN)
        value_total[0:n, :] += dot(short, grad, TN)
        out[rows, 0:HD] = query_grad.astype(jnp.bfloat16)
        out[rows, 3 * HD : 4 * HD] = attended.astype(jnp.bfloat16)
    out[:, HD : 2 * HD] = key_total[...].astype(jnp.bfloat16)
    out[:, 2 * HD : 3 * HD] = value_total[...].astype(jnp.bfloat16)


def feed_forward_kernel(
    scal, x, cot, norms, bias, weights, r0, r1, r2, r3,
    branch, input_part, keep, send, hidden_sums, norm_grads, cot_sums,
):
    first = scal[0] == 0
    hat, root = normalized(x[...].astype(jnp.float32))
    h = (hat * norms[2:3] + norms[3:4]).astype(jnp.bfloat16)
    h_own, h_other = halves(h, first)
    c_own, c_other = halves(cot[...], first)
    cot_sums[...] = jnp.sum(cot[...].astype(jnp.float32), axis=0, keepdims=True)
    outs = [0.0] * 4
    for r, other in enumerate((r0, r1, r2, r3)):
        piece = scal[1] ^ r
        in_own, in_other = weights[piece], other[0]
        down_own, down_other = weights[4 + piece], other[1]
        pre = dot(h_own, in_own) + dot(h_other, in_other) + bias[pl.ds(piece, 1), :]
        cumulative = 0.5 * (1.0 + lax.erf(pre * 0.7071067811865476))
        slope = cumulative + pre * (0.3989422804014327 * jnp.exp(-0.5 * pre * pre))
        act = (pre * cumulative).astype(jnp.bfloat16)
        act_grad = dot(c_own, down_own) + dot(c_other, down_other)
        grad = (act_grad * slope).astype(jnp.bfloat16)
        hidden_sums[pl.ds(piece, 1), :] = jnp.sum(
            grad.astype(jnp.float32), axis=0, keepdims=True
        )
        outs[0] += dot(act, down_own, NT)
        outs[1] += dot(act, down_other, NT)
        outs[2] += dot(grad, in_own, NT)
        outs[3] += dot(grad, in_other, NT)
        target = send if r % 2 else keep
        target[r // 2, 0] = grad
        target[r // 2, 1] = act
    branch[...] = whole(outs[0], outs[1], first)
    second = whole(outs[2], outs[3], first)
    norm_grads[0:1] = jnp.sum(second * hat, axis=0, keepdims=True)
    norm_grads[1:2] = jnp.sum(second, axis=0, keepdims=True)
    input_part[...] = norm_back(second, hat, root, norms[2:3])


def both_cores(scal, x, x_beside, cot, cot_beside, norms, at):
    first = scal[0] == 0
    tokens = jnp.concatenate([x[...], x_beside[...]], axis=0).astype(jnp.float32)
    hat, _ = normalized(tokens)
    h = (hat * norms[at : at + 1] + norms[at + 1 : at + 2]).astype(jnp.bfloat16)
    c = jnp.concatenate([cot[...], cot_beside[...]], axis=0)
    return list(zip(halves(h, first), halves(c, first)))


def unit_grads_kernel(
    scal, x, x_beside, cot, cot_beside, norms, keep, came, in_keep, in_send, down_keep, down_send
):
    for side, (h, c) in enumerate(both_cores(scal, x, x_beside, cot, cot_beside, norms, 2)):
        for far in range(2):
            grad = jnp.concatenate([keep[far, 0], came[far, 0]], axis=0)
            act = jnp.concatenate([keep[far, 1], came[far, 1]], axis=0)
            (in_send if side else in_keep)[far] = dot(h, grad, TN).astype(jnp.bfloat16)
            (down_send if far else down_keep)[side] = dot(c, act, TN).astype(jnp.bfloat16)


def combine_kernel(in_keep, in_came, down_keep, down_came, own, in_send, down_send):
    pairs = ((in_keep, in_came, in_send), (down_keep, down_came, down_send))
    for k, (keep, came, send) in enumerate(pairs):
        total = keep[...].astype(jnp.float32) + came[...].astype(jnp.float32)
        own[k] = total[0].astype(jnp.bfloat16)
        send[0] = total[1].astype(jnp.bfloat16)


def turn_kernel(scal, cosine, sine, back, keep, send, sums):
    low = low_lanes(keep.shape[1])
    for r in range(4):
        head = scal[1] ^ r
        grads = jnp.concatenate([back[head], back[4 + head]], axis=0)
        left = turned(grads[:, :128].astype(jnp.float32), cosine[...], -sine[...])
        left = left.astype(jnp.bfloat16)
        right = grads[:, 128:]
        target = send if r % 2 else keep
        target[r // 2, :, :128] = left
        target[r // 2, :, 128:] = right
        right = jnp.where(low, right.astype(jnp.float32), 0.0)
        wide = jnp.concatenate([left.astype(jnp.float32), right], axis=1)
        sums[pl.ds(head, 1), :] = jnp.sum(wide, axis=0, keepdims=True)


def split_last(piece):
    wide = piece.astype(jnp.float32)
    lane = lax.broadcasted_iota(jnp.int32, (1, wide.shape[1]), 1)
    share = (lane < 3 * HD).astype(jnp.float32)
    pre_grad = (wide * share).astype(jnp.bfloat16)
    attended = (wide * (1.0 - share)).astype(jnp.bfloat16)
    return pre_grad, attended


def head_grads_kernel(
    scal, x, x_beside, cot, cot_beside, norms, keep, came, totals, *outs
):
    both = totals[...].reshape(64, 256)
    coarse = both.astype(jnp.bfloat16)
    fine = (both - coarse.astype(jnp.float32)).astype(jnp.bfloat16)
    sides = both_cores(scal, x, x_beside, cot, cot_beside, norms, 0)
    a_keep, a_send, b_keep, b_send = outs
    for far in range(2):
        piece = jnp.concatenate([keep[far], came[far]], axis=0)
        pre_grad, attended = split_last(piece)
        for side, (h, c) in enumerate(sides):
            grad = (dot(h, pre_grad, TN) + dot(c, attended, TN)).astype(jnp.bfloat16)
            target = a_send if side else a_keep
            target[far, 0:256] = grad[0:256]
            target[far, 256:320] = coarse
            target[far, 320:384] = fine
            (b_send if far else b_keep)[side] = grad[256:512]


def combine_heads_kernel(a_keep, a_came, b_keep, b_came, a_own, a_send, b_own, b_send):
    for targets, at in (((a_own, b_own), 0), ((a_send, b_send), 1)):
        total = a_keep[at].astype(jnp.float32) + a_came[at].astype(jnp.float32)
        targets[0][0:256] = total[0:256].astype(jnp.bfloat16)
        tail = total[256:320] + total[320:384]
        coarse = tail.astype(jnp.bfloat16)
        targets[0][256:320] = coarse
        targets[0][320:384] = (tail - coarse.astype(jnp.float32)).astype(jnp.bfloat16)
        total = b_keep[at].astype(jnp.float32) + b_came[at].astype(jnp.float32)
        targets[1][...] = total.astype(jnp.bfloat16)


def add_kernel(near, came, kept, passed):
    add_up([((near, came), [kept, passed])])


def gather_kernel(
    scal, x, norms, keep, send, weights, r0, r1, r2, r3, ff_branch, ff_part,
    norm_two, cot_sums, unit_sums, qkv_sums, near, far, totals, parts,
):
    first = scal[0] == 0
    hat, root = normalized(x[...].astype(jnp.float32))
    outs = [0.0] * 4
    for r, other in enumerate((r0, r1, r2, r3)):
        mine, theirs = weights[scal[1] ^ r], other[0]
        pre_grad, attended = split_last((send if r % 2 else keep)[r // 2])
        outs[0] += dot(attended, mine, NT)
        outs[1] += dot(attended, theirs, NT)
        outs[2] += dot(pre_grad, mine, NT)
        outs[3] += dot(pre_grad, theirs, NT)
    branch = ff_branch[...] + whole(outs[0], outs[1], first)
    grad = whole(outs[2], outs[3], first)
    totals[...] = jnp.zeros_like(totals)
    rows = [jnp.sum(grad * hat, axis=0, keepdims=True), jnp.sum(grad, axis=0, keepdims=True)]
    rows += [norm_two[0:1], norm_two[1:2], cot_sums[...]]
    for i, row in enumerate(rows):
        for q in range(4):
            at = 4 * (i % 2) + q
            totals[i // 2, at : at + 1, :] = row[:, 256 * q : 256 * q + 256]
    totals[3 + scal[2], 0:4, :] = qkv_sums[...]
    totals[3 + scal[2], 4:8, :] = unit_sums[...]
    input_part = ff_part[...] + norm_back(grad, hat, root, norms[0:1])
    for q in range(4):
        parts[q, 0] = branch[64 * q : 64 * q + 64].astype(jnp.bfloat16)
        parts[q, 1] = input_part[64 * q : 64 * q + 64].astype(jnp.bfloat16)
    for r in range(4):
        (far if r % 2 else near)[r // 2] = parts[scal[2] ^ r]


def finish_rows_kernel(scal, x, cot, bias, near, far, beside, block_output, input_grad):
    for r in range(4):
        q = scal[2] ^ r
        piece = beside.at[r // 2] if r % 2 else (far if r else near)
        block_output[q] = x[q].astype(jnp.float32) + piece[0].astype(jnp.float32) + bias[...]
        input_grad[q] = cot[q].astype(jnp.float32) + piece[1].astype(jnp.float32)


def gram_of_piece(total, momenta, grads, grams):
    short = total.astype(jnp.bfloat16)
    grads[0] = short
    update = 1.95 * short.astype(jnp.float32) + 0.9025 * momenta[0]
    gram = dot(update, update, TN, lax.Precision.HIGHEST)
    for j in range(4):
        cut = slice(j * HD, (j + 1) * HD)
        grams[0, j] = gram[cut, cut]


def unit_gram_kernel(place, own, in_came, down_came, momenta, *refs):
    grads, grams = refs[-2:]
    a = in_came[0].astype(jnp.float32)
    b = down_came[0].astype(jnp.float32)
    other = jnp.where(pl.program_id(0) == 0, a, b)
    gram_of_piece(own[0].astype(jnp.float32) + other, momenta, grads, grams)


def head_gram_kernel(place, a_own, a_came, b_own, b_came, momenta, *refs):
    grads, grams, totals = refs[-3:]
    a = a_own[...].astype(jnp.float32) + a_came[...].astype(jnp.float32)
    b = b_own[...].astype(jnp.float32) + b_came[...].astype(jnp.float32)
    gram_of_piece(jnp.concatenate([a[0:256], b], axis=0), momenta, grads, grams)
    totals[...] = (a[256:320] + a[320:384]).reshape(8, 8, 256)


def gram_of(kernel, first, others, momenta, place, shapes, after=()):
    chunks = momenta.shape[0] // 4
    piece = pl.BlockSpec((1, 512, 256), lambda i, s: (i, 0, 0))
    block = pl.BlockSpec((1, 512, 256), lambda i, s: (4 * i + s[1], 0, 0))
    return pl.pallas_call(
        kernel,
        grid_spec=pltpu.PrefetchScalarGridSpec(
            num_scalar_prefetch=1,
            grid=(chunks,),
            in_specs=[piece if first.ndim == 3 else full(first)]
            + [full(other) for other in others]
            + [block]
            + [corner(a) for a in after],
            out_specs=[piece, pl.BlockSpec((1, 4, HD, HD), lambda i, s: (i, 0, 0, 0))]
            + [full(shape) for shape in shapes],
        ),
        out_shape=[
            jax.ShapeDtypeStruct((chunks, 512, 256), jnp.bfloat16),
            jax.ShapeDtypeStruct((chunks, 4, HD, HD), jnp.float32),
            *map(out_hbm, shapes),
        ],
        compiler_params=limits(20),
        cost_estimate=takes(2.5),
        name="gram",
    )(place, *map(in_hbm, [first, *others, momenta, *after]))


def newton_kernel(counts, mine, theirs, *refs):
    taken = sum(counts)
    out = refs[taken]
    add_up(grouped(refs, counts, refs[taken + 1 :]))
    linear, square, cubic = quintic
    shape = (HD, HD)
    eye = lax.broadcasted_iota(jnp.int32, shape, 0) == lax.broadcasted_iota(jnp.int32, shape, 1)
    full = lax.Precision.HIGHEST
    chunks = mine.shape[0]
    places = [(i, j) for i in range(chunks) for j in range(4)]
    states = []
    for i, j in places:
        gram = mine[i, j] + theirs[i, j]
        trace = jnp.sum(jnp.where(eye, gram, 0.0), axis=(0, 1), keepdims=True)
        scale = 1.0 / (jnp.sqrt(trace) + muon_epsilon)
        states.append([gram * scale * scale, None, scale])
    for iteration in range(NEWTON):
        squares = [dot(s[0], s[0], precision=full) for s in states]
        steps = [
            jnp.where(eye, linear, 0.0) + square * s[0] + cubic * sq
            for s, sq in zip(states, squares)
        ]
        if iteration == 0:
            halfway = [dot(s[0], m, precision=full) for s, m in zip(states, steps)]
            for s, m in zip(states, steps):
                s[1] = m
        elif iteration < NEWTON - 1:
            both = [
                dot(jnp.concatenate([s[0], s[1]], axis=0), m, precision=full)
                for s, m in zip(states, steps)
            ]
            halfway = [x[:HD] for x in both]
            for s, x in zip(states, both):
                s[1] = x[HD:]
        else:
            for s, m in zip(states, steps):
                s[1] = dot(s[1], m, precision=full)
        if iteration < NEWTON - 1:
            for s, x, m in zip(states, halfway, steps):
                s[0] = dot(x, m, precision=full)
    for (i, j), s in zip(places, states):
        mix = s[1] * s[2]
        coarse = mix.astype(jnp.bfloat16)
        fine = (mix - coarse.astype(jnp.float32)).astype(jnp.bfloat16)
        rows, lanes = slice(64 * (j // 2), 64 * (j // 2) + 64), slice(128 * (j % 2), 128 * (j % 2) + 128)
        out[i, rows, lanes] = jnp.concatenate([coarse, fine], axis=1)


def newton(mine, theirs, sums, after=()):
    flat = [part for group in sums for part in group]
    operands = [mine, theirs, *flat]
    return launch(
        functools.partial(newton_kernel, [len(group) for group in sums]),
        operands,
        [jax.ShapeDtypeStruct((mine.shape[0], 2 * HD, 256), jnp.bfloat16)]
        + [jax.ShapeDtypeStruct(group[0].shape, group[0].dtype) for group in sums],
        "newton",
        cost=3.5,
        specs=[full(a) for a in operands],
        after=after,
    )


def update_kernel(
    n, head, scal, g0, g1, g2, g3, q0, q1, q2, q3, momenta, native_momenta, native, *refs
):
    grads, weights, moved, mixing, first, second, steps = refs[-7:]
    place_of = members_of(head)

    @pl.when((pl.program_id(0) == 0) & (pl.program_id(1) == 0))
    def _():
        mixing[...] = jnp.zeros_like(mixing)

    @pl.when(pl.program_id(1) == 0)
    def _():
        for r, q in enumerate((q0, q1, q2, q3)):
            for j in range(4):
                at = slice(HD * (j // 2), HD * (j // 2) + HD), slice(128 * (j % 2), 128 * (j % 2) + 128)
                wide = q[(0,) * (len(q.shape) - 2) + at].astype(jnp.float32)
                other = pltpu.roll(wide, HD, 1)
                below = low_lanes(HD) == (j % 2 == 0)
                rows = slice(j * HD, (j + 1) * HD)
                lanes = slice(128 * (j // 2), 128 * (j // 2) + 128)
                pair = (wide, other) if j % 2 == 0 else (other, wide)
                for level in range(2):
                    part = jnp.where(below, pair[level], 0.0)
                    mixing[r, level, rows, lanes] = part.astype(jnp.bfloat16)

    low = low_lanes(n)
    for r, piece in enumerate((g0, g1, g2, g3)):
        place = scal[1] ^ r
        grad = piece[(0,) * (len(piece.shape) - 2)].astype(jnp.float32)
        update = 1.95 * grad + 0.9025 * momenta[place]
        coarse = update.astype(jnp.bfloat16)
        fine = (update - coarse.astype(jnp.float32)).astype(jnp.bfloat16)
        settled = dot(coarse, mixing[r, 0]) + dot(coarse, mixing[r, 1]) + dot(fine, mixing[r, 0])
        for half in range(2):
            k = 2 * r + half
            first[k] = grad[:, half * 128 : (half + 1) * 128]
            second[k] = settled[:, half * 128 : (half + 1) * 128]
            for source, target in ((first, grads), (second, steps)):
                even = source[k, pl.ds(0, n, stride=2), :]
                odd = source[k, pl.ds(1, n, stride=2), :]
                lines = (
                    jnp.where(low, even, pltpu.roll(odd, 64, 1)),
                    jnp.where(low, pltpu.roll(even, 64, 1), odd),
                )
                for w in range(2):
                    group, line = place_of(place, 2 * half + w)
                    target[group, pl.ds(line, n, stride=8), :] = lines[w]
    moved[...] = momentum_decay * native_momenta[...] + grads[...]
    weight = native[...]
    weights[...] = weight - muon_rate * (4.0 * steps[...] + weight_decay * weight)


def update(
    first, scal, own, far, mix, mix_far, beside, momenta, native_momenta, native, before=(), after=(), n=128
):
    chunks = own.shape[0]
    block = pl.BlockSpec((2, 8 * n, 128), lambda k, i: (first + k, i, 0))
    piece = pl.BlockSpec((1, 2 * n, 256), lambda k, i: (k, i, 0))
    factor = pl.BlockSpec((1, 2 * HD, 256), lambda k, i: (k, 0, 0))
    pieces, factors = [piece, None, piece, None], [factor, None, factor, None]
    for r in (0, 1):
        pieces[2 * r + 1] = pl.BlockSpec((1, 1, 2 * n, 256), lambda k, i, r=r: (r, k, i, 0))
        factors[2 * r + 1] = pl.BlockSpec((1, 1, 2 * HD, 256), lambda k, i, r=r: (r, k, 4, 0))
    grads, mixes = [own, beside, far, beside], [mix, beside, mix_far, beside]
    return launch(
        functools.partial(update_kernel, n, first == 0),
        [scal, *grads, *mixes, momenta, native_view(native_momenta), native_view(native), *before],
        [jax.ShapeDtypeStruct((6, 2048, 128), jnp.float32)] * 3,
        "update",
        specs=[mem(pltpu.SMEM)]
        + pieces
        + factors
        + [pl.BlockSpec((4, 2 * n, 256), lambda k, i: (k, i, 0)), block, block]
        + [mem(pl.ANY)] * len(before),
        after=after,
        vmem=32,
        cost=5.5 * chunks,
        grid=(chunks, 256 // n),
        out_specs=[block] * 3,
        scratch_shapes=[
            pltpu.VMEM((4, 2, 256, 256), jnp.bfloat16),
            pltpu.VMEM((8, 2 * n, 128), jnp.float32),
            pltpu.VMEM((8, 2 * n, 128), jnp.float32),
            pltpu.VMEM((2, 8 * n, 128), jnp.float32),
        ],
        input_output_aliases={12 + i: i for i in range(len(before))},
    )


def whole_device(
    inputs, cotangent, matrices, momenta, small, small_first, small_second, segments, positions
):
    blk_at = lax.axis_index("blk")
    ctx_at = lax.axis_index("ctx")
    tp_at = lax.axis_index("tp")
    scal = jnp.stack([blk_at, ctx_at, tp_at]).astype(jnp.int32)
    sequences, local_rows, width = inputs.shape
    tokens = sequences * local_rows
    both = ("blk", "ctx")
    f32, bf16 = jnp.float32, jnp.bfloat16
    shaped = jax.ShapeDtypeStruct

    def hop(values, by):
        return lax.ppermute(values, both, [(i, i ^ by) for i in range(8)])

    def hop_tp(values, by):
        return lax.ppermute(values, "tp", [(i, i ^ by) for i in range(4)])

    def tied(values, *results):
        return lax.optimization_barrier((values, *results))[0]

    def spread(piece):
        c = hop(piece, 2)
        return [piece, hop(piece, 1), c, hop(c, 1)]

    x = inputs.reshape(tokens, width)
    cot = cotangent.reshape(tokens, width)
    norms = small[: 4 * width].reshape(4, width)
    qkv_start = 6 * width + tp_at * 4 * 3 * HD
    qkv_bias = lax.dynamic_slice_in_dim(small, qkv_start, 4 * 3 * HD).reshape(4, 3 * HD)
    qkv_bias = jnp.pad(qkv_bias, ((0, 0), (0, HD)))
    unit_start = 6 * width + H * 3 * HD + tp_at * 1024
    unit_bias = lax.dynamic_slice_in_dim(small, unit_start, 1024).reshape(4, 256)
    lane = jnp.arange(128) % HD
    frequency = rope_base ** (-2.0 * (lane % 8).astype(f32) / ROTARY)
    angles = positions.astype(f32).reshape(tokens, 1) * frequency
    cosine = jnp.where(lane < ROTARY, jnp.cos(angles), 1.0)
    sign = jnp.where(lane < 8, -1.0, jnp.where(lane < ROTARY, 1.0, 0.0))
    sine = jnp.sin(angles) * sign

    head_weights, mine = relayout(scal, matrices, bf16, 0, 1, mine=True)
    first_hop = hop(mine, 4)
    unit_weights, mine_units = relayout(scal, matrices, bf16, 1, 2, mine=True, after=(mine,))
    first_hop = tied(first_hop, mine_units)
    other_heads = spread(first_hop)
    (piled_heads,) = relayout(scal, momenta, f32, 0, 1, after=(mine_units, first_hop))
    units_near = hop(tied(mine_units, first_hop), 4)
    units_far = hop(units_near, 2)
    x_beside = hop(x, 1)
    cot_beside = hop(cot, 1)

    send = launch(
        project_kernel,
        [scal, x, cot, norms, qkv_bias, cosine, sine, head_weights]
        + [piece[0] for piece in other_heads],
        shaped((8, local_rows, 256), bf16),
        "project",
        after=(piled_heads, units_near),
    )
    arrived = lax.all_to_all(send, both, split_axis=0, concat_axis=0, tiled=True)
    units_far = tied(units_far, send)
    other_units = [units_near, hop(tied(units_near, send), 1), units_far, hop(units_far, 1)]
    ff_branch, ff_part, unit_keep, unit_send, unit_sums, norm_two, cot_sums = launch(
        feed_forward_kernel,
        [scal, x, cot, norms, unit_bias, unit_weights, *other_units],
        [
            shaped((tokens, width), f32),
            shaped((tokens, width), f32),
            shaped((2, 2, tokens, 256), bf16),
            shaped((2, 2, tokens, 256), bf16),
            shaped((4, 256), f32),
            shaped((2, width), f32),
            shaped((1, width), f32),
        ],
        "feed_forward",
        cost=5.5,
        after=(send,),
    )
    documents = lax.dynamic_index_in_dim(segments, blk_at, 0, keepdims=False)
    length = documents.shape[0]
    attended = launch(
        attention_kernel,
        [arrived.reshape(length, 256), documents.reshape(length, 1)],
        shaped((length, 256), bf16),
        "attention",
        cost=6,
        specs=[full(arrived.reshape(length, 256)), pl.BlockSpec((length, 1), lambda *_: (0, 0))],
        after=(unit_sums,),
        scratch_shapes=[pltpu.VMEM((length, HD), f32)] * 2,
    )
    back = lax.all_to_all(
        attended.reshape(8, local_rows, 256), both, split_axis=0, concat_axis=0, tiled=True
    )

    in_keep, in_send, down_keep, down_send = launch(
        unit_grads_kernel,
        [scal, x, x_beside, cot, cot_beside, norms, unit_keep, hop(unit_send, 1)],
        [shaped((2, 512, 256), bf16)] * 4,
        "unit_grads",
        cost=3.5,
        after=(attended,),
    )
    (piled_units,) = relayout(scal, momenta, f32, 1, 2, after=(in_keep,))
    head_keep, head_send, qkv_sums = launch(
        turn_kernel,
        [scal, cosine, sine, back],
        [shaped((2, tokens, 256), bf16)] * 2 + [shaped((4, 256), f32)],
        "turn",
        cost=2,
        after=(piled_units,),
    )
    sums = [norm_two, cot_sums, unit_sums, qkv_sums]
    near, far, totals = launch(
        gather_kernel,
        [scal, x, norms, head_keep, head_send, head_weights, *other_heads, ff_branch, ff_part, *sums],
        [shaped((2, 2, 64, width), bf16)] * 2 + [shaped((8, 8, 256), f32)],
        "gather",
        after=(in_keep,),
        scratch_shapes=[pltpu.VMEM((4, 2, 64, width), bf16)],
    )
    a_keep, a_send, b_keep, b_send = launch(
        head_grads_kernel,
        [scal, x, x_beside, cot, cot_beside, norms, head_keep, hop(head_send, 1), totals],
        [shaped((2, 384, 256), bf16)] * 2 + [shaped((2, 256, 256), bf16)] * 2,
        "head_grads",
        cost=4,
    )
    came = hop_tp(far, 1)
    a_came, b_came = hop(a_send, 4), hop(b_send, 2)
    operands = [in_keep, hop(in_send, 4), down_keep, hop(down_send, 2)]
    own, in_send, down_send = launch(
        combine_kernel,
        operands,
        [shaped((2, 512, 256), bf16)] + [shaped((1, 512, 256), bf16)] * 2,
        "combine",
        specs=[full(a) for a in operands],
        cost=2,
        after=(a_keep,),
    )
    in_came, down_came = hop(in_send, 2), hop(down_send, 4)
    kept, passed = launch(
        add_kernel,
        [near, came],
        [shaped((2, 64, width), bf16)] * 2,
        "add",
        specs=[full(near)] * 2,
        after=(in_send,),
    )
    passed = hop_tp(passed, 2)
    operands = [a_keep, a_came, b_keep, b_came]
    a_own, a_send, b_own, b_send = launch(
        combine_heads_kernel,
        operands,
        [shaped((384, 256), bf16)] * 2 + [shaped((256, 256), bf16)] * 2,
        "combine_heads",
        specs=[full(a) for a in operands],
        after=(kept,),
    )
    a_came, b_came = hop(a_send, 2), hop(b_send, 4)
    unit_sum, unit_grams = gram_of(
        unit_gram_kernel,
        own,
        [in_came, down_came],
        piled_units,
        scal,
        [],
        after=(a_own,),
    )
    unit_theirs = hop(unit_grams, 4)
    unit_far = hop(unit_sum, 2)
    head_sum, head_grams, totals = gram_of(
        head_gram_kernel,
        a_own,
        [a_came, b_own, b_came],
        piled_heads,
        scal,
        [shaped((8, 8, 256), f32)],
        after=(unit_sum,),
    )
    head_theirs = hop(head_grams, 4)
    head_far = hop(head_sum, 2)
    unit_mix, total = newton(unit_grams, unit_theirs, [(kept, passed)], after=(head_sum,))
    total_far = hop_tp(total, 2)
    unit_mix_far = hop(unit_mix, 2)
    head_mix, totals = newton(
        head_grams,
        head_theirs,
        [(totals, hop(totals, 1))],
        after=(unit_mix, unit_far),
    )
    head_mix_far = hop(head_mix, 2)

    def to_beside(*pieces):
        return hop(jnp.stack([jnp.concatenate(pair, axis=1) for pair in pieces]), 1)

    beside = to_beside((unit_sum, unit_mix), (unit_far, tied(unit_mix_far, head_mix)))
    totals_came = hop_tp(totals, 1)
    before = update(
        1, scal, unit_sum, unit_far, unit_mix, unit_mix_far, beside, piled_units, momenta, matrices,
        after=(head_mix,),
    )
    head_far, head_mix_far = tied((head_far, head_mix_far), before[0])
    beside = to_beside((head_sum, head_mix), (head_far, head_mix_far))
    outs = update(
        0, scal, head_sum, head_far, head_mix, head_mix_far, beside, piled_heads, momenta, matrices,
        before,
    )
    total_beside = hop_tp(tied(jnp.stack([total, total_far]), head_mix), 1)
    totals = totals + totals_came
    totals = totals + tied(hop_tp(totals, 2), before[0])

    block_output, input_grad = launch(
        finish_rows_kernel,
        [
            scal,
            x.reshape(4, 64, width),
            cot.reshape(4, 64, width),
            (small[4 * width : 5 * width] + small[5 * width : 6 * width]).reshape(1, width),
            total,
            total_far,
            total_beside,
        ],
        [shaped((4, 64, width), f32)] * 2,
        "finish_rows",
        cost=2,
        after=(before[0],),
    )

    cot_total = totals[2, :4].reshape(-1) * 0.25
    small_grads = jnp.concatenate(
        [
            totals[:2].reshape(-1),
            cot_total,
            cot_total,
            totals[3:7, :4, : 3 * HD].reshape(-1),
            totals[3:7, 4:].reshape(-1),
        ]
    )
    return (
        block_output.reshape(inputs.shape),
        input_grad.reshape(inputs.shape),
        native_back(outs[0]),
        native_back(outs[1]),
        native_back(outs[2]),
        small_grads,
        *small_step(small, small_first, small_second, small_grads),
    )


def small_step(small, small_first, small_second, small_grads):
    new_first = adam_first * small_first + (1.0 - adam_first) * small_grads
    new_second = adam_second * small_second + (1.0 - adam_second) * small_grads * small_grads
    corrected = new_first / (1.0 - adam_first**STEP)
    spread = jnp.sqrt(new_second / (1.0 - adam_second**STEP))
    new_small = small - small_rate * corrected / (spread + adam_epsilon)
    return new_first, new_second, new_small


def solution(mesh):
    in_specs = (
        P(None, ("blk", "ctx"), None),
        P(None, ("blk", "ctx"), None),
        P("tp", "blk"),
        P("tp", "blk"),
        P(),
        P(),
        P(),
        P(),
        P(None, ("blk", "ctx")),
    )
    out_specs = (
        P(None, ("blk", "ctx"), None),
        P(None, ("blk", "ctx"), None),
        P("tp", "blk"),
        P("tp", "blk"),
        P("tp", "blk"),
        P(),
        P(),
        P(),
        P(),
    )
    one_each = mesh.shape["blk"] == SEQS and mesh.shape["ctx"] * mesh.shape["tp"] == H
    one_each = one_each and mesh.shape["tp"] == 4
    return jax.shard_map(
        whole_device if one_each else on_device, mesh=mesh, in_specs=in_specs, out_specs=out_specs, check_vma=False
    )
```

```python
import functools

import jax
import jax.numpy as jnp
from jax import lax
from jax.experimental import pallas as pl
from jax.experimental.pallas import tpu as pltpu
from jax.sharding import PartitionSpec as P

MODEL_DIM = 1024
H = 16
HD = 64
FF = 4096
ROTARY = 16
NEWTON = 5
STEP = 10
SEQS = 2


norm_epsilon = 1e-05
rope_base = 10000.0
masked_score = -1e30
momentum_decay = 0.95
muon_rate = 0.2
weight_decay = 0.01
muon_epsilon = 1e-07
quintic = (3.4445, -4.775, 2.0315)
adam_first = 0.9
adam_second = 0.95
adam_epsilon = 1e-08
small_rate = 0.2


def passed_along(x, axis, by):
    devices = lax.axis_size(axis)
    pairs = [(i, i + by) for i in range(devices) if 0 <= i + by < devices]
    return lax.ppermute(x, axis, pairs)


def shifted(x, axis, by):
    devices = lax.axis_size(axis)
    return lax.ppermute(x, axis, [(i, (i + by) % devices) for i in range(devices)])


def as_sent(x):

    def short(part):
        return part.astype(jnp.bfloat16) if part.dtype == jnp.float32 else part

    return jax.tree.map(short, x)


def layer_norm(values, scaling, offset):
    centre = jnp.mean(values, axis=-1, keepdims=True)
    centred = values - centre
    spread = jnp.mean(centred * centred, axis=-1, keepdims=True)
    return centred * lax.rsqrt(spread + norm_epsilon) * scaling + offset


def rope_tables(positions):
    halfway = ROTARY // 2
    frequency = rope_base ** (-2.0 * jnp.arange(halfway, dtype=jnp.float32) / ROTARY)
    angles = positions.astype(jnp.float32)[..., None] * frequency
    return (jnp.cos(angles)[:, :, None, :], jnp.sin(angles)[:, :, None, :])


def rotate(values, cosine, sine):
    halfway = ROTARY // 2
    former = values[..., :halfway]
    latter = values[..., halfway:ROTARY]
    return jnp.concatenate(
        [former * cosine - latter * sine, latter * cosine + former * sine, values[..., ROTARY:]],
        axis=-1,
    )


def exact_gelu(values):
    return jax.nn.gelu(values, approximate=False)


def newton_schulz(blocks):
    frobenius = jnp.sqrt(jnp.sum(blocks * blocks, axis=(1, 2), keepdims=True))
    current = blocks / (frobenius + muon_epsilon)
    linear_term, square_term, cubic_term = quintic
    for iteration in range(NEWTON):
        gram_matrix = jnp.einsum("mde,mdf->mef", current, current, precision=lax.Precision.HIGHEST)
        polynomial = square_term * gram_matrix + cubic_term * jnp.einsum(
            "mef,mfg->meg", gram_matrix, gram_matrix, precision=lax.Precision.HIGHEST
        )
        current = linear_term * current + jnp.einsum(
            "mde,mef->mdf", current, polynomial, precision=lax.Precision.HIGHEST
        )
    return current


def to_heads(values):
    return lax.all_to_all(values, "ctx", split_axis=3, concat_axis=1, tiled=True)


def to_positions(values):
    return lax.all_to_all(values, "ctx", split_axis=1, concat_axis=3, tiled=True)


def pass_keys(pair):
    return passed_along(pair, "blk", 1)


def pass_grads(pair_grad):
    return shifted(pair_grad.astype(jnp.bfloat16), "blk", 1).astype(pair_grad.dtype)


def allowed_pairs(segments, query_block, key_block, block_rows):
    query_place = query_block * block_rows + jnp.arange(block_rows, dtype=jnp.int32)
    key_place = key_block * block_rows + jnp.arange(block_rows, dtype=jnp.int32)
    query_doc = lax.dynamic_slice_in_dim(segments, query_block * block_rows, block_rows, 1)
    key_doc = lax.dynamic_slice_in_dim(segments, key_block * block_rows, block_rows, 1)
    causal = key_place[None, :] <= query_place[:, None]
    return (causal[None] & (query_doc[:, :, None] == key_doc[:, None, :]))[:, None]


def masked_scores(queries, keys, allowed):
    score_scale = HD ** (-0.5)
    scores = (
        jnp.einsum("sqhe,skhe->shqk", queries, keys, preferred_element_type=jnp.float32)
        * score_scale
    )
    return jnp.where(allowed, scores, masked_score)


def on_device(
    inputs, cotangent, matrices, momenta, small, small_first, small_second, segments, positions
):
    tensor_size = lax.axis_size("tp")
    cycle_size = lax.axis_size("blk")
    context_size = lax.axis_size("ctx")
    tensor_index = lax.axis_index("tp")
    cycle_index = lax.axis_index("blk")
    sequences, local_rows, model_width = inputs.shape
    per_group = matrices.shape[0]
    head_count = H // tensor_size
    unit_blocks = FF // HD // tensor_size
    block_rows = local_rows * context_size
    gathered = lax.all_gather(matrices.astype(jnp.bfloat16), "blk", axis=1, tiled=True).reshape(
        per_group, model_width, HD
    )
    query_key_value_weight = gathered[: 3 * head_count]
    projection_out_weight = gathered[3 * head_count : 4 * head_count]
    input_weight = gathered[4 * head_count : 4 * head_count + unit_blocks]
    down_projection_weight = gathered[4 * head_count + unit_blocks :]
    qkv_start = 6 * model_width + tensor_index * head_count * 3 * HD
    query_key_value_bias = lax.dynamic_slice_in_dim(small, qkv_start, head_count * 3 * HD).reshape(
        head_count, 3, HD
    )
    unit_start = 6 * model_width + H * 3 * HD + tensor_index * unit_blocks * HD
    hidden_unit_bias = lax.dynamic_slice_in_dim(small, unit_start, unit_blocks * HD).reshape(
        unit_blocks, HD
    )
    residual = inputs.astype(jnp.float32)

    def both_norms(values, gain_one, offset_one, gain_two, offset_two):
        return (layer_norm(values, gain_one, offset_one), layer_norm(values, gain_two, offset_two))

    (normed_one, normed_two), norm_back = jax.vjp(
        both_norms,
        residual,
        small[0:model_width],
        small[model_width : 2 * model_width],
        small[2 * model_width : 3 * model_width],
        small[3 * model_width : 4 * model_width],
    )
    first_input = normed_one.astype(jnp.bfloat16)
    second_input = normed_two.astype(jnp.bfloat16)
    projected = jnp.einsum(
        "pgk,jka->pgja", first_input, query_key_value_weight, preferred_element_type=jnp.float32
    )
    projected = projected.reshape(sequences, local_rows, 3, head_count, HD) + jnp.transpose(
        query_key_value_bias, (1, 0, 2)
    )
    cosine, sine = rope_tables(positions)

    def turn_pair(query_pre, key_pre):
        return (rotate(query_pre, cosine, sine), rotate(key_pre, cosine, sine))

    (query_turned, key_turned), turn_back = jax.vjp(
        turn_pair, projected[:, :, 0], projected[:, :, 1]
    )
    stacked = jnp.stack([query_turned, key_turned, projected[:, :, 2]], axis=2).astype(jnp.bfloat16)
    by_heads = to_heads(stacked)
    queries = by_heads[:, :, 0]
    head_local = queries.shape[2]

    def forward_visit(state, pair, source):
        row_max, row_total, weighted = state
        allowed = allowed_pairs(segments, cycle_index, source, block_rows)
        scores = masked_scores(queries, pair[:, :, 0], allowed)
        new_max = jnp.maximum(row_max, jnp.max(scores, axis=-1))
        weights = jnp.where(allowed, jnp.exp(scores - new_max[..., None]), 0.0)
        rescale = jnp.exp(row_max - new_max)
        row_total = row_total * rescale + jnp.sum(weights, axis=-1)
        weighted = weighted * rescale[..., None] + jnp.einsum(
            "shqk,skhe->shqe",
            weights.astype(jnp.bfloat16),
            pair[:, :, 1],
            preferred_element_type=jnp.float32,
        )
        return (new_max, row_total, weighted)

    def forward_hop(hop_index, carry):
        pair, state = carry
        source = (cycle_index - hop_index) % cycle_size
        state = forward_visit(state, pair, source)
        return (pass_keys(pair), state)

    start_state = (
        jnp.full((sequences, head_local, block_rows), masked_score, jnp.float32),
        jnp.zeros((sequences, head_local, block_rows), jnp.float32),
        jnp.zeros((sequences, head_local, block_rows, HD), jnp.float32),
    )
    pair, state = lax.fori_loop(0, cycle_size - 1, forward_hop, (by_heads[:, :, 1:], start_state))
    row_max, row_total, weighted = forward_visit(state, pair, (cycle_index + 1) % cycle_size)
    log_total = row_max + jnp.log(row_total)
    attended_rows = jnp.transpose(weighted / row_total[..., None], (0, 2, 1, 3))
    attention_result = to_positions(attended_rows.astype(jnp.bfloat16)[:, :, None])[:, :, 0]
    attention_branch = jnp.einsum(
        "roxu,xcu->roc", attention_result, projection_out_weight, preferred_element_type=jnp.float32
    )
    hidden_preactivation = (
        jnp.einsum("ptr,kra->ptka", second_input, input_weight, preferred_element_type=jnp.float32)
        + hidden_unit_bias
    )
    activated_hidden, gelu_back = jax.vjp(exact_gelu, hidden_preactivation)
    activated_reduced = activated_hidden.astype(jnp.bfloat16)
    perceptron_branch = jnp.einsum(
        "xkzp,zop->xko",
        activated_reduced,
        down_projection_weight,
        preferred_element_type=jnp.float32,
    )
    branches = lax.psum((attention_branch + perceptron_branch).astype(jnp.bfloat16), "tp").astype(
        jnp.float32
    )
    block_output = (
        residual
        + branches
        + small[4 * model_width : 5 * model_width]
        + small[5 * model_width : 6 * model_width]
    )
    act_grad = jnp.einsum(
        "ptr,kra->ptka", cotangent, down_projection_weight, preferred_element_type=jnp.float32
    )
    hidden_gradient = gelu_back(act_grad)[0].astype(jnp.bfloat16)
    down_grad = jnp.einsum(
        "gup,guzb->zpb", cotangent, activated_reduced, preferred_element_type=jnp.float32
    )
    in_grad = jnp.einsum(
        "gup,guzb->zpb", second_input, hidden_gradient, preferred_element_type=jnp.float32
    )
    second_grad = jnp.einsum(
        "xkzp,zop->xko", hidden_gradient, input_weight, preferred_element_type=jnp.float32
    )
    attended_grad = jnp.einsum(
        "pgk,jka->pgja", cotangent, projection_out_weight, preferred_element_type=jnp.float32
    ).astype(jnp.bfloat16)
    outproj_grad = jnp.einsum(
        "ztu,ztqi->qui", cotangent, attention_result, preferred_element_type=jnp.float32
    )
    grad_heads = to_heads(attended_grad[:, :, None])[:, :, 0]
    row_delta = jnp.transpose(
        jnp.sum(grad_heads.astype(jnp.float32) * attended_rows, axis=-1), (0, 2, 1)
    )

    def backward_visit(query_grad, pair, source):
        allowed = allowed_pairs(segments, cycle_index, source, block_rows)
        scores = masked_scores(queries, pair[:, :, 0], allowed)
        probabilities = jnp.where(allowed, jnp.exp(scores - log_total[..., None]), 0.0)
        value_grad = jnp.einsum(
            "shqk,sqhe->skhe",
            probabilities.astype(jnp.bfloat16),
            grad_heads,
            preferred_element_type=jnp.float32,
        )
        prob_grad = jnp.einsum(
            "sqhe,skhe->shqk", grad_heads, pair[:, :, 1], preferred_element_type=jnp.float32
        )
        score_grad = (probabilities * (prob_grad - row_delta[..., None])).astype(jnp.bfloat16)
        score_scale = HD ** (-0.5)
        query_grad = (
            query_grad
            + jnp.einsum(
                "shqk,skhe->sqhe", score_grad, pair[:, :, 0], preferred_element_type=jnp.float32
            )
            * score_scale
        )
        key_grad = (
            jnp.einsum("shqk,sqhe->skhe", score_grad, queries, preferred_element_type=jnp.float32)
            * score_scale
        )
        return (query_grad, jnp.stack([key_grad, value_grad], axis=2))

    def backward_hop(hop_index, carry):
        pair, pair_grad, query_grad = carry
        source = (cycle_index - hop_index) % cycle_size
        query_grad, visit_grad = backward_visit(query_grad, pair, source)
        return (pass_keys(pair), pass_grads(pair_grad + visit_grad), query_grad)

    zero_pair = jnp.zeros(by_heads[:, :, 1:].shape, jnp.float32)
    pair, pair_grad, query_grad = lax.fori_loop(
        0,
        cycle_size - 1,
        backward_hop,
        (by_heads[:, :, 1:], zero_pair, jnp.zeros(queries.shape, jnp.float32)),
    )
    query_grad, visit_grad = backward_visit(query_grad, pair, (cycle_index + 1) % cycle_size)
    pair_grad = pass_grads(pair_grad + visit_grad)
    head_grads = jnp.concatenate([query_grad[:, :, None], pair_grad], axis=2).astype(jnp.bfloat16)
    position_grads = to_positions(head_grads).astype(jnp.float32)
    query_pre_grad, key_pre_grad = turn_back((position_grads[:, :, 0], position_grads[:, :, 1]))
    projected_grad = jnp.stack(
        [query_pre_grad, key_pre_grad, position_grads[:, :, 2]], axis=2
    ).astype(jnp.bfloat16)
    flattened_gradient = projected_grad.reshape(sequences, local_rows, 3 * head_count, HD)
    query_key_value_gradient = jnp.einsum(
        "ztu,ztqi->qui", first_input, flattened_gradient, preferred_element_type=jnp.float32
    )
    first_grad = jnp.einsum(
        "roxu,xcu->roc",
        flattened_gradient,
        query_key_value_weight,
        preferred_element_type=jnp.float32,
    )
    input_part, gain_one_grad, offset_one_grad, gain_two_grad, offset_two_grad = norm_back(
        (first_grad, second_grad)
    )
    input_grad = cotangent.astype(jnp.float32) + lax.psum(
        input_part.astype(jnp.bfloat16), "tp"
    ).astype(jnp.float32)
    owner_share = jnp.where(tensor_index == 0, 1.0, 0.0).astype(jnp.float32)
    bias_grad = jnp.sum(cotangent.astype(jnp.float32), axis=(0, 1)) * owner_share
    qkv_bias_grad = jnp.transpose(
        jnp.sum(projected_grad.astype(jnp.float32), axis=(0, 1)), (1, 0, 2)
    ).reshape(-1)
    unit_bias_grad = jnp.sum(hidden_gradient.astype(jnp.float32), axis=(0, 1)).reshape(-1)
    local_small = jnp.concatenate(
        [
            gain_one_grad,
            offset_one_grad,
            gain_two_grad,
            offset_two_grad,
            bias_grad,
            bias_grad,
            jnp.zeros((small.shape[0] - 6 * model_width,), jnp.float32),
        ]
    )
    local_small = lax.dynamic_update_slice_in_dim(local_small, qkv_bias_grad, qkv_start, 0)
    local_small = lax.dynamic_update_slice_in_dim(local_small, unit_bias_grad, unit_start, 0)
    small_grads = lax.psum(local_small, ("blk", "ctx", "tp"))
    local_grad = jnp.concatenate(
        [query_key_value_gradient, outproj_grad, in_grad, down_grad], axis=0
    ).reshape(per_group, -1)
    shares = lax.psum_scatter(
        local_grad.astype(jnp.bfloat16), "blk", scatter_dimension=1, tiled=True
    )
    matrix_grads = lax.psum(shares, "ctx").astype(jnp.float32)
    new_momenta = momentum_decay * momenta + matrix_grads
    update = matrix_grads + momentum_decay * new_momenta
    per_owner = per_group // cycle_size
    sectioned = update.reshape(cycle_size, per_owner, update.shape[1])
    pieces = lax.all_to_all(
        sectioned.astype(jnp.bfloat16), "blk", split_axis=0, concat_axis=2, tiled=True
    ).astype(sectioned.dtype)
    piece_count = pieces.shape[1]
    settled_blocks = newton_schulz(pieces.reshape(piece_count, MODEL_DIM, HD)).reshape(
        1, piece_count, MODEL_DIM * HD
    )
    settled = lax.all_to_all(
        as_sent(settled_blocks), "blk", split_axis=2, concat_axis=0, tiled=True
    ).astype(settled_blocks.dtype)
    orthogonal_all = settled.reshape(per_group, -1)
    muon_scale = max(1.0, MODEL_DIM / HD) ** 0.5
    new_matrices = matrices - muon_rate * (muon_scale * orthogonal_all + weight_decay * matrices)
    new_first = adam_first * small_first + (1.0 - adam_first) * small_grads
    new_second = adam_second * small_second + (1.0 - adam_second) * small_grads * small_grads
    corrected = new_first / (1.0 - adam_first**STEP)
    spread = jnp.sqrt(new_second / (1.0 - adam_second**STEP))
    new_small = small - small_rate * corrected / (spread + adam_epsilon)
    return (
        block_output,
        input_grad,
        matrix_grads,
        new_matrices,
        new_momenta,
        small_grads,
        new_first,
        new_second,
        new_small,
    )


def native_view(array):
    rows, columns = array.shape
    tiled = array.reshape(rows // 8, 8, columns // 128, 128).transpose(0, 2, 1, 3)
    return tiled.reshape(rows // 8, columns // 16, 128)


def native_back(array):
    groups, rows, _ = array.shape
    return array.reshape(groups, rows // 8, 8, 128).transpose(0, 2, 1, 3).reshape(groups * 8, rows * 16)


def members_of(head):
    if head:
        return lambda piece, j: (j // 2, 4 * (j % 2) + piece)
    return lambda piece, j: (piece // 2, 4 * (piece % 2) + j)


def mem(kind=pltpu.VMEM):
    return pl.BlockSpec(memory_space=kind)


def limits(mebibytes):
    return pltpu.CompilerParams(vmem_limit_bytes=mebibytes << 20)


def low_lanes(rows):
    return lax.broadcasted_iota(jnp.int32, (rows, 128), 1) < HD


def dot(a, b, dims=((1,), (0,)), precision=None):
    return lax.dot_general(
        a, b, (dims, ((), ())), precision=precision, preferred_element_type=jnp.float32
    )


NT = ((1,), (1,))
TN = ((0,), (0,))


def corner(array):
    block = (1,) * (array.ndim - 2) + (min(16, array.shape[-2]), 128)
    return pl.BlockSpec(block, lambda *_: (0,) * array.ndim)


def takes(microseconds):
    return pl.CostEstimate(
        flops=int(microseconds * 1.15e9), transcendentals=0, bytes_accessed=int(1e6)
    )


def in_hbm(array):
    if array.size * array.dtype.itemsize < 1 << 21:
        return array
    return pltpu.with_memory_space_constraint(array, pltpu.HBM)


def out_hbm(shape):
    if shape.size * shape.dtype.itemsize < 1 << 20:
        return shape
    return pltpu.HBM(shape.shape, shape.dtype)


def full(array):
    return pl.BlockSpec(array.shape, lambda *_: (0,) * array.ndim)


def launch(kernel, operands, out_shapes, name, specs=None, after=(), vmem=20, cost=3, **more):
    taken = len(operands)
    body = kernel
    if after:
        body = lambda *refs: kernel(*refs[:taken], *refs[taken + len(after) :])
    if specs is None:
        specs = [mem(pltpu.SMEM)] + [full(a) for a in operands[1:]]
    if "out_specs" not in more:
        more["out_specs"] = jax.tree.map(full, out_shapes)
    more.setdefault("grid", (1,))
    return pl.pallas_call(
        body,
        in_specs=list(specs) + [corner(a) for a in after],
        out_shape=jax.tree.map(out_hbm, out_shapes),
        compiler_params=limits(vmem),
        cost_estimate=takes(cost),
        name=name,
        **more,
    )(*map(in_hbm, operands), *map(in_hbm, after))


def relayout_kernel(n, first, count, scal, src, out, *refs):
    fetched, paired, packed, arrivals, departures = refs[-5:]
    low = low_lanes(n)
    place_of = members_of(first == 0)
    steps = [(k, i) for k in range(count) for i in range(256 // n)]

    def fetch(k, i, group):
        rows = pl.ds(i * 8 * n, 8 * n)
        return pltpu.make_async_copy(
            src.at[2 * first + 2 * k + group, rows],
            fetched.at[2 * k + group, rows],
            arrivals.at[2 * k + group, i],
        )

    def leave(k, i):
        rows = pl.ds(i * 2 * n, 2 * n)
        return pltpu.make_async_copy(
            packed.at[pl.ds(4 * k, 4), rows], out.at[pl.ds(4 * k, 4), rows], departures.at[k, i]
        )

    for k, i in steps:
        for group in range(2):
            fetch(k, i, group).start()
    for k, i in steps:
        for group in range(2):
            fetch(k, i, group).wait()
        for piece in range(4):
            for half in range(2):
                pair = []
                for j in (2 * half, 2 * half + 1):
                    group, line = place_of(piece, j)
                    rows = pl.ds(i * 8 * n + line, n, stride=8)
                    pair.append(fetched[2 * k + group, rows, :])
                a, b = pair
                at = 2 * piece + half
                paired[at, pl.ds(0, n, stride=2), :] = jnp.where(low, a, pltpu.roll(b, 64, 1))
                paired[at, pl.ds(1, n, stride=2), :] = jnp.where(low, pltpu.roll(a, 64, 1), b)
                lanes = slice(half * 128, (half + 1) * 128)
                rows = slice(i * 2 * n, (i + 1) * 2 * n)
                packed[4 * k + piece, rows, lanes] = paired[at].astype(packed.dtype)
        leave(k, i).start()
    if len(refs) == 6:
        for k in range(count):
            refs[0][k] = packed[4 * k + scal[1]]
    for k, i in steps:
        leave(k, i).wait()


def relayout(scal, array, dtype, first, count, mine=False, n=128, after=()):
    shapes = [jax.ShapeDtypeStruct((4 * count, 512, 256), dtype)]
    specs = [mem(pl.ANY)]
    if mine:
        shapes.append(jax.ShapeDtypeStruct((count, 512, 256), dtype))
        specs.append(full(shapes[1]))
    return launch(
        functools.partial(relayout_kernel, n, first, count),
        [scal, native_view(array)],
        shapes,
        "relayout",
        specs=[mem(pltpu.SMEM), mem(pl.ANY)],
        after=after,
        cost=0.2 * count,
        vmem=24,
        out_specs=specs,
        scratch_shapes=[
            pltpu.VMEM((2 * count, 2048, 128), jnp.float32),
            pltpu.VMEM((8, 2 * n, 128), jnp.float32),
            pltpu.VMEM((4 * count, 512, 256), dtype),
            pltpu.SemaphoreType.DMA((2 * count, 256 // n)),
            pltpu.SemaphoreType.DMA((count, 256 // n)),
        ],
    )


def add_up(groups):
    for parts, target in groups:
        values = [part[...].astype(jnp.float32) for part in parts]
        while len(values) > 1:
            values = [sum(values[i : i + 2]) for i in range(0, len(values), 2)]
        if isinstance(target, list):
            for i, part in enumerate(target):
                part[...] = values[0][i].astype(part.dtype)
        else:
            target[...] = values[0].astype(target.dtype)


def grouped(refs, counts, targets):
    refs = iter(refs)
    return [([next(refs) for _ in range(n)], target) for n, target in zip(counts, targets)]


def normalized(x):
    centred = x - jnp.mean(x, axis=-1, keepdims=True)
    spread = jnp.mean(centred * centred, axis=-1, keepdims=True)
    root = lax.rsqrt(spread + norm_epsilon)
    return centred * root, root


def halves(values, first):
    left, right = values[:, :512], values[:, 512:]
    return jnp.where(first, left, right), jnp.where(first, right, left)


def whole(own, other, first):
    return jnp.concatenate([jnp.where(first, own, other), jnp.where(first, other, own)], axis=1)


def norm_back(grad, hat, root, gain):
    scaled = grad * gain
    along = jnp.mean(scaled * hat, axis=-1, keepdims=True)
    return root * (scaled - jnp.mean(scaled, axis=-1, keepdims=True) - hat * along)


def turned(values, cosine, sine):
    lane = lax.broadcasted_iota(jnp.int32, values.shape, 1) % HD
    other = jnp.where(lane < 8, pltpu.roll(values, 120, 1), pltpu.roll(values, 8, 1))
    return values * cosine + other * sine


def project_kernel(scal, x, cot, norms, bias, cosine, sine, own, r0, r1, r2, r3, send):
    first = scal[0] == 0
    hat, _ = normalized(x[...].astype(jnp.float32))
    h = (hat * norms[0:1] + norms[1:2]).astype(jnp.bfloat16)
    h_own, h_other = halves(h, first)
    c_own, c_other = halves(cot[...], first)
    tokens = h.shape[0]
    low = low_lanes(tokens)
    for r, other in enumerate((r0, r1, r2, r3)):
        head = scal[1] ^ r
        mine = own[head]
        theirs = other[...]
        pre = dot(h_own, mine) + dot(h_other, theirs) + bias[pl.ds(head, 1), :]
        back = dot(c_own, mine[:, 128:]) + dot(c_other, theirs[:, 128:])
        left = turned(pre[:, :128], cosine[...], sine[...]).astype(jnp.bfloat16)
        right = jnp.where(low, pre[:, 128:], back).astype(jnp.bfloat16)
        for s in range(2):
            rows = slice(128 * s, 128 * s + 128)
            send[4 * s + head, :, :128] = left[rows]
            send[4 * s + head, :, 128:] = right[rows]


def attention_kernel(rows_ref, seg, out, key_total, value_total):
    key_total[...] = jnp.zeros_like(key_total)
    value_total[...] = jnp.zeros_like(value_total)
    step = 256
    for block in range(rows_ref.shape[0] // step):
        rows = slice(block * step, (block + 1) * step)
        n = (block + 1) * step
        query = rows_ref[rows, 0:HD] * jnp.bfloat16(0.125)
        grad = rows_ref[rows, 3 * HD : 4 * HD]
        keys = rows_ref[0:n, HD : 2 * HD]
        values = rows_ref[0:n, 2 * HD : 3 * HD]
        scores = dot(query, keys, NT)
        query_place = block * step + lax.broadcasted_iota(jnp.int32, (step, n), 0)
        key_place = lax.broadcasted_iota(jnp.int32, (step, n), 1)
        allowed = (key_place <= query_place) & (key_place >= seg[rows, :])
        scores = jnp.where(allowed, scores, masked_score)
        weights = jnp.exp(scores - jnp.max(scores, axis=-1, keepdims=True))
        weights = jnp.where(allowed, weights, 0.0)
        weights = weights * (1.0 / jnp.sum(weights, axis=-1, keepdims=True))
        short = weights.astype(jnp.bfloat16)
        attended = dot(short, values)
        weight_grad = dot(grad, values, NT)
        delta = jnp.sum(weights * weight_grad, axis=-1, keepdims=True)
        score_grad = (weights * (weight_grad - delta)).astype(jnp.bfloat16)
        query_grad = dot(score_grad, keys) * 0.125
        key_total[0:n, :] += dot(score_grad, query, TN)
        value_total[0:n, :] += dot(short, grad, TN)
        out[rows, 0:HD] = query_grad.astype(jnp.bfloat16)
        out[rows, 3 * HD : 4 * HD] = attended.astype(jnp.bfloat16)
    out[:, HD : 2 * HD] = key_total[...].astype(jnp.bfloat16)
    out[:, 2 * HD : 3 * HD] = value_total[...].astype(jnp.bfloat16)


def feed_forward_kernel(
    scal, x, cot, norms, bias, weights, r0, r1, r2, r3,
    branch, input_part, keep, send, hidden_sums, norm_grads, cot_sums,
):
    first = scal[0] == 0
    hat, root = normalized(x[...].astype(jnp.float32))
    h = (hat * norms[2:3] + norms[3:4]).astype(jnp.bfloat16)
    h_own, h_other = halves(h, first)
    c_own, c_other = halves(cot[...], first)
    cot_sums[...] = jnp.sum(cot[...].astype(jnp.float32), axis=0, keepdims=True)
    outs = [0.0] * 4
    for r, other in enumerate((r0, r1, r2, r3)):
        piece = scal[1] ^ r
        in_own, in_other = weights[piece], other[0]
        down_own, down_other = weights[4 + piece], other[1]
        pre = dot(h_own, in_own) + dot(h_other, in_other) + bias[pl.ds(piece, 1), :]
        cumulative = 0.5 * (1.0 + lax.erf(pre * 0.7071067811865476))
        slope = cumulative + pre * (0.3989422804014327 * jnp.exp(-0.5 * pre * pre))
        act = (pre * cumulative).astype(jnp.bfloat16)
        act_grad = dot(c_own, down_own) + dot(c_other, down_other)
        grad = (act_grad * slope).astype(jnp.bfloat16)
        hidden_sums[pl.ds(piece, 1), :] = jnp.sum(
            grad.astype(jnp.float32), axis=0, keepdims=True
        )
        outs[0] += dot(act, down_own, NT)
        outs[1] += dot(act, down_other, NT)
        outs[2] += dot(grad, in_own, NT)
        outs[3] += dot(grad, in_other, NT)
        target = send if r % 2 else keep
        target[r // 2, 0] = grad
        target[r // 2, 1] = act
    branch[...] = whole(outs[0], outs[1], first)
    second = whole(outs[2], outs[3], first)
    norm_grads[0:1] = jnp.sum(second * hat, axis=0, keepdims=True)
    norm_grads[1:2] = jnp.sum(second, axis=0, keepdims=True)
    input_part[...] = norm_back(second, hat, root, norms[2:3])


def both_cores(scal, x, x_beside, cot, cot_beside, norms, at):
    first = scal[0] == 0
    tokens = jnp.concatenate([x[...], x_beside[...]], axis=0).astype(jnp.float32)
    hat, _ = normalized(tokens)
    h = (hat * norms[at : at + 1] + norms[at + 1 : at + 2]).astype(jnp.bfloat16)
    c = jnp.concatenate([cot[...], cot_beside[...]], axis=0)
    return list(zip(halves(h, first), halves(c, first)))


def unit_grads_kernel(
    scal, x, x_beside, cot, cot_beside, norms, keep, came, in_keep, in_send, down_keep, down_send
):
    for side, (h, c) in enumerate(both_cores(scal, x, x_beside, cot, cot_beside, norms, 2)):
        for far in range(2):
            grad = jnp.concatenate([keep[far, 0], came[far, 0]], axis=0)
            act = jnp.concatenate([keep[far, 1], came[far, 1]], axis=0)
            (in_send if side else in_keep)[far] = dot(h, grad, TN).astype(jnp.bfloat16)
            (down_send if far else down_keep)[side] = dot(c, act, TN).astype(jnp.bfloat16)


def combine_kernel(in_keep, in_came, down_keep, down_came, own, in_send, down_send):
    pairs = ((in_keep, in_came, in_send), (down_keep, down_came, down_send))
    for k, (keep, came, send) in enumerate(pairs):
        total = keep[...].astype(jnp.float32) + came[...].astype(jnp.float32)
        own[k] = total[0].astype(jnp.bfloat16)
        send[0] = total[1].astype(jnp.bfloat16)


def turn_kernel(scal, cosine, sine, back, keep, send, sums):
    low = low_lanes(keep.shape[1])
    for r in range(4):
        head = scal[1] ^ r
        grads = jnp.concatenate([back[head], back[4 + head]], axis=0)
        left = turned(grads[:, :128].astype(jnp.float32), cosine[...], -sine[...])
        left = left.astype(jnp.bfloat16)
        right = grads[:, 128:]
        target = send if r % 2 else keep
        target[r // 2, :, :128] = left
        target[r // 2, :, 128:] = right
        right = jnp.where(low, right.astype(jnp.float32), 0.0)
        wide = jnp.concatenate([left.astype(jnp.float32), right], axis=1)
        sums[pl.ds(head, 1), :] = jnp.sum(wide, axis=0, keepdims=True)


def split_last(piece):
    wide = piece.astype(jnp.float32)
    lane = lax.broadcasted_iota(jnp.int32, (1, wide.shape[1]), 1)
    share = (lane < 3 * HD).astype(jnp.float32)
    pre_grad = (wide * share).astype(jnp.bfloat16)
    attended = (wide * (1.0 - share)).astype(jnp.bfloat16)
    return pre_grad, attended


def head_grads_kernel(
    scal, x, x_beside, cot, cot_beside, norms, keep, came, totals, *outs
):
    both = totals[...].reshape(64, 256)
    coarse = both.astype(jnp.bfloat16)
    fine = (both - coarse.astype(jnp.float32)).astype(jnp.bfloat16)
    sides = both_cores(scal, x, x_beside, cot, cot_beside, norms, 0)
    a_keep, a_send, b_keep, b_send = outs
    for far in range(2):
        piece = jnp.concatenate([keep[far], came[far]], axis=0)
        pre_grad, attended = split_last(piece)
        for side, (h, c) in enumerate(sides):
            grad = (dot(h, pre_grad, TN) + dot(c, attended, TN)).astype(jnp.bfloat16)
            target = a_send if side else a_keep
            target[far, 0:256] = grad[0:256]
            target[far, 256:320] = coarse
            target[far, 320:384] = fine
            (b_send if far else b_keep)[side] = grad[256:512]


def combine_heads_kernel(a_keep, a_came, b_keep, b_came, a_own, a_send, b_own, b_send):
    for targets, at in (((a_own, b_own), 0), ((a_send, b_send), 1)):
        total = a_keep[at].astype(jnp.float32) + a_came[at].astype(jnp.float32)
        targets[0][0:256] = total[0:256].astype(jnp.bfloat16)
        tail = total[256:320] + total[320:384]
        coarse = tail.astype(jnp.bfloat16)
        targets[0][256:320] = coarse
        targets[0][320:384] = (tail - coarse.astype(jnp.float32)).astype(jnp.bfloat16)
        total = b_keep[at].astype(jnp.float32) + b_came[at].astype(jnp.float32)
        targets[1][...] = total.astype(jnp.bfloat16)


def add_kernel(near, came, kept, passed):
    add_up([((near, came), [kept, passed])])


def total_kernel(kept, came, total):
    add_up([((kept, came), total)])


def gather_kernel(
    scal, x, norms, keep, send, weights, r0, r1, r2, r3, ff_branch, ff_part,
    norm_two, cot_sums, unit_sums, qkv_sums, near, far, totals, parts,
):
    first = scal[0] == 0
    hat, root = normalized(x[...].astype(jnp.float32))
    outs = [0.0] * 4
    for r, other in enumerate((r0, r1, r2, r3)):
        mine, theirs = weights[scal[1] ^ r], other[0]
        pre_grad, attended = split_last((send if r % 2 else keep)[r // 2])
        outs[0] += dot(attended, mine, NT)
        outs[1] += dot(attended, theirs, NT)
        outs[2] += dot(pre_grad, mine, NT)
        outs[3] += dot(pre_grad, theirs, NT)
    branch = ff_branch[...] + whole(outs[0], outs[1], first)
    grad = whole(outs[2], outs[3], first)
    totals[...] = jnp.zeros_like(totals)
    rows = [jnp.sum(grad * hat, axis=0, keepdims=True), jnp.sum(grad, axis=0, keepdims=True)]
    rows += [norm_two[0:1], norm_two[1:2], cot_sums[...]]
    for i, row in enumerate(rows):
        for q in range(4):
            at = 4 * (i % 2) + q
            totals[i // 2, at : at + 1, :] = row[:, 256 * q : 256 * q + 256]
    totals[3 + scal[2], 0:4, :] = qkv_sums[...]
    totals[3 + scal[2], 4:8, :] = unit_sums[...]
    input_part = ff_part[...] + norm_back(grad, hat, root, norms[0:1])
    for q in range(4):
        parts[q, 0] = branch[64 * q : 64 * q + 64].astype(jnp.bfloat16)
        parts[q, 1] = input_part[64 * q : 64 * q + 64].astype(jnp.bfloat16)
    for r in range(4):
        (far if r % 2 else near)[r // 2] = parts[scal[2] ^ r]


def finish_rows_kernel(scal, x, cot, bias, r0, r1, r2, r3, block_output, input_grad):
    for r, piece in enumerate((r0, r1, r2, r3)):
        q = scal[2] ^ r
        block_output[q] = x[q].astype(jnp.float32) + piece[0].astype(jnp.float32) + bias[...]
        input_grad[q] = cot[q].astype(jnp.float32) + piece[1].astype(jnp.float32)


def gram_of_piece(total, momenta, grads, grams):
    short = total.astype(jnp.bfloat16)
    grads[0] = short
    update = 1.95 * short.astype(jnp.float32) + 0.9025 * momenta[0]
    gram = dot(update, update, TN, lax.Precision.HIGHEST)
    for j in range(4):
        cut = slice(j * HD, (j + 1) * HD)
        grams[0, j] = gram[cut, cut]


def unit_gram_kernel(place, own, in_came, down_came, momenta, *refs):
    grads, grams = refs[-2:]
    a = in_came[0].astype(jnp.float32)
    b = down_came[0].astype(jnp.float32)
    other = jnp.where(pl.program_id(0) == 0, a, b)
    gram_of_piece(own[0].astype(jnp.float32) + other, momenta, grads, grams)


def head_gram_kernel(place, a_own, a_came, b_own, b_came, momenta, *refs):
    grads, grams, totals = refs[-3:]
    a = a_own[...].astype(jnp.float32) + a_came[...].astype(jnp.float32)
    b = b_own[...].astype(jnp.float32) + b_came[...].astype(jnp.float32)
    gram_of_piece(jnp.concatenate([a[0:256], b], axis=0), momenta, grads, grams)
    totals[...] = (a[256:320] + a[320:384]).reshape(8, 8, 256)


def gram_of(kernel, first, others, momenta, place, shapes, after=()):
    chunks = momenta.shape[0] // 4
    piece = pl.BlockSpec((1, 512, 256), lambda i, s: (i, 0, 0))
    block = pl.BlockSpec((1, 512, 256), lambda i, s: (4 * i + s[1], 0, 0))
    return pl.pallas_call(
        kernel,
        grid_spec=pltpu.PrefetchScalarGridSpec(
            num_scalar_prefetch=1,
            grid=(chunks,),
            in_specs=[piece if first.ndim == 3 else full(first)]
            + [full(other) for other in others]
            + [block]
            + [corner(a) for a in after],
            out_specs=[piece, pl.BlockSpec((1, 4, HD, HD), lambda i, s: (i, 0, 0, 0))]
            + [full(shape) for shape in shapes],
        ),
        out_shape=[
            jax.ShapeDtypeStruct((chunks, 512, 256), jnp.bfloat16),
            jax.ShapeDtypeStruct((chunks, 4, HD, HD), jnp.float32),
            *map(out_hbm, shapes),
        ],
        compiler_params=limits(20),
        cost_estimate=takes(2.5),
        name="gram",
    )(place, *map(in_hbm, [first, *others, momenta, *after]))


def newton_kernel(counts, mine, theirs, *refs):
    taken = sum(counts)
    out = refs[taken]
    add_up(grouped(refs, counts, refs[taken + 1 :]))
    linear, square, cubic = quintic
    shape = (HD, HD)
    eye = lax.broadcasted_iota(jnp.int32, shape, 0) == lax.broadcasted_iota(jnp.int32, shape, 1)
    full = lax.Precision.HIGHEST
    chunks = mine.shape[0]
    places = [(i, j) for i in range(chunks) for j in range(4)]
    states = []
    for i, j in places:
        gram = mine[i, j] + theirs[i, j]
        trace = jnp.sum(jnp.where(eye, gram, 0.0), axis=(0, 1), keepdims=True)
        scale = 1.0 / (jnp.sqrt(trace) + muon_epsilon)
        states.append([gram * scale * scale, None, scale])
    for iteration in range(NEWTON):
        squares = [dot(s[0], s[0], precision=full) for s in states]
        steps = [
            jnp.where(eye, linear, 0.0) + square * s[0] + cubic * sq
            for s, sq in zip(states, squares)
        ]
        if iteration == 0:
            halfway = [dot(s[0], m, precision=full) for s, m in zip(states, steps)]
            for s, m in zip(states, steps):
                s[1] = m
        elif iteration < NEWTON - 1:
            both = [
                dot(jnp.concatenate([s[0], s[1]], axis=0), m, precision=full)
                for s, m in zip(states, steps)
            ]
            halfway = [x[:HD] for x in both]
            for s, x in zip(states, both):
                s[1] = x[HD:]
        else:
            for s, m in zip(states, steps):
                s[1] = dot(s[1], m, precision=full)
        if iteration < NEWTON - 1:
            for s, x, m in zip(states, halfway, steps):
                s[0] = dot(x, m, precision=full)
    for (i, j), s in zip(places, states):
        mix = s[1] * s[2]
        coarse = mix.astype(jnp.bfloat16)
        fine = (mix - coarse.astype(jnp.float32)).astype(jnp.bfloat16)
        rows, lanes = slice(64 * (j // 2), 64 * (j // 2) + 64), slice(128 * (j % 2), 128 * (j % 2) + 128)
        out[i, rows, lanes] = jnp.concatenate([coarse, fine], axis=1)


def newton(mine, theirs, sums, after=()):
    flat = [part for group in sums for part in group]
    operands = [mine, theirs, *flat]
    return launch(
        functools.partial(newton_kernel, [len(group) for group in sums]),
        operands,
        [jax.ShapeDtypeStruct((mine.shape[0], 2 * HD, 256), jnp.bfloat16)]
        + [jax.ShapeDtypeStruct(group[0].shape, group[0].dtype) for group in sums],
        "newton",
        cost=3.5,
        specs=[full(a) for a in operands],
        after=after,
    )


def update_kernel(
    n, head, scal, g0, g1, g2, g3, q0, q1, q2, q3, momenta, native_momenta, native, *refs
):
    grads, weights, moved, mixing, first, second, steps = refs[-7:]
    place_of = members_of(head)

    @pl.when((pl.program_id(0) == 0) & (pl.program_id(1) == 0))
    def _():
        mixing[...] = jnp.zeros_like(mixing)

    @pl.when(pl.program_id(1) == 0)
    def _():
        for r, q in enumerate((q0, q1, q2, q3)):
            for j in range(4):
                at = slice(HD * (j // 2), HD * (j // 2) + HD), slice(128 * (j % 2), 128 * (j % 2) + 128)
                wide = q[(0,) * (len(q.shape) - 2) + at].astype(jnp.float32)
                other = pltpu.roll(wide, HD, 1)
                below = low_lanes(HD) == (j % 2 == 0)
                rows = slice(j * HD, (j + 1) * HD)
                lanes = slice(128 * (j // 2), 128 * (j // 2) + 128)
                pair = (wide, other) if j % 2 == 0 else (other, wide)
                for level in range(2):
                    part = jnp.where(below, pair[level], 0.0)
                    mixing[r, level, rows, lanes] = part.astype(jnp.bfloat16)

    low = low_lanes(n)
    for r, piece in enumerate((g0, g1, g2, g3)):
        place = scal[1] ^ r
        grad = piece[(0,) * (len(piece.shape) - 2)].astype(jnp.float32)
        update = 1.95 * grad + 0.9025 * momenta[place]
        coarse = update.astype(jnp.bfloat16)
        fine = (update - coarse.astype(jnp.float32)).astype(jnp.bfloat16)
        settled = dot(coarse, mixing[r, 0]) + dot(coarse, mixing[r, 1]) + dot(fine, mixing[r, 0])
        for half in range(2):
            k = 2 * r + half
            first[k] = grad[:, half * 128 : (half + 1) * 128]
            second[k] = settled[:, half * 128 : (half + 1) * 128]
            for source, target in ((first, grads), (second, steps)):
                even = source[k, pl.ds(0, n, stride=2), :]
                odd = source[k, pl.ds(1, n, stride=2), :]
                lines = (
                    jnp.where(low, even, pltpu.roll(odd, 64, 1)),
                    jnp.where(low, pltpu.roll(even, 64, 1), odd),
                )
                for w in range(2):
                    group, line = place_of(place, 2 * half + w)
                    target[group, pl.ds(line, n, stride=8), :] = lines[w]
    moved[...] = momentum_decay * native_momenta[...] + grads[...]
    weight = native[...]
    weights[...] = weight - muon_rate * (4.0 * steps[...] + weight_decay * weight)


def update(
    first, scal, own, far, mix, mix_far, beside, momenta, native_momenta, native, before=(), after=(), n=128
):
    chunks = own.shape[0]
    block = pl.BlockSpec((2, 8 * n, 128), lambda k, i: (first + k, i, 0))
    piece = pl.BlockSpec((1, 2 * n, 256), lambda k, i: (k, i, 0))
    factor = pl.BlockSpec((1, 2 * HD, 256), lambda k, i: (k, 0, 0))
    pieces, factors = [piece, None, piece, None], [factor, None, factor, None]
    for r in (0, 1):
        pieces[2 * r + 1] = pl.BlockSpec((1, 1, 2 * n, 256), lambda k, i, r=r: (r, k, i, 0))
        factors[2 * r + 1] = pl.BlockSpec((1, 1, 2 * HD, 256), lambda k, i, r=r: (r, k, 4, 0))
    grads, mixes = [own, beside, far, beside], [mix, beside, mix_far, beside]
    return launch(
        functools.partial(update_kernel, n, first == 0),
        [scal, *grads, *mixes, momenta, native_view(native_momenta), native_view(native), *before],
        [jax.ShapeDtypeStruct((6, 2048, 128), jnp.float32)] * 3,
        "update",
        specs=[mem(pltpu.SMEM)]
        + pieces
        + factors
        + [pl.BlockSpec((4, 2 * n, 256), lambda k, i: (k, i, 0)), block, block]
        + [mem(pl.ANY)] * len(before),
        after=after,
        vmem=32,
        cost=0.5 * chunks,
        grid=(chunks, 256 // n),
        out_specs=[block] * 3,
        scratch_shapes=[
            pltpu.VMEM((4, 2, 256, 256), jnp.bfloat16),
            pltpu.VMEM((8, 2 * n, 128), jnp.float32),
            pltpu.VMEM((8, 2 * n, 128), jnp.float32),
            pltpu.VMEM((2, 8 * n, 128), jnp.float32),
        ],
        input_output_aliases={12 + i: i for i in range(len(before))},
    )


def whole_device(
    inputs, cotangent, matrices, momenta, small, small_first, small_second, segments, positions
):
    blk_at = lax.axis_index("blk")
    ctx_at = lax.axis_index("ctx")
    tp_at = lax.axis_index("tp")
    scal = jnp.stack([blk_at, ctx_at, tp_at]).astype(jnp.int32)
    sequences, local_rows, width = inputs.shape
    tokens = sequences * local_rows
    both = ("blk", "ctx")
    f32, bf16 = jnp.float32, jnp.bfloat16
    shaped = jax.ShapeDtypeStruct

    def hop(values, by):
        return lax.ppermute(values, both, [(i, i ^ by) for i in range(8)])

    def hop_tp(values, by):
        return lax.ppermute(values, "tp", [(i, i ^ by) for i in range(4)])

    def tied(values, *results):
        return lax.optimization_barrier((values, *results))[0]

    def spread(piece):
        c = hop(piece, 2)
        return [piece, hop(piece, 1), c, hop(c, 1)]

    x = inputs.reshape(tokens, width)
    cot = cotangent.reshape(tokens, width)
    norms = small[: 4 * width].reshape(4, width)
    qkv_start = 6 * width + tp_at * 4 * 3 * HD
    qkv_bias = lax.dynamic_slice_in_dim(small, qkv_start, 4 * 3 * HD).reshape(4, 3 * HD)
    qkv_bias = jnp.pad(qkv_bias, ((0, 0), (0, HD)))
    unit_start = 6 * width + H * 3 * HD + tp_at * 1024
    unit_bias = lax.dynamic_slice_in_dim(small, unit_start, 1024).reshape(4, 256)
    lane = jnp.arange(128) % HD
    frequency = rope_base ** (-2.0 * (lane % 8).astype(f32) / ROTARY)
    angles = positions.astype(f32).reshape(tokens, 1) * frequency
    cosine = jnp.where(lane < ROTARY, jnp.cos(angles), 1.0)
    sign = jnp.where(lane < 8, -1.0, jnp.where(lane < ROTARY, 1.0, 0.0))
    sine = jnp.sin(angles) * sign

    head_weights, mine = relayout(scal, matrices, bf16, 0, 1, mine=True)
    first_hop = hop(mine, 4)
    unit_weights, mine_units = relayout(scal, matrices, bf16, 1, 2, mine=True, after=(mine,))
    first_hop = tied(first_hop, mine_units)
    other_heads = spread(first_hop)
    units_near = hop(tied(mine_units, first_hop), 4)
    x_beside = hop(x, 1)
    cot_beside = hop(cot, 1)

    send = launch(
        project_kernel,
        [scal, x, cot, norms, qkv_bias, cosine, sine, head_weights]
        + [piece[0] for piece in other_heads],
        shaped((8, local_rows, 256), bf16),
        "project",
    )
    arrived = lax.all_to_all(tied(send, units_near), both, split_axis=0, concat_axis=0, tiled=True)
    (piled_heads,) = relayout(scal, momenta, f32, 0, 1, after=(send,))
    units_near = tied(units_near, send)
    units_far = hop(units_near, 2)
    units_beside = hop(units_near, 1)
    documents = lax.dynamic_index_in_dim(segments, blk_at, 0, keepdims=False)
    length = documents.shape[0]
    attended = launch(
        attention_kernel,
        [arrived.reshape(length, 256), documents.reshape(length, 1)],
        shaped((length, 256), bf16),
        "attention",
        cost=6,
        specs=[full(arrived.reshape(length, 256)), pl.BlockSpec((length, 1), lambda *_: (0, 0))],
        after=(piled_heads,),
        scratch_shapes=[pltpu.VMEM((length, HD), f32)] * 2,
    )
    back = lax.all_to_all(
        attended.reshape(8, local_rows, 256), both, split_axis=0, concat_axis=0, tiled=True
    )

    units_far = tied(units_far, attended)
    other_units = [units_near, units_beside, units_far, hop(units_far, 1)]
    ff_branch, ff_part, unit_keep, unit_send, unit_sums, norm_two, cot_sums = launch(
        feed_forward_kernel,
        [scal, x, cot, norms, unit_bias, unit_weights, *other_units],
        [
            shaped((tokens, width), f32),
            shaped((tokens, width), f32),
            shaped((2, 2, tokens, 256), bf16),
            shaped((2, 2, tokens, 256), bf16),
            shaped((4, 256), f32),
            shaped((2, width), f32),
            shaped((1, width), f32),
        ],
        "feed_forward",
        cost=5.5,
        after=(attended,),
    )
    head_keep, head_send, qkv_sums = launch(
        turn_kernel,
        [scal, cosine, sine, back],
        [shaped((2, tokens, 256), bf16)] * 2 + [shaped((4, 256), f32)],
        "turn",
        cost=2,
        after=(unit_sums,),
    )
    in_keep, in_send, down_keep, down_send = launch(
        unit_grads_kernel,
        [scal, x, x_beside, cot, cot_beside, norms, unit_keep, hop(unit_send, 1)],
        [shaped((2, 512, 256), bf16)] * 4,
        "unit_grads",
        cost=3.5,
        after=(qkv_sums,),
    )
    sums = [norm_two, cot_sums, unit_sums, qkv_sums]
    near, far, totals = launch(
        gather_kernel,
        [scal, x, norms, head_keep, head_send, head_weights, *other_heads, ff_branch, ff_part, *sums],
        [shaped((2, 2, 64, width), bf16)] * 2 + [shaped((8, 8, 256), f32)],
        "gather",
        after=(in_keep,),
        scratch_shapes=[pltpu.VMEM((4, 2, 64, width), bf16)],
    )
    a_keep, a_send, b_keep, b_send = launch(
        head_grads_kernel,
        [scal, x, x_beside, cot, cot_beside, norms, head_keep, hop(head_send, 1), totals],
        [shaped((2, 384, 256), bf16)] * 2 + [shaped((2, 256, 256), bf16)] * 2,
        "head_grads",
        cost=4,
    )
    (piled_units,) = relayout(scal, momenta, f32, 1, 2, after=(a_keep,))
    came = hop_tp(far, 1)
    a_came, b_came = hop(a_send, 4), hop(b_send, 2)
    operands = [in_keep, hop(in_send, 4), down_keep, hop(down_send, 2)]
    own, in_send, down_send = launch(
        combine_kernel,
        operands,
        [shaped((2, 512, 256), bf16)] + [shaped((1, 512, 256), bf16)] * 2,
        "combine",
        specs=[full(a) for a in operands],
        cost=2,
        after=(piled_units,),
    )
    in_came, down_came = hop(in_send, 2), hop(down_send, 4)
    kept, passed = launch(
        add_kernel,
        [near, came],
        [shaped((2, 64, width), bf16)] * 2,
        "add",
        specs=[full(near)] * 2,
        after=(in_send,),
    )
    passed = hop_tp(passed, 2)
    operands = [a_keep, a_came, b_keep, b_came]
    a_own, a_send, b_own, b_send = launch(
        combine_heads_kernel,
        operands,
        [shaped((384, 256), bf16)] * 2 + [shaped((256, 256), bf16)] * 2,
        "combine_heads",
        specs=[full(a) for a in operands],
        after=(kept,),
    )
    a_came, b_came = hop(a_send, 2), hop(b_send, 4)
    unit_sum, unit_grams = gram_of(
        unit_gram_kernel,
        own,
        [in_came, down_came],
        piled_units,
        scal,
        [],
        after=(a_own,),
    )
    unit_theirs = hop(unit_grams, 4)
    unit_far = hop(unit_sum, 2)
    head_sum, head_grams, totals = gram_of(
        head_gram_kernel,
        a_own,
        [a_came, b_own, b_came],
        piled_heads,
        scal,
        [shaped((8, 8, 256), f32)],
        after=(unit_sum,),
    )
    head_theirs = hop(head_grams, 4)
    head_far = hop(head_sum, 2)
    total = launch(
        total_kernel,
        [kept, passed],
        shaped((2, 64, width), bf16),
        "total",
        cost=1,
        specs=[full(kept)] * 2,
        after=(head_sum,),
    )
    total_far, total_beside = hop_tp(total, 2), hop_tp(total, 1)
    (unit_mix,) = newton(unit_grams, unit_theirs, [], after=(total,))
    unit_mix_far = hop(unit_mix, 2)
    head_mix, totals = newton(
        head_grams,
        head_theirs,
        [(totals, hop(totals, 1))],
        after=(unit_mix, unit_far),
    )
    head_mix_far = hop(head_mix, 2)

    def to_beside(*pieces):
        return hop(jnp.stack([jnp.concatenate(pair, axis=1) for pair in pieces]), 1)

    beside = to_beside((unit_sum, unit_mix), (unit_far, tied(unit_mix_far, head_mix)))
    totals_came = hop_tp(totals, 1)
    before = update(
        1, scal, unit_sum, unit_far, unit_mix, unit_mix_far, beside, piled_units, momenta, matrices,
        after=(head_mix, total_far),
    )
    head_far, head_mix_far = tied((head_far, head_mix_far), before[0])
    beside = to_beside((head_sum, head_mix), (head_far, head_mix_far))
    outs = update(
        0, scal, head_sum, head_far, head_mix, head_mix_far, beside, piled_heads, momenta, matrices,
        before,
    )
    total_far = tied(total_far, head_mix)
    total_last = hop_tp(total_far, 1)
    totals = totals + tied(totals_came, before[0])
    totals = tied(totals + hop_tp(totals, 2), outs[0])

    block_output, input_grad = launch(
        finish_rows_kernel,
        [
            scal,
            x.reshape(4, 64, width),
            cot.reshape(4, 64, width),
            (small[4 * width : 5 * width] + small[5 * width : 6 * width]).reshape(1, width),
            total,
            total_beside,
            total_far,
            total_last,
        ],
        [shaped((4, 64, width), f32)] * 2,
        "finish_rows",
        cost=2,
        after=(outs[0],),
    )

    cot_total = totals[2, :4].reshape(-1) * 0.25
    small_grads = jnp.concatenate(
        [
            totals[:2].reshape(-1),
            cot_total,
            cot_total,
            totals[3:7, :4, : 3 * HD].reshape(-1),
            totals[3:7, 4:].reshape(-1),
        ]
    )
    return (
        block_output.reshape(inputs.shape),
        input_grad.reshape(inputs.shape),
        native_back(outs[0]),
        native_back(outs[1]),
        native_back(outs[2]),
        small_grads,
        *small_step(small, small_first, small_second, small_grads),
    )


def small_step(small, small_first, small_second, small_grads):
    new_first = adam_first * small_first + (1.0 - adam_first) * small_grads
    new_second = adam_second * small_second + (1.0 - adam_second) * small_grads * small_grads
    corrected = new_first / (1.0 - adam_first**STEP)
    spread = jnp.sqrt(new_second / (1.0 - adam_second**STEP))
    new_small = small - small_rate * corrected / (spread + adam_epsilon)
    return new_first, new_second, new_small


def solution(mesh):
    in_specs = (
        P(None, ("blk", "ctx"), None),
        P(None, ("blk", "ctx"), None),
        P("tp", "blk"),
        P("tp", "blk"),
        P(),
        P(),
        P(),
        P(),
        P(None, ("blk", "ctx")),
    )
    out_specs = (
        P(None, ("blk", "ctx"), None),
        P(None, ("blk", "ctx"), None),
        P("tp", "blk"),
        P("tp", "blk"),
        P("tp", "blk"),
        P(),
        P(),
        P(),
        P(),
    )
    one_each = mesh.shape["blk"] == SEQS and mesh.shape["ctx"] * mesh.shape["tp"] == H
    one_each = one_each and mesh.shape["tp"] == 4
    return jax.shard_map(
        whole_device if one_each else on_device, mesh=mesh, in_specs=in_specs, out_specs=out_specs, check_vma=False
    )
```

```python
import functools

import jax
import jax.numpy as jnp
from jax import lax
from jax.experimental import pallas as pl
from jax.experimental.pallas import tpu as pltpu
from jax.sharding import PartitionSpec as P

MODEL_DIM = 1024
H = 16
HD = 64
FF = 4096
ROTARY = 16
NEWTON = 5
STEP = 10
SEQS = 2


norm_epsilon = 1e-05
rope_base = 10000.0
masked_score = -1e30
momentum_decay = 0.95
muon_rate = 0.2
weight_decay = 0.01
muon_epsilon = 1e-07
quintic = (3.4445, -4.775, 2.0315)
adam_first = 0.9
adam_second = 0.95
adam_epsilon = 1e-08
small_rate = 0.2


def passed_along(x, axis, by):
    devices = lax.axis_size(axis)
    pairs = [(i, i + by) for i in range(devices) if 0 <= i + by < devices]
    return lax.ppermute(x, axis, pairs)


def shifted(x, axis, by):
    devices = lax.axis_size(axis)
    return lax.ppermute(x, axis, [(i, (i + by) % devices) for i in range(devices)])


def as_sent(x):

    def short(part):
        return part.astype(jnp.bfloat16) if part.dtype == jnp.float32 else part

    return jax.tree.map(short, x)


def layer_norm(values, scaling, offset):
    centre = jnp.mean(values, axis=-1, keepdims=True)
    centred = values - centre
    spread = jnp.mean(centred * centred, axis=-1, keepdims=True)
    return centred * lax.rsqrt(spread + norm_epsilon) * scaling + offset


def rope_tables(positions):
    halfway = ROTARY // 2
    frequency = rope_base ** (-2.0 * jnp.arange(halfway, dtype=jnp.float32) / ROTARY)
    angles = positions.astype(jnp.float32)[..., None] * frequency
    return (jnp.cos(angles)[:, :, None, :], jnp.sin(angles)[:, :, None, :])


def rotate(values, cosine, sine):
    halfway = ROTARY // 2
    former = values[..., :halfway]
    latter = values[..., halfway:ROTARY]
    return jnp.concatenate(
        [former * cosine - latter * sine, latter * cosine + former * sine, values[..., ROTARY:]],
        axis=-1,
    )


def exact_gelu(values):
    return jax.nn.gelu(values, approximate=False)


def newton_schulz(blocks):
    frobenius = jnp.sqrt(jnp.sum(blocks * blocks, axis=(1, 2), keepdims=True))
    current = blocks / (frobenius + muon_epsilon)
    linear_term, square_term, cubic_term = quintic
    for iteration in range(NEWTON):
        gram_matrix = jnp.einsum("mde,mdf->mef", current, current, precision=lax.Precision.HIGHEST)
        polynomial = square_term * gram_matrix + cubic_term * jnp.einsum(
            "mef,mfg->meg", gram_matrix, gram_matrix, precision=lax.Precision.HIGHEST
        )
        current = linear_term * current + jnp.einsum(
            "mde,mef->mdf", current, polynomial, precision=lax.Precision.HIGHEST
        )
    return current


def to_heads(values):
    return lax.all_to_all(values, "ctx", split_axis=3, concat_axis=1, tiled=True)


def to_positions(values):
    return lax.all_to_all(values, "ctx", split_axis=1, concat_axis=3, tiled=True)


def pass_keys(pair):
    return passed_along(pair, "blk", 1)


def pass_grads(pair_grad):
    return shifted(pair_grad.astype(jnp.bfloat16), "blk", 1).astype(pair_grad.dtype)


def allowed_pairs(segments, query_block, key_block, block_rows):
    query_place = query_block * block_rows + jnp.arange(block_rows, dtype=jnp.int32)
    key_place = key_block * block_rows + jnp.arange(block_rows, dtype=jnp.int32)
    query_doc = lax.dynamic_slice_in_dim(segments, query_block * block_rows, block_rows, 1)
    key_doc = lax.dynamic_slice_in_dim(segments, key_block * block_rows, block_rows, 1)
    causal = key_place[None, :] <= query_place[:, None]
    return (causal[None] & (query_doc[:, :, None] == key_doc[:, None, :]))[:, None]


def masked_scores(queries, keys, allowed):
    score_scale = HD ** (-0.5)
    scores = (
        jnp.einsum("sqhe,skhe->shqk", queries, keys, preferred_element_type=jnp.float32)
        * score_scale
    )
    return jnp.where(allowed, scores, masked_score)


def on_device(
    inputs, cotangent, matrices, momenta, small, small_first, small_second, segments, positions
):
    tensor_size = lax.axis_size("tp")
    cycle_size = lax.axis_size("blk")
    context_size = lax.axis_size("ctx")
    tensor_index = lax.axis_index("tp")
    cycle_index = lax.axis_index("blk")
    sequences, local_rows, model_width = inputs.shape
    per_group = matrices.shape[0]
    head_count = H // tensor_size
    unit_blocks = FF // HD // tensor_size
    block_rows = local_rows * context_size
    gathered = lax.all_gather(matrices.astype(jnp.bfloat16), "blk", axis=1, tiled=True).reshape(
        per_group, model_width, HD
    )
    query_key_value_weight = gathered[: 3 * head_count]
    projection_out_weight = gathered[3 * head_count : 4 * head_count]
    input_weight = gathered[4 * head_count : 4 * head_count + unit_blocks]
    down_projection_weight = gathered[4 * head_count + unit_blocks :]
    qkv_start = 6 * model_width + tensor_index * head_count * 3 * HD
    query_key_value_bias = lax.dynamic_slice_in_dim(small, qkv_start, head_count * 3 * HD).reshape(
        head_count, 3, HD
    )
    unit_start = 6 * model_width + H * 3 * HD + tensor_index * unit_blocks * HD
    hidden_unit_bias = lax.dynamic_slice_in_dim(small, unit_start, unit_blocks * HD).reshape(
        unit_blocks, HD
    )
    residual = inputs.astype(jnp.float32)

    def both_norms(values, gain_one, offset_one, gain_two, offset_two):
        return (layer_norm(values, gain_one, offset_one), layer_norm(values, gain_two, offset_two))

    (normed_one, normed_two), norm_back = jax.vjp(
        both_norms,
        residual,
        small[0:model_width],
        small[model_width : 2 * model_width],
        small[2 * model_width : 3 * model_width],
        small[3 * model_width : 4 * model_width],
    )
    first_input = normed_one.astype(jnp.bfloat16)
    second_input = normed_two.astype(jnp.bfloat16)
    projected = jnp.einsum(
        "pgk,jka->pgja", first_input, query_key_value_weight, preferred_element_type=jnp.float32
    )
    projected = projected.reshape(sequences, local_rows, 3, head_count, HD) + jnp.transpose(
        query_key_value_bias, (1, 0, 2)
    )
    cosine, sine = rope_tables(positions)

    def turn_pair(query_pre, key_pre):
        return (rotate(query_pre, cosine, sine), rotate(key_pre, cosine, sine))

    (query_turned, key_turned), turn_back = jax.vjp(
        turn_pair, projected[:, :, 0], projected[:, :, 1]
    )
    stacked = jnp.stack([query_turned, key_turned, projected[:, :, 2]], axis=2).astype(jnp.bfloat16)
    by_heads = to_heads(stacked)
    queries = by_heads[:, :, 0]
    head_local = queries.shape[2]

    def forward_visit(state, pair, source):
        row_max, row_total, weighted = state
        allowed = allowed_pairs(segments, cycle_index, source, block_rows)
        scores = masked_scores(queries, pair[:, :, 0], allowed)
        new_max = jnp.maximum(row_max, jnp.max(scores, axis=-1))
        weights = jnp.where(allowed, jnp.exp(scores - new_max[..., None]), 0.0)
        rescale = jnp.exp(row_max - new_max)
        row_total = row_total * rescale + jnp.sum(weights, axis=-1)
        weighted = weighted * rescale[..., None] + jnp.einsum(
            "shqk,skhe->shqe",
            weights.astype(jnp.bfloat16),
            pair[:, :, 1],
            preferred_element_type=jnp.float32,
        )
        return (new_max, row_total, weighted)

    def forward_hop(hop_index, carry):
        pair, state = carry
        source = (cycle_index - hop_index) % cycle_size
        state = forward_visit(state, pair, source)
        return (pass_keys(pair), state)

    start_state = (
        jnp.full((sequences, head_local, block_rows), masked_score, jnp.float32),
        jnp.zeros((sequences, head_local, block_rows), jnp.float32),
        jnp.zeros((sequences, head_local, block_rows, HD), jnp.float32),
    )
    pair, state = lax.fori_loop(0, cycle_size - 1, forward_hop, (by_heads[:, :, 1:], start_state))
    row_max, row_total, weighted = forward_visit(state, pair, (cycle_index + 1) % cycle_size)
    log_total = row_max + jnp.log(row_total)
    attended_rows = jnp.transpose(weighted / row_total[..., None], (0, 2, 1, 3))
    attention_result = to_positions(attended_rows.astype(jnp.bfloat16)[:, :, None])[:, :, 0]
    attention_branch = jnp.einsum(
        "roxu,xcu->roc", attention_result, projection_out_weight, preferred_element_type=jnp.float32
    )
    hidden_preactivation = (
        jnp.einsum("ptr,kra->ptka", second_input, input_weight, preferred_element_type=jnp.float32)
        + hidden_unit_bias
    )
    activated_hidden, gelu_back = jax.vjp(exact_gelu, hidden_preactivation)
    activated_reduced = activated_hidden.astype(jnp.bfloat16)
    perceptron_branch = jnp.einsum(
        "xkzp,zop->xko",
        activated_reduced,
        down_projection_weight,
        preferred_element_type=jnp.float32,
    )
    branches = lax.psum((attention_branch + perceptron_branch).astype(jnp.bfloat16), "tp").astype(
        jnp.float32
    )
    block_output = (
        residual
        + branches
        + small[4 * model_width : 5 * model_width]
        + small[5 * model_width : 6 * model_width]
    )
    act_grad = jnp.einsum(
        "ptr,kra->ptka", cotangent, down_projection_weight, preferred_element_type=jnp.float32
    )
    hidden_gradient = gelu_back(act_grad)[0].astype(jnp.bfloat16)
    down_grad = jnp.einsum(
        "gup,guzb->zpb", cotangent, activated_reduced, preferred_element_type=jnp.float32
    )
    in_grad = jnp.einsum(
        "gup,guzb->zpb", second_input, hidden_gradient, preferred_element_type=jnp.float32
    )
    second_grad = jnp.einsum(
        "xkzp,zop->xko", hidden_gradient, input_weight, preferred_element_type=jnp.float32
    )
    attended_grad = jnp.einsum(
        "pgk,jka->pgja", cotangent, projection_out_weight, preferred_element_type=jnp.float32
    ).astype(jnp.bfloat16)
    outproj_grad = jnp.einsum(
        "ztu,ztqi->qui", cotangent, attention_result, preferred_element_type=jnp.float32
    )
    grad_heads = to_heads(attended_grad[:, :, None])[:, :, 0]
    row_delta = jnp.transpose(
        jnp.sum(grad_heads.astype(jnp.float32) * attended_rows, axis=-1), (0, 2, 1)
    )

    def backward_visit(query_grad, pair, source):
        allowed = allowed_pairs(segments, cycle_index, source, block_rows)
        scores = masked_scores(queries, pair[:, :, 0], allowed)
        probabilities = jnp.where(allowed, jnp.exp(scores - log_total[..., None]), 0.0)
        value_grad = jnp.einsum(
            "shqk,sqhe->skhe",
            probabilities.astype(jnp.bfloat16),
            grad_heads,
            preferred_element_type=jnp.float32,
        )
        prob_grad = jnp.einsum(
            "sqhe,skhe->shqk", grad_heads, pair[:, :, 1], preferred_element_type=jnp.float32
        )
        score_grad = (probabilities * (prob_grad - row_delta[..., None])).astype(jnp.bfloat16)
        score_scale = HD ** (-0.5)
        query_grad = (
            query_grad
            + jnp.einsum(
                "shqk,skhe->sqhe", score_grad, pair[:, :, 0], preferred_element_type=jnp.float32
            )
            * score_scale
        )
        key_grad = (
            jnp.einsum("shqk,sqhe->skhe", score_grad, queries, preferred_element_type=jnp.float32)
            * score_scale
        )
        return (query_grad, jnp.stack([key_grad, value_grad], axis=2))

    def backward_hop(hop_index, carry):
        pair, pair_grad, query_grad = carry
        source = (cycle_index - hop_index) % cycle_size
        query_grad, visit_grad = backward_visit(query_grad, pair, source)
        return (pass_keys(pair), pass_grads(pair_grad + visit_grad), query_grad)

    zero_pair = jnp.zeros(by_heads[:, :, 1:].shape, jnp.float32)
    pair, pair_grad, query_grad = lax.fori_loop(
        0,
        cycle_size - 1,
        backward_hop,
        (by_heads[:, :, 1:], zero_pair, jnp.zeros(queries.shape, jnp.float32)),
    )
    query_grad, visit_grad = backward_visit(query_grad, pair, (cycle_index + 1) % cycle_size)
    pair_grad = pass_grads(pair_grad + visit_grad)
    head_grads = jnp.concatenate([query_grad[:, :, None], pair_grad], axis=2).astype(jnp.bfloat16)
    position_grads = to_positions(head_grads).astype(jnp.float32)
    query_pre_grad, key_pre_grad = turn_back((position_grads[:, :, 0], position_grads[:, :, 1]))
    projected_grad = jnp.stack(
        [query_pre_grad, key_pre_grad, position_grads[:, :, 2]], axis=2
    ).astype(jnp.bfloat16)
    flattened_gradient = projected_grad.reshape(sequences, local_rows, 3 * head_count, HD)
    query_key_value_gradient = jnp.einsum(
        "ztu,ztqi->qui", first_input, flattened_gradient, preferred_element_type=jnp.float32
    )
    first_grad = jnp.einsum(
        "roxu,xcu->roc",
        flattened_gradient,
        query_key_value_weight,
        preferred_element_type=jnp.float32,
    )
    input_part, gain_one_grad, offset_one_grad, gain_two_grad, offset_two_grad = norm_back(
        (first_grad, second_grad)
    )
    input_grad = cotangent.astype(jnp.float32) + lax.psum(
        input_part.astype(jnp.bfloat16), "tp"
    ).astype(jnp.float32)
    owner_share = jnp.where(tensor_index == 0, 1.0, 0.0).astype(jnp.float32)
    bias_grad = jnp.sum(cotangent.astype(jnp.float32), axis=(0, 1)) * owner_share
    qkv_bias_grad = jnp.transpose(
        jnp.sum(projected_grad.astype(jnp.float32), axis=(0, 1)), (1, 0, 2)
    ).reshape(-1)
    unit_bias_grad = jnp.sum(hidden_gradient.astype(jnp.float32), axis=(0, 1)).reshape(-1)
    local_small = jnp.concatenate(
        [
            gain_one_grad,
            offset_one_grad,
            gain_two_grad,
            offset_two_grad,
            bias_grad,
            bias_grad,
            jnp.zeros((small.shape[0] - 6 * model_width,), jnp.float32),
        ]
    )
    local_small = lax.dynamic_update_slice_in_dim(local_small, qkv_bias_grad, qkv_start, 0)
    local_small = lax.dynamic_update_slice_in_dim(local_small, unit_bias_grad, unit_start, 0)
    small_grads = lax.psum(local_small, ("blk", "ctx", "tp"))
    local_grad = jnp.concatenate(
        [query_key_value_gradient, outproj_grad, in_grad, down_grad], axis=0
    ).reshape(per_group, -1)
    shares = lax.psum_scatter(
        local_grad.astype(jnp.bfloat16), "blk", scatter_dimension=1, tiled=True
    )
    matrix_grads = lax.psum(shares, "ctx").astype(jnp.float32)
    new_momenta = momentum_decay * momenta + matrix_grads
    update = matrix_grads + momentum_decay * new_momenta
    per_owner = per_group // cycle_size
    sectioned = update.reshape(cycle_size, per_owner, update.shape[1])
    pieces = lax.all_to_all(
        sectioned.astype(jnp.bfloat16), "blk", split_axis=0, concat_axis=2, tiled=True
    ).astype(sectioned.dtype)
    piece_count = pieces.shape[1]
    settled_blocks = newton_schulz(pieces.reshape(piece_count, MODEL_DIM, HD)).reshape(
        1, piece_count, MODEL_DIM * HD
    )
    settled = lax.all_to_all(
        as_sent(settled_blocks), "blk", split_axis=2, concat_axis=0, tiled=True
    ).astype(settled_blocks.dtype)
    orthogonal_all = settled.reshape(per_group, -1)
    muon_scale = max(1.0, MODEL_DIM / HD) ** 0.5
    new_matrices = matrices - muon_rate * (muon_scale * orthogonal_all + weight_decay * matrices)
    new_first = adam_first * small_first + (1.0 - adam_first) * small_grads
    new_second = adam_second * small_second + (1.0 - adam_second) * small_grads * small_grads
    corrected = new_first / (1.0 - adam_first**STEP)
    spread = jnp.sqrt(new_second / (1.0 - adam_second**STEP))
    new_small = small - small_rate * corrected / (spread + adam_epsilon)
    return (
        block_output,
        input_grad,
        matrix_grads,
        new_matrices,
        new_momenta,
        small_grads,
        new_first,
        new_second,
        new_small,
    )


def native_view(array):
    rows, columns = array.shape
    tiled = array.reshape(rows // 8, 8, columns // 128, 128).transpose(0, 2, 1, 3)
    return tiled.reshape(rows // 8, columns // 16, 128)


def native_back(array):
    groups, rows, _ = array.shape
    return array.reshape(groups, rows // 8, 8, 128).transpose(0, 2, 1, 3).reshape(groups * 8, rows * 16)


def members_of(head):
    if head:
        return lambda piece, j: (j // 2, 4 * (j % 2) + piece)
    return lambda piece, j: (piece // 2, 4 * (piece % 2) + j)


def mem(kind=pltpu.VMEM):
    return pl.BlockSpec(memory_space=kind)


def limits(mebibytes):
    return pltpu.CompilerParams(vmem_limit_bytes=mebibytes << 20)


def low_lanes(rows):
    return lax.broadcasted_iota(jnp.int32, (rows, 128), 1) < HD


def dot(a, b, dims=((1,), (0,)), precision=None):
    return lax.dot_general(
        a, b, (dims, ((), ())), precision=precision, preferred_element_type=jnp.float32
    )


NT = ((1,), (1,))
TN = ((0,), (0,))


def corner(array):
    block = (1,) * (array.ndim - 2) + (min(16, array.shape[-2]), 128)
    return pl.BlockSpec(block, lambda *_: (0,) * array.ndim)


def takes(microseconds):
    return pl.CostEstimate(
        flops=int(microseconds * 1.15e9), transcendentals=0, bytes_accessed=int(1e6)
    )


def in_hbm(array):
    if array.size * array.dtype.itemsize < 1 << 21:
        return array
    return pltpu.with_memory_space_constraint(array, pltpu.HBM)


def out_hbm(shape):
    if shape.size * shape.dtype.itemsize < 1 << 20:
        return shape
    return pltpu.HBM(shape.shape, shape.dtype)


def full(array):
    return pl.BlockSpec(array.shape, lambda *_: (0,) * array.ndim)


def launch(kernel, operands, out_shapes, name, specs=None, after=(), vmem=20, cost=3, **more):
    taken = len(operands)
    body = kernel
    if after:
        body = lambda *refs: kernel(*refs[:taken], *refs[taken + len(after) :])
    if specs is None:
        specs = [mem(pltpu.SMEM)] + [full(a) for a in operands[1:]]
    if "out_specs" not in more:
        more["out_specs"] = jax.tree.map(full, out_shapes)
    more.setdefault("grid", (1,))
    return pl.pallas_call(
        body,
        in_specs=list(specs) + [corner(a) for a in after],
        out_shape=jax.tree.map(out_hbm, out_shapes),
        compiler_params=limits(vmem),
        cost_estimate=takes(cost),
        name=name,
        **more,
    )(*map(in_hbm, operands), *map(in_hbm, after))


def relayout_kernel(n, first, count, scal, src, out, *refs):
    fetched, paired, packed, arrivals, departures = refs[-5:]
    low = low_lanes(n)
    place_of = members_of(first == 0)
    steps = [(k, i) for k in range(count) for i in range(256 // n)]

    def fetch(k, i, group):
        rows = pl.ds(i * 8 * n, 8 * n)
        return pltpu.make_async_copy(
            src.at[2 * first + 2 * k + group, rows],
            fetched.at[2 * k + group, rows],
            arrivals.at[2 * k + group, i],
        )

    def leave(k, i):
        rows = pl.ds(i * 2 * n, 2 * n)
        return pltpu.make_async_copy(
            packed.at[pl.ds(4 * k, 4), rows], out.at[pl.ds(4 * k, 4), rows], departures.at[k, i]
        )

    for k, i in steps:
        for group in range(2):
            fetch(k, i, group).start()
    for k, i in steps:
        for group in range(2):
            fetch(k, i, group).wait()
        for piece in range(4):
            for half in range(2):
                pair = []
                for j in (2 * half, 2 * half + 1):
                    group, line = place_of(piece, j)
                    rows = pl.ds(i * 8 * n + line, n, stride=8)
                    pair.append(fetched[2 * k + group, rows, :])
                a, b = pair
                at = 2 * piece + half
                paired[at, pl.ds(0, n, stride=2), :] = jnp.where(low, a, pltpu.roll(b, 64, 1))
                paired[at, pl.ds(1, n, stride=2), :] = jnp.where(low, pltpu.roll(a, 64, 1), b)
                lanes = slice(half * 128, (half + 1) * 128)
                rows = slice(i * 2 * n, (i + 1) * 2 * n)
                packed[4 * k + piece, rows, lanes] = paired[at].astype(packed.dtype)
        leave(k, i).start()
    if len(refs) == 6:
        for k in range(count):
            refs[0][k] = packed[4 * k + scal[1]]
    for k, i in steps:
        leave(k, i).wait()


def relayout(scal, array, dtype, first, count, mine=False, n=128, after=()):
    shapes = [jax.ShapeDtypeStruct((4 * count, 512, 256), dtype)]
    specs = [mem(pl.ANY)]
    if mine:
        shapes.append(jax.ShapeDtypeStruct((count, 512, 256), dtype))
        specs.append(full(shapes[1]))
    return launch(
        functools.partial(relayout_kernel, n, first, count),
        [scal, native_view(array)],
        shapes,
        "relayout",
        specs=[mem(pltpu.SMEM), mem(pl.ANY)],
        after=after,
        cost=0.2 * count,
        vmem=24,
        out_specs=specs,
        scratch_shapes=[
            pltpu.VMEM((2 * count, 2048, 128), jnp.float32),
            pltpu.VMEM((8, 2 * n, 128), jnp.float32),
            pltpu.VMEM((4 * count, 512, 256), dtype),
            pltpu.SemaphoreType.DMA((2 * count, 256 // n)),
            pltpu.SemaphoreType.DMA((count, 256 // n)),
        ],
    )


def add_up(groups):
    for parts, target in groups:
        values = [part[...].astype(jnp.float32) for part in parts]
        while len(values) > 1:
            values = [sum(values[i : i + 2]) for i in range(0, len(values), 2)]
        if isinstance(target, list):
            for i, part in enumerate(target):
                part[...] = values[0][i].astype(part.dtype)
        else:
            target[...] = values[0].astype(target.dtype)


def grouped(refs, counts, targets):
    refs = iter(refs)
    return [([next(refs) for _ in range(n)], target) for n, target in zip(counts, targets)]


def normalized(x):
    centred = x - jnp.mean(x, axis=-1, keepdims=True)
    spread = jnp.mean(centred * centred, axis=-1, keepdims=True)
    root = lax.rsqrt(spread + norm_epsilon)
    return centred * root, root


def halves(values, first):
    left, right = values[:, :512], values[:, 512:]
    return jnp.where(first, left, right), jnp.where(first, right, left)


def whole(own, other, first):
    return jnp.concatenate([jnp.where(first, own, other), jnp.where(first, other, own)], axis=1)


def norm_back(grad, hat, root, gain):
    scaled = grad * gain
    along = jnp.mean(scaled * hat, axis=-1, keepdims=True)
    return root * (scaled - jnp.mean(scaled, axis=-1, keepdims=True) - hat * along)


def turned(values, cosine, sine):
    lane = lax.broadcasted_iota(jnp.int32, values.shape, 1) % HD
    other = jnp.where(lane < 8, pltpu.roll(values, 120, 1), pltpu.roll(values, 8, 1))
    return values * cosine + other * sine


def project_kernel(scal, x, cot, norms, bias, cosine, sine, own, r0, r1, r2, r3, send):
    first = scal[0] == 0
    hat, _ = normalized(x[...].astype(jnp.float32))
    h = (hat * norms[0:1] + norms[1:2]).astype(jnp.bfloat16)
    h_own, h_other = halves(h, first)
    c_own, c_other = halves(cot[...], first)
    tokens = h.shape[0]
    low = low_lanes(tokens)
    for r, other in enumerate((r0, r1, r2, r3)):
        head = scal[1] ^ r
        mine = own[head]
        theirs = other[...]
        pre = dot(h_own, mine) + dot(h_other, theirs) + bias[pl.ds(head, 1), :]
        back = dot(c_own, mine[:, 128:]) + dot(c_other, theirs[:, 128:])
        left = turned(pre[:, :128], cosine[...], sine[...]).astype(jnp.bfloat16)
        right = jnp.where(low, pre[:, 128:], back).astype(jnp.bfloat16)
        for s in range(2):
            rows = slice(128 * s, 128 * s + 128)
            send[4 * s + head, :, :128] = left[rows]
            send[4 * s + head, :, 128:] = right[rows]


def attention_kernel(rows_ref, seg, out, key_total, value_total):
    key_total[...] = jnp.zeros_like(key_total)
    value_total[...] = jnp.zeros_like(value_total)
    step = 256
    for block in range(rows_ref.shape[0] // step):
        rows = slice(block * step, (block + 1) * step)
        n = (block + 1) * step
        query = rows_ref[rows, 0:HD] * jnp.bfloat16(0.125)
        grad = rows_ref[rows, 3 * HD : 4 * HD]
        keys = rows_ref[0:n, HD : 2 * HD]
        values = rows_ref[0:n, 2 * HD : 3 * HD]
        scores = dot(query, keys, NT)
        query_place = block * step + lax.broadcasted_iota(jnp.int32, (step, n), 0)
        key_place = lax.broadcasted_iota(jnp.int32, (step, n), 1)
        allowed = (key_place <= query_place) & (key_place >= seg[rows, :])
        scores = jnp.where(allowed, scores, masked_score)
        weights = jnp.exp(scores - jnp.max(scores, axis=-1, keepdims=True))
        weights = jnp.where(allowed, weights, 0.0)
        weights = weights * (1.0 / jnp.sum(weights, axis=-1, keepdims=True))
        short = weights.astype(jnp.bfloat16)
        attended = dot(short, values)
        weight_grad = dot(grad, values, NT)
        delta = jnp.sum(weights * weight_grad, axis=-1, keepdims=True)
        score_grad = (weights * (weight_grad - delta)).astype(jnp.bfloat16)
        query_grad = dot(score_grad, keys) * 0.125
        key_total[0:n, :] += dot(score_grad, query, TN)
        value_total[0:n, :] += dot(short, grad, TN)
        out[rows, 0:HD] = query_grad.astype(jnp.bfloat16)
        out[rows, 3 * HD : 4 * HD] = attended.astype(jnp.bfloat16)
    out[:, HD : 2 * HD] = key_total[...].astype(jnp.bfloat16)
    out[:, 2 * HD : 3 * HD] = value_total[...].astype(jnp.bfloat16)


def feed_forward_kernel(
    scal, x, cot, norms, bias, weights, r0, r1, r2, r3,
    branch, input_part, keep, send, hidden_sums, norm_grads, cot_sums,
):
    first = scal[0] == 0
    hat, root = normalized(x[...].astype(jnp.float32))
    h = (hat * norms[2:3] + norms[3:4]).astype(jnp.bfloat16)
    h_own, h_other = halves(h, first)
    c_own, c_other = halves(cot[...], first)
    cot_sums[...] = jnp.sum(cot[...].astype(jnp.float32), axis=0, keepdims=True)
    outs = [0.0] * 4
    for r, other in enumerate((r0, r1, r2, r3)):
        piece = scal[1] ^ r
        in_own, in_other = weights[piece], other[0]
        down_own, down_other = weights[4 + piece], other[1]
        pre = dot(h_own, in_own) + dot(h_other, in_other) + bias[pl.ds(piece, 1), :]
        cumulative = 0.5 * (1.0 + lax.erf(pre * 0.7071067811865476))
        slope = cumulative + pre * (0.3989422804014327 * jnp.exp(-0.5 * pre * pre))
        act = (pre * cumulative).astype(jnp.bfloat16)
        act_grad = dot(c_own, down_own) + dot(c_other, down_other)
        grad = (act_grad * slope).astype(jnp.bfloat16)
        hidden_sums[pl.ds(piece, 1), :] = jnp.sum(
            grad.astype(jnp.float32), axis=0, keepdims=True
        )
        outs[0] += dot(act, down_own, NT)
        outs[1] += dot(act, down_other, NT)
        outs[2] += dot(grad, in_own, NT)
        outs[3] += dot(grad, in_other, NT)
        target = send if r % 2 else keep
        target[r // 2, 0] = grad
        target[r // 2, 1] = act
    branch[...] = whole(outs[0], outs[1], first)
    second = whole(outs[2], outs[3], first)
    norm_grads[0:1] = jnp.sum(second * hat, axis=0, keepdims=True)
    norm_grads[1:2] = jnp.sum(second, axis=0, keepdims=True)
    input_part[...] = norm_back(second, hat, root, norms[2:3])


def both_cores(scal, x, x_beside, cot, cot_beside, norms, at):
    first = scal[0] == 0
    tokens = jnp.concatenate([x[...], x_beside[...]], axis=0).astype(jnp.float32)
    hat, _ = normalized(tokens)
    h = (hat * norms[at : at + 1] + norms[at + 1 : at + 2]).astype(jnp.bfloat16)
    c = jnp.concatenate([cot[...], cot_beside[...]], axis=0)
    return list(zip(halves(h, first), halves(c, first)))


def unit_grads_kernel(
    scal, x, x_beside, cot, cot_beside, norms, keep, came, in_keep, in_send, down_keep, down_send
):
    for side, (h, c) in enumerate(both_cores(scal, x, x_beside, cot, cot_beside, norms, 2)):
        for far in range(2):
            grad = jnp.concatenate([keep[far, 0], came[far, 0]], axis=0)
            act = jnp.concatenate([keep[far, 1], came[far, 1]], axis=0)
            (in_send if side else in_keep)[far] = dot(h, grad, TN).astype(jnp.bfloat16)
            (down_send if far else down_keep)[side] = dot(c, act, TN).astype(jnp.bfloat16)


def combine_kernel(in_keep, in_came, down_keep, down_came, own, in_send, down_send):
    pairs = ((in_keep, in_came, in_send), (down_keep, down_came, down_send))
    for k, (keep, came, send) in enumerate(pairs):
        total = keep[...].astype(jnp.float32) + came[...].astype(jnp.float32)
        own[k] = total[0].astype(jnp.bfloat16)
        send[0] = total[1].astype(jnp.bfloat16)


def turn_kernel(scal, cosine, sine, back, keep, send, sums):
    low = low_lanes(keep.shape[1])
    for r in range(4):
        head = scal[1] ^ r
        grads = jnp.concatenate([back[head], back[4 + head]], axis=0)
        left = turned(grads[:, :128].astype(jnp.float32), cosine[...], -sine[...])
        left = left.astype(jnp.bfloat16)
        right = grads[:, 128:]
        target = send if r % 2 else keep
        target[r // 2, :, :128] = left
        target[r // 2, :, 128:] = right
        right = jnp.where(low, right.astype(jnp.float32), 0.0)
        wide = jnp.concatenate([left.astype(jnp.float32), right], axis=1)
        sums[pl.ds(head, 1), :] = jnp.sum(wide, axis=0, keepdims=True)


def split_last(piece):
    wide = piece.astype(jnp.float32)
    lane = lax.broadcasted_iota(jnp.int32, (1, wide.shape[1]), 1)
    share = (lane < 3 * HD).astype(jnp.float32)
    pre_grad = (wide * share).astype(jnp.bfloat16)
    attended = (wide * (1.0 - share)).astype(jnp.bfloat16)
    return pre_grad, attended


def head_grads_kernel(
    scal, x, x_beside, cot, cot_beside, norms, keep, came, totals, *outs
):
    both = totals[...].reshape(64, 256)
    coarse = both.astype(jnp.bfloat16)
    fine = (both - coarse.astype(jnp.float32)).astype(jnp.bfloat16)
    sides = both_cores(scal, x, x_beside, cot, cot_beside, norms, 0)
    a_keep, a_send, b_keep, b_send = outs
    for far in range(2):
        piece = jnp.concatenate([keep[far], came[far]], axis=0)
        pre_grad, attended = split_last(piece)
        for side, (h, c) in enumerate(sides):
            grad = (dot(h, pre_grad, TN) + dot(c, attended, TN)).astype(jnp.bfloat16)
            target = a_send if side else a_keep
            target[far, 0:256] = grad[0:256]
            target[far, 256:320] = coarse
            target[far, 320:384] = fine
            (b_send if far else b_keep)[side] = grad[256:512]


def combine_heads_kernel(a_keep, a_came, b_keep, b_came, a_own, a_send, b_own, b_send):
    for targets, at in (((a_own, b_own), 0), ((a_send, b_send), 1)):
        total = a_keep[at].astype(jnp.float32) + a_came[at].astype(jnp.float32)
        targets[0][0:256] = total[0:256].astype(jnp.bfloat16)
        tail = total[256:320] + total[320:384]
        coarse = tail.astype(jnp.bfloat16)
        targets[0][256:320] = coarse
        targets[0][320:384] = (tail - coarse.astype(jnp.float32)).astype(jnp.bfloat16)
        total = b_keep[at].astype(jnp.float32) + b_came[at].astype(jnp.float32)
        targets[1][...] = total.astype(jnp.bfloat16)


def add_kernel(near, came, kept, passed):
    add_up([((near, came), [kept, passed])])


def gather_kernel(
    scal, x, norms, keep, send, weights, r0, r1, r2, r3, ff_branch, ff_part,
    norm_two, cot_sums, unit_sums, qkv_sums, near, far, totals, parts,
):
    first = scal[0] == 0
    hat, root = normalized(x[...].astype(jnp.float32))
    outs = [0.0] * 4
    for r, other in enumerate((r0, r1, r2, r3)):
        mine, theirs = weights[scal[1] ^ r], other[0]
        pre_grad, attended = split_last((send if r % 2 else keep)[r // 2])
        outs[0] += dot(attended, mine, NT)
        outs[1] += dot(attended, theirs, NT)
        outs[2] += dot(pre_grad, mine, NT)
        outs[3] += dot(pre_grad, theirs, NT)
    branch = ff_branch[...] + whole(outs[0], outs[1], first)
    grad = whole(outs[2], outs[3], first)
    totals[...] = jnp.zeros_like(totals)
    rows = [jnp.sum(grad * hat, axis=0, keepdims=True), jnp.sum(grad, axis=0, keepdims=True)]
    rows += [norm_two[0:1], norm_two[1:2], cot_sums[...]]
    for i, row in enumerate(rows):
        for q in range(4):
            at = 4 * (i % 2) + q
            totals[i // 2, at : at + 1, :] = row[:, 256 * q : 256 * q + 256]
    totals[3 + scal[2], 0:4, :] = qkv_sums[...]
    totals[3 + scal[2], 4:8, :] = unit_sums[...]
    input_part = ff_part[...] + norm_back(grad, hat, root, norms[0:1])
    for q in range(4):
        parts[q, 0] = branch[64 * q : 64 * q + 64].astype(jnp.bfloat16)
        parts[q, 1] = input_part[64 * q : 64 * q + 64].astype(jnp.bfloat16)
    for r in range(4):
        (far if r % 2 else near)[r // 2] = parts[scal[2] ^ r]


def finish_rows_kernel(scal, x, cot, bias, near, far, beside, block_output, input_grad):
    for r in range(4):
        q = scal[2] ^ r
        piece = beside.at[r // 2] if r % 2 else (far if r else near)
        block_output[q] = x[q].astype(jnp.float32) + piece[0].astype(jnp.float32) + bias[...]
        input_grad[q] = cot[q].astype(jnp.float32) + piece[1].astype(jnp.float32)


def gram_of_piece(total, momenta, grads, grams):
    short = total.astype(jnp.bfloat16)
    grads[0] = short
    update = 1.95 * short.astype(jnp.float32) + 0.9025 * momenta[0]
    gram = dot(update, update, TN, lax.Precision.HIGHEST)
    for j in range(4):
        cut = slice(j * HD, (j + 1) * HD)
        grams[0, j] = gram[cut, cut]


def unit_gram_kernel(place, own, in_came, down_came, momenta, kept, came, *refs):
    grads, grams, total = refs[-3:]

    @pl.when(pl.program_id(0) == 0)
    def _():
        add_up([((kept, came), total)])

    a = in_came[0].astype(jnp.float32)
    b = down_came[0].astype(jnp.float32)
    other = jnp.where(pl.program_id(0) == 0, a, b)
    gram_of_piece(own[0].astype(jnp.float32) + other, momenta, grads, grams)


def head_gram_kernel(place, a_own, a_came, b_own, b_came, momenta, *refs):
    grads, grams, totals = refs[-3:]
    a = a_own[...].astype(jnp.float32) + a_came[...].astype(jnp.float32)
    b = b_own[...].astype(jnp.float32) + b_came[...].astype(jnp.float32)
    gram_of_piece(jnp.concatenate([a[0:256], b], axis=0), momenta, grads, grams)
    totals[...] = (a[256:320] + a[320:384]).reshape(8, 8, 256)


def gram_of(kernel, first, others, momenta, place, more, shapes, after=()):
    chunks = momenta.shape[0] // 4
    piece = pl.BlockSpec((1, 512, 256), lambda i, s: (i, 0, 0))
    block = pl.BlockSpec((1, 512, 256), lambda i, s: (4 * i + s[1], 0, 0))
    return pl.pallas_call(
        kernel,
        grid_spec=pltpu.PrefetchScalarGridSpec(
            num_scalar_prefetch=1,
            grid=(chunks,),
            in_specs=[piece if first.ndim == 3 else full(first)]
            + [full(other) for other in others]
            + [block]
            + [full(part) for part in more]
            + [corner(a) for a in after],
            out_specs=[piece, pl.BlockSpec((1, 4, HD, HD), lambda i, s: (i, 0, 0, 0))]
            + [full(shape) for shape in shapes],
        ),
        out_shape=[
            jax.ShapeDtypeStruct((chunks, 512, 256), jnp.bfloat16),
            jax.ShapeDtypeStruct((chunks, 4, HD, HD), jnp.float32),
            *map(out_hbm, shapes),
        ],
        compiler_params=limits(20),
        cost_estimate=takes(2.5),
        name="gram",
    )(place, *map(in_hbm, [first, *others, momenta, *more, *after]))


def newton_kernel(counts, mine, theirs, *refs):
    taken = sum(counts)
    out = refs[taken]
    add_up(grouped(refs, counts, refs[taken + 1 :]))
    linear, square, cubic = quintic
    shape = (HD, HD)
    eye = lax.broadcasted_iota(jnp.int32, shape, 0) == lax.broadcasted_iota(jnp.int32, shape, 1)
    full = lax.Precision.HIGHEST
    chunks = mine.shape[0]
    places = [(i, j) for i in range(chunks) for j in range(4)]
    states = []
    for i, j in places:
        gram = mine[i, j] + theirs[i, j]
        trace = jnp.sum(jnp.where(eye, gram, 0.0), axis=(0, 1), keepdims=True)
        scale = 1.0 / (jnp.sqrt(trace) + muon_epsilon)
        states.append([gram * scale * scale, None, scale])
    for iteration in range(NEWTON):
        squares = [dot(s[0], s[0], precision=full) for s in states]
        steps = [
            jnp.where(eye, linear, 0.0) + square * s[0] + cubic * sq
            for s, sq in zip(states, squares)
        ]
        if iteration == 0:
            halfway = [dot(s[0], m, precision=full) for s, m in zip(states, steps)]
            for s, m in zip(states, steps):
                s[1] = m
        elif iteration < NEWTON - 1:
            both = [
                dot(jnp.concatenate([s[0], s[1]], axis=0), m, precision=full)
                for s, m in zip(states, steps)
            ]
            halfway = [x[:HD] for x in both]
            for s, x in zip(states, both):
                s[1] = x[HD:]
        else:
            for s, m in zip(states, steps):
                s[1] = dot(s[1], m, precision=full)
        if iteration < NEWTON - 1:
            for s, x, m in zip(states, halfway, steps):
                s[0] = dot(x, m, precision=full)
    for (i, j), s in zip(places, states):
        mix = s[1] * s[2]
        coarse = mix.astype(jnp.bfloat16)
        fine = (mix - coarse.astype(jnp.float32)).astype(jnp.bfloat16)
        rows, lanes = slice(64 * (j // 2), 64 * (j // 2) + 64), slice(128 * (j % 2), 128 * (j % 2) + 128)
        out[i, rows, lanes] = jnp.concatenate([coarse, fine], axis=1)


def newton(mine, theirs, sums, after=()):
    flat = [part for group in sums for part in group]
    operands = [mine, theirs, *flat]
    return launch(
        functools.partial(newton_kernel, [len(group) for group in sums]),
        operands,
        [jax.ShapeDtypeStruct((mine.shape[0], 2 * HD, 256), jnp.bfloat16)]
        + [jax.ShapeDtypeStruct(group[0].shape, group[0].dtype) for group in sums],
        "newton",
        cost=3.5,
        specs=[full(a) for a in operands],
        after=after,
    )


def update_kernel(
    n, head, scal, g0, g1, g2, g3, q0, q1, q2, q3, momenta, native_momenta, native, *refs
):
    grads, weights, moved, mixing, first, second, steps = refs[-7:]
    place_of = members_of(head)

    @pl.when((pl.program_id(0) == 0) & (pl.program_id(1) == 0))
    def _():
        mixing[...] = jnp.zeros_like(mixing)

    @pl.when(pl.program_id(1) == 0)
    def _():
        for r, q in enumerate((q0, q1, q2, q3)):
            for j in range(4):
                at = slice(HD * (j // 2), HD * (j // 2) + HD), slice(128 * (j % 2), 128 * (j % 2) + 128)
                wide = q[(0,) * (len(q.shape) - 2) + at].astype(jnp.float32)
                other = pltpu.roll(wide, HD, 1)
                below = low_lanes(HD) == (j % 2 == 0)
                rows = slice(j * HD, (j + 1) * HD)
                lanes = slice(128 * (j // 2), 128 * (j // 2) + 128)
                pair = (wide, other) if j % 2 == 0 else (other, wide)
                for level in range(2):
                    part = jnp.where(below, pair[level], 0.0)
                    mixing[r, level, rows, lanes] = part.astype(jnp.bfloat16)

    low = low_lanes(n)
    for r, piece in enumerate((g0, g1, g2, g3)):
        place = scal[1] ^ r
        grad = piece[(0,) * (len(piece.shape) - 2)].astype(jnp.float32)
        update = 1.95 * grad + 0.9025 * momenta[place]
        coarse = update.astype(jnp.bfloat16)
        fine = (update - coarse.astype(jnp.float32)).astype(jnp.bfloat16)
        settled = dot(coarse, mixing[r, 0]) + dot(coarse, mixing[r, 1]) + dot(fine, mixing[r, 0])
        for half in range(2):
            k = 2 * r + half
            first[k] = grad[:, half * 128 : (half + 1) * 128]
            second[k] = settled[:, half * 128 : (half + 1) * 128]
            for source, target in ((first, grads), (second, steps)):
                even = source[k, pl.ds(0, n, stride=2), :]
                odd = source[k, pl.ds(1, n, stride=2), :]
                lines = (
                    jnp.where(low, even, pltpu.roll(odd, 64, 1)),
                    jnp.where(low, pltpu.roll(even, 64, 1), odd),
                )
                for w in range(2):
                    group, line = place_of(place, 2 * half + w)
                    target[group, pl.ds(line, n, stride=8), :] = lines[w]
    moved[...] = momentum_decay * native_momenta[...] + grads[...]
    weight = native[...]
    weights[...] = weight - muon_rate * (4.0 * steps[...] + weight_decay * weight)


def update(
    first, scal, own, far, mix, mix_far, beside, momenta, native_momenta, native, before=(), after=(), n=128
):
    chunks = own.shape[0]
    block = pl.BlockSpec((2, 8 * n, 128), lambda k, i: (first + k, i, 0))
    piece = pl.BlockSpec((1, 2 * n, 256), lambda k, i: (k, i, 0))
    factor = pl.BlockSpec((1, 2 * HD, 256), lambda k, i: (k, 0, 0))
    pieces, factors = [piece, None, piece, None], [factor, None, factor, None]
    for r in (0, 1):
        pieces[2 * r + 1] = pl.BlockSpec((1, 1, 2 * n, 256), lambda k, i, r=r: (r, k, i, 0))
        factors[2 * r + 1] = pl.BlockSpec((1, 1, 2 * HD, 256), lambda k, i, r=r: (r, k, 4, 0))
    grads, mixes = [own, beside, far, beside], [mix, beside, mix_far, beside]
    return launch(
        functools.partial(update_kernel, n, first == 0),
        [scal, *grads, *mixes, momenta, native_view(native_momenta), native_view(native), *before],
        [jax.ShapeDtypeStruct((6, 2048, 128), jnp.float32)] * 3,
        "update",
        specs=[mem(pltpu.SMEM)]
        + pieces
        + factors
        + [pl.BlockSpec((4, 2 * n, 256), lambda k, i: (k, i, 0)), block, block]
        + [mem(pl.ANY)] * len(before),
        after=after,
        vmem=32,
        cost=0.5 * chunks,
        grid=(chunks, 256 // n),
        out_specs=[block] * 3,
        scratch_shapes=[
            pltpu.VMEM((4, 2, 256, 256), jnp.bfloat16),
            pltpu.VMEM((8, 2 * n, 128), jnp.float32),
            pltpu.VMEM((8, 2 * n, 128), jnp.float32),
            pltpu.VMEM((2, 8 * n, 128), jnp.float32),
        ],
        input_output_aliases={12 + i: i for i in range(len(before))},
    )


def whole_device(
    inputs, cotangent, matrices, momenta, small, small_first, small_second, segments, positions
):
    blk_at = lax.axis_index("blk")
    ctx_at = lax.axis_index("ctx")
    tp_at = lax.axis_index("tp")
    scal = jnp.stack([blk_at, ctx_at, tp_at]).astype(jnp.int32)
    sequences, local_rows, width = inputs.shape
    tokens = sequences * local_rows
    both = ("blk", "ctx")
    f32, bf16 = jnp.float32, jnp.bfloat16
    shaped = jax.ShapeDtypeStruct

    def hop(values, by):
        return lax.ppermute(values, both, [(i, i ^ by) for i in range(8)])

    def hop_tp(values, by):
        return lax.ppermute(values, "tp", [(i, i ^ by) for i in range(4)])

    def tied(values, *results):
        return lax.optimization_barrier((values, *results))[0]

    def spread(piece):
        c = hop(piece, 2)
        return [piece, hop(piece, 1), c, hop(c, 1)]

    x = inputs.reshape(tokens, width)
    cot = cotangent.reshape(tokens, width)
    norms = small[: 4 * width].reshape(4, width)
    qkv_start = 6 * width + tp_at * 4 * 3 * HD
    qkv_bias = lax.dynamic_slice_in_dim(small, qkv_start, 4 * 3 * HD).reshape(4, 3 * HD)
    qkv_bias = jnp.pad(qkv_bias, ((0, 0), (0, HD)))
    unit_start = 6 * width + H * 3 * HD + tp_at * 1024
    unit_bias = lax.dynamic_slice_in_dim(small, unit_start, 1024).reshape(4, 256)
    lane = jnp.arange(128) % HD
    frequency = rope_base ** (-2.0 * (lane % 8).astype(f32) / ROTARY)
    angles = positions.astype(f32).reshape(tokens, 1) * frequency
    cosine = jnp.where(lane < ROTARY, jnp.cos(angles), 1.0)
    sign = jnp.where(lane < 8, -1.0, jnp.where(lane < ROTARY, 1.0, 0.0))
    sine = jnp.sin(angles) * sign

    head_weights, mine = relayout(scal, matrices, bf16, 0, 1, mine=True)
    first_hop = hop(mine, 4)
    unit_weights, mine_units = relayout(scal, matrices, bf16, 1, 2, mine=True, after=(mine,))
    first_hop = tied(first_hop, mine_units)
    other_heads = spread(first_hop)
    units_near = hop(tied(mine_units, first_hop), 4)
    x_beside = hop(x, 1)
    cot_beside = hop(cot, 1)

    send = launch(
        project_kernel,
        [scal, x, cot, norms, qkv_bias, cosine, sine, head_weights]
        + [piece[0] for piece in other_heads],
        shaped((8, local_rows, 256), bf16),
        "project",
    )
    arrived = lax.all_to_all(send, both, split_axis=0, concat_axis=0, tiled=True)
    (piled_heads,) = relayout(scal, momenta, f32, 0, 1, after=(send,))
    units_near = tied(units_near, send)
    units_far = hop(units_near, 2)
    units_beside = hop(units_near, 1)
    documents = lax.dynamic_index_in_dim(segments, blk_at, 0, keepdims=False)
    length = documents.shape[0]
    attended = launch(
        attention_kernel,
        [arrived.reshape(length, 256), documents.reshape(length, 1)],
        shaped((length, 256), bf16),
        "attention",
        cost=6,
        specs=[full(arrived.reshape(length, 256)), pl.BlockSpec((length, 1), lambda *_: (0, 0))],
        after=(piled_heads,),
        scratch_shapes=[pltpu.VMEM((length, HD), f32)] * 2,
    )
    back = lax.all_to_all(
        attended.reshape(8, local_rows, 256), both, split_axis=0, concat_axis=0, tiled=True
    )

    units_far = tied(units_far, attended)
    other_units = [units_near, units_beside, units_far, hop(units_far, 1)]
    ff_branch, ff_part, unit_keep, unit_send, unit_sums, norm_two, cot_sums = launch(
        feed_forward_kernel,
        [scal, x, cot, norms, unit_bias, unit_weights, *other_units],
        [
            shaped((tokens, width), f32),
            shaped((tokens, width), f32),
            shaped((2, 2, tokens, 256), bf16),
            shaped((2, 2, tokens, 256), bf16),
            shaped((4, 256), f32),
            shaped((2, width), f32),
            shaped((1, width), f32),
        ],
        "feed_forward",
        cost=0.3,
        after=(attended,),
    )
    head_keep, head_send, qkv_sums = launch(
        turn_kernel,
        [scal, cosine, sine, back],
        [shaped((2, tokens, 256), bf16)] * 2 + [shaped((4, 256), f32)],
        "turn",
        cost=2,
        after=(unit_sums,),
    )
    in_keep, in_send, down_keep, down_send = launch(
        unit_grads_kernel,
        [scal, x, x_beside, cot, cot_beside, norms, unit_keep, hop(unit_send, 1)],
        [shaped((2, 512, 256), bf16)] * 4,
        "unit_grads",
        cost=3.5,
        after=(qkv_sums,),
    )
    sums = [norm_two, cot_sums, unit_sums, qkv_sums]
    near, far, totals = launch(
        gather_kernel,
        [scal, x, norms, head_keep, head_send, head_weights, *other_heads, ff_branch, ff_part, *sums],
        [shaped((2, 2, 64, width), bf16)] * 2 + [shaped((8, 8, 256), f32)],
        "gather",
        after=(in_keep,),
        scratch_shapes=[pltpu.VMEM((4, 2, 64, width), bf16)],
    )
    a_keep, a_send, b_keep, b_send = launch(
        head_grads_kernel,
        [scal, x, x_beside, cot, cot_beside, norms, head_keep, hop(head_send, 1), totals],
        [shaped((2, 384, 256), bf16)] * 2 + [shaped((2, 256, 256), bf16)] * 2,
        "head_grads",
        cost=4,
    )
    (piled_units,) = relayout(scal, momenta, f32, 1, 2, after=(a_keep,))
    came = hop_tp(far, 1)
    a_came, b_came = hop(a_send, 4), hop(b_send, 2)
    operands = [in_keep, hop(in_send, 4), down_keep, hop(down_send, 2)]
    own, in_send, down_send = launch(
        combine_kernel,
        operands,
        [shaped((2, 512, 256), bf16)] + [shaped((1, 512, 256), bf16)] * 2,
        "combine",
        specs=[full(a) for a in operands],
        cost=2,
        after=(piled_units,),
    )
    in_came, down_came = hop(in_send, 2), hop(down_send, 4)
    kept, passed = launch(
        add_kernel,
        [near, came],
        [shaped((2, 64, width), bf16)] * 2,
        "add",
        specs=[full(near)] * 2,
        after=(in_send,),
    )
    passed = hop_tp(passed, 2)
    operands = [a_keep, a_came, b_keep, b_came]
    a_own, a_send, b_own, b_send = launch(
        combine_heads_kernel,
        operands,
        [shaped((384, 256), bf16)] * 2 + [shaped((256, 256), bf16)] * 2,
        "combine_heads",
        specs=[full(a) for a in operands],
        after=(kept,),
    )
    a_came, b_came = hop(a_send, 2), hop(b_send, 4)
    unit_sum, unit_grams, total = gram_of(
        unit_gram_kernel,
        own,
        [in_came, down_came],
        piled_units,
        scal,
        [kept, passed],
        [shaped((2, 64, width), bf16)],
        after=(a_own,),
    )
    unit_theirs = hop(unit_grams, 4)
    unit_far = hop(unit_sum, 2)
    total_far = hop_tp(total, 2)
    head_sum, head_grams, totals = gram_of(
        head_gram_kernel,
        a_own,
        [a_came, b_own, b_came],
        piled_heads,
        scal,
        [],
        [shaped((8, 8, 256), f32)],
        after=(unit_sum,),
    )
    head_theirs = hop(head_grams, 4)
    head_far = hop(head_sum, 2)
    (unit_mix,) = newton(unit_grams, unit_theirs, [], after=(head_sum,))
    unit_mix_far = hop(unit_mix, 2)
    head_mix, totals = newton(
        head_grams,
        head_theirs,
        [(totals, hop(totals, 1))],
        after=(unit_mix, unit_far, total_far),
    )
    head_mix_far = hop(head_mix, 2)

    def to_beside(*pieces):
        return hop(jnp.stack([jnp.concatenate(pair, axis=1) for pair in pieces]), 1)

    beside = to_beside((unit_sum, unit_mix), (unit_far, tied(unit_mix_far, head_mix)))
    totals_came = hop_tp(totals, 1)
    before = update(
        1, scal, unit_sum, unit_far, unit_mix, unit_mix_far, beside, piled_units, momenta, matrices,
        after=(head_mix, totals_came),
    )
    head_far, head_mix_far = tied((head_far, head_mix_far), before[0])
    beside = to_beside((head_sum, head_mix), (head_far, head_mix_far))
    outs = update(
        0, scal, head_sum, head_far, head_mix, head_mix_far, beside, piled_heads, momenta, matrices,
        before,
    )
    total_beside = hop_tp(tied(jnp.stack([total, total_far]), head_mix), 1)
    totals = totals + totals_came
    totals = totals + tied(hop_tp(totals, 2), outs[0])

    block_output, input_grad = launch(
        finish_rows_kernel,
        [
            scal,
            x.reshape(4, 64, width),
            cot.reshape(4, 64, width),
            (small[4 * width : 5 * width] + small[5 * width : 6 * width]).reshape(1, width),
            total,
            total_far,
            total_beside,
        ],
        [shaped((4, 64, width), f32)] * 2,
        "finish_rows",
        cost=2,
        after=(outs[0], totals),
    )

    cot_total = totals[2, :4].reshape(-1) * 0.25
    small_grads = jnp.concatenate(
        [
            totals[:2].reshape(-1),
            cot_total,
            cot_total,
            totals[3:7, :4, : 3 * HD].reshape(-1),
            totals[3:7, 4:].reshape(-1),
        ]
    )
    return (
        block_output.reshape(inputs.shape),
        input_grad.reshape(inputs.shape),
        native_back(outs[0]),
        native_back(outs[1]),
        native_back(outs[2]),
        small_grads,
        *small_step(small, small_first, small_second, small_grads),
    )


def small_step(small, small_first, small_second, small_grads):
    new_first = adam_first * small_first + (1.0 - adam_first) * small_grads
    new_second = adam_second * small_second + (1.0 - adam_second) * small_grads * small_grads
    corrected = new_first / (1.0 - adam_first**STEP)
    spread = jnp.sqrt(new_second / (1.0 - adam_second**STEP))
    new_small = small - small_rate * corrected / (spread + adam_epsilon)
    return new_first, new_second, new_small


def solution(mesh):
    in_specs = (
        P(None, ("blk", "ctx"), None),
        P(None, ("blk", "ctx"), None),
        P("tp", "blk"),
        P("tp", "blk"),
        P(),
        P(),
        P(),
        P(),
        P(None, ("blk", "ctx")),
    )
    out_specs = (
        P(None, ("blk", "ctx"), None),
        P(None, ("blk", "ctx"), None),
        P("tp", "blk"),
        P("tp", "blk"),
        P("tp", "blk"),
        P(),
        P(),
        P(),
        P(),
    )
    one_each = mesh.shape["blk"] == SEQS and mesh.shape["ctx"] * mesh.shape["tp"] == H
    one_each = one_each and mesh.shape["tp"] == 4
    return jax.shard_map(
        whole_device if one_each else on_device, mesh=mesh, in_specs=in_specs, out_specs=out_specs, check_vma=False
    )
```

```python
import functools

import jax
import jax.numpy as jnp
from jax import lax
from jax.experimental import pallas as pl
from jax.experimental.pallas import tpu as pltpu
from jax.sharding import PartitionSpec as P

MODEL_DIM = 1024
H = 16
HD = 64
FF = 4096
ROTARY = 16
NEWTON = 5
STEP = 10
SEQS = 2


norm_epsilon = 1e-05
rope_base = 10000.0
masked_score = -1e30
momentum_decay = 0.95
muon_rate = 0.2
weight_decay = 0.01
muon_epsilon = 1e-07
quintic = (3.4445, -4.775, 2.0315)
adam_first = 0.9
adam_second = 0.95
adam_epsilon = 1e-08
small_rate = 0.2


def passed_along(x, axis, by):
    devices = lax.axis_size(axis)
    pairs = [(i, i + by) for i in range(devices) if 0 <= i + by < devices]
    return lax.ppermute(x, axis, pairs)


def shifted(x, axis, by):
    devices = lax.axis_size(axis)
    return lax.ppermute(x, axis, [(i, (i + by) % devices) for i in range(devices)])


def as_sent(x):

    def short(part):
        return part.astype(jnp.bfloat16) if part.dtype == jnp.float32 else part

    return jax.tree.map(short, x)


def layer_norm(values, scaling, offset):
    centre = jnp.mean(values, axis=-1, keepdims=True)
    centred = values - centre
    spread = jnp.mean(centred * centred, axis=-1, keepdims=True)
    return centred * lax.rsqrt(spread + norm_epsilon) * scaling + offset


def rope_tables(positions):
    halfway = ROTARY // 2
    frequency = rope_base ** (-2.0 * jnp.arange(halfway, dtype=jnp.float32) / ROTARY)
    angles = positions.astype(jnp.float32)[..., None] * frequency
    return (jnp.cos(angles)[:, :, None, :], jnp.sin(angles)[:, :, None, :])


def rotate(values, cosine, sine):
    halfway = ROTARY // 2
    former = values[..., :halfway]
    latter = values[..., halfway:ROTARY]
    return jnp.concatenate(
        [former * cosine - latter * sine, latter * cosine + former * sine, values[..., ROTARY:]],
        axis=-1,
    )


def exact_gelu(values):
    return jax.nn.gelu(values, approximate=False)


def newton_schulz(blocks):
    frobenius = jnp.sqrt(jnp.sum(blocks * blocks, axis=(1, 2), keepdims=True))
    current = blocks / (frobenius + muon_epsilon)
    linear_term, square_term, cubic_term = quintic
    for iteration in range(NEWTON):
        gram_matrix = jnp.einsum("mde,mdf->mef", current, current, precision=lax.Precision.HIGHEST)
        polynomial = square_term * gram_matrix + cubic_term * jnp.einsum(
            "mef,mfg->meg", gram_matrix, gram_matrix, precision=lax.Precision.HIGHEST
        )
        current = linear_term * current + jnp.einsum(
            "mde,mef->mdf", current, polynomial, precision=lax.Precision.HIGHEST
        )
    return current


def to_heads(values):
    return lax.all_to_all(values, "ctx", split_axis=3, concat_axis=1, tiled=True)


def to_positions(values):
    return lax.all_to_all(values, "ctx", split_axis=1, concat_axis=3, tiled=True)


def pass_keys(pair):
    return passed_along(pair, "blk", 1)


def pass_grads(pair_grad):
    return shifted(pair_grad.astype(jnp.bfloat16), "blk", 1).astype(pair_grad.dtype)


def allowed_pairs(segments, query_block, key_block, block_rows):
    query_place = query_block * block_rows + jnp.arange(block_rows, dtype=jnp.int32)
    key_place = key_block * block_rows + jnp.arange(block_rows, dtype=jnp.int32)
    query_doc = lax.dynamic_slice_in_dim(segments, query_block * block_rows, block_rows, 1)
    key_doc = lax.dynamic_slice_in_dim(segments, key_block * block_rows, block_rows, 1)
    causal = key_place[None, :] <= query_place[:, None]
    return (causal[None] & (query_doc[:, :, None] == key_doc[:, None, :]))[:, None]


def masked_scores(queries, keys, allowed):
    score_scale = HD ** (-0.5)
    scores = (
        jnp.einsum("sqhe,skhe->shqk", queries, keys, preferred_element_type=jnp.float32)
        * score_scale
    )
    return jnp.where(allowed, scores, masked_score)


def on_device(
    inputs, cotangent, matrices, momenta, small, small_first, small_second, segments, positions
):
    tensor_size = lax.axis_size("tp")
    cycle_size = lax.axis_size("blk")
    context_size = lax.axis_size("ctx")
    tensor_index = lax.axis_index("tp")
    cycle_index = lax.axis_index("blk")
    sequences, local_rows, model_width = inputs.shape
    per_group = matrices.shape[0]
    head_count = H // tensor_size
    unit_blocks = FF // HD // tensor_size
    block_rows = local_rows * context_size
    gathered = lax.all_gather(matrices.astype(jnp.bfloat16), "blk", axis=1, tiled=True).reshape(
        per_group, model_width, HD
    )
    query_key_value_weight = gathered[: 3 * head_count]
    projection_out_weight = gathered[3 * head_count : 4 * head_count]
    input_weight = gathered[4 * head_count : 4 * head_count + unit_blocks]
    down_projection_weight = gathered[4 * head_count + unit_blocks :]
    qkv_start = 6 * model_width + tensor_index * head_count * 3 * HD
    query_key_value_bias = lax.dynamic_slice_in_dim(small, qkv_start, head_count * 3 * HD).reshape(
        head_count, 3, HD
    )
    unit_start = 6 * model_width + H * 3 * HD + tensor_index * unit_blocks * HD
    hidden_unit_bias = lax.dynamic_slice_in_dim(small, unit_start, unit_blocks * HD).reshape(
        unit_blocks, HD
    )
    residual = inputs.astype(jnp.float32)

    def both_norms(values, gain_one, offset_one, gain_two, offset_two):
        return (layer_norm(values, gain_one, offset_one), layer_norm(values, gain_two, offset_two))

    (normed_one, normed_two), norm_back = jax.vjp(
        both_norms,
        residual,
        small[0:model_width],
        small[model_width : 2 * model_width],
        small[2 * model_width : 3 * model_width],
        small[3 * model_width : 4 * model_width],
    )
    first_input = normed_one.astype(jnp.bfloat16)
    second_input = normed_two.astype(jnp.bfloat16)
    projected = jnp.einsum(
        "pgk,jka->pgja", first_input, query_key_value_weight, preferred_element_type=jnp.float32
    )
    projected = projected.reshape(sequences, local_rows, 3, head_count, HD) + jnp.transpose(
        query_key_value_bias, (1, 0, 2)
    )
    cosine, sine = rope_tables(positions)

    def turn_pair(query_pre, key_pre):
        return (rotate(query_pre, cosine, sine), rotate(key_pre, cosine, sine))

    (query_turned, key_turned), turn_back = jax.vjp(
        turn_pair, projected[:, :, 0], projected[:, :, 1]
    )
    stacked = jnp.stack([query_turned, key_turned, projected[:, :, 2]], axis=2).astype(jnp.bfloat16)
    by_heads = to_heads(stacked)
    queries = by_heads[:, :, 0]
    head_local = queries.shape[2]

    def forward_visit(state, pair, source):
        row_max, row_total, weighted = state
        allowed = allowed_pairs(segments, cycle_index, source, block_rows)
        scores = masked_scores(queries, pair[:, :, 0], allowed)
        new_max = jnp.maximum(row_max, jnp.max(scores, axis=-1))
        weights = jnp.where(allowed, jnp.exp(scores - new_max[..., None]), 0.0)
        rescale = jnp.exp(row_max - new_max)
        row_total = row_total * rescale + jnp.sum(weights, axis=-1)
        weighted = weighted * rescale[..., None] + jnp.einsum(
            "shqk,skhe->shqe",
            weights.astype(jnp.bfloat16),
            pair[:, :, 1],
            preferred_element_type=jnp.float32,
        )
        return (new_max, row_total, weighted)

    def forward_hop(hop_index, carry):
        pair, state = carry
        source = (cycle_index - hop_index) % cycle_size
        state = forward_visit(state, pair, source)
        return (pass_keys(pair), state)

    start_state = (
        jnp.full((sequences, head_local, block_rows), masked_score, jnp.float32),
        jnp.zeros((sequences, head_local, block_rows), jnp.float32),
        jnp.zeros((sequences, head_local, block_rows, HD), jnp.float32),
    )
    pair, state = lax.fori_loop(0, cycle_size - 1, forward_hop, (by_heads[:, :, 1:], start_state))
    row_max, row_total, weighted = forward_visit(state, pair, (cycle_index + 1) % cycle_size)
    log_total = row_max + jnp.log(row_total)
    attended_rows = jnp.transpose(weighted / row_total[..., None], (0, 2, 1, 3))
    attention_result = to_positions(attended_rows.astype(jnp.bfloat16)[:, :, None])[:, :, 0]
    attention_branch = jnp.einsum(
        "roxu,xcu->roc", attention_result, projection_out_weight, preferred_element_type=jnp.float32
    )
    hidden_preactivation = (
        jnp.einsum("ptr,kra->ptka", second_input, input_weight, preferred_element_type=jnp.float32)
        + hidden_unit_bias
    )
    activated_hidden, gelu_back = jax.vjp(exact_gelu, hidden_preactivation)
    activated_reduced = activated_hidden.astype(jnp.bfloat16)
    perceptron_branch = jnp.einsum(
        "xkzp,zop->xko",
        activated_reduced,
        down_projection_weight,
        preferred_element_type=jnp.float32,
    )
    branches = lax.psum((attention_branch + perceptron_branch).astype(jnp.bfloat16), "tp").astype(
        jnp.float32
    )
    block_output = (
        residual
        + branches
        + small[4 * model_width : 5 * model_width]
        + small[5 * model_width : 6 * model_width]
    )
    act_grad = jnp.einsum(
        "ptr,kra->ptka", cotangent, down_projection_weight, preferred_element_type=jnp.float32
    )
    hidden_gradient = gelu_back(act_grad)[0].astype(jnp.bfloat16)
    down_grad = jnp.einsum(
        "gup,guzb->zpb", cotangent, activated_reduced, preferred_element_type=jnp.float32
    )
    in_grad = jnp.einsum(
        "gup,guzb->zpb", second_input, hidden_gradient, preferred_element_type=jnp.float32
    )
    second_grad = jnp.einsum(
        "xkzp,zop->xko", hidden_gradient, input_weight, preferred_element_type=jnp.float32
    )
    attended_grad = jnp.einsum(
        "pgk,jka->pgja", cotangent, projection_out_weight, preferred_element_type=jnp.float32
    ).astype(jnp.bfloat16)
    outproj_grad = jnp.einsum(
        "ztu,ztqi->qui", cotangent, attention_result, preferred_element_type=jnp.float32
    )
    grad_heads = to_heads(attended_grad[:, :, None])[:, :, 0]
    row_delta = jnp.transpose(
        jnp.sum(grad_heads.astype(jnp.float32) * attended_rows, axis=-1), (0, 2, 1)
    )

    def backward_visit(query_grad, pair, source):
        allowed = allowed_pairs(segments, cycle_index, source, block_rows)
        scores = masked_scores(queries, pair[:, :, 0], allowed)
        probabilities = jnp.where(allowed, jnp.exp(scores - log_total[..., None]), 0.0)
        value_grad = jnp.einsum(
            "shqk,sqhe->skhe",
            probabilities.astype(jnp.bfloat16),
            grad_heads,
            preferred_element_type=jnp.float32,
        )
        prob_grad = jnp.einsum(
            "sqhe,skhe->shqk", grad_heads, pair[:, :, 1], preferred_element_type=jnp.float32
        )
        score_grad = (probabilities * (prob_grad - row_delta[..., None])).astype(jnp.bfloat16)
        score_scale = HD ** (-0.5)
        query_grad = (
            query_grad
            + jnp.einsum(
                "shqk,skhe->sqhe", score_grad, pair[:, :, 0], preferred_element_type=jnp.float32
            )
            * score_scale
        )
        key_grad = (
            jnp.einsum("shqk,sqhe->skhe", score_grad, queries, preferred_element_type=jnp.float32)
            * score_scale
        )
        return (query_grad, jnp.stack([key_grad, value_grad], axis=2))

    def backward_hop(hop_index, carry):
        pair, pair_grad, query_grad = carry
        source = (cycle_index - hop_index) % cycle_size
        query_grad, visit_grad = backward_visit(query_grad, pair, source)
        return (pass_keys(pair), pass_grads(pair_grad + visit_grad), query_grad)

    zero_pair = jnp.zeros(by_heads[:, :, 1:].shape, jnp.float32)
    pair, pair_grad, query_grad = lax.fori_loop(
        0,
        cycle_size - 1,
        backward_hop,
        (by_heads[:, :, 1:], zero_pair, jnp.zeros(queries.shape, jnp.float32)),
    )
    query_grad, visit_grad = backward_visit(query_grad, pair, (cycle_index + 1) % cycle_size)
    pair_grad = pass_grads(pair_grad + visit_grad)
    head_grads = jnp.concatenate([query_grad[:, :, None], pair_grad], axis=2).astype(jnp.bfloat16)
    position_grads = to_positions(head_grads).astype(jnp.float32)
    query_pre_grad, key_pre_grad = turn_back((position_grads[:, :, 0], position_grads[:, :, 1]))
    projected_grad = jnp.stack(
        [query_pre_grad, key_pre_grad, position_grads[:, :, 2]], axis=2
    ).astype(jnp.bfloat16)
    flattened_gradient = projected_grad.reshape(sequences, local_rows, 3 * head_count, HD)
    query_key_value_gradient = jnp.einsum(
        "ztu,ztqi->qui", first_input, flattened_gradient, preferred_element_type=jnp.float32
    )
    first_grad = jnp.einsum(
        "roxu,xcu->roc",
        flattened_gradient,
        query_key_value_weight,
        preferred_element_type=jnp.float32,
    )
    input_part, gain_one_grad, offset_one_grad, gain_two_grad, offset_two_grad = norm_back(
        (first_grad, second_grad)
    )
    input_grad = cotangent.astype(jnp.float32) + lax.psum(
        input_part.astype(jnp.bfloat16), "tp"
    ).astype(jnp.float32)
    owner_share = jnp.where(tensor_index == 0, 1.0, 0.0).astype(jnp.float32)
    bias_grad = jnp.sum(cotangent.astype(jnp.float32), axis=(0, 1)) * owner_share
    qkv_bias_grad = jnp.transpose(
        jnp.sum(projected_grad.astype(jnp.float32), axis=(0, 1)), (1, 0, 2)
    ).reshape(-1)
    unit_bias_grad = jnp.sum(hidden_gradient.astype(jnp.float32), axis=(0, 1)).reshape(-1)
    local_small = jnp.concatenate(
        [
            gain_one_grad,
            offset_one_grad,
            gain_two_grad,
            offset_two_grad,
            bias_grad,
            bias_grad,
            jnp.zeros((small.shape[0] - 6 * model_width,), jnp.float32),
        ]
    )
    local_small = lax.dynamic_update_slice_in_dim(local_small, qkv_bias_grad, qkv_start, 0)
    local_small = lax.dynamic_update_slice_in_dim(local_small, unit_bias_grad, unit_start, 0)
    small_grads = lax.psum(local_small, ("blk", "ctx", "tp"))
    local_grad = jnp.concatenate(
        [query_key_value_gradient, outproj_grad, in_grad, down_grad], axis=0
    ).reshape(per_group, -1)
    shares = lax.psum_scatter(
        local_grad.astype(jnp.bfloat16), "blk", scatter_dimension=1, tiled=True
    )
    matrix_grads = lax.psum(shares, "ctx").astype(jnp.float32)
    new_momenta = momentum_decay * momenta + matrix_grads
    update = matrix_grads + momentum_decay * new_momenta
    per_owner = per_group // cycle_size
    sectioned = update.reshape(cycle_size, per_owner, update.shape[1])
    pieces = lax.all_to_all(
        sectioned.astype(jnp.bfloat16), "blk", split_axis=0, concat_axis=2, tiled=True
    ).astype(sectioned.dtype)
    piece_count = pieces.shape[1]
    settled_blocks = newton_schulz(pieces.reshape(piece_count, MODEL_DIM, HD)).reshape(
        1, piece_count, MODEL_DIM * HD
    )
    settled = lax.all_to_all(
        as_sent(settled_blocks), "blk", split_axis=2, concat_axis=0, tiled=True
    ).astype(settled_blocks.dtype)
    orthogonal_all = settled.reshape(per_group, -1)
    muon_scale = max(1.0, MODEL_DIM / HD) ** 0.5
    new_matrices = matrices - muon_rate * (muon_scale * orthogonal_all + weight_decay * matrices)
    new_first = adam_first * small_first + (1.0 - adam_first) * small_grads
    new_second = adam_second * small_second + (1.0 - adam_second) * small_grads * small_grads
    corrected = new_first / (1.0 - adam_first**STEP)
    spread = jnp.sqrt(new_second / (1.0 - adam_second**STEP))
    new_small = small - small_rate * corrected / (spread + adam_epsilon)
    return (
        block_output,
        input_grad,
        matrix_grads,
        new_matrices,
        new_momenta,
        small_grads,
        new_first,
        new_second,
        new_small,
    )


def native_view(array):
    rows, columns = array.shape
    tiled = array.reshape(rows // 8, 8, columns // 128, 128).transpose(0, 2, 1, 3)
    return tiled.reshape(rows // 8, columns // 16, 128)


def native_back(array):
    groups, rows, _ = array.shape
    return array.reshape(groups, rows // 8, 8, 128).transpose(0, 2, 1, 3).reshape(groups * 8, rows * 16)


def members_of(head):
    if head:
        return lambda piece, j: (j // 2, 4 * (j % 2) + piece)
    return lambda piece, j: (piece // 2, 4 * (piece % 2) + j)


def mem(kind=pltpu.VMEM):
    return pl.BlockSpec(memory_space=kind)


def limits(mebibytes):
    return pltpu.CompilerParams(vmem_limit_bytes=mebibytes << 20)


def low_lanes(rows):
    return lax.broadcasted_iota(jnp.int32, (rows, 128), 1) < HD


def dot(a, b, dims=((1,), (0,)), precision=None):
    return lax.dot_general(
        a, b, (dims, ((), ())), precision=precision, preferred_element_type=jnp.float32
    )


NT = ((1,), (1,))
TN = ((0,), (0,))


def corner(array):
    block = (1,) * (array.ndim - 2) + (min(16, array.shape[-2]), 128)
    return pl.BlockSpec(block, lambda *_: (0,) * array.ndim)


def takes(microseconds):
    return pl.CostEstimate(
        flops=int(microseconds * 1.15e9), transcendentals=0, bytes_accessed=int(1e6)
    )


def in_hbm(array):
    if array.size * array.dtype.itemsize < 1 << 21:
        return array
    return pltpu.with_memory_space_constraint(array, pltpu.HBM)


def out_hbm(shape):
    if shape.size * shape.dtype.itemsize < 1 << 20:
        return shape
    return pltpu.HBM(shape.shape, shape.dtype)


def full(array):
    return pl.BlockSpec(array.shape, lambda *_: (0,) * array.ndim)


def launch(kernel, operands, out_shapes, name, specs=None, after=(), vmem=16, cost=3, **more):
    taken = len(operands)
    body = kernel
    if after:
        body = lambda *refs: kernel(*refs[:taken], *refs[taken + len(after) :])
    if specs is None:
        specs = [mem(pltpu.SMEM)] + [full(a) for a in operands[1:]]
    if "out_specs" not in more:
        more["out_specs"] = jax.tree.map(full, out_shapes)
    more.setdefault("grid", (1,))
    return pl.pallas_call(
        body,
        in_specs=list(specs) + [corner(a) for a in after],
        out_shape=jax.tree.map(out_hbm, out_shapes),
        compiler_params=limits(vmem),
        cost_estimate=takes(cost),
        name=name,
        **more,
    )(*map(in_hbm, operands), *map(in_hbm, after))


def relayout_kernel(n, first, count, scal, src, out, *refs):
    fetched, paired, packed, arrivals, departures = refs[-5:]
    low = low_lanes(n)
    place_of = members_of(first == 0)
    steps = [(k, i) for k in range(count) for i in range(256 // n)]

    def fetch(k, i, group):
        rows = pl.ds(i * 8 * n, 8 * n)
        return pltpu.make_async_copy(
            src.at[2 * first + 2 * k + group, rows],
            fetched.at[2 * k + group, rows],
            arrivals.at[2 * k + group, i],
        )

    def leave(k, i):
        rows = pl.ds(i * 2 * n, 2 * n)
        return pltpu.make_async_copy(
            packed.at[pl.ds(4 * k, 4), rows], out.at[pl.ds(4 * k, 4), rows], departures.at[k, i]
        )

    for k, i in steps:
        for group in range(2):
            fetch(k, i, group).start()
    for k, i in steps:
        for group in range(2):
            fetch(k, i, group).wait()
        for piece in range(4):
            for half in range(2):
                pair = []
                for j in (2 * half, 2 * half + 1):
                    group, line = place_of(piece, j)
                    rows = pl.ds(i * 8 * n + line, n, stride=8)
                    pair.append(fetched[2 * k + group, rows, :])
                a, b = pair
                at = 2 * piece + half
                paired[at, pl.ds(0, n, stride=2), :] = jnp.where(low, a, pltpu.roll(b, 64, 1))
                paired[at, pl.ds(1, n, stride=2), :] = jnp.where(low, pltpu.roll(a, 64, 1), b)
                lanes = slice(half * 128, (half + 1) * 128)
                rows = slice(i * 2 * n, (i + 1) * 2 * n)
                packed[4 * k + piece, rows, lanes] = paired[at].astype(packed.dtype)
        leave(k, i).start()
    if len(refs) == 6:
        for k in range(count):
            refs[0][k] = packed[4 * k + scal[1]]
    for k, i in steps:
        leave(k, i).wait()


def relayout(scal, array, dtype, first, count, mine=False, n=128, after=()):
    shapes = [jax.ShapeDtypeStruct((4 * count, 512, 256), dtype)]
    specs = [mem(pl.ANY)]
    if mine:
        shapes.append(jax.ShapeDtypeStruct((count, 512, 256), dtype))
        specs.append(full(shapes[1]))
    return launch(
        functools.partial(relayout_kernel, n, first, count),
        [scal, native_view(array)],
        shapes,
        "relayout",
        specs=[mem(pltpu.SMEM), mem(pl.ANY)],
        after=after,
        cost=0.2 * count,
        vmem=14,
        out_specs=specs,
        scratch_shapes=[
            pltpu.VMEM((2 * count, 2048, 128), jnp.float32),
            pltpu.VMEM((8, 2 * n, 128), jnp.float32),
            pltpu.VMEM((4 * count, 512, 256), dtype),
            pltpu.SemaphoreType.DMA((2 * count, 256 // n)),
            pltpu.SemaphoreType.DMA((count, 256 // n)),
        ],
    )


def add_up(groups):
    for parts, target in groups:
        values = [part[...].astype(jnp.float32) for part in parts]
        while len(values) > 1:
            values = [sum(values[i : i + 2]) for i in range(0, len(values), 2)]
        if isinstance(target, list):
            for i, part in enumerate(target):
                part[...] = values[0][i].astype(part.dtype)
        else:
            target[...] = values[0].astype(target.dtype)


def grouped(refs, counts, targets):
    refs = iter(refs)
    return [([next(refs) for _ in range(n)], target) for n, target in zip(counts, targets)]


def normalized(x):
    centred = x - jnp.mean(x, axis=-1, keepdims=True)
    spread = jnp.mean(centred * centred, axis=-1, keepdims=True)
    root = lax.rsqrt(spread + norm_epsilon)
    return centred * root, root


def halves(values, first):
    left, right = values[:, :512], values[:, 512:]
    return jnp.where(first, left, right), jnp.where(first, right, left)


def whole(own, other, first):
    return jnp.concatenate([jnp.where(first, own, other), jnp.where(first, other, own)], axis=1)


def norm_back(grad, hat, root, gain):
    scaled = grad * gain
    along = jnp.mean(scaled * hat, axis=-1, keepdims=True)
    return root * (scaled - jnp.mean(scaled, axis=-1, keepdims=True) - hat * along)


def turned(values, cosine, sine):
    lane = lax.broadcasted_iota(jnp.int32, values.shape, 1) % HD
    other = jnp.where(lane < 8, pltpu.roll(values, 120, 1), pltpu.roll(values, 8, 1))
    return values * cosine + other * sine


def project_kernel(scal, x, cot, norms, bias, cosine, sine, own, r0, r1, r2, r3, send):
    first = scal[0] == 0
    hat, _ = normalized(x[...].astype(jnp.float32))
    h = (hat * norms[0:1] + norms[1:2]).astype(jnp.bfloat16)
    h_own, h_other = halves(h, first)
    c_own, c_other = halves(cot[...], first)
    tokens = h.shape[0]
    low = low_lanes(tokens)
    for r, other in enumerate((r0, r1, r2, r3)):
        head = scal[1] ^ r
        mine = own[head]
        theirs = other[...]
        pre = dot(h_own, mine) + dot(h_other, theirs) + bias[pl.ds(head, 1), :]
        back = dot(c_own, mine[:, 128:]) + dot(c_other, theirs[:, 128:])
        left = turned(pre[:, :128], cosine[...], sine[...]).astype(jnp.bfloat16)
        right = jnp.where(low, pre[:, 128:], back).astype(jnp.bfloat16)
        for s in range(2):
            rows = slice(128 * s, 128 * s + 128)
            send[4 * s + head, :, :128] = left[rows]
            send[4 * s + head, :, 128:] = right[rows]


def attention_kernel(rows_ref, seg, out, key_total, value_total):
    key_total[...] = jnp.zeros_like(key_total)
    value_total[...] = jnp.zeros_like(value_total)
    step = 256
    for block in range(rows_ref.shape[0] // step):
        rows = slice(block * step, (block + 1) * step)
        n = (block + 1) * step
        query = rows_ref[rows, 0:HD] * jnp.bfloat16(0.125)
        grad = rows_ref[rows, 3 * HD : 4 * HD]
        keys = rows_ref[0:n, HD : 2 * HD]
        values = rows_ref[0:n, 2 * HD : 3 * HD]
        scores = dot(query, keys, NT)
        query_place = block * step + lax.broadcasted_iota(jnp.int32, (step, n), 0)
        key_place = lax.broadcasted_iota(jnp.int32, (step, n), 1)
        allowed = (key_place <= query_place) & (key_place >= seg[rows, :])
        scores = jnp.where(allowed, scores, masked_score)
        weights = jnp.exp(scores - jnp.max(scores, axis=-1, keepdims=True))
        weights = jnp.where(allowed, weights, 0.0)
        weights = weights * (1.0 / jnp.sum(weights, axis=-1, keepdims=True))
        short = weights.astype(jnp.bfloat16)
        attended = dot(short, values)
        weight_grad = dot(grad, values, NT)
        delta = jnp.sum(weights * weight_grad, axis=-1, keepdims=True)
        score_grad = (weights * (weight_grad - delta)).astype(jnp.bfloat16)
        query_grad = dot(score_grad, keys) * 0.125
        key_total[0:n, :] += dot(score_grad, query, TN)
        value_total[0:n, :] += dot(short, grad, TN)
        out[rows, 0:HD] = query_grad.astype(jnp.bfloat16)
        out[rows, 3 * HD : 4 * HD] = attended.astype(jnp.bfloat16)
    out[:, HD : 2 * HD] = key_total[...].astype(jnp.bfloat16)
    out[:, 2 * HD : 3 * HD] = value_total[...].astype(jnp.bfloat16)


def feed_forward_kernel(
    scal, x, cot, norms, bias, weights, r0, r1, r2, r3,
    branch, input_part, keep, send, hidden_sums, norm_grads, cot_sums,
):
    first = scal[0] == 0
    hat, root = normalized(x[...].astype(jnp.float32))
    h = (hat * norms[2:3] + norms[3:4]).astype(jnp.bfloat16)
    h_own, h_other = halves(h, first)
    c_own, c_other = halves(cot[...], first)
    cot_sums[...] = jnp.sum(cot[...].astype(jnp.float32), axis=0, keepdims=True)
    outs = [0.0] * 4
    for r, other in enumerate((r0, r1, r2, r3)):
        piece = scal[1] ^ r
        in_own, in_other = weights[piece], other[0]
        down_own, down_other = weights[4 + piece], other[1]
        pre = dot(h_own, in_own) + dot(h_other, in_other) + bias[pl.ds(piece, 1), :]
        cumulative = 0.5 * (1.0 + lax.erf(pre * 0.7071067811865476))
        slope = cumulative + pre * (0.3989422804014327 * jnp.exp(-0.5 * pre * pre))
        act = (pre * cumulative).astype(jnp.bfloat16)
        act_grad = dot(c_own, down_own) + dot(c_other, down_other)
        grad = (act_grad * slope).astype(jnp.bfloat16)
        hidden_sums[pl.ds(piece, 1), :] = jnp.sum(
            grad.astype(jnp.float32), axis=0, keepdims=True
        )
        outs[0] += dot(act, down_own, NT)
        outs[1] += dot(act, down_other, NT)
        outs[2] += dot(grad, in_own, NT)
        outs[3] += dot(grad, in_other, NT)
        target = send if r % 2 else keep
        target[r // 2, 0] = grad
        target[r // 2, 1] = act
    branch[...] = whole(outs[0], outs[1], first)
    second = whole(outs[2], outs[3], first)
    norm_grads[0:1] = jnp.sum(second * hat, axis=0, keepdims=True)
    norm_grads[1:2] = jnp.sum(second, axis=0, keepdims=True)
    input_part[...] = norm_back(second, hat, root, norms[2:3])


def both_cores(scal, x, x_beside, cot, cot_beside, norms, at):
    first = scal[0] == 0
    tokens = jnp.concatenate([x[...], x_beside[...]], axis=0).astype(jnp.float32)
    hat, _ = normalized(tokens)
    h = (hat * norms[at : at + 1] + norms[at + 1 : at + 2]).astype(jnp.bfloat16)
    c = jnp.concatenate([cot[...], cot_beside[...]], axis=0)
    return list(zip(halves(h, first), halves(c, first)))


def unit_grads_kernel(
    scal, x, x_beside, cot, cot_beside, norms, keep, came, in_keep, in_send, down_keep, down_send
):
    for side, (h, c) in enumerate(both_cores(scal, x, x_beside, cot, cot_beside, norms, 2)):
        for far in range(2):
            grad = jnp.concatenate([keep[far, 0], came[far, 0]], axis=0)
            act = jnp.concatenate([keep[far, 1], came[far, 1]], axis=0)
            (in_send if side else in_keep)[far] = dot(h, grad, TN).astype(jnp.bfloat16)
            (down_send if far else down_keep)[side] = dot(c, act, TN).astype(jnp.bfloat16)


def combine_kernel(
    in_keep, in_came, down_keep, down_came, totals, totals_came, own, in_send, down_send, totals_sum
):
    add_up([((totals, totals_came), totals_sum)])
    pairs = ((in_keep, in_came, in_send), (down_keep, down_came, down_send))
    for k, (keep, came, send) in enumerate(pairs):
        total = keep[...].astype(jnp.float32) + came[...].astype(jnp.float32)
        own[k] = total[0].astype(jnp.bfloat16)
        send[0] = total[1].astype(jnp.bfloat16)


def turn_kernel(scal, cosine, sine, back, keep, send, sums):
    low = low_lanes(keep.shape[1])
    for r in range(4):
        head = scal[1] ^ r
        grads = jnp.concatenate([back[head], back[4 + head]], axis=0)
        left = turned(grads[:, :128].astype(jnp.float32), cosine[...], -sine[...])
        left = left.astype(jnp.bfloat16)
        right = grads[:, 128:]
        target = send if r % 2 else keep
        target[r // 2, :, :128] = left
        target[r // 2, :, 128:] = right
        right = jnp.where(low, right.astype(jnp.float32), 0.0)
        wide = jnp.concatenate([left.astype(jnp.float32), right], axis=1)
        sums[pl.ds(head, 1), :] = jnp.sum(wide, axis=0, keepdims=True)


def split_last(piece):
    wide = piece.astype(jnp.float32)
    lane = lax.broadcasted_iota(jnp.int32, (1, wide.shape[1]), 1)
    share = (lane < 3 * HD).astype(jnp.float32)
    pre_grad = (wide * share).astype(jnp.bfloat16)
    attended = (wide * (1.0 - share)).astype(jnp.bfloat16)
    return pre_grad, attended


def head_grads_kernel(
    scal, x, x_beside, cot, cot_beside, norms, keep, came, totals, totals_came, *outs
):
    add_up([((totals, totals_came), outs[4])])
    sides = both_cores(scal, x, x_beside, cot, cot_beside, norms, 0)
    a_keep, a_send, b_keep, b_send = outs[:4]
    for far in range(2):
        piece = jnp.concatenate([keep[far], came[far]], axis=0)
        pre_grad, attended = split_last(piece)
        for side, (h, c) in enumerate(sides):
            grad = (dot(h, pre_grad, TN) + dot(c, attended, TN)).astype(jnp.bfloat16)
            (a_send if side else a_keep)[far] = grad[0:256]
            (b_send if far else b_keep)[side] = grad[256:512]


def combine_heads_kernel(
    a_keep, a_came, b_keep, b_came, totals, totals_came, a_own, a_send, b_own, b_send, totals_sum
):
    add_up(
        [
            ((a_keep, a_came), [a_own, a_send]),
            ((b_keep, b_came), [b_own, b_send]),
            ((totals, totals_came), totals_sum),
        ]
    )


def add_kernel(near, came, kept, passed):
    add_up([((near, came), [kept, passed])])


def gather_kernel(
    scal, x, norms, keep, send, weights, r0, r1, r2, r3, ff_branch, ff_part,
    norm_two, cot_sums, unit_sums, qkv_sums, near, far, totals, parts,
):
    first = scal[0] == 0
    hat, root = normalized(x[...].astype(jnp.float32))
    outs = [0.0] * 4
    for r, other in enumerate((r0, r1, r2, r3)):
        mine, theirs = weights[scal[1] ^ r], other[0]
        pre_grad, attended = split_last((send if r % 2 else keep)[r // 2])
        outs[0] += dot(attended, mine, NT)
        outs[1] += dot(attended, theirs, NT)
        outs[2] += dot(pre_grad, mine, NT)
        outs[3] += dot(pre_grad, theirs, NT)
    branch = ff_branch[...] + whole(outs[0], outs[1], first)
    grad = whole(outs[2], outs[3], first)
    totals[...] = jnp.zeros_like(totals)
    rows = [jnp.sum(grad * hat, axis=0, keepdims=True), jnp.sum(grad, axis=0, keepdims=True)]
    rows += [norm_two[0:1], norm_two[1:2], cot_sums[...]]
    for i, row in enumerate(rows):
        for q in range(4):
            at = 4 * (i % 2) + q
            totals[i // 2, at : at + 1, :] = row[:, 256 * q : 256 * q + 256]
    totals[3 + scal[2], 0:4, :] = qkv_sums[...]
    totals[3 + scal[2], 4:8, :] = unit_sums[...]
    input_part = ff_part[...] + norm_back(grad, hat, root, norms[0:1])
    for q in range(4):
        parts[q, 0] = branch[64 * q : 64 * q + 64].astype(jnp.bfloat16)
        parts[q, 1] = input_part[64 * q : 64 * q + 64].astype(jnp.bfloat16)
    for r in range(4):
        (far if r % 2 else near)[r // 2] = parts[scal[2] ^ r]


def finish_rows_kernel(scal, x, cot, bias, r0, r1, r2, r3, block_output, input_grad):
    for r, piece in enumerate((r0, r1, r2, r3)):
        q = scal[2] ^ r
        block_output[q] = x[q].astype(jnp.float32) + piece[0].astype(jnp.float32) + bias[...]
        input_grad[q] = cot[q].astype(jnp.float32) + piece[1].astype(jnp.float32)


def gram_of_piece(total, momenta, grads, grams):
    short = total.astype(jnp.bfloat16)
    grads[0] = short
    update = 1.95 * short.astype(jnp.float32) + 0.9025 * momenta[0]
    gram = dot(update, update, TN, lax.Precision.HIGHEST)
    for j in range(4):
        cut = slice(j * HD, (j + 1) * HD)
        grams[0, j] = gram[cut, cut]


def unit_gram_kernel(place, own, in_came, down_came, momenta, totals, totals_came, *refs):
    grads, grams, totals_sum = refs[-3:]

    @pl.when(pl.program_id(0) == 0)
    def _():
        add_up([((totals, totals_came), totals_sum)])

    a = in_came[0].astype(jnp.float32)
    b = down_came[0].astype(jnp.float32)
    other = jnp.where(pl.program_id(0) == 0, a, b)
    gram_of_piece(own[0].astype(jnp.float32) + other, momenta, grads, grams)


def head_gram_kernel(place, a_own, a_came, b_own, b_came, momenta, *refs):
    grads, grams = refs[-2:]
    a = a_own[...].astype(jnp.float32) + a_came[...].astype(jnp.float32)
    b = b_own[...].astype(jnp.float32) + b_came[...].astype(jnp.float32)
    gram_of_piece(jnp.concatenate([a, b], axis=0), momenta, grads, grams)


def gram_of(kernel, first, others, momenta, place, more, shapes, after=()):
    chunks = momenta.shape[0] // 4
    piece = pl.BlockSpec((1, 512, 256), lambda i, s: (i, 0, 0))
    block = pl.BlockSpec((1, 512, 256), lambda i, s: (4 * i + s[1], 0, 0))
    return pl.pallas_call(
        kernel,
        grid_spec=pltpu.PrefetchScalarGridSpec(
            num_scalar_prefetch=1,
            grid=(chunks,),
            in_specs=[piece if first.ndim == 3 else full(first)]
            + [full(other) for other in others]
            + [block]
            + [full(part) for part in more]
            + [corner(a) for a in after],
            out_specs=[piece, pl.BlockSpec((1, 4, HD, HD), lambda i, s: (i, 0, 0, 0))]
            + [full(shape) for shape in shapes],
        ),
        out_shape=[
            jax.ShapeDtypeStruct((chunks, 512, 256), jnp.bfloat16),
            jax.ShapeDtypeStruct((chunks, 4, HD, HD), jnp.float32),
            *map(out_hbm, shapes),
        ],
        compiler_params=limits(12),
        cost_estimate=takes(2.5),
        name="gram",
    )(place, *map(in_hbm, [first, *others, momenta, *more, *after]))


def newton_kernel(counts, mine, theirs, *refs):
    taken = sum(counts)
    out = refs[taken]
    add_up(grouped(refs, counts, refs[taken + 1 :]))
    linear, square, cubic = quintic
    shape = (HD, HD)
    eye = lax.broadcasted_iota(jnp.int32, shape, 0) == lax.broadcasted_iota(jnp.int32, shape, 1)
    full = lax.Precision.HIGHEST
    chunks = mine.shape[0]
    places = [(i, j) for i in range(chunks) for j in range(4)]
    states = []
    for i, j in places:
        gram = mine[i, j] + theirs[i, j]
        trace = jnp.sum(jnp.where(eye, gram, 0.0), axis=(0, 1), keepdims=True)
        scale = 1.0 / (jnp.sqrt(trace) + muon_epsilon)
        states.append([gram * scale * scale, None, scale])
    for iteration in range(NEWTON):
        squares = [dot(s[0], s[0], precision=full) for s in states]
        steps = [
            jnp.where(eye, linear, 0.0) + square * s[0] + cubic * sq
            for s, sq in zip(states, squares)
        ]
        if iteration == 0:
            halfway = [dot(s[0], m, precision=full) for s, m in zip(states, steps)]
            for s, m in zip(states, steps):
                s[1] = m
        elif iteration < NEWTON - 1:
            both = [
                dot(jnp.concatenate([s[0], s[1]], axis=0), m, precision=full)
                for s, m in zip(states, steps)
            ]
            halfway = [x[:HD] for x in both]
            for s, x in zip(states, both):
                s[1] = x[HD:]
        else:
            for s, m in zip(states, steps):
                s[1] = dot(s[1], m, precision=full)
        if iteration < NEWTON - 1:
            for s, x, m in zip(states, halfway, steps):
                s[0] = dot(x, m, precision=full)
    for (i, j), s in zip(places, states):
        mix = s[1] * s[2]
        coarse = mix.astype(jnp.bfloat16)
        fine = (mix - coarse.astype(jnp.float32)).astype(jnp.bfloat16)
        rows, lanes = slice(64 * (j // 2), 64 * (j // 2) + 64), slice(128 * (j % 2), 128 * (j % 2) + 128)
        out[i, rows, lanes] = jnp.concatenate([coarse, fine], axis=1)


def newton(mine, theirs, sums, after=()):
    flat = [part for group in sums for part in group]
    operands = [mine, theirs, *flat]
    return launch(
        functools.partial(newton_kernel, [len(group) for group in sums]),
        operands,
        [jax.ShapeDtypeStruct((mine.shape[0], 2 * HD, 256), jnp.bfloat16)]
        + [jax.ShapeDtypeStruct(group[0].shape, group[0].dtype) for group in sums],
        "newton",
        cost=3.5,
        specs=[full(a) for a in operands],
        after=after,
    )


def update_kernel(
    n, head, scal, g0, g1, g2, g3, q0, q1, q2, q3, momenta, native_momenta, native, *refs
):
    grads, weights, moved, mixing, first, second, steps = refs[-7:]
    place_of = members_of(head)

    @pl.when((pl.program_id(0) == 0) & (pl.program_id(1) == 0))
    def _():
        mixing[...] = jnp.zeros_like(mixing)

    @pl.when(pl.program_id(1) == 0)
    def _():
        for r, q in enumerate((q0, q1, q2, q3)):
            for j in range(4):
                at = slice(HD * (j // 2), HD * (j // 2) + HD), slice(128 * (j % 2), 128 * (j % 2) + 128)
                wide = q[(0,) * (len(q.shape) - 2) + at].astype(jnp.float32)
                other = pltpu.roll(wide, HD, 1)
                below = low_lanes(HD) == (j % 2 == 0)
                rows = slice(j * HD, (j + 1) * HD)
                lanes = slice(128 * (j // 2), 128 * (j // 2) + 128)
                pair = (wide, other) if j % 2 == 0 else (other, wide)
                for level in range(2):
                    part = jnp.where(below, pair[level], 0.0)
                    mixing[r, level, rows, lanes] = part.astype(jnp.bfloat16)

    low = low_lanes(n)
    for r, piece in enumerate((g0, g1, g2, g3)):
        place = scal[1] ^ r
        grad = piece[(0,) * (len(piece.shape) - 2)].astype(jnp.float32)
        update = 1.95 * grad + 0.9025 * momenta[place]
        coarse = update.astype(jnp.bfloat16)
        fine = (update - coarse.astype(jnp.float32)).astype(jnp.bfloat16)
        settled = dot(coarse, mixing[r, 0]) + dot(coarse, mixing[r, 1]) + dot(fine, mixing[r, 0])
        for half in range(2):
            k = 2 * r + half
            first[k] = grad[:, half * 128 : (half + 1) * 128]
            second[k] = settled[:, half * 128 : (half + 1) * 128]
            for source, target in ((first, grads), (second, steps)):
                even = source[k, pl.ds(0, n, stride=2), :]
                odd = source[k, pl.ds(1, n, stride=2), :]
                lines = (
                    jnp.where(low, even, pltpu.roll(odd, 64, 1)),
                    jnp.where(low, pltpu.roll(even, 64, 1), odd),
                )
                for w in range(2):
                    group, line = place_of(place, 2 * half + w)
                    target[group, pl.ds(line, n, stride=8), :] = lines[w]
    moved[...] = momentum_decay * native_momenta[...] + grads[...]
    weight = native[...]
    weights[...] = weight - muon_rate * (4.0 * steps[...] + weight_decay * weight)


def update(
    first, scal, own, far, mix, mix_far, beside, momenta, native_momenta, native, before=(), after=(), n=128
):
    chunks = own.shape[0]
    block = pl.BlockSpec((2, 8 * n, 128), lambda k, i: (first + k, i, 0))
    piece = pl.BlockSpec((1, 2 * n, 256), lambda k, i: (k, i, 0))
    factor = pl.BlockSpec((1, 2 * HD, 256), lambda k, i: (k, 0, 0))
    pieces, factors = [piece, None, piece, None], [factor, None, factor, None]
    for r in (0, 1):
        pieces[2 * r + 1] = pl.BlockSpec((1, 1, 2 * n, 256), lambda k, i, r=r: (r, k, i, 0))
        factors[2 * r + 1] = pl.BlockSpec((1, 1, 2 * HD, 256), lambda k, i, r=r: (r, k, 4, 0))
    grads, mixes = [own, beside, far, beside], [mix, beside, mix_far, beside]
    return launch(
        functools.partial(update_kernel, n, first == 0),
        [scal, *grads, *mixes, momenta, native_view(native_momenta), native_view(native), *before],
        [jax.ShapeDtypeStruct((6, 2048, 128), jnp.float32)] * 3,
        "update",
        specs=[mem(pltpu.SMEM)]
        + pieces
        + factors
        + [pl.BlockSpec((4, 2 * n, 256), lambda k, i: (k, i, 0)), block, block]
        + [mem(pl.ANY)] * len(before),
        after=after,
        vmem=24,
        cost=0.5 * chunks,
        grid=(chunks, 256 // n),
        out_specs=[block] * 3,
        scratch_shapes=[
            pltpu.VMEM((4, 2, 256, 256), jnp.bfloat16),
            pltpu.VMEM((8, 2 * n, 128), jnp.float32),
            pltpu.VMEM((8, 2 * n, 128), jnp.float32),
            pltpu.VMEM((2, 8 * n, 128), jnp.float32),
        ],
        input_output_aliases={12 + i: i for i in range(len(before))},
    )


def whole_device(
    inputs, cotangent, matrices, momenta, small, small_first, small_second, segments, positions
):
    blk_at = lax.axis_index("blk")
    ctx_at = lax.axis_index("ctx")
    tp_at = lax.axis_index("tp")
    scal = jnp.stack([blk_at, ctx_at, tp_at]).astype(jnp.int32)
    sequences, local_rows, width = inputs.shape
    tokens = sequences * local_rows
    both = ("blk", "ctx")
    f32, bf16 = jnp.float32, jnp.bfloat16
    shaped = jax.ShapeDtypeStruct

    def hop(values, by):
        return lax.ppermute(values, both, [(i, i ^ by) for i in range(8)])

    def hop_tp(values, by):
        return lax.ppermute(values, "tp", [(i, i ^ by) for i in range(4)])

    def tied(values, *results):
        return lax.optimization_barrier((values, *results))[0]

    def spread(piece):
        c = hop(piece, 2)
        return [piece, hop(piece, 1), c, hop(c, 1)]

    x = inputs.reshape(tokens, width)
    cot = cotangent.reshape(tokens, width)
    norms = small[: 4 * width].reshape(4, width)
    qkv_start = 6 * width + tp_at * 4 * 3 * HD
    qkv_bias = lax.dynamic_slice_in_dim(small, qkv_start, 4 * 3 * HD).reshape(4, 3 * HD)
    qkv_bias = jnp.pad(qkv_bias, ((0, 0), (0, HD)))
    unit_start = 6 * width + H * 3 * HD + tp_at * 1024
    unit_bias = lax.dynamic_slice_in_dim(small, unit_start, 1024).reshape(4, 256)
    lane = jnp.arange(128) % HD
    frequency = rope_base ** (-2.0 * (lane % 8).astype(f32) / ROTARY)
    angles = positions.astype(f32).reshape(tokens, 1) * frequency
    cosine = jnp.where(lane < ROTARY, jnp.cos(angles), 1.0)
    sign = jnp.where(lane < 8, -1.0, jnp.where(lane < ROTARY, 1.0, 0.0))
    sine = jnp.sin(angles) * sign

    head_weights, mine = relayout(scal, matrices, bf16, 0, 1, mine=True)
    first_hop = hop(mine, 4)
    unit_weights, mine_units = relayout(scal, matrices, bf16, 1, 2, mine=True, after=(mine,))
    first_hop = tied(first_hop, mine_units)
    other_heads = spread(first_hop)
    units_near = hop(tied(mine_units, first_hop), 4)
    x_beside = hop(x, 1)
    cot_beside = hop(cot, 1)

    send = launch(
        project_kernel,
        [scal, x, cot, norms, qkv_bias, cosine, sine, head_weights]
        + [piece[0] for piece in other_heads],
        shaped((8, local_rows, 256), bf16),
        "project",
    )
    arrived = lax.all_to_all(send, both, split_axis=0, concat_axis=0, tiled=True)
    (piled_heads,) = relayout(scal, momenta, f32, 0, 1, after=(send,))
    units_near = tied(units_near, send)
    units_far = hop(units_near, 2)
    units_beside = hop(units_near, 1)
    documents = lax.dynamic_index_in_dim(segments, blk_at, 0, keepdims=False)
    length = documents.shape[0]
    attended = launch(
        attention_kernel,
        [arrived.reshape(length, 256), documents.reshape(length, 1)],
        shaped((length, 256), bf16),
        "attention",
        vmem=20,
        cost=6,
        specs=[full(arrived.reshape(length, 256)), pl.BlockSpec((length, 1), lambda *_: (0, 0))],
        after=(piled_heads,),
        scratch_shapes=[pltpu.VMEM((length, HD), f32)] * 2,
    )
    back = lax.all_to_all(
        attended.reshape(8, local_rows, 256), both, split_axis=0, concat_axis=0, tiled=True
    )

    units_far = tied(units_far, attended)
    other_units = [units_near, units_beside, units_far, hop(units_far, 1)]
    ff_branch, ff_part, unit_keep, unit_send, unit_sums, norm_two, cot_sums = launch(
        feed_forward_kernel,
        [scal, x, cot, norms, unit_bias, unit_weights, *other_units],
        [
            shaped((tokens, width), f32),
            shaped((tokens, width), f32),
            shaped((2, 2, tokens, 256), bf16),
            shaped((2, 2, tokens, 256), bf16),
            shaped((4, 256), f32),
            shaped((2, width), f32),
            shaped((1, width), f32),
        ],
        "feed_forward",
        vmem=20,
        cost=0.3,
        after=(attended,),
    )
    head_keep, head_send, qkv_sums = launch(
        turn_kernel,
        [scal, cosine, sine, back],
        [shaped((2, tokens, 256), bf16)] * 2 + [shaped((4, 256), f32)],
        "turn",
        cost=2,
        after=(unit_sums,),
    )
    in_keep, in_send, down_keep, down_send = launch(
        unit_grads_kernel,
        [scal, x, x_beside, cot, cot_beside, norms, unit_keep, hop(unit_send, 1)],
        [shaped((2, 512, 256), bf16)] * 4,
        "unit_grads",
        cost=3.5,
        after=(qkv_sums,),
    )
    sums = [norm_two, cot_sums, unit_sums, qkv_sums]
    near, far, totals = launch(
        gather_kernel,
        [scal, x, norms, head_keep, head_send, head_weights, *other_heads, ff_branch, ff_part, *sums],
        [shaped((2, 2, 64, width), bf16)] * 2 + [shaped((8, 8, 256), f32)],
        "gather",
        cost=0.5,
        after=(in_keep,),
        scratch_shapes=[pltpu.VMEM((4, 2, 64, width), bf16)],
    )
    came = hop_tp(far, 1)
    totals_shape = shaped((8, 8, 256), f32)
    a_keep, a_send, b_keep, b_send, totals = launch(
        head_grads_kernel,
        [
            scal, x, x_beside, cot, cot_beside, norms, head_keep, hop(head_send, 1),
            totals, hop_tp(totals, 1),
        ],
        [shaped((2, 256, 256), bf16)] * 4 + [totals_shape],
        "head_grads",
        cost=0.5,
    )
    (piled_units,) = relayout(scal, momenta, f32, 1, 2, after=(a_keep,))
    a_came, b_came = hop(a_send, 4), hop(b_send, 2)
    operands = [in_keep, hop(in_send, 4), down_keep, hop(down_send, 2), totals, hop_tp(totals, 2)]
    own, in_send, down_send, totals = launch(
        combine_kernel,
        operands,
        [shaped((2, 512, 256), bf16)] + [shaped((1, 512, 256), bf16)] * 2 + [totals_shape],
        "combine",
        specs=[full(a) for a in operands],
        cost=2,
        after=(piled_units,),
    )
    in_came, down_came = hop(in_send, 2), hop(down_send, 4)
    kept, passed = launch(
        add_kernel,
        [near, came],
        [shaped((2, 64, width), bf16)] * 2,
        "add",
        specs=[full(near)] * 2,
        cost=1,
        after=(in_send,),
    )
    passed = hop_tp(passed, 2)
    operands = [a_keep, a_came, b_keep, b_came, totals, hop(totals, 1)]
    a_own, a_send, b_own, b_send, totals = launch(
        combine_heads_kernel,
        operands,
        [shaped((256, 256), bf16)] * 4 + [totals_shape],
        "combine_heads",
        specs=[full(a) for a in operands],
        after=(kept,),
    )
    a_came, b_came = hop(a_send, 2), hop(b_send, 4)
    unit_sum, unit_grams, totals = gram_of(
        unit_gram_kernel,
        own,
        [in_came, down_came],
        piled_units,
        scal,
        [totals, hop(totals, 4)],
        [totals_shape],
        after=(a_own,),
    )
    unit_theirs = hop(unit_grams, 4)
    unit_far = hop(unit_sum, 2)
    head_sum, head_grams = gram_of(
        head_gram_kernel,
        a_own,
        [a_came, b_own, b_came],
        piled_heads,
        scal,
        [],
        [],
        after=(unit_sum,),
    )
    head_theirs = hop(head_grams, 4)
    head_far = hop(head_sum, 2)
    unit_mix, totals, total = newton(
        unit_grams, unit_theirs, [(totals, hop(totals, 2)), (kept, passed)], after=(head_sum,)
    )
    total_far, total_beside = hop_tp(total, 2), hop_tp(total, 1)
    unit_mix_far = hop(unit_mix, 2)
    (head_mix,) = newton(head_grams, head_theirs, [], after=(unit_mix, unit_far))
    head_mix_far = hop(head_mix, 2)

    def to_beside(*pieces):
        return hop(jnp.stack([jnp.concatenate(pair, axis=1) for pair in pieces]), 1)

    beside = to_beside((unit_sum, unit_mix), (unit_far, tied(unit_mix_far, head_mix)))
    before = update(
        1, scal, unit_sum, unit_far, unit_mix, unit_mix_far, beside, piled_units, momenta, matrices,
        after=(head_mix,),
    )
    head_far, head_mix_far = tied((head_far, head_mix_far), before[0])
    beside = to_beside((head_sum, head_mix), (head_far, head_mix_far))
    outs = update(
        0, scal, head_sum, head_far, head_mix, head_mix_far, beside, piled_heads, momenta, matrices,
        before,
    )
    total_far = tied(total_far, before[0])
    bias = (small[4 * width : 5 * width] + small[5 * width : 6 * width]).reshape(1, width)
    block_output, input_grad = launch(
        finish_rows_kernel,
        [
            scal,
            x.reshape(4, 64, width),
            cot.reshape(4, 64, width),
            bias,
            total,
            total_beside,
            total_far,
            hop_tp(total_far, 1),
        ],
        [shaped((4, 64, width), f32)] * 2,
        "finish_rows",
        cost=2,
        after=(outs[0],),
    )
    cot_total = totals[2, :4].reshape(-1) * 0.25
    small_grads = jnp.concatenate(
        [
            totals[:2].reshape(-1),
            cot_total,
            cot_total,
            totals[3:7, :4, : 3 * HD].reshape(-1),
            totals[3:7, 4:].reshape(-1),
        ]
    )
    return (
        block_output.reshape(inputs.shape),
        input_grad.reshape(inputs.shape),
        native_back(outs[0]),
        native_back(outs[1]),
        native_back(outs[2]),
        small_grads,
        *small_step(small, small_first, small_second, small_grads),
    )


def small_step(small, small_first, small_second, small_grads):
    new_first = adam_first * small_first + (1.0 - adam_first) * small_grads
    new_second = adam_second * small_second + (1.0 - adam_second) * small_grads * small_grads
    corrected = new_first / (1.0 - adam_first**STEP)
    spread = jnp.sqrt(new_second / (1.0 - adam_second**STEP))
    new_small = small - small_rate * corrected / (spread + adam_epsilon)
    return new_first, new_second, new_small


def solution(mesh):
    in_specs = (
        P(None, ("blk", "ctx"), None),
        P(None, ("blk", "ctx"), None),
        P("tp", "blk"),
        P("tp", "blk"),
        P(),
        P(),
        P(),
        P(),
        P(None, ("blk", "ctx")),
    )
    out_specs = (
        P(None, ("blk", "ctx"), None),
        P(None, ("blk", "ctx"), None),
        P("tp", "blk"),
        P("tp", "blk"),
        P("tp", "blk"),
        P(),
        P(),
        P(),
        P(),
    )
    one_each = mesh.shape["blk"] == SEQS and mesh.shape["ctx"] * mesh.shape["tp"] == H
    one_each = one_each and mesh.shape["tp"] == 4
    return jax.shard_map(
        whole_device if one_each else on_device, mesh=mesh, in_specs=in_specs, out_specs=out_specs, check_vma=False
    )
```

```python
import functools

import jax
import jax.numpy as jnp
from jax import lax
from jax.experimental import pallas as pl
from jax.experimental.pallas import tpu as pltpu
from jax.sharding import PartitionSpec as P

MODEL_DIM = 1024
H = 16
HD = 64
FF = 4096
ROTARY = 16
NEWTON = 5
STEP = 10
SEQS = 2


norm_epsilon = 1e-05
rope_base = 10000.0
masked_score = -1e30
momentum_decay = 0.95
muon_rate = 0.2
weight_decay = 0.01
muon_epsilon = 1e-07
quintic = (3.4445, -4.775, 2.0315)
adam_first = 0.9
adam_second = 0.95
adam_epsilon = 1e-08
small_rate = 0.2


def passed_along(x, axis, by):
    devices = lax.axis_size(axis)
    pairs = [(i, i + by) for i in range(devices) if 0 <= i + by < devices]
    return lax.ppermute(x, axis, pairs)


def shifted(x, axis, by):
    devices = lax.axis_size(axis)
    return lax.ppermute(x, axis, [(i, (i + by) % devices) for i in range(devices)])


def as_sent(x):

    def short(part):
        return part.astype(jnp.bfloat16) if part.dtype == jnp.float32 else part

    return jax.tree.map(short, x)


def layer_norm(values, scaling, offset):
    centre = jnp.mean(values, axis=-1, keepdims=True)
    centred = values - centre
    spread = jnp.mean(centred * centred, axis=-1, keepdims=True)
    return centred * lax.rsqrt(spread + norm_epsilon) * scaling + offset


def rope_tables(positions):
    halfway = ROTARY // 2
    frequency = rope_base ** (-2.0 * jnp.arange(halfway, dtype=jnp.float32) / ROTARY)
    angles = positions.astype(jnp.float32)[..., None] * frequency
    return (jnp.cos(angles)[:, :, None, :], jnp.sin(angles)[:, :, None, :])


def rotate(values, cosine, sine):
    halfway = ROTARY // 2
    former = values[..., :halfway]
    latter = values[..., halfway:ROTARY]
    return jnp.concatenate(
        [former * cosine - latter * sine, latter * cosine + former * sine, values[..., ROTARY:]],
        axis=-1,
    )


def exact_gelu(values):
    return jax.nn.gelu(values, approximate=False)


def newton_schulz(blocks):
    frobenius = jnp.sqrt(jnp.sum(blocks * blocks, axis=(1, 2), keepdims=True))
    current = blocks / (frobenius + muon_epsilon)
    linear_term, square_term, cubic_term = quintic
    for iteration in range(NEWTON):
        gram_matrix = jnp.einsum("mde,mdf->mef", current, current, precision=lax.Precision.HIGHEST)
        polynomial = square_term * gram_matrix + cubic_term * jnp.einsum(
            "mef,mfg->meg", gram_matrix, gram_matrix, precision=lax.Precision.HIGHEST
        )
        current = linear_term * current + jnp.einsum(
            "mde,mef->mdf", current, polynomial, precision=lax.Precision.HIGHEST
        )
    return current


def to_heads(values):
    return lax.all_to_all(values, "ctx", split_axis=3, concat_axis=1, tiled=True)


def to_positions(values):
    return lax.all_to_all(values, "ctx", split_axis=1, concat_axis=3, tiled=True)


def pass_keys(pair):
    return passed_along(pair, "blk", 1)


def pass_grads(pair_grad):
    return shifted(pair_grad.astype(jnp.bfloat16), "blk", 1).astype(pair_grad.dtype)


def allowed_pairs(segments, query_block, key_block, block_rows):
    query_place = query_block * block_rows + jnp.arange(block_rows, dtype=jnp.int32)
    key_place = key_block * block_rows + jnp.arange(block_rows, dtype=jnp.int32)
    query_doc = lax.dynamic_slice_in_dim(segments, query_block * block_rows, block_rows, 1)
    key_doc = lax.dynamic_slice_in_dim(segments, key_block * block_rows, block_rows, 1)
    causal = key_place[None, :] <= query_place[:, None]
    return (causal[None] & (query_doc[:, :, None] == key_doc[:, None, :]))[:, None]


def masked_scores(queries, keys, allowed):
    score_scale = HD ** (-0.5)
    scores = (
        jnp.einsum("sqhe,skhe->shqk", queries, keys, preferred_element_type=jnp.float32)
        * score_scale
    )
    return jnp.where(allowed, scores, masked_score)


def on_device(
    inputs, cotangent, matrices, momenta, small, small_first, small_second, segments, positions
):
    tensor_size = lax.axis_size("tp")
    cycle_size = lax.axis_size("blk")
    context_size = lax.axis_size("ctx")
    tensor_index = lax.axis_index("tp")
    cycle_index = lax.axis_index("blk")
    sequences, local_rows, model_width = inputs.shape
    per_group = matrices.shape[0]
    head_count = H // tensor_size
    unit_blocks = FF // HD // tensor_size
    block_rows = local_rows * context_size
    gathered = lax.all_gather(matrices.astype(jnp.bfloat16), "blk", axis=1, tiled=True).reshape(
        per_group, model_width, HD
    )
    query_key_value_weight = gathered[: 3 * head_count]
    projection_out_weight = gathered[3 * head_count : 4 * head_count]
    input_weight = gathered[4 * head_count : 4 * head_count + unit_blocks]
    down_projection_weight = gathered[4 * head_count + unit_blocks :]
    qkv_start = 6 * model_width + tensor_index * head_count * 3 * HD
    query_key_value_bias = lax.dynamic_slice_in_dim(small, qkv_start, head_count * 3 * HD).reshape(
        head_count, 3, HD
    )
    unit_start = 6 * model_width + H * 3 * HD + tensor_index * unit_blocks * HD
    hidden_unit_bias = lax.dynamic_slice_in_dim(small, unit_start, unit_blocks * HD).reshape(
        unit_blocks, HD
    )
    residual = inputs.astype(jnp.float32)

    def both_norms(values, gain_one, offset_one, gain_two, offset_two):
        return (layer_norm(values, gain_one, offset_one), layer_norm(values, gain_two, offset_two))

    (normed_one, normed_two), norm_back = jax.vjp(
        both_norms,
        residual,
        small[0:model_width],
        small[model_width : 2 * model_width],
        small[2 * model_width : 3 * model_width],
        small[3 * model_width : 4 * model_width],
    )
    first_input = normed_one.astype(jnp.bfloat16)
    second_input = normed_two.astype(jnp.bfloat16)
    projected = jnp.einsum(
        "pgk,jka->pgja", first_input, query_key_value_weight, preferred_element_type=jnp.float32
    )
    projected = projected.reshape(sequences, local_rows, 3, head_count, HD) + jnp.transpose(
        query_key_value_bias, (1, 0, 2)
    )
    cosine, sine = rope_tables(positions)

    def turn_pair(query_pre, key_pre):
        return (rotate(query_pre, cosine, sine), rotate(key_pre, cosine, sine))

    (query_turned, key_turned), turn_back = jax.vjp(
        turn_pair, projected[:, :, 0], projected[:, :, 1]
    )
    stacked = jnp.stack([query_turned, key_turned, projected[:, :, 2]], axis=2).astype(jnp.bfloat16)
    by_heads = to_heads(stacked)
    queries = by_heads[:, :, 0]
    head_local = queries.shape[2]

    def forward_visit(state, pair, source):
        row_max, row_total, weighted = state
        allowed = allowed_pairs(segments, cycle_index, source, block_rows)
        scores = masked_scores(queries, pair[:, :, 0], allowed)
        new_max = jnp.maximum(row_max, jnp.max(scores, axis=-1))
        weights = jnp.where(allowed, jnp.exp(scores - new_max[..., None]), 0.0)
        rescale = jnp.exp(row_max - new_max)
        row_total = row_total * rescale + jnp.sum(weights, axis=-1)
        weighted = weighted * rescale[..., None] + jnp.einsum(
            "shqk,skhe->shqe",
            weights.astype(jnp.bfloat16),
            pair[:, :, 1],
            preferred_element_type=jnp.float32,
        )
        return (new_max, row_total, weighted)

    def forward_hop(hop_index, carry):
        pair, state = carry
        source = (cycle_index - hop_index) % cycle_size
        state = forward_visit(state, pair, source)
        return (pass_keys(pair), state)

    start_state = (
        jnp.full((sequences, head_local, block_rows), masked_score, jnp.float32),
        jnp.zeros((sequences, head_local, block_rows), jnp.float32),
        jnp.zeros((sequences, head_local, block_rows, HD), jnp.float32),
    )
    pair, state = lax.fori_loop(0, cycle_size - 1, forward_hop, (by_heads[:, :, 1:], start_state))
    row_max, row_total, weighted = forward_visit(state, pair, (cycle_index + 1) % cycle_size)
    log_total = row_max + jnp.log(row_total)
    attended_rows = jnp.transpose(weighted / row_total[..., None], (0, 2, 1, 3))
    attention_result = to_positions(attended_rows.astype(jnp.bfloat16)[:, :, None])[:, :, 0]
    attention_branch = jnp.einsum(
        "roxu,xcu->roc", attention_result, projection_out_weight, preferred_element_type=jnp.float32
    )
    hidden_preactivation = (
        jnp.einsum("ptr,kra->ptka", second_input, input_weight, preferred_element_type=jnp.float32)
        + hidden_unit_bias
    )
    activated_hidden, gelu_back = jax.vjp(exact_gelu, hidden_preactivation)
    activated_reduced = activated_hidden.astype(jnp.bfloat16)
    perceptron_branch = jnp.einsum(
        "xkzp,zop->xko",
        activated_reduced,
        down_projection_weight,
        preferred_element_type=jnp.float32,
    )
    branches = lax.psum((attention_branch + perceptron_branch).astype(jnp.bfloat16), "tp").astype(
        jnp.float32
    )
    block_output = (
        residual
        + branches
        + small[4 * model_width : 5 * model_width]
        + small[5 * model_width : 6 * model_width]
    )
    act_grad = jnp.einsum(
        "ptr,kra->ptka", cotangent, down_projection_weight, preferred_element_type=jnp.float32
    )
    hidden_gradient = gelu_back(act_grad)[0].astype(jnp.bfloat16)
    down_grad = jnp.einsum(
        "gup,guzb->zpb", cotangent, activated_reduced, preferred_element_type=jnp.float32
    )
    in_grad = jnp.einsum(
        "gup,guzb->zpb", second_input, hidden_gradient, preferred_element_type=jnp.float32
    )
    second_grad = jnp.einsum(
        "xkzp,zop->xko", hidden_gradient, input_weight, preferred_element_type=jnp.float32
    )
    attended_grad = jnp.einsum(
        "pgk,jka->pgja", cotangent, projection_out_weight, preferred_element_type=jnp.float32
    ).astype(jnp.bfloat16)
    outproj_grad = jnp.einsum(
        "ztu,ztqi->qui", cotangent, attention_result, preferred_element_type=jnp.float32
    )
    grad_heads = to_heads(attended_grad[:, :, None])[:, :, 0]
    row_delta = jnp.transpose(
        jnp.sum(grad_heads.astype(jnp.float32) * attended_rows, axis=-1), (0, 2, 1)
    )

    def backward_visit(query_grad, pair, source):
        allowed = allowed_pairs(segments, cycle_index, source, block_rows)
        scores = masked_scores(queries, pair[:, :, 0], allowed)
        probabilities = jnp.where(allowed, jnp.exp(scores - log_total[..., None]), 0.0)
        value_grad = jnp.einsum(
            "shqk,sqhe->skhe",
            probabilities.astype(jnp.bfloat16),
            grad_heads,
            preferred_element_type=jnp.float32,
        )
        prob_grad = jnp.einsum(
            "sqhe,skhe->shqk", grad_heads, pair[:, :, 1], preferred_element_type=jnp.float32
        )
        score_grad = (probabilities * (prob_grad - row_delta[..., None])).astype(jnp.bfloat16)
        score_scale = HD ** (-0.5)
        query_grad = (
            query_grad
            + jnp.einsum(
                "shqk,skhe->sqhe", score_grad, pair[:, :, 0], preferred_element_type=jnp.float32
            )
            * score_scale
        )
        key_grad = (
            jnp.einsum("shqk,sqhe->skhe", score_grad, queries, preferred_element_type=jnp.float32)
            * score_scale
        )
        return (query_grad, jnp.stack([key_grad, value_grad], axis=2))

    def backward_hop(hop_index, carry):
        pair, pair_grad, query_grad = carry
        source = (cycle_index - hop_index) % cycle_size
        query_grad, visit_grad = backward_visit(query_grad, pair, source)
        return (pass_keys(pair), pass_grads(pair_grad + visit_grad), query_grad)

    zero_pair = jnp.zeros(by_heads[:, :, 1:].shape, jnp.float32)
    pair, pair_grad, query_grad = lax.fori_loop(
        0,
        cycle_size - 1,
        backward_hop,
        (by_heads[:, :, 1:], zero_pair, jnp.zeros(queries.shape, jnp.float32)),
    )
    query_grad, visit_grad = backward_visit(query_grad, pair, (cycle_index + 1) % cycle_size)
    pair_grad = pass_grads(pair_grad + visit_grad)
    head_grads = jnp.concatenate([query_grad[:, :, None], pair_grad], axis=2).astype(jnp.bfloat16)
    position_grads = to_positions(head_grads).astype(jnp.float32)
    query_pre_grad, key_pre_grad = turn_back((position_grads[:, :, 0], position_grads[:, :, 1]))
    projected_grad = jnp.stack(
        [query_pre_grad, key_pre_grad, position_grads[:, :, 2]], axis=2
    ).astype(jnp.bfloat16)
    flattened_gradient = projected_grad.reshape(sequences, local_rows, 3 * head_count, HD)
    query_key_value_gradient = jnp.einsum(
        "ztu,ztqi->qui", first_input, flattened_gradient, preferred_element_type=jnp.float32
    )
    first_grad = jnp.einsum(
        "roxu,xcu->roc",
        flattened_gradient,
        query_key_value_weight,
        preferred_element_type=jnp.float32,
    )
    input_part, gain_one_grad, offset_one_grad, gain_two_grad, offset_two_grad = norm_back(
        (first_grad, second_grad)
    )
    input_grad = cotangent.astype(jnp.float32) + lax.psum(
        input_part.astype(jnp.bfloat16), "tp"
    ).astype(jnp.float32)
    owner_share = jnp.where(tensor_index == 0, 1.0, 0.0).astype(jnp.float32)
    bias_grad = jnp.sum(cotangent.astype(jnp.float32), axis=(0, 1)) * owner_share
    qkv_bias_grad = jnp.transpose(
        jnp.sum(projected_grad.astype(jnp.float32), axis=(0, 1)), (1, 0, 2)
    ).reshape(-1)
    unit_bias_grad = jnp.sum(hidden_gradient.astype(jnp.float32), axis=(0, 1)).reshape(-1)
    local_small = jnp.concatenate(
        [
            gain_one_grad,
            offset_one_grad,
            gain_two_grad,
            offset_two_grad,
            bias_grad,
            bias_grad,
            jnp.zeros((small.shape[0] - 6 * model_width,), jnp.float32),
        ]
    )
    local_small = lax.dynamic_update_slice_in_dim(local_small, qkv_bias_grad, qkv_start, 0)
    local_small = lax.dynamic_update_slice_in_dim(local_small, unit_bias_grad, unit_start, 0)
    small_grads = lax.psum(local_small, ("blk", "ctx", "tp"))
    local_grad = jnp.concatenate(
        [query_key_value_gradient, outproj_grad, in_grad, down_grad], axis=0
    ).reshape(per_group, -1)
    shares = lax.psum_scatter(
        local_grad.astype(jnp.bfloat16), "blk", scatter_dimension=1, tiled=True
    )
    matrix_grads = lax.psum(shares, "ctx").astype(jnp.float32)
    new_momenta = momentum_decay * momenta + matrix_grads
    update = matrix_grads + momentum_decay * new_momenta
    per_owner = per_group // cycle_size
    sectioned = update.reshape(cycle_size, per_owner, update.shape[1])
    pieces = lax.all_to_all(
        sectioned.astype(jnp.bfloat16), "blk", split_axis=0, concat_axis=2, tiled=True
    ).astype(sectioned.dtype)
    piece_count = pieces.shape[1]
    settled_blocks = newton_schulz(pieces.reshape(piece_count, MODEL_DIM, HD)).reshape(
        1, piece_count, MODEL_DIM * HD
    )
    settled = lax.all_to_all(
        as_sent(settled_blocks), "blk", split_axis=2, concat_axis=0, tiled=True
    ).astype(settled_blocks.dtype)
    orthogonal_all = settled.reshape(per_group, -1)
    muon_scale = max(1.0, MODEL_DIM / HD) ** 0.5
    new_matrices = matrices - muon_rate * (muon_scale * orthogonal_all + weight_decay * matrices)
    new_first = adam_first * small_first + (1.0 - adam_first) * small_grads
    new_second = adam_second * small_second + (1.0 - adam_second) * small_grads * small_grads
    corrected = new_first / (1.0 - adam_first**STEP)
    spread = jnp.sqrt(new_second / (1.0 - adam_second**STEP))
    new_small = small - small_rate * corrected / (spread + adam_epsilon)
    return (
        block_output,
        input_grad,
        matrix_grads,
        new_matrices,
        new_momenta,
        small_grads,
        new_first,
        new_second,
        new_small,
    )


def native_view(array):
    rows, columns = array.shape
    tiled = array.reshape(rows // 8, 8, columns // 128, 128).transpose(0, 2, 1, 3)
    return tiled.reshape(rows // 8, columns // 16, 128)


def native_back(array):
    groups, rows, _ = array.shape
    return array.reshape(groups, rows // 8, 8, 128).transpose(0, 2, 1, 3).reshape(groups * 8, rows * 16)


def members_of(head):
    if head:
        return lambda piece, j: (j // 2, 4 * (j % 2) + piece)
    return lambda piece, j: (piece // 2, 4 * (piece % 2) + j)


def mem(kind=pltpu.VMEM):
    return pl.BlockSpec(memory_space=kind)


def limits(mebibytes):
    return pltpu.CompilerParams(vmem_limit_bytes=mebibytes << 20)


def low_lanes(rows):
    return lax.broadcasted_iota(jnp.int32, (rows, 128), 1) < HD


def dot(a, b, dims=((1,), (0,)), precision=None):
    return lax.dot_general(
        a, b, (dims, ((), ())), precision=precision, preferred_element_type=jnp.float32
    )


NT = ((1,), (1,))
TN = ((0,), (0,))


def corner(array):
    block = (1,) * (array.ndim - 2) + (min(16, array.shape[-2]), 128)
    return pl.BlockSpec(block, lambda *_: (0,) * array.ndim)


def takes(microseconds):
    return pl.CostEstimate(
        flops=int(microseconds * 1.15e9), transcendentals=0, bytes_accessed=int(1e6)
    )


def in_hbm(array):
    if array.size * array.dtype.itemsize < 1 << 21:
        return array
    return pltpu.with_memory_space_constraint(array, pltpu.HBM)


def out_hbm(shape):
    if shape.size * shape.dtype.itemsize < 1 << 20:
        return shape
    return pltpu.HBM(shape.shape, shape.dtype)


def full(array):
    return pl.BlockSpec(array.shape, lambda *_: (0,) * array.ndim)


def launch(kernel, operands, out_shapes, name, specs=None, after=(), vmem=16, cost=3, **more):
    taken = len(operands)
    body = kernel
    if after:
        body = lambda *refs: kernel(*refs[:taken], *refs[taken + len(after) :])
    if specs is None:
        specs = [mem(pltpu.SMEM)] + [full(a) for a in operands[1:]]
    if "out_specs" not in more:
        more["out_specs"] = jax.tree.map(full, out_shapes)
    more.setdefault("grid", (1,))
    return pl.pallas_call(
        body,
        in_specs=list(specs) + [corner(a) for a in after],
        out_shape=jax.tree.map(out_hbm, out_shapes),
        compiler_params=limits(vmem),
        cost_estimate=takes(cost),
        name=name,
        **more,
    )(*map(in_hbm, operands), *map(in_hbm, after))


def relayout_kernel(n, first, count, scal, src, out, *refs):
    fetched, paired, packed, arrivals, departures = refs[-5:]
    low = low_lanes(n)
    place_of = members_of(first == 0)
    steps = [(k, i) for k in range(count) for i in range(256 // n)]

    def fetch(k, i, group):
        rows = pl.ds(i * 8 * n, 8 * n)
        return pltpu.make_async_copy(
            src.at[2 * first + 2 * k + group, rows],
            fetched.at[2 * k + group, rows],
            arrivals.at[2 * k + group, i],
        )

    def leave(k, i):
        rows = pl.ds(i * 2 * n, 2 * n)
        return pltpu.make_async_copy(
            packed.at[pl.ds(4 * k, 4), rows], out.at[pl.ds(4 * k, 4), rows], departures.at[k, i]
        )

    for k, i in steps:
        for group in range(2):
            fetch(k, i, group).start()
    for k, i in steps:
        for group in range(2):
            fetch(k, i, group).wait()
        for piece in range(4):
            for half in range(2):
                pair = []
                for j in (2 * half, 2 * half + 1):
                    group, line = place_of(piece, j)
                    rows = pl.ds(i * 8 * n + line, n, stride=8)
                    pair.append(fetched[2 * k + group, rows, :])
                a, b = pair
                at = 2 * piece + half
                paired[at, pl.ds(0, n, stride=2), :] = jnp.where(low, a, pltpu.roll(b, 64, 1))
                paired[at, pl.ds(1, n, stride=2), :] = jnp.where(low, pltpu.roll(a, 64, 1), b)
                lanes = slice(half * 128, (half + 1) * 128)
                rows = slice(i * 2 * n, (i + 1) * 2 * n)
                packed[4 * k + piece, rows, lanes] = paired[at].astype(packed.dtype)
        leave(k, i).start()
    if len(refs) == 6:
        for k in range(count):
            refs[0][k] = packed[4 * k + scal[1]]
    for k, i in steps:
        leave(k, i).wait()


def relayout(scal, array, dtype, first, count, mine=False, n=128, after=()):
    shapes = [jax.ShapeDtypeStruct((4 * count, 512, 256), dtype)]
    specs = [mem(pl.ANY)]
    if mine:
        shapes.append(jax.ShapeDtypeStruct((count, 512, 256), dtype))
        specs.append(full(shapes[1]))
    return launch(
        functools.partial(relayout_kernel, n, first, count),
        [scal, native_view(array)],
        shapes,
        "relayout",
        specs=[mem(pltpu.SMEM), mem(pl.ANY)],
        after=after,
        cost=0.2 * count,
        vmem=14,
        out_specs=specs,
        scratch_shapes=[
            pltpu.VMEM((2 * count, 2048, 128), jnp.float32),
            pltpu.VMEM((8, 2 * n, 128), jnp.float32),
            pltpu.VMEM((4 * count, 512, 256), dtype),
            pltpu.SemaphoreType.DMA((2 * count, 256 // n)),
            pltpu.SemaphoreType.DMA((count, 256 // n)),
        ],
    )


def add_up(groups):
    for parts, target in groups:
        values = [part[...].astype(jnp.float32) for part in parts]
        while len(values) > 1:
            values = [sum(values[i : i + 2]) for i in range(0, len(values), 2)]
        if isinstance(target, list):
            for i, part in enumerate(target):
                part[...] = values[0][i].astype(part.dtype)
        else:
            target[...] = values[0].astype(target.dtype)


def grouped(refs, counts, targets):
    refs = iter(refs)
    return [([next(refs) for _ in range(n)], target) for n, target in zip(counts, targets)]


def normalized(x):
    centred = x - jnp.mean(x, axis=-1, keepdims=True)
    spread = jnp.mean(centred * centred, axis=-1, keepdims=True)
    root = lax.rsqrt(spread + norm_epsilon)
    return centred * root, root


def halves(values, first):
    left, right = values[:, :512], values[:, 512:]
    return jnp.where(first, left, right), jnp.where(first, right, left)


def whole(own, other, first):
    return jnp.concatenate([jnp.where(first, own, other), jnp.where(first, other, own)], axis=1)


def norm_back(grad, hat, root, gain):
    scaled = grad * gain
    along = jnp.mean(scaled * hat, axis=-1, keepdims=True)
    return root * (scaled - jnp.mean(scaled, axis=-1, keepdims=True) - hat * along)


def turned(values, cosine, sine):
    lane = lax.broadcasted_iota(jnp.int32, values.shape, 1) % HD
    other = jnp.where(lane < 8, pltpu.roll(values, 120, 1), pltpu.roll(values, 8, 1))
    return values * cosine + other * sine


def project_kernel(scal, x, cot, norms, bias, cosine, sine, own, r0, r1, r2, r3, send):
    first = scal[0] == 0
    hat, _ = normalized(x[...].astype(jnp.float32))
    h = (hat * norms[0:1] + norms[1:2]).astype(jnp.bfloat16)
    h_own, h_other = halves(h, first)
    c_own, c_other = halves(cot[...], first)
    tokens = h.shape[0]
    low = low_lanes(tokens)
    for r, other in enumerate((r0, r1, r2, r3)):
        head = scal[1] ^ r
        mine = own[head]
        theirs = other[...]
        pre = dot(h_own, mine) + dot(h_other, theirs) + bias[pl.ds(head, 1), :]
        back = dot(c_own, mine[:, 128:]) + dot(c_other, theirs[:, 128:])
        left = turned(pre[:, :128], cosine[...], sine[...]).astype(jnp.bfloat16)
        right = jnp.where(low, pre[:, 128:], back).astype(jnp.bfloat16)
        for s in range(2):
            rows = slice(128 * s, 128 * s + 128)
            send[4 * s + head, :, :128] = left[rows]
            send[4 * s + head, :, 128:] = right[rows]


def attention_kernel(rows_ref, seg, out, key_total, value_total):
    key_total[...] = jnp.zeros_like(key_total)
    value_total[...] = jnp.zeros_like(value_total)
    step = 256
    for block in range(rows_ref.shape[0] // step):
        rows = slice(block * step, (block + 1) * step)
        n = (block + 1) * step
        query = rows_ref[rows, 0:HD] * jnp.bfloat16(0.125)
        grad = rows_ref[rows, 3 * HD : 4 * HD]
        keys = rows_ref[0:n, HD : 2 * HD]
        values = rows_ref[0:n, 2 * HD : 3 * HD]
        scores = dot(query, keys, NT)
        query_place = block * step + lax.broadcasted_iota(jnp.int32, (step, n), 0)
        key_place = lax.broadcasted_iota(jnp.int32, (step, n), 1)
        allowed = (key_place <= query_place) & (key_place >= seg[rows, :])
        scores = jnp.where(allowed, scores, masked_score)
        weights = jnp.exp(scores - jnp.max(scores, axis=-1, keepdims=True))
        weights = jnp.where(allowed, weights, 0.0)
        weights = weights * (1.0 / jnp.sum(weights, axis=-1, keepdims=True))
        short = weights.astype(jnp.bfloat16)
        attended = dot(short, values)
        weight_grad = dot(grad, values, NT)
        delta = jnp.sum(weights * weight_grad, axis=-1, keepdims=True)
        score_grad = (weights * (weight_grad - delta)).astype(jnp.bfloat16)
        query_grad = dot(score_grad, keys) * 0.125
        key_total[0:n, :] += dot(score_grad, query, TN)
        value_total[0:n, :] += dot(short, grad, TN)
        out[rows, 0:HD] = query_grad.astype(jnp.bfloat16)
        out[rows, 3 * HD : 4 * HD] = attended.astype(jnp.bfloat16)
    out[:, HD : 2 * HD] = key_total[...].astype(jnp.bfloat16)
    out[:, 2 * HD : 3 * HD] = value_total[...].astype(jnp.bfloat16)


def feed_forward_kernel(
    scal, x, cot, norms, bias, weights, r0, r1, r2, r3,
    branch, input_part, keep, send, hidden_sums, norm_grads, cot_sums,
):
    first = scal[0] == 0
    hat, root = normalized(x[...].astype(jnp.float32))
    h = (hat * norms[2:3] + norms[3:4]).astype(jnp.bfloat16)
    h_own, h_other = halves(h, first)
    c_own, c_other = halves(cot[...], first)
    cot_sums[...] = jnp.sum(cot[...].astype(jnp.float32), axis=0, keepdims=True)
    outs = [0.0] * 4
    for r, other in enumerate((r0, r1, r2, r3)):
        piece = scal[1] ^ r
        in_own, in_other = weights[piece], other[0]
        down_own, down_other = weights[4 + piece], other[1]
        pre = dot(h_own, in_own) + dot(h_other, in_other) + bias[pl.ds(piece, 1), :]
        cumulative = 0.5 * (1.0 + lax.erf(pre * 0.7071067811865476))
        slope = cumulative + pre * (0.3989422804014327 * jnp.exp(-0.5 * pre * pre))
        act = (pre * cumulative).astype(jnp.bfloat16)
        act_grad = dot(c_own, down_own) + dot(c_other, down_other)
        grad = (act_grad * slope).astype(jnp.bfloat16)
        hidden_sums[pl.ds(piece, 1), :] = jnp.sum(
            grad.astype(jnp.float32), axis=0, keepdims=True
        )
        outs[0] += dot(act, down_own, NT)
        outs[1] += dot(act, down_other, NT)
        outs[2] += dot(grad, in_own, NT)
        outs[3] += dot(grad, in_other, NT)
        target = send if r % 2 else keep
        target[r // 2, 0] = grad
        target[r // 2, 1] = act
    branch[...] = whole(outs[0], outs[1], first)
    second = whole(outs[2], outs[3], first)
    norm_grads[0:1] = jnp.sum(second * hat, axis=0, keepdims=True)
    norm_grads[1:2] = jnp.sum(second, axis=0, keepdims=True)
    input_part[...] = norm_back(second, hat, root, norms[2:3])


def both_cores(scal, x, x_beside, cot, cot_beside, norms, at):
    first = scal[0] == 0
    tokens = jnp.concatenate([x[...], x_beside[...]], axis=0).astype(jnp.float32)
    hat, _ = normalized(tokens)
    h = (hat * norms[at : at + 1] + norms[at + 1 : at + 2]).astype(jnp.bfloat16)
    c = jnp.concatenate([cot[...], cot_beside[...]], axis=0)
    return list(zip(halves(h, first), halves(c, first)))


def unit_grads_kernel(
    scal, x, x_beside, cot, cot_beside, norms, keep, came, in_keep, in_send, down_keep, down_send
):
    for side, (h, c) in enumerate(both_cores(scal, x, x_beside, cot, cot_beside, norms, 2)):
        for far in range(2):
            grad = jnp.concatenate([keep[far, 0], came[far, 0]], axis=0)
            act = jnp.concatenate([keep[far, 1], came[far, 1]], axis=0)
            (in_send if side else in_keep)[far] = dot(h, grad, TN).astype(jnp.bfloat16)
            (down_send if far else down_keep)[side] = dot(c, act, TN).astype(jnp.bfloat16)


def combine_kernel(in_keep, in_came, down_keep, down_came, own, in_send, down_send):
    pairs = ((in_keep, in_came, in_send), (down_keep, down_came, down_send))
    for k, (keep, came, send) in enumerate(pairs):
        total = keep[...].astype(jnp.float32) + came[...].astype(jnp.float32)
        own[k] = total[0].astype(jnp.bfloat16)
        send[0] = total[1].astype(jnp.bfloat16)


def turn_kernel(scal, cosine, sine, back, keep, send, sums):
    low = low_lanes(keep.shape[1])
    for r in range(4):
        head = scal[1] ^ r
        grads = jnp.concatenate([back[head], back[4 + head]], axis=0)
        left = turned(grads[:, :128].astype(jnp.float32), cosine[...], -sine[...])
        left = left.astype(jnp.bfloat16)
        right = grads[:, 128:]
        target = send if r % 2 else keep
        target[r // 2, :, :128] = left
        target[r // 2, :, 128:] = right
        right = jnp.where(low, right.astype(jnp.float32), 0.0)
        wide = jnp.concatenate([left.astype(jnp.float32), right], axis=1)
        sums[pl.ds(head, 1), :] = jnp.sum(wide, axis=0, keepdims=True)


def split_last(piece):
    wide = piece.astype(jnp.float32)
    lane = lax.broadcasted_iota(jnp.int32, (1, wide.shape[1]), 1)
    share = (lane < 3 * HD).astype(jnp.float32)
    pre_grad = (wide * share).astype(jnp.bfloat16)
    attended = (wide * (1.0 - share)).astype(jnp.bfloat16)
    return pre_grad, attended


def head_grads_kernel(
    scal, x, x_beside, cot, cot_beside, norms, keep, came, totals, totals_came, *outs
):
    add_up([((totals, totals_came), outs[4])])
    sides = both_cores(scal, x, x_beside, cot, cot_beside, norms, 0)
    a_keep, a_send, b_keep, b_send = outs[:4]
    for far in range(2):
        piece = jnp.concatenate([keep[far], came[far]], axis=0)
        pre_grad, attended = split_last(piece)
        for side, (h, c) in enumerate(sides):
            grad = (dot(h, pre_grad, TN) + dot(c, attended, TN)).astype(jnp.bfloat16)
            (a_send if side else a_keep)[far] = grad[0:256]
            (b_send if far else b_keep)[side] = grad[256:512]


def combine_heads_kernel(
    a_keep, a_came, b_keep, b_came, totals, totals_came, a_own, a_send, b_own, b_send, totals_sum
):
    add_up(
        [
            ((a_keep, a_came), [a_own, a_send]),
            ((b_keep, b_came), [b_own, b_send]),
            ((totals, totals_came), totals_sum),
        ]
    )


def add_kernel(near, came, kept, passed):
    add_up([((near, came), [kept, passed])])


def gather_kernel(
    scal, x, norms, keep, send, weights, r0, r1, r2, r3, ff_branch, ff_part,
    norm_two, cot_sums, unit_sums, qkv_sums, near, far, totals, parts,
):
    first = scal[0] == 0
    hat, root = normalized(x[...].astype(jnp.float32))
    outs = [0.0] * 4
    for r, other in enumerate((r0, r1, r2, r3)):
        mine, theirs = weights[scal[1] ^ r], other[0]
        pre_grad, attended = split_last((send if r % 2 else keep)[r // 2])
        outs[0] += dot(attended, mine, NT)
        outs[1] += dot(attended, theirs, NT)
        outs[2] += dot(pre_grad, mine, NT)
        outs[3] += dot(pre_grad, theirs, NT)
    branch = ff_branch[...] + whole(outs[0], outs[1], first)
    grad = whole(outs[2], outs[3], first)
    totals[...] = jnp.zeros_like(totals)
    rows = [jnp.sum(grad * hat, axis=0, keepdims=True), jnp.sum(grad, axis=0, keepdims=True)]
    rows += [norm_two[0:1], norm_two[1:2], cot_sums[...]]
    for i, row in enumerate(rows):
        for q in range(4):
            at = 4 * (i % 2) + q
            totals[i // 2, at : at + 1, :] = row[:, 256 * q : 256 * q + 256]
    totals[3 + scal[2], 0:4, :] = qkv_sums[...]
    totals[3 + scal[2], 4:8, :] = unit_sums[...]
    input_part = ff_part[...] + norm_back(grad, hat, root, norms[0:1])
    for q in range(4):
        parts[q, 0] = branch[64 * q : 64 * q + 64].astype(jnp.bfloat16)
        parts[q, 1] = input_part[64 * q : 64 * q + 64].astype(jnp.bfloat16)
    for r in range(4):
        (far if r % 2 else near)[r // 2] = parts[scal[2] ^ r]


def finish_rows_kernel(scal, x, cot, bias, r0, r1, r2, r3, block_output, input_grad):
    for r, piece in enumerate((r0, r1, r2, r3)):
        q = scal[2] ^ r
        block_output[q] = x[q].astype(jnp.float32) + piece[0].astype(jnp.float32) + bias[...]
        input_grad[q] = cot[q].astype(jnp.float32) + piece[1].astype(jnp.float32)


def gram_of_piece(total, momenta, grads, grams):
    short = total.astype(jnp.bfloat16)
    grads[0] = short
    update = 1.95 * short.astype(jnp.float32) + 0.9025 * momenta[0]
    gram = dot(update, update, TN, lax.Precision.HIGHEST)
    for j in range(4):
        cut = slice(j * HD, (j + 1) * HD)
        grams[0, j] = gram[cut, cut]


def unit_gram_kernel(place, own, in_came, down_came, momenta, totals, totals_came, *refs):
    grads, grams, totals_sum = refs[-3:]

    @pl.when(pl.program_id(0) == 0)
    def _():
        add_up([((totals, totals_came), totals_sum)])

    a = in_came[0].astype(jnp.float32)
    b = down_came[0].astype(jnp.float32)
    other = jnp.where(pl.program_id(0) == 0, a, b)
    gram_of_piece(own[0].astype(jnp.float32) + other, momenta, grads, grams)


def head_gram_kernel(place, a_own, a_came, b_own, b_came, momenta, *refs):
    grads, grams = refs[-2:]
    a = a_own[...].astype(jnp.float32) + a_came[...].astype(jnp.float32)
    b = b_own[...].astype(jnp.float32) + b_came[...].astype(jnp.float32)
    gram_of_piece(jnp.concatenate([a, b], axis=0), momenta, grads, grams)


def gram_of(kernel, first, others, momenta, place, more, shapes, after=()):
    chunks = momenta.shape[0] // 4
    piece = pl.BlockSpec((1, 512, 256), lambda i, s: (i, 0, 0))
    block = pl.BlockSpec((1, 512, 256), lambda i, s: (4 * i + s[1], 0, 0))
    return pl.pallas_call(
        kernel,
        grid_spec=pltpu.PrefetchScalarGridSpec(
            num_scalar_prefetch=1,
            grid=(chunks,),
            in_specs=[piece if first.ndim == 3 else full(first)]
            + [full(other) for other in others]
            + [block]
            + [full(part) for part in more]
            + [corner(a) for a in after],
            out_specs=[piece, pl.BlockSpec((1, 4, HD, HD), lambda i, s: (i, 0, 0, 0))]
            + [full(shape) for shape in shapes],
        ),
        out_shape=[
            jax.ShapeDtypeStruct((chunks, 512, 256), jnp.bfloat16),
            jax.ShapeDtypeStruct((chunks, 4, HD, HD), jnp.float32),
            *map(out_hbm, shapes),
        ],
        compiler_params=limits(12),
        cost_estimate=takes(2.5),
        name="gram",
    )(place, *map(in_hbm, [first, *others, momenta, *more, *after]))


def newton_kernel(counts, mine, theirs, *refs):
    taken = sum(counts)
    out = refs[taken]
    add_up(grouped(refs, counts, refs[taken + 1 :]))
    linear, square, cubic = quintic
    shape = (HD, HD)
    eye = lax.broadcasted_iota(jnp.int32, shape, 0) == lax.broadcasted_iota(jnp.int32, shape, 1)
    full = lax.Precision.HIGHEST
    chunks = mine.shape[0]
    places = [(i, j) for i in range(chunks) for j in range(4)]
    states = []
    for i, j in places:
        gram = mine[i, j] + theirs[i, j]
        trace = jnp.sum(jnp.where(eye, gram, 0.0), axis=(0, 1), keepdims=True)
        scale = 1.0 / (jnp.sqrt(trace) + muon_epsilon)
        states.append([gram * scale * scale, None, scale])
    for iteration in range(NEWTON):
        squares = [dot(s[0], s[0], precision=full) for s in states]
        steps = [
            jnp.where(eye, linear, 0.0) + square * s[0] + cubic * sq
            for s, sq in zip(states, squares)
        ]
        if iteration == 0:
            halfway = [dot(s[0], m, precision=full) for s, m in zip(states, steps)]
            for s, m in zip(states, steps):
                s[1] = m
        elif iteration < NEWTON - 1:
            both = [
                dot(jnp.concatenate([s[0], s[1]], axis=0), m, precision=full)
                for s, m in zip(states, steps)
            ]
            halfway = [x[:HD] for x in both]
            for s, x in zip(states, both):
                s[1] = x[HD:]
        else:
            for s, m in zip(states, steps):
                s[1] = dot(s[1], m, precision=full)
        if iteration < NEWTON - 1:
            for s, x, m in zip(states, halfway, steps):
                s[0] = dot(x, m, precision=full)
    for (i, j), s in zip(places, states):
        mix = s[1] * s[2]
        coarse = mix.astype(jnp.bfloat16)
        fine = (mix - coarse.astype(jnp.float32)).astype(jnp.bfloat16)
        rows, lanes = slice(64 * (j // 2), 64 * (j // 2) + 64), slice(128 * (j % 2), 128 * (j % 2) + 128)
        out[i, rows, lanes] = jnp.concatenate([coarse, fine], axis=1)


def newton(mine, theirs, sums, after=()):
    flat = [part for group in sums for part in group]
    operands = [mine, theirs, *flat]
    return launch(
        functools.partial(newton_kernel, [len(group) for group in sums]),
        operands,
        [jax.ShapeDtypeStruct((mine.shape[0], 2 * HD, 256), jnp.bfloat16)]
        + [jax.ShapeDtypeStruct(group[0].shape, group[0].dtype) for group in sums],
        "newton",
        cost=3.5,
        specs=[full(a) for a in operands],
        after=after,
    )


def update_kernel(
    n, head, scal, g0, g1, g2, g3, q0, q1, q2, q3, momenta, native_momenta, native, *refs
):
    grads, weights, moved, mixing, first, second, steps = refs[-7:]
    place_of = members_of(head)

    @pl.when((pl.program_id(0) == 0) & (pl.program_id(1) == 0))
    def _():
        mixing[...] = jnp.zeros_like(mixing)

    @pl.when(pl.program_id(1) == 0)
    def _():
        for r, q in enumerate((q0, q1, q2, q3)):
            for j in range(4):
                at = slice(HD * (j // 2), HD * (j // 2) + HD), slice(128 * (j % 2), 128 * (j % 2) + 128)
                wide = q[(0,) * (len(q.shape) - 2) + at].astype(jnp.float32)
                other = pltpu.roll(wide, HD, 1)
                below = low_lanes(HD) == (j % 2 == 0)
                rows = slice(j * HD, (j + 1) * HD)
                lanes = slice(128 * (j // 2), 128 * (j // 2) + 128)
                pair = (wide, other) if j % 2 == 0 else (other, wide)
                for level in range(2):
                    part = jnp.where(below, pair[level], 0.0)
                    mixing[r, level, rows, lanes] = part.astype(jnp.bfloat16)

    low = low_lanes(n)
    for r, piece in enumerate((g0, g1, g2, g3)):
        place = scal[1] ^ r
        grad = piece[(0,) * (len(piece.shape) - 2)].astype(jnp.float32)
        update = 1.95 * grad + 0.9025 * momenta[place]
        coarse = update.astype(jnp.bfloat16)
        fine = (update - coarse.astype(jnp.float32)).astype(jnp.bfloat16)
        settled = dot(coarse, mixing[r, 0]) + dot(coarse, mixing[r, 1]) + dot(fine, mixing[r, 0])
        for half in range(2):
            k = 2 * r + half
            first[k] = grad[:, half * 128 : (half + 1) * 128]
            second[k] = settled[:, half * 128 : (half + 1) * 128]
            for source, target in ((first, grads), (second, steps)):
                even = source[k, pl.ds(0, n, stride=2), :]
                odd = source[k, pl.ds(1, n, stride=2), :]
                lines = (
                    jnp.where(low, even, pltpu.roll(odd, 64, 1)),
                    jnp.where(low, pltpu.roll(even, 64, 1), odd),
                )
                for w in range(2):
                    group, line = place_of(place, 2 * half + w)
                    target[group, pl.ds(line, n, stride=8), :] = lines[w]
    moved[...] = momentum_decay * native_momenta[...] + grads[...]
    weight = native[...]
    weights[...] = weight - muon_rate * (4.0 * steps[...] + weight_decay * weight)


def update(
    first, scal, own, far, mix, mix_far, beside, momenta, native_momenta, native, before=(), after=(), n=128
):
    chunks = own.shape[0]
    block = pl.BlockSpec((2, 8 * n, 128), lambda k, i: (first + k, i, 0))
    piece = pl.BlockSpec((1, 2 * n, 256), lambda k, i: (k, i, 0))
    factor = pl.BlockSpec((1, 2 * HD, 256), lambda k, i: (k, 0, 0))
    pieces, factors = [piece, None, piece, None], [factor, None, factor, None]
    for r in (0, 1):
        pieces[2 * r + 1] = pl.BlockSpec((1, 1, 2 * n, 256), lambda k, i, r=r: (r, k, i, 0))
        factors[2 * r + 1] = pl.BlockSpec((1, 1, 2 * HD, 256), lambda k, i, r=r: (r, k, 4, 0))
    grads, mixes = [own, beside, far, beside], [mix, beside, mix_far, beside]
    return launch(
        functools.partial(update_kernel, n, first == 0),
        [scal, *grads, *mixes, momenta, native_view(native_momenta), native_view(native), *before],
        [jax.ShapeDtypeStruct((6, 2048, 128), jnp.float32)] * 3,
        "update",
        specs=[mem(pltpu.SMEM)]
        + pieces
        + factors
        + [pl.BlockSpec((4, 2 * n, 256), lambda k, i: (k, i, 0)), block, block]
        + [mem(pl.ANY)] * len(before),
        after=after,
        vmem=24,
        cost=0.5 * chunks,
        grid=(chunks, 256 // n),
        out_specs=[block] * 3,
        scratch_shapes=[
            pltpu.VMEM((4, 2, 256, 256), jnp.bfloat16),
            pltpu.VMEM((8, 2 * n, 128), jnp.float32),
            pltpu.VMEM((8, 2 * n, 128), jnp.float32),
            pltpu.VMEM((2, 8 * n, 128), jnp.float32),
        ],
        input_output_aliases={12 + i: i for i in range(len(before))},
    )


def whole_device(
    inputs, cotangent, matrices, momenta, small, small_first, small_second, segments, positions
):
    blk_at = lax.axis_index("blk")
    ctx_at = lax.axis_index("ctx")
    tp_at = lax.axis_index("tp")
    scal = jnp.stack([blk_at, ctx_at, tp_at]).astype(jnp.int32)
    sequences, local_rows, width = inputs.shape
    tokens = sequences * local_rows
    both = ("blk", "ctx")
    f32, bf16 = jnp.float32, jnp.bfloat16
    shaped = jax.ShapeDtypeStruct

    def hop(values, by):
        return lax.ppermute(values, both, [(i, i ^ by) for i in range(8)])

    def hop_tp(values, by):
        return lax.ppermute(values, "tp", [(i, i ^ by) for i in range(4)])

    def tied(values, *results):
        return lax.optimization_barrier((values, *results))[0]

    def spread(piece):
        c = hop(piece, 2)
        return [piece, hop(piece, 1), c, hop(c, 1)]

    x = inputs.reshape(tokens, width)
    cot = cotangent.reshape(tokens, width)
    norms = small[: 4 * width].reshape(4, width)
    qkv_start = 6 * width + tp_at * 4 * 3 * HD
    qkv_bias = lax.dynamic_slice_in_dim(small, qkv_start, 4 * 3 * HD).reshape(4, 3 * HD)
    qkv_bias = jnp.pad(qkv_bias, ((0, 0), (0, HD)))
    unit_start = 6 * width + H * 3 * HD + tp_at * 1024
    unit_bias = lax.dynamic_slice_in_dim(small, unit_start, 1024).reshape(4, 256)
    lane = jnp.arange(128) % HD
    frequency = rope_base ** (-2.0 * (lane % 8).astype(f32) / ROTARY)
    angles = positions.astype(f32).reshape(tokens, 1) * frequency
    cosine = jnp.where(lane < ROTARY, jnp.cos(angles), 1.0)
    sign = jnp.where(lane < 8, -1.0, jnp.where(lane < ROTARY, 1.0, 0.0))
    sine = jnp.sin(angles) * sign

    head_weights, mine = relayout(scal, matrices, bf16, 0, 1, mine=True)
    first_hop = hop(mine, 4)
    unit_weights, mine_units = relayout(scal, matrices, bf16, 1, 2, mine=True, after=(mine,))
    first_hop = tied(first_hop, mine_units)
    other_heads = spread(first_hop)
    units_near = hop(tied(mine_units, first_hop), 4)
    x_beside = hop(x, 1)
    cot_beside = hop(cot, 1)

    send = launch(
        project_kernel,
        [scal, x, cot, norms, qkv_bias, cosine, sine, head_weights]
        + [piece[0] for piece in other_heads],
        shaped((8, local_rows, 256), bf16),
        "project",
        after=(units_near,),
    )
    arrived = lax.all_to_all(send, both, split_axis=0, concat_axis=0, tiled=True)
    (piled_heads,) = relayout(scal, momenta, f32, 0, 1, after=(send,))
    units_far = hop(units_near, 2)
    units_beside = hop(units_near, 1)
    documents = lax.dynamic_index_in_dim(segments, blk_at, 0, keepdims=False)
    length = documents.shape[0]
    attended = launch(
        attention_kernel,
        [arrived.reshape(length, 256), documents.reshape(length, 1)],
        shaped((length, 256), bf16),
        "attention",
        vmem=20,
        cost=6,
        specs=[full(arrived.reshape(length, 256)), pl.BlockSpec((length, 1), lambda *_: (0, 0))],
        after=(piled_heads,),
        scratch_shapes=[pltpu.VMEM((length, HD), f32)] * 2,
    )
    back = lax.all_to_all(
        attended.reshape(8, local_rows, 256), both, split_axis=0, concat_axis=0, tiled=True
    )

    units_far = tied(units_far, attended)
    other_units = [units_near, units_beside, units_far, hop(units_far, 1)]
    ff_branch, ff_part, unit_keep, unit_send, unit_sums, norm_two, cot_sums = launch(
        feed_forward_kernel,
        [scal, x, cot, norms, unit_bias, unit_weights, *other_units],
        [
            shaped((tokens, width), f32),
            shaped((tokens, width), f32),
            shaped((2, 2, tokens, 256), bf16),
            shaped((2, 2, tokens, 256), bf16),
            shaped((4, 256), f32),
            shaped((2, width), f32),
            shaped((1, width), f32),
        ],
        "feed_forward",
        vmem=20,
        cost=0.3,
        after=(attended,),
    )
    head_keep, head_send, qkv_sums = launch(
        turn_kernel,
        [scal, cosine, sine, back],
        [shaped((2, tokens, 256), bf16)] * 2 + [shaped((4, 256), f32)],
        "turn",
        cost=2,
        after=(unit_sums,),
    )
    in_keep, in_send, down_keep, down_send = launch(
        unit_grads_kernel,
        [scal, x, x_beside, cot, cot_beside, norms, unit_keep, hop(unit_send, 1)],
        [shaped((2, 512, 256), bf16)] * 4,
        "unit_grads",
        cost=3.5,
        after=(qkv_sums,),
    )
    sums = [norm_two, cot_sums, unit_sums, qkv_sums]
    near, far, totals = launch(
        gather_kernel,
        [scal, x, norms, head_keep, head_send, head_weights, *other_heads, ff_branch, ff_part, *sums],
        [shaped((2, 2, 64, width), bf16)] * 2 + [shaped((8, 8, 256), f32)],
        "gather",
        cost=0.5,
        after=(in_keep,),
        scratch_shapes=[pltpu.VMEM((4, 2, 64, width), bf16)],
    )
    came = hop_tp(far, 1)
    totals_shape = shaped((8, 8, 256), f32)
    a_keep, a_send, b_keep, b_send, totals = launch(
        head_grads_kernel,
        [
            scal, x, x_beside, cot, cot_beside, norms, head_keep, hop(head_send, 1),
            totals, hop(totals, 1),
        ],
        [shaped((2, 256, 256), bf16)] * 4 + [totals_shape],
        "head_grads",
        cost=0.5,
    )
    (piled_units,) = relayout(scal, momenta, f32, 1, 2, after=(a_keep,))
    a_came, b_came = hop(a_send, 4), hop(b_send, 2)
    operands = [in_keep, hop(in_send, 4), down_keep, hop(down_send, 2)]
    own, in_send, down_send = launch(
        combine_kernel,
        operands,
        [shaped((2, 512, 256), bf16)] + [shaped((1, 512, 256), bf16)] * 2,
        "combine",
        specs=[full(a) for a in operands],
        cost=2,
        after=(piled_units,),
    )
    in_came, down_came = hop(in_send, 2), hop(down_send, 4)
    kept, passed = launch(
        add_kernel,
        [near, came],
        [shaped((2, 64, width), bf16)] * 2,
        "add",
        specs=[full(near)] * 2,
        cost=1,
        after=(in_send,),
    )
    passed = hop_tp(passed, 2)
    operands = [a_keep, a_came, b_keep, b_came, totals, hop(totals, 4)]
    a_own, a_send, b_own, b_send, totals = launch(
        combine_heads_kernel,
        operands,
        [shaped((256, 256), bf16)] * 4 + [totals_shape],
        "combine_heads",
        specs=[full(a) for a in operands],
        after=(kept,),
    )
    a_came, b_came = hop(a_send, 2), hop(b_send, 4)
    unit_sum, unit_grams, totals = gram_of(
        unit_gram_kernel,
        own,
        [in_came, down_came],
        piled_units,
        scal,
        [totals, hop(totals, 2)],
        [totals_shape],
        after=(a_own,),
    )
    unit_theirs = hop(unit_grams, 4)
    unit_far = hop(unit_sum, 2)
    head_sum, head_grams = gram_of(
        head_gram_kernel,
        a_own,
        [a_came, b_own, b_came],
        piled_heads,
        scal,
        [],
        [],
        after=(unit_sum,),
    )
    head_theirs = hop(head_grams, 4)
    head_far = hop(head_sum, 2)
    unit_mix, totals, total = newton(
        unit_grams, unit_theirs, [(totals, hop_tp(totals, 1)), (kept, passed)], after=(head_sum,)
    )
    total_far, total_beside = hop_tp(total, 2), hop_tp(total, 1)
    unit_mix_far = hop(unit_mix, 2)
    head_mix, totals = newton(
        head_grams, head_theirs, [(totals, hop_tp(totals, 2))], after=(unit_mix, unit_far)
    )
    head_mix_far = hop(head_mix, 2)

    def to_beside(*pieces):
        return hop(jnp.stack([jnp.concatenate(pair, axis=1) for pair in pieces]), 1)

    beside = to_beside((unit_sum, unit_mix), (unit_far, tied(unit_mix_far, head_mix)))
    before = update(
        1, scal, unit_sum, unit_far, unit_mix, unit_mix_far, beside, piled_units, momenta, matrices,
        after=(head_mix,),
    )
    head_far, head_mix_far = tied((head_far, head_mix_far), before[0])
    beside = to_beside((head_sum, head_mix), (head_far, head_mix_far))
    outs = update(
        0, scal, head_sum, head_far, head_mix, head_mix_far, beside, piled_heads, momenta, matrices,
        before,
    )
    total_far = tied(total_far, before[0])
    bias = (small[4 * width : 5 * width] + small[5 * width : 6 * width]).reshape(1, width)
    block_output, input_grad = launch(
        finish_rows_kernel,
        [
            scal,
            x.reshape(4, 64, width),
            cot.reshape(4, 64, width),
            bias,
            total,
            total_beside,
            total_far,
            hop_tp(total_far, 1),
        ],
        [shaped((4, 64, width), f32)] * 2,
        "finish_rows",
        cost=2,
        after=(outs[0],),
    )
    totals = tied(totals, before[0])
    cot_total = totals[2, :4].reshape(-1) * 0.25
    small_grads = jnp.concatenate(
        [
            totals[:2].reshape(-1),
            cot_total,
            cot_total,
            totals[3:7, :4, : 3 * HD].reshape(-1),
            totals[3:7, 4:].reshape(-1),
        ]
    )
    return (
        block_output.reshape(inputs.shape),
        input_grad.reshape(inputs.shape),
        native_back(outs[0]),
        native_back(outs[1]),
        native_back(outs[2]),
        small_grads,
        *small_step(small, small_first, small_second, small_grads),
    )


def small_step(small, small_first, small_second, small_grads):
    new_first = adam_first * small_first + (1.0 - adam_first) * small_grads
    new_second = adam_second * small_second + (1.0 - adam_second) * small_grads * small_grads
    corrected = new_first / (1.0 - adam_first**STEP)
    spread = jnp.sqrt(new_second / (1.0 - adam_second**STEP))
    new_small = small - small_rate * corrected / (spread + adam_epsilon)
    return new_first, new_second, new_small


def solution(mesh):
    in_specs = (
        P(None, ("blk", "ctx"), None),
        P(None, ("blk", "ctx"), None),
        P("tp", "blk"),
        P("tp", "blk"),
        P(),
        P(),
        P(),
        P(),
        P(None, ("blk", "ctx")),
    )
    out_specs = (
        P(None, ("blk", "ctx"), None),
        P(None, ("blk", "ctx"), None),
        P("tp", "blk"),
        P("tp", "blk"),
        P("tp", "blk"),
        P(),
        P(),
        P(),
        P(),
    )
    one_each = mesh.shape["blk"] == SEQS and mesh.shape["ctx"] * mesh.shape["tp"] == H
    one_each = one_each and mesh.shape["tp"] == 4
    return jax.shard_map(
        whole_device if one_each else on_device, mesh=mesh, in_specs=in_specs, out_specs=out_specs, check_vma=False
    )
```

```python
import functools

import jax
import jax.numpy as jnp
from jax import lax
from jax.experimental import pallas as pl
from jax.experimental.pallas import tpu as pltpu
from jax.sharding import PartitionSpec as P

MODEL_DIM = 1024
H = 16
HD = 64
FF = 4096
ROTARY = 16
NEWTON = 5
STEP = 10
SEQS = 2


norm_epsilon = 1e-05
rope_base = 10000.0
masked_score = -1e30
momentum_decay = 0.95
muon_rate = 0.2
weight_decay = 0.01
muon_epsilon = 1e-07
quintic = (3.4445, -4.775, 2.0315)
adam_first = 0.9
adam_second = 0.95
adam_epsilon = 1e-08
small_rate = 0.2


def passed_along(x, axis, by):
    devices = lax.axis_size(axis)
    pairs = [(i, i + by) for i in range(devices) if 0 <= i + by < devices]
    return lax.ppermute(x, axis, pairs)


def shifted(x, axis, by):
    devices = lax.axis_size(axis)
    return lax.ppermute(x, axis, [(i, (i + by) % devices) for i in range(devices)])


def as_sent(x):

    def short(part):
        return part.astype(jnp.bfloat16) if part.dtype == jnp.float32 else part

    return jax.tree.map(short, x)


def layer_norm(values, scaling, offset):
    centre = jnp.mean(values, axis=-1, keepdims=True)
    centred = values - centre
    spread = jnp.mean(centred * centred, axis=-1, keepdims=True)
    return centred * lax.rsqrt(spread + norm_epsilon) * scaling + offset


def rope_tables(positions):
    halfway = ROTARY // 2
    frequency = rope_base ** (-2.0 * jnp.arange(halfway, dtype=jnp.float32) / ROTARY)
    angles = positions.astype(jnp.float32)[..., None] * frequency
    return (jnp.cos(angles)[:, :, None, :], jnp.sin(angles)[:, :, None, :])


def rotate(values, cosine, sine):
    halfway = ROTARY // 2
    former = values[..., :halfway]
    latter = values[..., halfway:ROTARY]
    return jnp.concatenate(
        [former * cosine - latter * sine, latter * cosine + former * sine, values[..., ROTARY:]],
        axis=-1,
    )


def exact_gelu(values):
    return jax.nn.gelu(values, approximate=False)


def newton_schulz(blocks):
    frobenius = jnp.sqrt(jnp.sum(blocks * blocks, axis=(1, 2), keepdims=True))
    current = blocks / (frobenius + muon_epsilon)
    linear_term, square_term, cubic_term = quintic
    for iteration in range(NEWTON):
        gram_matrix = jnp.einsum("mde,mdf->mef", current, current, precision=lax.Precision.HIGHEST)
        polynomial = square_term * gram_matrix + cubic_term * jnp.einsum(
            "mef,mfg->meg", gram_matrix, gram_matrix, precision=lax.Precision.HIGHEST
        )
        current = linear_term * current + jnp.einsum(
            "mde,mef->mdf", current, polynomial, precision=lax.Precision.HIGHEST
        )
    return current


def to_heads(values):
    return lax.all_to_all(values, "ctx", split_axis=3, concat_axis=1, tiled=True)


def to_positions(values):
    return lax.all_to_all(values, "ctx", split_axis=1, concat_axis=3, tiled=True)


def pass_keys(pair):
    return passed_along(pair, "blk", 1)


def pass_grads(pair_grad):
    return shifted(pair_grad.astype(jnp.bfloat16), "blk", 1).astype(pair_grad.dtype)


def allowed_pairs(segments, query_block, key_block, block_rows):
    query_place = query_block * block_rows + jnp.arange(block_rows, dtype=jnp.int32)
    key_place = key_block * block_rows + jnp.arange(block_rows, dtype=jnp.int32)
    query_doc = lax.dynamic_slice_in_dim(segments, query_block * block_rows, block_rows, 1)
    key_doc = lax.dynamic_slice_in_dim(segments, key_block * block_rows, block_rows, 1)
    causal = key_place[None, :] <= query_place[:, None]
    return (causal[None] & (query_doc[:, :, None] == key_doc[:, None, :]))[:, None]


def masked_scores(queries, keys, allowed):
    score_scale = HD ** (-0.5)
    scores = (
        jnp.einsum("sqhe,skhe->shqk", queries, keys, preferred_element_type=jnp.float32)
        * score_scale
    )
    return jnp.where(allowed, scores, masked_score)


def on_device(
    inputs, cotangent, matrices, momenta, small, small_first, small_second, segments, positions
):
    tensor_size = lax.axis_size("tp")
    cycle_size = lax.axis_size("blk")
    context_size = lax.axis_size("ctx")
    tensor_index = lax.axis_index("tp")
    cycle_index = lax.axis_index("blk")
    sequences, local_rows, model_width = inputs.shape
    per_group = matrices.shape[0]
    head_count = H // tensor_size
    unit_blocks = FF // HD // tensor_size
    block_rows = local_rows * context_size
    gathered = lax.all_gather(matrices.astype(jnp.bfloat16), "blk", axis=1, tiled=True).reshape(
        per_group, model_width, HD
    )
    query_key_value_weight = gathered[: 3 * head_count]
    projection_out_weight = gathered[3 * head_count : 4 * head_count]
    input_weight = gathered[4 * head_count : 4 * head_count + unit_blocks]
    down_projection_weight = gathered[4 * head_count + unit_blocks :]
    qkv_start = 6 * model_width + tensor_index * head_count * 3 * HD
    query_key_value_bias = lax.dynamic_slice_in_dim(small, qkv_start, head_count * 3 * HD).reshape(
        head_count, 3, HD
    )
    unit_start = 6 * model_width + H * 3 * HD + tensor_index * unit_blocks * HD
    hidden_unit_bias = lax.dynamic_slice_in_dim(small, unit_start, unit_blocks * HD).reshape(
        unit_blocks, HD
    )
    residual = inputs.astype(jnp.float32)

    def both_norms(values, gain_one, offset_one, gain_two, offset_two):
        return (layer_norm(values, gain_one, offset_one), layer_norm(values, gain_two, offset_two))

    (normed_one, normed_two), norm_back = jax.vjp(
        both_norms,
        residual,
        small[0:model_width],
        small[model_width : 2 * model_width],
        small[2 * model_width : 3 * model_width],
        small[3 * model_width : 4 * model_width],
    )
    first_input = normed_one.astype(jnp.bfloat16)
    second_input = normed_two.astype(jnp.bfloat16)
    projected = jnp.einsum(
        "pgk,jka->pgja", first_input, query_key_value_weight, preferred_element_type=jnp.float32
    )
    projected = projected.reshape(sequences, local_rows, 3, head_count, HD) + jnp.transpose(
        query_key_value_bias, (1, 0, 2)
    )
    cosine, sine = rope_tables(positions)

    def turn_pair(query_pre, key_pre):
        return (rotate(query_pre, cosine, sine), rotate(key_pre, cosine, sine))

    (query_turned, key_turned), turn_back = jax.vjp(
        turn_pair, projected[:, :, 0], projected[:, :, 1]
    )
    stacked = jnp.stack([query_turned, key_turned, projected[:, :, 2]], axis=2).astype(jnp.bfloat16)
    by_heads = to_heads(stacked)
    queries = by_heads[:, :, 0]
    head_local = queries.shape[2]

    def forward_visit(state, pair, source):
        row_max, row_total, weighted = state
        allowed = allowed_pairs(segments, cycle_index, source, block_rows)
        scores = masked_scores(queries, pair[:, :, 0], allowed)
        new_max = jnp.maximum(row_max, jnp.max(scores, axis=-1))
        weights = jnp.where(allowed, jnp.exp(scores - new_max[..., None]), 0.0)
        rescale = jnp.exp(row_max - new_max)
        row_total = row_total * rescale + jnp.sum(weights, axis=-1)
        weighted = weighted * rescale[..., None] + jnp.einsum(
            "shqk,skhe->shqe",
            weights.astype(jnp.bfloat16),
            pair[:, :, 1],
            preferred_element_type=jnp.float32,
        )
        return (new_max, row_total, weighted)

    def forward_hop(hop_index, carry):
        pair, state = carry
        source = (cycle_index - hop_index) % cycle_size
        state = forward_visit(state, pair, source)
        return (pass_keys(pair), state)

    start_state = (
        jnp.full((sequences, head_local, block_rows), masked_score, jnp.float32),
        jnp.zeros((sequences, head_local, block_rows), jnp.float32),
        jnp.zeros((sequences, head_local, block_rows, HD), jnp.float32),
    )
    pair, state = lax.fori_loop(0, cycle_size - 1, forward_hop, (by_heads[:, :, 1:], start_state))
    row_max, row_total, weighted = forward_visit(state, pair, (cycle_index + 1) % cycle_size)
    log_total = row_max + jnp.log(row_total)
    attended_rows = jnp.transpose(weighted / row_total[..., None], (0, 2, 1, 3))
    attention_result = to_positions(attended_rows.astype(jnp.bfloat16)[:, :, None])[:, :, 0]
    attention_branch = jnp.einsum(
        "roxu,xcu->roc", attention_result, projection_out_weight, preferred_element_type=jnp.float32
    )
    hidden_preactivation = (
        jnp.einsum("ptr,kra->ptka", second_input, input_weight, preferred_element_type=jnp.float32)
        + hidden_unit_bias
    )
    activated_hidden, gelu_back = jax.vjp(exact_gelu, hidden_preactivation)
    activated_reduced = activated_hidden.astype(jnp.bfloat16)
    perceptron_branch = jnp.einsum(
        "xkzp,zop->xko",
        activated_reduced,
        down_projection_weight,
        preferred_element_type=jnp.float32,
    )
    branches = lax.psum((attention_branch + perceptron_branch).astype(jnp.bfloat16), "tp").astype(
        jnp.float32
    )
    block_output = (
        residual
        + branches
        + small[4 * model_width : 5 * model_width]
        + small[5 * model_width : 6 * model_width]
    )
    act_grad = jnp.einsum(
        "ptr,kra->ptka", cotangent, down_projection_weight, preferred_element_type=jnp.float32
    )
    hidden_gradient = gelu_back(act_grad)[0].astype(jnp.bfloat16)
    down_grad = jnp.einsum(
        "gup,guzb->zpb", cotangent, activated_reduced, preferred_element_type=jnp.float32
    )
    in_grad = jnp.einsum(
        "gup,guzb->zpb", second_input, hidden_gradient, preferred_element_type=jnp.float32
    )
    second_grad = jnp.einsum(
        "xkzp,zop->xko", hidden_gradient, input_weight, preferred_element_type=jnp.float32
    )
    attended_grad = jnp.einsum(
        "pgk,jka->pgja", cotangent, projection_out_weight, preferred_element_type=jnp.float32
    ).astype(jnp.bfloat16)
    outproj_grad = jnp.einsum(
        "ztu,ztqi->qui", cotangent, attention_result, preferred_element_type=jnp.float32
    )
    grad_heads = to_heads(attended_grad[:, :, None])[:, :, 0]
    row_delta = jnp.transpose(
        jnp.sum(grad_heads.astype(jnp.float32) * attended_rows, axis=-1), (0, 2, 1)
    )

    def backward_visit(query_grad, pair, source):
        allowed = allowed_pairs(segments, cycle_index, source, block_rows)
        scores = masked_scores(queries, pair[:, :, 0], allowed)
        probabilities = jnp.where(allowed, jnp.exp(scores - log_total[..., None]), 0.0)
        value_grad = jnp.einsum(
            "shqk,sqhe->skhe",
            probabilities.astype(jnp.bfloat16),
            grad_heads,
            preferred_element_type=jnp.float32,
        )
        prob_grad = jnp.einsum(
            "sqhe,skhe->shqk", grad_heads, pair[:, :, 1], preferred_element_type=jnp.float32
        )
        score_grad = (probabilities * (prob_grad - row_delta[..., None])).astype(jnp.bfloat16)
        score_scale = HD ** (-0.5)
        query_grad = (
            query_grad
            + jnp.einsum(
                "shqk,skhe->sqhe", score_grad, pair[:, :, 0], preferred_element_type=jnp.float32
            )
            * score_scale
        )
        key_grad = (
            jnp.einsum("shqk,sqhe->skhe", score_grad, queries, preferred_element_type=jnp.float32)
            * score_scale
        )
        return (query_grad, jnp.stack([key_grad, value_grad], axis=2))

    def backward_hop(hop_index, carry):
        pair, pair_grad, query_grad = carry
        source = (cycle_index - hop_index) % cycle_size
        query_grad, visit_grad = backward_visit(query_grad, pair, source)
        return (pass_keys(pair), pass_grads(pair_grad + visit_grad), query_grad)

    zero_pair = jnp.zeros(by_heads[:, :, 1:].shape, jnp.float32)
    pair, pair_grad, query_grad = lax.fori_loop(
        0,
        cycle_size - 1,
        backward_hop,
        (by_heads[:, :, 1:], zero_pair, jnp.zeros(queries.shape, jnp.float32)),
    )
    query_grad, visit_grad = backward_visit(query_grad, pair, (cycle_index + 1) % cycle_size)
    pair_grad = pass_grads(pair_grad + visit_grad)
    head_grads = jnp.concatenate([query_grad[:, :, None], pair_grad], axis=2).astype(jnp.bfloat16)
    position_grads = to_positions(head_grads).astype(jnp.float32)
    query_pre_grad, key_pre_grad = turn_back((position_grads[:, :, 0], position_grads[:, :, 1]))
    projected_grad = jnp.stack(
        [query_pre_grad, key_pre_grad, position_grads[:, :, 2]], axis=2
    ).astype(jnp.bfloat16)
    flattened_gradient = projected_grad.reshape(sequences, local_rows, 3 * head_count, HD)
    query_key_value_gradient = jnp.einsum(
        "ztu,ztqi->qui", first_input, flattened_gradient, preferred_element_type=jnp.float32
    )
    first_grad = jnp.einsum(
        "roxu,xcu->roc",
        flattened_gradient,
        query_key_value_weight,
        preferred_element_type=jnp.float32,
    )
    input_part, gain_one_grad, offset_one_grad, gain_two_grad, offset_two_grad = norm_back(
        (first_grad, second_grad)
    )
    input_grad = cotangent.astype(jnp.float32) + lax.psum(
        input_part.astype(jnp.bfloat16), "tp"
    ).astype(jnp.float32)
    owner_share = jnp.where(tensor_index == 0, 1.0, 0.0).astype(jnp.float32)
    bias_grad = jnp.sum(cotangent.astype(jnp.float32), axis=(0, 1)) * owner_share
    qkv_bias_grad = jnp.transpose(
        jnp.sum(projected_grad.astype(jnp.float32), axis=(0, 1)), (1, 0, 2)
    ).reshape(-1)
    unit_bias_grad = jnp.sum(hidden_gradient.astype(jnp.float32), axis=(0, 1)).reshape(-1)
    local_small = jnp.concatenate(
        [
            gain_one_grad,
            offset_one_grad,
            gain_two_grad,
            offset_two_grad,
            bias_grad,
            bias_grad,
            jnp.zeros((small.shape[0] - 6 * model_width,), jnp.float32),
        ]
    )
    local_small = lax.dynamic_update_slice_in_dim(local_small, qkv_bias_grad, qkv_start, 0)
    local_small = lax.dynamic_update_slice_in_dim(local_small, unit_bias_grad, unit_start, 0)
    small_grads = lax.psum(local_small, ("blk", "ctx", "tp"))
    local_grad = jnp.concatenate(
        [query_key_value_gradient, outproj_grad, in_grad, down_grad], axis=0
    ).reshape(per_group, -1)
    shares = lax.psum_scatter(
        local_grad.astype(jnp.bfloat16), "blk", scatter_dimension=1, tiled=True
    )
    matrix_grads = lax.psum(shares, "ctx").astype(jnp.float32)
    new_momenta = momentum_decay * momenta + matrix_grads
    update = matrix_grads + momentum_decay * new_momenta
    per_owner = per_group // cycle_size
    sectioned = update.reshape(cycle_size, per_owner, update.shape[1])
    pieces = lax.all_to_all(
        sectioned.astype(jnp.bfloat16), "blk", split_axis=0, concat_axis=2, tiled=True
    ).astype(sectioned.dtype)
    piece_count = pieces.shape[1]
    settled_blocks = newton_schulz(pieces.reshape(piece_count, MODEL_DIM, HD)).reshape(
        1, piece_count, MODEL_DIM * HD
    )
    settled = lax.all_to_all(
        as_sent(settled_blocks), "blk", split_axis=2, concat_axis=0, tiled=True
    ).astype(settled_blocks.dtype)
    orthogonal_all = settled.reshape(per_group, -1)
    muon_scale = max(1.0, MODEL_DIM / HD) ** 0.5
    new_matrices = matrices - muon_rate * (muon_scale * orthogonal_all + weight_decay * matrices)
    new_first = adam_first * small_first + (1.0 - adam_first) * small_grads
    new_second = adam_second * small_second + (1.0 - adam_second) * small_grads * small_grads
    corrected = new_first / (1.0 - adam_first**STEP)
    spread = jnp.sqrt(new_second / (1.0 - adam_second**STEP))
    new_small = small - small_rate * corrected / (spread + adam_epsilon)
    return (
        block_output,
        input_grad,
        matrix_grads,
        new_matrices,
        new_momenta,
        small_grads,
        new_first,
        new_second,
        new_small,
    )


def native_view(array):
    rows, columns = array.shape
    tiled = array.reshape(rows // 8, 8, columns // 128, 128).transpose(0, 2, 1, 3)
    return tiled.reshape(rows // 8, columns // 16, 128)


def native_back(array):
    groups, rows, _ = array.shape
    return array.reshape(groups, rows // 8, 8, 128).transpose(0, 2, 1, 3).reshape(groups * 8, rows * 16)


def members_of(head):
    if head:
        return lambda piece, j: (j // 2, 4 * (j % 2) + piece)
    return lambda piece, j: (piece // 2, 4 * (piece % 2) + j)


def mem(kind=pltpu.VMEM):
    return pl.BlockSpec(memory_space=kind)


def limits(mebibytes):
    return pltpu.CompilerParams(vmem_limit_bytes=mebibytes << 20)


def low_lanes(rows):
    return lax.broadcasted_iota(jnp.int32, (rows, 128), 1) < HD


def dot(a, b, dims=((1,), (0,)), precision=None):
    return lax.dot_general(
        a, b, (dims, ((), ())), precision=precision, preferred_element_type=jnp.float32
    )


NT = ((1,), (1,))
TN = ((0,), (0,))


def corner(array):
    block = (1,) * (array.ndim - 2) + (min(16, array.shape[-2]), 128)
    return pl.BlockSpec(block, lambda *_: (0,) * array.ndim)


def takes(microseconds):
    return pl.CostEstimate(
        flops=int(microseconds * 1.15e9), transcendentals=0, bytes_accessed=int(1e6)
    )


def in_hbm(array):
    if array.size * array.dtype.itemsize < 1 << 21:
        return array
    return pltpu.with_memory_space_constraint(array, pltpu.HBM)


def out_hbm(shape):
    if shape.size * shape.dtype.itemsize < 1 << 20:
        return shape
    return pltpu.HBM(shape.shape, shape.dtype)


def full(array):
    return pl.BlockSpec(array.shape, lambda *_: (0,) * array.ndim)


def launch(kernel, operands, out_shapes, name, specs=None, after=(), vmem=16, cost=3, **more):
    taken = len(operands)
    body = kernel
    if after:
        body = lambda *refs: kernel(*refs[:taken], *refs[taken + len(after) :])
    if specs is None:
        specs = [mem(pltpu.SMEM)] + [full(a) for a in operands[1:]]
    if "out_specs" not in more:
        more["out_specs"] = jax.tree.map(full, out_shapes)
    more.setdefault("grid", (1,))
    return pl.pallas_call(
        body,
        in_specs=list(specs) + [corner(a) for a in after],
        out_shape=jax.tree.map(out_hbm, out_shapes),
        compiler_params=limits(vmem),
        cost_estimate=takes(cost),
        name=name,
        **more,
    )(*map(in_hbm, operands), *map(in_hbm, after))


def relayout_kernel(n, first, count, scal, src, out, *refs):
    fetched, paired, packed, arrivals, departures = refs[-5:]
    low = low_lanes(n)
    place_of = members_of(first == 0)
    steps = [(k, i) for k in range(count) for i in range(256 // n)]

    def fetch(k, i, group):
        rows = pl.ds(i * 8 * n, 8 * n)
        return pltpu.make_async_copy(
            src.at[2 * first + 2 * k + group, rows],
            fetched.at[2 * k + group, rows],
            arrivals.at[2 * k + group, i],
        )

    def leave(k, i):
        rows = pl.ds(i * 2 * n, 2 * n)
        return pltpu.make_async_copy(
            packed.at[pl.ds(4 * k, 4), rows], out.at[pl.ds(4 * k, 4), rows], departures.at[k, i]
        )

    for k, i in steps:
        for group in range(2):
            fetch(k, i, group).start()
    for k, i in steps:
        for group in range(2):
            fetch(k, i, group).wait()
        for piece in range(4):
            for half in range(2):
                pair = []
                for j in (2 * half, 2 * half + 1):
                    group, line = place_of(piece, j)
                    rows = pl.ds(i * 8 * n + line, n, stride=8)
                    pair.append(fetched[2 * k + group, rows, :])
                a, b = pair
                at = 2 * piece + half
                paired[at, pl.ds(0, n, stride=2), :] = jnp.where(low, a, pltpu.roll(b, 64, 1))
                paired[at, pl.ds(1, n, stride=2), :] = jnp.where(low, pltpu.roll(a, 64, 1), b)
                lanes = slice(half * 128, (half + 1) * 128)
                rows = slice(i * 2 * n, (i + 1) * 2 * n)
                packed[4 * k + piece, rows, lanes] = paired[at].astype(packed.dtype)
        leave(k, i).start()
    if len(refs) == 6:
        for k in range(count):
            refs[0][k] = packed[4 * k + scal[1]]
    for k, i in steps:
        leave(k, i).wait()


def relayout(scal, array, dtype, first, count, mine=False, n=128, after=()):
    shapes = [jax.ShapeDtypeStruct((4 * count, 512, 256), dtype)]
    specs = [mem(pl.ANY)]
    if mine:
        shapes.append(jax.ShapeDtypeStruct((count, 512, 256), dtype))
        specs.append(full(shapes[1]))
    return launch(
        functools.partial(relayout_kernel, n, first, count),
        [scal, native_view(array)],
        shapes,
        "relayout",
        specs=[mem(pltpu.SMEM), mem(pl.ANY)],
        after=after,
        cost=0.2 * count,
        vmem=14,
        out_specs=specs,
        scratch_shapes=[
            pltpu.VMEM((2 * count, 2048, 128), jnp.float32),
            pltpu.VMEM((8, 2 * n, 128), jnp.float32),
            pltpu.VMEM((4 * count, 512, 256), dtype),
            pltpu.SemaphoreType.DMA((2 * count, 256 // n)),
            pltpu.SemaphoreType.DMA((count, 256 // n)),
        ],
    )


def add_up(groups):
    for parts, target in groups:
        values = [part[...].astype(jnp.float32) for part in parts]
        while len(values) > 1:
            values = [sum(values[i : i + 2]) for i in range(0, len(values), 2)]
        if isinstance(target, list):
            for i, part in enumerate(target):
                part[...] = values[0][i].astype(part.dtype)
        else:
            target[...] = values[0].astype(target.dtype)


def grouped(refs, counts, targets):
    refs = iter(refs)
    return [([next(refs) for _ in range(n)], target) for n, target in zip(counts, targets)]


def normalized(x):
    centred = x - jnp.mean(x, axis=-1, keepdims=True)
    spread = jnp.mean(centred * centred, axis=-1, keepdims=True)
    root = lax.rsqrt(spread + norm_epsilon)
    return centred * root, root


def halves(values, first):
    left, right = values[:, :512], values[:, 512:]
    return jnp.where(first, left, right), jnp.where(first, right, left)


def whole(own, other, first):
    return jnp.concatenate([jnp.where(first, own, other), jnp.where(first, other, own)], axis=1)


def norm_back(grad, hat, root, gain):
    scaled = grad * gain
    along = jnp.mean(scaled * hat, axis=-1, keepdims=True)
    return root * (scaled - jnp.mean(scaled, axis=-1, keepdims=True) - hat * along)


def turned(values, cosine, sine):
    lane = lax.broadcasted_iota(jnp.int32, values.shape, 1) % HD
    other = jnp.where(lane < 8, pltpu.roll(values, 120, 1), pltpu.roll(values, 8, 1))
    return values * cosine + other * sine


def project_kernel(scal, x, cot, norms, bias, cosine, sine, own, r0, r1, r2, r3, send):
    first = scal[0] == 0
    hat, _ = normalized(x[...].astype(jnp.float32))
    h = (hat * norms[0:1] + norms[1:2]).astype(jnp.bfloat16)
    h_own, h_other = halves(h, first)
    c_own, c_other = halves(cot[...], first)
    tokens = h.shape[0]
    low = low_lanes(tokens)
    for r, other in enumerate((r0, r1, r2, r3)):
        head = scal[1] ^ r
        mine = own[head]
        theirs = other[...]
        pre = dot(h_own, mine) + dot(h_other, theirs) + bias[pl.ds(head, 1), :]
        back = dot(c_own, mine[:, 128:]) + dot(c_other, theirs[:, 128:])
        left = turned(pre[:, :128], cosine[...], sine[...]).astype(jnp.bfloat16)
        right = jnp.where(low, pre[:, 128:], back).astype(jnp.bfloat16)
        for s in range(2):
            rows = slice(128 * s, 128 * s + 128)
            send[4 * s + head, :, :128] = left[rows]
            send[4 * s + head, :, 128:] = right[rows]


def attention_kernel(rows_ref, seg, out, key_total, value_total):
    key_total[...] = jnp.zeros_like(key_total)
    value_total[...] = jnp.zeros_like(value_total)
    step = 256
    for block in range(rows_ref.shape[0] // step):
        rows = slice(block * step, (block + 1) * step)
        n = (block + 1) * step
        query = rows_ref[rows, 0:HD] * jnp.bfloat16(0.125)
        grad = rows_ref[rows, 3 * HD : 4 * HD]
        keys = rows_ref[0:n, HD : 2 * HD]
        values = rows_ref[0:n, 2 * HD : 3 * HD]
        scores = dot(query, keys, NT)
        query_place = block * step + lax.broadcasted_iota(jnp.int32, (step, n), 0)
        key_place = lax.broadcasted_iota(jnp.int32, (step, n), 1)
        allowed = (key_place <= query_place) & (key_place >= seg[rows, :])
        scores = jnp.where(allowed, scores, masked_score)
        weights = jnp.exp(scores - jnp.max(scores, axis=-1, keepdims=True))
        weights = jnp.where(allowed, weights, 0.0)
        weights = weights * (1.0 / jnp.sum(weights, axis=-1, keepdims=True))
        short = weights.astype(jnp.bfloat16)
        attended = dot(short, values)
        weight_grad = dot(grad, values, NT)
        delta = jnp.sum(weights * weight_grad, axis=-1, keepdims=True)
        score_grad = (weights * (weight_grad - delta)).astype(jnp.bfloat16)
        query_grad = dot(score_grad, keys) * 0.125
        key_total[0:n, :] += dot(score_grad, query, TN)
        value_total[0:n, :] += dot(short, grad, TN)
        out[rows, 0:HD] = query_grad.astype(jnp.bfloat16)
        out[rows, 3 * HD : 4 * HD] = attended.astype(jnp.bfloat16)
    out[:, HD : 2 * HD] = key_total[...].astype(jnp.bfloat16)
    out[:, 2 * HD : 3 * HD] = value_total[...].astype(jnp.bfloat16)


def feed_forward_kernel(
    scal, x, cot, norms, bias, weights, r0, r1, r2, r3,
    branch, input_part, keep, send, hidden_sums, norm_grads, cot_sums,
):
    first = scal[0] == 0
    hat, root = normalized(x[...].astype(jnp.float32))
    h = (hat * norms[2:3] + norms[3:4]).astype(jnp.bfloat16)
    h_own, h_other = halves(h, first)
    c_own, c_other = halves(cot[...], first)
    cot_sums[...] = jnp.sum(cot[...].astype(jnp.float32), axis=0, keepdims=True)
    outs = [0.0] * 4
    for r, other in enumerate((r0, r1, r2, r3)):
        piece = scal[1] ^ r
        in_own, in_other = weights[piece], other[0]
        down_own, down_other = weights[4 + piece], other[1]
        pre = dot(h_own, in_own) + dot(h_other, in_other) + bias[pl.ds(piece, 1), :]
        cumulative = 0.5 * (1.0 + lax.erf(pre * 0.7071067811865476))
        slope = cumulative + pre * (0.3989422804014327 * jnp.exp(-0.5 * pre * pre))
        act = (pre * cumulative).astype(jnp.bfloat16)
        act_grad = dot(c_own, down_own) + dot(c_other, down_other)
        grad = (act_grad * slope).astype(jnp.bfloat16)
        hidden_sums[pl.ds(piece, 1), :] = jnp.sum(
            grad.astype(jnp.float32), axis=0, keepdims=True
        )
        outs[0] += dot(act, down_own, NT)
        outs[1] += dot(act, down_other, NT)
        outs[2] += dot(grad, in_own, NT)
        outs[3] += dot(grad, in_other, NT)
        target = send if r % 2 else keep
        target[r // 2, 0] = grad
        target[r // 2, 1] = act
    branch[...] = whole(outs[0], outs[1], first)
    second = whole(outs[2], outs[3], first)
    norm_grads[0:1] = jnp.sum(second * hat, axis=0, keepdims=True)
    norm_grads[1:2] = jnp.sum(second, axis=0, keepdims=True)
    input_part[...] = norm_back(second, hat, root, norms[2:3])


def both_cores(scal, x, x_beside, cot, cot_beside, norms, at):
    first = scal[0] == 0
    tokens = jnp.concatenate([x[...], x_beside[...]], axis=0).astype(jnp.float32)
    hat, _ = normalized(tokens)
    h = (hat * norms[at : at + 1] + norms[at + 1 : at + 2]).astype(jnp.bfloat16)
    c = jnp.concatenate([cot[...], cot_beside[...]], axis=0)
    return list(zip(halves(h, first), halves(c, first)))


def unit_grads_kernel(
    scal, x, x_beside, cot, cot_beside, norms, keep, came, in_keep, in_send, down_keep, down_send
):
    for side, (h, c) in enumerate(both_cores(scal, x, x_beside, cot, cot_beside, norms, 2)):
        for far in range(2):
            grad = jnp.concatenate([keep[far, 0], came[far, 0]], axis=0)
            act = jnp.concatenate([keep[far, 1], came[far, 1]], axis=0)
            (in_send if side else in_keep)[far] = dot(h, grad, TN).astype(jnp.bfloat16)
            (down_send if far else down_keep)[side] = dot(c, act, TN).astype(jnp.bfloat16)


def combine_kernel(in_keep, in_came, down_keep, down_came, own, in_send, down_send):
    pairs = ((in_keep, in_came, in_send), (down_keep, down_came, down_send))
    for k, (keep, came, send) in enumerate(pairs):
        total = keep[...].astype(jnp.float32) + came[...].astype(jnp.float32)
        own[k] = total[0].astype(jnp.bfloat16)
        send[0] = total[1].astype(jnp.bfloat16)


def turn_kernel(scal, cosine, sine, back, keep, send, sums):
    low = low_lanes(keep.shape[1])
    for r in range(4):
        head = scal[1] ^ r
        grads = jnp.concatenate([back[head], back[4 + head]], axis=0)
        left = turned(grads[:, :128].astype(jnp.float32), cosine[...], -sine[...])
        left = left.astype(jnp.bfloat16)
        right = grads[:, 128:]
        target = send if r % 2 else keep
        target[r // 2, :, :128] = left
        target[r // 2, :, 128:] = right
        right = jnp.where(low, right.astype(jnp.float32), 0.0)
        wide = jnp.concatenate([left.astype(jnp.float32), right], axis=1)
        sums[pl.ds(head, 1), :] = jnp.sum(wide, axis=0, keepdims=True)


def split_last(piece):
    wide = piece.astype(jnp.float32)
    lane = lax.broadcasted_iota(jnp.int32, (1, wide.shape[1]), 1)
    share = (lane < 3 * HD).astype(jnp.float32)
    pre_grad = (wide * share).astype(jnp.bfloat16)
    attended = (wide * (1.0 - share)).astype(jnp.bfloat16)
    return pre_grad, attended


def head_grads_kernel(
    scal, x, x_beside, cot, cot_beside, norms, keep, came, totals, totals_came, *outs
):
    add_up([((totals, totals_came), outs[4])])
    sides = both_cores(scal, x, x_beside, cot, cot_beside, norms, 0)
    a_keep, a_send, b_keep, b_send = outs[:4]
    for far in range(2):
        piece = jnp.concatenate([keep[far], came[far]], axis=0)
        pre_grad, attended = split_last(piece)
        for side, (h, c) in enumerate(sides):
            grad = (dot(h, pre_grad, TN) + dot(c, attended, TN)).astype(jnp.bfloat16)
            (a_send if side else a_keep)[far] = grad[0:256]
            (b_send if far else b_keep)[side] = grad[256:512]


def combine_heads_kernel(
    a_keep, a_came, b_keep, b_came, totals, totals_came, a_own, a_send, b_own, b_send, totals_sum
):
    add_up(
        [
            ((a_keep, a_came), [a_own, a_send]),
            ((b_keep, b_came), [b_own, b_send]),
            ((totals, totals_came), totals_sum),
        ]
    )


def add_kernel(near, came, kept, passed):
    add_up([((near, came), [kept, passed])])


def gather_kernel(
    scal, x, norms, keep, send, weights, r0, r1, r2, r3, ff_branch, ff_part,
    norm_two, cot_sums, unit_sums, qkv_sums, near, far, totals, parts,
):
    first = scal[0] == 0
    hat, root = normalized(x[...].astype(jnp.float32))
    outs = [0.0] * 4
    for r, other in enumerate((r0, r1, r2, r3)):
        mine, theirs = weights[scal[1] ^ r], other[0]
        pre_grad, attended = split_last((send if r % 2 else keep)[r // 2])
        outs[0] += dot(attended, mine, NT)
        outs[1] += dot(attended, theirs, NT)
        outs[2] += dot(pre_grad, mine, NT)
        outs[3] += dot(pre_grad, theirs, NT)
    branch = ff_branch[...] + whole(outs[0], outs[1], first)
    grad = whole(outs[2], outs[3], first)
    totals[...] = jnp.zeros_like(totals)
    rows = [jnp.sum(grad * hat, axis=0, keepdims=True), jnp.sum(grad, axis=0, keepdims=True)]
    rows += [norm_two[0:1], norm_two[1:2], cot_sums[...]]
    for i, row in enumerate(rows):
        for q in range(4):
            at = 4 * (i % 2) + q
            totals[i // 2, at : at + 1, :] = row[:, 256 * q : 256 * q + 256]
    totals[3 + scal[2], 0:4, :] = qkv_sums[...]
    totals[3 + scal[2], 4:8, :] = unit_sums[...]
    input_part = ff_part[...] + norm_back(grad, hat, root, norms[0:1])
    for q in range(4):
        parts[q, 0] = branch[64 * q : 64 * q + 64].astype(jnp.bfloat16)
        parts[q, 1] = input_part[64 * q : 64 * q + 64].astype(jnp.bfloat16)
    for r in range(4):
        (far if r % 2 else near)[r // 2] = parts[scal[2] ^ r]


def finish_rows_kernel(scal, x, cot, bias, r0, r1, r2, r3, block_output, input_grad):
    for r, piece in enumerate((r0, r1, r2, r3)):
        q = scal[2] ^ r
        block_output[q] = x[q].astype(jnp.float32) + piece[0].astype(jnp.float32) + bias[...]
        input_grad[q] = cot[q].astype(jnp.float32) + piece[1].astype(jnp.float32)


def gram_of_piece(total, momenta, grads, grams):
    short = total.astype(jnp.bfloat16)
    grads[0] = short
    update = 1.95 * short.astype(jnp.float32) + 0.9025 * momenta[0]
    gram = dot(update, update, TN, lax.Precision.HIGHEST)
    for j in range(4):
        cut = slice(j * HD, (j + 1) * HD)
        grams[0, j] = gram[cut, cut]


def unit_gram_kernel(place, own, in_came, down_came, momenta, totals, totals_came, *refs):
    grads, grams, totals_sum = refs[-3:]

    @pl.when(pl.program_id(0) == 0)
    def _():
        add_up([((totals, totals_came), totals_sum)])

    a = in_came[0].astype(jnp.float32)
    b = down_came[0].astype(jnp.float32)
    other = jnp.where(pl.program_id(0) == 0, a, b)
    gram_of_piece(own[0].astype(jnp.float32) + other, momenta, grads, grams)


def head_gram_kernel(place, a_own, a_came, b_own, b_came, momenta, *refs):
    grads, grams = refs[-2:]
    a = a_own[...].astype(jnp.float32) + a_came[...].astype(jnp.float32)
    b = b_own[...].astype(jnp.float32) + b_came[...].astype(jnp.float32)
    gram_of_piece(jnp.concatenate([a, b], axis=0), momenta, grads, grams)


def gram_of(kernel, first, others, momenta, place, more, shapes, after=()):
    chunks = momenta.shape[0] // 4
    piece = pl.BlockSpec((1, 512, 256), lambda i, s: (i, 0, 0))
    block = pl.BlockSpec((1, 512, 256), lambda i, s: (4 * i + s[1], 0, 0))
    return pl.pallas_call(
        kernel,
        grid_spec=pltpu.PrefetchScalarGridSpec(
            num_scalar_prefetch=1,
            grid=(chunks,),
            in_specs=[piece if first.ndim == 3 else full(first)]
            + [full(other) for other in others]
            + [block]
            + [full(part) for part in more]
            + [corner(a) for a in after],
            out_specs=[piece, pl.BlockSpec((1, 4, HD, HD), lambda i, s: (i, 0, 0, 0))]
            + [full(shape) for shape in shapes],
        ),
        out_shape=[
            jax.ShapeDtypeStruct((chunks, 512, 256), jnp.bfloat16),
            jax.ShapeDtypeStruct((chunks, 4, HD, HD), jnp.float32),
            *map(out_hbm, shapes),
        ],
        compiler_params=limits(12),
        cost_estimate=takes(2.5),
        name="gram",
    )(place, *map(in_hbm, [first, *others, momenta, *more, *after]))


def newton_kernel(counts, mine, theirs, *refs):
    taken = sum(counts)
    out = refs[taken]
    add_up(grouped(refs, counts, refs[taken + 1 :]))
    linear, square, cubic = quintic
    shape = (HD, HD)
    eye = lax.broadcasted_iota(jnp.int32, shape, 0) == lax.broadcasted_iota(jnp.int32, shape, 1)
    full = lax.Precision.HIGHEST
    chunks = mine.shape[0]
    places = [(i, j) for i in range(chunks) for j in range(4)]
    states = []
    for i, j in places:
        gram = mine[i, j] + theirs[i, j]
        trace = jnp.sum(jnp.where(eye, gram, 0.0), axis=(0, 1), keepdims=True)
        scale = 1.0 / (jnp.sqrt(trace) + muon_epsilon)
        states.append([gram * scale * scale, None, scale])
    for iteration in range(NEWTON):
        squares = [dot(s[0], s[0], precision=full) for s in states]
        steps = [
            jnp.where(eye, linear, 0.0) + square * s[0] + cubic * sq
            for s, sq in zip(states, squares)
        ]
        if iteration == 0:
            halfway = [dot(s[0], m, precision=full) for s, m in zip(states, steps)]
            for s, m in zip(states, steps):
                s[1] = m
        elif iteration < NEWTON - 1:
            both = [
                dot(jnp.concatenate([s[0], s[1]], axis=0), m, precision=full)
                for s, m in zip(states, steps)
            ]
            halfway = [x[:HD] for x in both]
            for s, x in zip(states, both):
                s[1] = x[HD:]
        else:
            for s, m in zip(states, steps):
                s[1] = dot(s[1], m, precision=full)
        if iteration < NEWTON - 1:
            for s, x, m in zip(states, halfway, steps):
                s[0] = dot(x, m, precision=full)
    for (i, j), s in zip(places, states):
        mix = s[1] * s[2]
        coarse = mix.astype(jnp.bfloat16)
        fine = (mix - coarse.astype(jnp.float32)).astype(jnp.bfloat16)
        rows, lanes = slice(64 * (j // 2), 64 * (j // 2) + 64), slice(128 * (j % 2), 128 * (j % 2) + 128)
        out[i, rows, lanes] = jnp.concatenate([coarse, fine], axis=1)


def newton(mine, theirs, sums, after=()):
    flat = [part for group in sums for part in group]
    operands = [mine, theirs, *flat]
    return launch(
        functools.partial(newton_kernel, [len(group) for group in sums]),
        operands,
        [jax.ShapeDtypeStruct((mine.shape[0], 2 * HD, 256), jnp.bfloat16)]
        + [jax.ShapeDtypeStruct(group[0].shape, group[0].dtype) for group in sums],
        "newton",
        cost=3.5,
        specs=[full(a) for a in operands],
        after=after,
    )


def update_kernel(
    n, head, scal, g0, g1, g2, g3, q0, q1, q2, q3, momenta, native_momenta, native, *refs
):
    grads, weights, moved, mixing, first, second, steps = refs[-7:]
    place_of = members_of(head)

    @pl.when((pl.program_id(0) == 0) & (pl.program_id(1) == 0))
    def _():
        mixing[...] = jnp.zeros_like(mixing)

    @pl.when(pl.program_id(1) == 0)
    def _():
        for r, q in enumerate((q0, q1, q2, q3)):
            for j in range(4):
                at = slice(HD * (j // 2), HD * (j // 2) + HD), slice(128 * (j % 2), 128 * (j % 2) + 128)
                wide = q[(0,) * (len(q.shape) - 2) + at].astype(jnp.float32)
                other = pltpu.roll(wide, HD, 1)
                below = low_lanes(HD) == (j % 2 == 0)
                rows = slice(j * HD, (j + 1) * HD)
                lanes = slice(128 * (j // 2), 128 * (j // 2) + 128)
                pair = (wide, other) if j % 2 == 0 else (other, wide)
                for level in range(2):
                    part = jnp.where(below, pair[level], 0.0)
                    mixing[r, level, rows, lanes] = part.astype(jnp.bfloat16)

    low = low_lanes(n)
    for r, piece in enumerate((g0, g1, g2, g3)):
        place = scal[1] ^ r
        grad = piece[(0,) * (len(piece.shape) - 2)].astype(jnp.float32)
        update = 1.95 * grad + 0.9025 * momenta[place]
        coarse = update.astype(jnp.bfloat16)
        fine = (update - coarse.astype(jnp.float32)).astype(jnp.bfloat16)
        settled = dot(coarse, mixing[r, 0]) + dot(coarse, mixing[r, 1]) + dot(fine, mixing[r, 0])
        for half in range(2):
            k = 2 * r + half
            first[k] = grad[:, half * 128 : (half + 1) * 128]
            second[k] = settled[:, half * 128 : (half + 1) * 128]
            for source, target in ((first, grads), (second, steps)):
                even = source[k, pl.ds(0, n, stride=2), :]
                odd = source[k, pl.ds(1, n, stride=2), :]
                lines = (
                    jnp.where(low, even, pltpu.roll(odd, 64, 1)),
                    jnp.where(low, pltpu.roll(even, 64, 1), odd),
                )
                for w in range(2):
                    group, line = place_of(place, 2 * half + w)
                    target[group, pl.ds(line, n, stride=8), :] = lines[w]
    moved[...] = momentum_decay * native_momenta[...] + grads[...]
    weight = native[...]
    weights[...] = weight - muon_rate * (4.0 * steps[...] + weight_decay * weight)


def update(
    first, scal, own, far, mix, mix_far, beside, momenta, native_momenta, native, before=(), after=(), n=128
):
    chunks = own.shape[0]
    block = pl.BlockSpec((2, 8 * n, 128), lambda k, i: (first + k, i, 0))
    piece = pl.BlockSpec((1, 2 * n, 256), lambda k, i: (k, i, 0))
    factor = pl.BlockSpec((1, 2 * HD, 256), lambda k, i: (k, 0, 0))
    pieces, factors = [piece, None, piece, None], [factor, None, factor, None]
    for r in (0, 1):
        pieces[2 * r + 1] = pl.BlockSpec((1, 1, 2 * n, 256), lambda k, i, r=r: (r, k, i, 0))
        factors[2 * r + 1] = pl.BlockSpec((1, 1, 2 * HD, 256), lambda k, i, r=r: (r, k, 4, 0))
    grads, mixes = [own, beside, far, beside], [mix, beside, mix_far, beside]
    return launch(
        functools.partial(update_kernel, n, first == 0),
        [scal, *grads, *mixes, momenta, native_view(native_momenta), native_view(native), *before],
        [jax.ShapeDtypeStruct((6, 2048, 128), jnp.float32)] * 3,
        "update",
        specs=[mem(pltpu.SMEM)]
        + pieces
        + factors
        + [pl.BlockSpec((4, 2 * n, 256), lambda k, i: (k, i, 0)), block, block]
        + [mem(pl.ANY)] * len(before),
        after=after,
        vmem=24,
        cost=0.5 * chunks,
        grid=(chunks, 256 // n),
        out_specs=[block] * 3,
        scratch_shapes=[
            pltpu.VMEM((4, 2, 256, 256), jnp.bfloat16),
            pltpu.VMEM((8, 2 * n, 128), jnp.float32),
            pltpu.VMEM((8, 2 * n, 128), jnp.float32),
            pltpu.VMEM((2, 8 * n, 128), jnp.float32),
        ],
        input_output_aliases={12 + i: i for i in range(len(before))},
    )


def whole_device(
    inputs, cotangent, matrices, momenta, small, small_first, small_second, segments, positions
):
    blk_at = lax.axis_index("blk")
    ctx_at = lax.axis_index("ctx")
    tp_at = lax.axis_index("tp")
    scal = jnp.stack([blk_at, ctx_at, tp_at]).astype(jnp.int32)
    sequences, local_rows, width = inputs.shape
    tokens = sequences * local_rows
    both = ("blk", "ctx")
    f32, bf16 = jnp.float32, jnp.bfloat16
    shaped = jax.ShapeDtypeStruct

    def hop(values, by):
        return lax.ppermute(values, both, [(i, i ^ by) for i in range(8)])

    def hop_tp(values, by):
        return lax.ppermute(values, "tp", [(i, i ^ by) for i in range(4)])

    def tied(values, *results):
        return lax.optimization_barrier((values, *results))[0]

    def spread(piece):
        c = hop(piece, 2)
        return [piece, hop(piece, 1), c, hop(c, 1)]

    x = inputs.reshape(tokens, width)
    cot = cotangent.reshape(tokens, width)
    norms = small[: 4 * width].reshape(4, width)
    qkv_start = 6 * width + tp_at * 4 * 3 * HD
    qkv_bias = lax.dynamic_slice_in_dim(small, qkv_start, 4 * 3 * HD).reshape(4, 3 * HD)
    qkv_bias = jnp.pad(qkv_bias, ((0, 0), (0, HD)))
    unit_start = 6 * width + H * 3 * HD + tp_at * 1024
    unit_bias = lax.dynamic_slice_in_dim(small, unit_start, 1024).reshape(4, 256)
    lane = jnp.arange(128) % HD
    frequency = rope_base ** (-2.0 * (lane % 8).astype(f32) / ROTARY)
    angles = positions.astype(f32).reshape(tokens, 1) * frequency
    cosine = jnp.where(lane < ROTARY, jnp.cos(angles), 1.0)
    sign = jnp.where(lane < 8, -1.0, jnp.where(lane < ROTARY, 1.0, 0.0))
    sine = jnp.sin(angles) * sign

    head_weights, mine = relayout(scal, matrices, bf16, 0, 1, mine=True)
    first_hop = hop(mine, 4)
    unit_weights, mine_units = relayout(scal, matrices, bf16, 1, 2, mine=True, after=(mine,))
    first_hop = tied(first_hop, mine_units)
    other_heads = spread(first_hop)
    units_near = hop(tied(mine_units, first_hop), 4)
    x_beside = hop(x, 1)
    cot_beside = hop(cot, 1)

    send = launch(
        project_kernel,
        [scal, x, cot, norms, qkv_bias, cosine, sine, head_weights]
        + [piece[0] for piece in other_heads],
        shaped((8, local_rows, 256), bf16),
        "project",
    )
    arrived = lax.all_to_all(send, both, split_axis=0, concat_axis=0, tiled=True)
    (piled_heads,) = relayout(scal, momenta, f32, 0, 1, after=(send,))
    units_near = tied(units_near, piled_heads)
    units_far = hop(units_near, 2)
    units_beside = hop(units_near, 1)
    documents = lax.dynamic_index_in_dim(segments, blk_at, 0, keepdims=False)
    length = documents.shape[0]
    attended = launch(
        attention_kernel,
        [arrived.reshape(length, 256), documents.reshape(length, 1)],
        shaped((length, 256), bf16),
        "attention",
        vmem=20,
        cost=6,
        specs=[full(arrived.reshape(length, 256)), pl.BlockSpec((length, 1), lambda *_: (0, 0))],
        after=(piled_heads,),
        scratch_shapes=[pltpu.VMEM((length, HD), f32)] * 2,
    )
    back = lax.all_to_all(
        attended.reshape(8, local_rows, 256), both, split_axis=0, concat_axis=0, tiled=True
    )

    (piled_units,) = relayout(scal, momenta, f32, 1, 2, after=(attended,))
    units_far = tied(units_far, piled_units)
    other_units = [units_near, units_beside, units_far, hop(units_far, 1)]
    ff_branch, ff_part, unit_keep, unit_send, unit_sums, norm_two, cot_sums = launch(
        feed_forward_kernel,
        [scal, x, cot, norms, unit_bias, unit_weights, *other_units],
        [
            shaped((tokens, width), f32),
            shaped((tokens, width), f32),
            shaped((2, 2, tokens, 256), bf16),
            shaped((2, 2, tokens, 256), bf16),
            shaped((4, 256), f32),
            shaped((2, width), f32),
            shaped((1, width), f32),
        ],
        "feed_forward",
        vmem=20,
        cost=0.3,
        after=(attended,),
    )
    head_keep, head_send, qkv_sums = launch(
        turn_kernel,
        [scal, cosine, sine, back],
        [shaped((2, tokens, 256), bf16)] * 2 + [shaped((4, 256), f32)],
        "turn",
        cost=2,
        after=(unit_sums,),
    )
    in_keep, in_send, down_keep, down_send = launch(
        unit_grads_kernel,
        [scal, x, x_beside, cot, cot_beside, norms, unit_keep, hop(unit_send, 1)],
        [shaped((2, 512, 256), bf16)] * 4,
        "unit_grads",
        cost=3.5,
        after=(qkv_sums,),
    )
    sums = [norm_two, cot_sums, unit_sums, qkv_sums]
    near, far, totals = launch(
        gather_kernel,
        [scal, x, norms, head_keep, head_send, head_weights, *other_heads, ff_branch, ff_part, *sums],
        [shaped((2, 2, 64, width), bf16)] * 2 + [shaped((8, 8, 256), f32)],
        "gather",
        cost=0.5,
        after=(in_keep,),
        scratch_shapes=[pltpu.VMEM((4, 2, 64, width), bf16)],
    )
    came = hop_tp(far, 1)
    totals_shape = shaped((8, 8, 256), f32)
    a_keep, a_send, b_keep, b_send, totals = launch(
        head_grads_kernel,
        [
            scal, x, x_beside, cot, cot_beside, norms, head_keep, hop(head_send, 1),
            totals, hop(totals, 1),
        ],
        [shaped((2, 256, 256), bf16)] * 4 + [totals_shape],
        "head_grads",
        cost=0.5,
    )
    a_came, b_came = hop(a_send, 4), hop(b_send, 2)
    operands = [in_keep, hop(in_send, 4), down_keep, hop(down_send, 2)]
    own, in_send, down_send = launch(
        combine_kernel,
        operands,
        [shaped((2, 512, 256), bf16)] + [shaped((1, 512, 256), bf16)] * 2,
        "combine",
        specs=[full(a) for a in operands],
        cost=2,
        after=(a_keep,),
    )
    in_came, down_came = hop(in_send, 2), hop(down_send, 4)
    kept, passed = launch(
        add_kernel,
        [near, came],
        [shaped((2, 64, width), bf16)] * 2,
        "add",
        specs=[full(near)] * 2,
        cost=1,
        after=(in_send,),
    )
    passed = hop_tp(passed, 2)
    operands = [a_keep, a_came, b_keep, b_came, totals, hop(totals, 4)]
    a_own, a_send, b_own, b_send, totals = launch(
        combine_heads_kernel,
        operands,
        [shaped((256, 256), bf16)] * 4 + [totals_shape],
        "combine_heads",
        specs=[full(a) for a in operands],
        after=(kept,),
    )
    a_came, b_came = hop(a_send, 2), hop(b_send, 4)
    unit_sum, unit_grams, totals = gram_of(
        unit_gram_kernel,
        own,
        [in_came, down_came],
        piled_units,
        scal,
        [totals, hop(totals, 2)],
        [totals_shape],
        after=(a_own,),
    )
    unit_theirs = hop(unit_grams, 4)
    unit_far = hop(unit_sum, 2)
    head_sum, head_grams = gram_of(
        head_gram_kernel,
        a_own,
        [a_came, b_own, b_came],
        piled_heads,
        scal,
        [],
        [],
        after=(unit_sum,),
    )
    head_theirs = hop(head_grams, 4)
    head_far = hop(head_sum, 2)
    unit_mix, totals, total = newton(
        unit_grams, unit_theirs, [(totals, hop_tp(totals, 1)), (kept, passed)], after=(head_sum,)
    )
    total_far, total_beside = hop_tp(total, 2), hop_tp(total, 1)
    unit_mix_far = hop(unit_mix, 2)
    (head_mix,) = newton(head_grams, head_theirs, [], after=(unit_mix, unit_far))
    head_mix_far = hop(head_mix, 2)

    def to_beside(*pieces):
        return hop(jnp.stack([jnp.concatenate(pair, axis=1) for pair in pieces]), 1)

    beside = to_beside((unit_sum, unit_mix), (unit_far, tied(unit_mix_far, head_mix)))
    before = update(
        1, scal, unit_sum, unit_far, unit_mix, unit_mix_far, beside, piled_units, momenta, matrices,
        after=(head_mix,),
    )
    head_far, head_mix_far = tied((head_far, head_mix_far), before[0])
    beside = to_beside((head_sum, head_mix), (head_far, head_mix_far))
    outs = update(
        0, scal, head_sum, head_far, head_mix, head_mix_far, beside, piled_heads, momenta, matrices,
        before,
    )
    total_far = tied(total_far, before[0])
    bias = (small[4 * width : 5 * width] + small[5 * width : 6 * width]).reshape(1, width)
    block_output, input_grad = launch(
        finish_rows_kernel,
        [
            scal,
            x.reshape(4, 64, width),
            cot.reshape(4, 64, width),
            bias,
            total,
            total_beside,
            total_far,
            hop_tp(total_far, 1),
        ],
        [shaped((4, 64, width), f32)] * 2,
        "finish_rows",
        cost=2,
        after=(outs[0],),
    )
    totals = totals + tied(hop_tp(totals, 2), before[0])
    cot_total = totals[2, :4].reshape(-1) * 0.25
    small_grads = jnp.concatenate(
        [
            totals[:2].reshape(-1),
            cot_total,
            cot_total,
            totals[3:7, :4, : 3 * HD].reshape(-1),
            totals[3:7, 4:].reshape(-1),
        ]
    )
    return (
        block_output.reshape(inputs.shape),
        input_grad.reshape(inputs.shape),
        native_back(outs[0]),
        native_back(outs[1]),
        native_back(outs[2]),
        small_grads,
        *small_step(small, small_first, small_second, small_grads),
    )


def small_step(small, small_first, small_second, small_grads):
    new_first = adam_first * small_first + (1.0 - adam_first) * small_grads
    new_second = adam_second * small_second + (1.0 - adam_second) * small_grads * small_grads
    corrected = new_first / (1.0 - adam_first**STEP)
    spread = jnp.sqrt(new_second / (1.0 - adam_second**STEP))
    new_small = small - small_rate * corrected / (spread + adam_epsilon)
    return new_first, new_second, new_small


def solution(mesh):
    in_specs = (
        P(None, ("blk", "ctx"), None),
        P(None, ("blk", "ctx"), None),
        P("tp", "blk"),
        P("tp", "blk"),
        P(),
        P(),
        P(),
        P(),
        P(None, ("blk", "ctx")),
    )
    out_specs = (
        P(None, ("blk", "ctx"), None),
        P(None, ("blk", "ctx"), None),
        P("tp", "blk"),
        P("tp", "blk"),
        P("tp", "blk"),
        P(),
        P(),
        P(),
        P(),
    )
    one_each = mesh.shape["blk"] == SEQS and mesh.shape["ctx"] * mesh.shape["tp"] == H
    one_each = one_each and mesh.shape["tp"] == 4
    return jax.shard_map(
        whole_device if one_each else on_device, mesh=mesh, in_specs=in_specs, out_specs=out_specs, check_vma=False
    )
```

```python
import functools

import jax
import jax.numpy as jnp
from jax import lax
from jax.experimental import pallas as pl
from jax.experimental.pallas import tpu as pltpu
from jax.sharding import PartitionSpec as P

MODEL_DIM = 1024
H = 16
HD = 64
FF = 4096
ROTARY = 16
NEWTON = 5
STEP = 10
SEQS = 2


norm_epsilon = 1e-05
rope_base = 10000.0
masked_score = -1e30
momentum_decay = 0.95
muon_rate = 0.2
weight_decay = 0.01
muon_epsilon = 1e-07
quintic = (3.4445, -4.775, 2.0315)
adam_first = 0.9
adam_second = 0.95
adam_epsilon = 1e-08
small_rate = 0.2


def passed_along(x, axis, by):
    devices = lax.axis_size(axis)
    pairs = [(i, i + by) for i in range(devices) if 0 <= i + by < devices]
    return lax.ppermute(x, axis, pairs)


def shifted(x, axis, by):
    devices = lax.axis_size(axis)
    return lax.ppermute(x, axis, [(i, (i + by) % devices) for i in range(devices)])


def as_sent(x):

    def short(part):
        return part.astype(jnp.bfloat16) if part.dtype == jnp.float32 else part

    return jax.tree.map(short, x)


def layer_norm(values, scaling, offset):
    centre = jnp.mean(values, axis=-1, keepdims=True)
    centred = values - centre
    spread = jnp.mean(centred * centred, axis=-1, keepdims=True)
    return centred * lax.rsqrt(spread + norm_epsilon) * scaling + offset


def rope_tables(positions):
    halfway = ROTARY // 2
    frequency = rope_base ** (-2.0 * jnp.arange(halfway, dtype=jnp.float32) / ROTARY)
    angles = positions.astype(jnp.float32)[..., None] * frequency
    return (jnp.cos(angles)[:, :, None, :], jnp.sin(angles)[:, :, None, :])


def rotate(values, cosine, sine):
    halfway = ROTARY // 2
    former = values[..., :halfway]
    latter = values[..., halfway:ROTARY]
    return jnp.concatenate(
        [former * cosine - latter * sine, latter * cosine + former * sine, values[..., ROTARY:]],
        axis=-1,
    )


def exact_gelu(values):
    return jax.nn.gelu(values, approximate=False)


def newton_schulz(blocks):
    frobenius = jnp.sqrt(jnp.sum(blocks * blocks, axis=(1, 2), keepdims=True))
    current = blocks / (frobenius + muon_epsilon)
    linear_term, square_term, cubic_term = quintic
    for iteration in range(NEWTON):
        gram_matrix = jnp.einsum("mde,mdf->mef", current, current, precision=lax.Precision.HIGHEST)
        polynomial = square_term * gram_matrix + cubic_term * jnp.einsum(
            "mef,mfg->meg", gram_matrix, gram_matrix, precision=lax.Precision.HIGHEST
        )
        current = linear_term * current + jnp.einsum(
            "mde,mef->mdf", current, polynomial, precision=lax.Precision.HIGHEST
        )
    return current


def to_heads(values):
    return lax.all_to_all(values, "ctx", split_axis=3, concat_axis=1, tiled=True)


def to_positions(values):
    return lax.all_to_all(values, "ctx", split_axis=1, concat_axis=3, tiled=True)


def pass_keys(pair):
    return passed_along(pair, "blk", 1)


def pass_grads(pair_grad):
    return shifted(pair_grad.astype(jnp.bfloat16), "blk", 1).astype(pair_grad.dtype)


def allowed_pairs(segments, query_block, key_block, block_rows):
    query_place = query_block * block_rows + jnp.arange(block_rows, dtype=jnp.int32)
    key_place = key_block * block_rows + jnp.arange(block_rows, dtype=jnp.int32)
    query_doc = lax.dynamic_slice_in_dim(segments, query_block * block_rows, block_rows, 1)
    key_doc = lax.dynamic_slice_in_dim(segments, key_block * block_rows, block_rows, 1)
    causal = key_place[None, :] <= query_place[:, None]
    return (causal[None] & (query_doc[:, :, None] == key_doc[:, None, :]))[:, None]


def masked_scores(queries, keys, allowed):
    score_scale = HD ** (-0.5)
    scores = (
        jnp.einsum("sqhe,skhe->shqk", queries, keys, preferred_element_type=jnp.float32)
        * score_scale
    )
    return jnp.where(allowed, scores, masked_score)


def on_device(
    inputs, cotangent, matrices, momenta, small, small_first, small_second, segments, positions
):
    tensor_size = lax.axis_size("tp")
    cycle_size = lax.axis_size("blk")
    context_size = lax.axis_size("ctx")
    tensor_index = lax.axis_index("tp")
    cycle_index = lax.axis_index("blk")
    sequences, local_rows, model_width = inputs.shape
    per_group = matrices.shape[0]
    head_count = H // tensor_size
    unit_blocks = FF // HD // tensor_size
    block_rows = local_rows * context_size
    gathered = lax.all_gather(matrices.astype(jnp.bfloat16), "blk", axis=1, tiled=True).reshape(
        per_group, model_width, HD
    )
    query_key_value_weight = gathered[: 3 * head_count]
    projection_out_weight = gathered[3 * head_count : 4 * head_count]
    input_weight = gathered[4 * head_count : 4 * head_count + unit_blocks]
    down_projection_weight = gathered[4 * head_count + unit_blocks :]
    qkv_start = 6 * model_width + tensor_index * head_count * 3 * HD
    query_key_value_bias = lax.dynamic_slice_in_dim(small, qkv_start, head_count * 3 * HD).reshape(
        head_count, 3, HD
    )
    unit_start = 6 * model_width + H * 3 * HD + tensor_index * unit_blocks * HD
    hidden_unit_bias = lax.dynamic_slice_in_dim(small, unit_start, unit_blocks * HD).reshape(
        unit_blocks, HD
    )
    residual = inputs.astype(jnp.float32)

    def both_norms(values, gain_one, offset_one, gain_two, offset_two):
        return (layer_norm(values, gain_one, offset_one), layer_norm(values, gain_two, offset_two))

    (normed_one, normed_two), norm_back = jax.vjp(
        both_norms,
        residual,
        small[0:model_width],
        small[model_width : 2 * model_width],
        small[2 * model_width : 3 * model_width],
        small[3 * model_width : 4 * model_width],
    )
    first_input = normed_one.astype(jnp.bfloat16)
    second_input = normed_two.astype(jnp.bfloat16)
    projected = jnp.einsum(
        "pgk,jka->pgja", first_input, query_key_value_weight, preferred_element_type=jnp.float32
    )
    projected = projected.reshape(sequences, local_rows, 3, head_count, HD) + jnp.transpose(
        query_key_value_bias, (1, 0, 2)
    )
    cosine, sine = rope_tables(positions)

    def turn_pair(query_pre, key_pre):
        return (rotate(query_pre, cosine, sine), rotate(key_pre, cosine, sine))

    (query_turned, key_turned), turn_back = jax.vjp(
        turn_pair, projected[:, :, 0], projected[:, :, 1]
    )
    stacked = jnp.stack([query_turned, key_turned, projected[:, :, 2]], axis=2).astype(jnp.bfloat16)
    by_heads = to_heads(stacked)
    queries = by_heads[:, :, 0]
    head_local = queries.shape[2]

    def forward_visit(state, pair, source):
        row_max, row_total, weighted = state
        allowed = allowed_pairs(segments, cycle_index, source, block_rows)
        scores = masked_scores(queries, pair[:, :, 0], allowed)
        new_max = jnp.maximum(row_max, jnp.max(scores, axis=-1))
        weights = jnp.where(allowed, jnp.exp(scores - new_max[..., None]), 0.0)
        rescale = jnp.exp(row_max - new_max)
        row_total = row_total * rescale + jnp.sum(weights, axis=-1)
        weighted = weighted * rescale[..., None] + jnp.einsum(
            "shqk,skhe->shqe",
            weights.astype(jnp.bfloat16),
            pair[:, :, 1],
            preferred_element_type=jnp.float32,
        )
        return (new_max, row_total, weighted)

    def forward_hop(hop_index, carry):
        pair, state = carry
        source = (cycle_index - hop_index) % cycle_size
        state = forward_visit(state, pair, source)
        return (pass_keys(pair), state)

    start_state = (
        jnp.full((sequences, head_local, block_rows), masked_score, jnp.float32),
        jnp.zeros((sequences, head_local, block_rows), jnp.float32),
        jnp.zeros((sequences, head_local, block_rows, HD), jnp.float32),
    )
    pair, state = lax.fori_loop(0, cycle_size - 1, forward_hop, (by_heads[:, :, 1:], start_state))
    row_max, row_total, weighted = forward_visit(state, pair, (cycle_index + 1) % cycle_size)
    log_total = row_max + jnp.log(row_total)
    attended_rows = jnp.transpose(weighted / row_total[..., None], (0, 2, 1, 3))
    attention_result = to_positions(attended_rows.astype(jnp.bfloat16)[:, :, None])[:, :, 0]
    attention_branch = jnp.einsum(
        "roxu,xcu->roc", attention_result, projection_out_weight, preferred_element_type=jnp.float32
    )
    hidden_preactivation = (
        jnp.einsum("ptr,kra->ptka", second_input, input_weight, preferred_element_type=jnp.float32)
        + hidden_unit_bias
    )
    activated_hidden, gelu_back = jax.vjp(exact_gelu, hidden_preactivation)
    activated_reduced = activated_hidden.astype(jnp.bfloat16)
    perceptron_branch = jnp.einsum(
        "xkzp,zop->xko",
        activated_reduced,
        down_projection_weight,
        preferred_element_type=jnp.float32,
    )
    branches = lax.psum((attention_branch + perceptron_branch).astype(jnp.bfloat16), "tp").astype(
        jnp.float32
    )
    block_output = (
        residual
        + branches
        + small[4 * model_width : 5 * model_width]
        + small[5 * model_width : 6 * model_width]
    )
    act_grad = jnp.einsum(
        "ptr,kra->ptka", cotangent, down_projection_weight, preferred_element_type=jnp.float32
    )
    hidden_gradient = gelu_back(act_grad)[0].astype(jnp.bfloat16)
    down_grad = jnp.einsum(
        "gup,guzb->zpb", cotangent, activated_reduced, preferred_element_type=jnp.float32
    )
    in_grad = jnp.einsum(
        "gup,guzb->zpb", second_input, hidden_gradient, preferred_element_type=jnp.float32
    )
    second_grad = jnp.einsum(
        "xkzp,zop->xko", hidden_gradient, input_weight, preferred_element_type=jnp.float32
    )
    attended_grad = jnp.einsum(
        "pgk,jka->pgja", cotangent, projection_out_weight, preferred_element_type=jnp.float32
    ).astype(jnp.bfloat16)
    outproj_grad = jnp.einsum(
        "ztu,ztqi->qui", cotangent, attention_result, preferred_element_type=jnp.float32
    )
    grad_heads = to_heads(attended_grad[:, :, None])[:, :, 0]
    row_delta = jnp.transpose(
        jnp.sum(grad_heads.astype(jnp.float32) * attended_rows, axis=-1), (0, 2, 1)
    )

    def backward_visit(query_grad, pair, source):
        allowed = allowed_pairs(segments, cycle_index, source, block_rows)
        scores = masked_scores(queries, pair[:, :, 0], allowed)
        probabilities = jnp.where(allowed, jnp.exp(scores - log_total[..., None]), 0.0)
        value_grad = jnp.einsum(
            "shqk,sqhe->skhe",
            probabilities.astype(jnp.bfloat16),
            grad_heads,
            preferred_element_type=jnp.float32,
        )
        prob_grad = jnp.einsum(
            "sqhe,skhe->shqk", grad_heads, pair[:, :, 1], preferred_element_type=jnp.float32
        )
        score_grad = (probabilities * (prob_grad - row_delta[..., None])).astype(jnp.bfloat16)
        score_scale = HD ** (-0.5)
        query_grad = (
            query_grad
            + jnp.einsum(
                "shqk,skhe->sqhe", score_grad, pair[:, :, 0], preferred_element_type=jnp.float32
            )
            * score_scale
        )
        key_grad = (
            jnp.einsum("shqk,sqhe->skhe", score_grad, queries, preferred_element_type=jnp.float32)
            * score_scale
        )
        return (query_grad, jnp.stack([key_grad, value_grad], axis=2))

    def backward_hop(hop_index, carry):
        pair, pair_grad, query_grad = carry
        source = (cycle_index - hop_index) % cycle_size
        query_grad, visit_grad = backward_visit(query_grad, pair, source)
        return (pass_keys(pair), pass_grads(pair_grad + visit_grad), query_grad)

    zero_pair = jnp.zeros(by_heads[:, :, 1:].shape, jnp.float32)
    pair, pair_grad, query_grad = lax.fori_loop(
        0,
        cycle_size - 1,
        backward_hop,
        (by_heads[:, :, 1:], zero_pair, jnp.zeros(queries.shape, jnp.float32)),
    )
    query_grad, visit_grad = backward_visit(query_grad, pair, (cycle_index + 1) % cycle_size)
    pair_grad = pass_grads(pair_grad + visit_grad)
    head_grads = jnp.concatenate([query_grad[:, :, None], pair_grad], axis=2).astype(jnp.bfloat16)
    position_grads = to_positions(head_grads).astype(jnp.float32)
    query_pre_grad, key_pre_grad = turn_back((position_grads[:, :, 0], position_grads[:, :, 1]))
    projected_grad = jnp.stack(
        [query_pre_grad, key_pre_grad, position_grads[:, :, 2]], axis=2
    ).astype(jnp.bfloat16)
    flattened_gradient = projected_grad.reshape(sequences, local_rows, 3 * head_count, HD)
    query_key_value_gradient = jnp.einsum(
        "ztu,ztqi->qui", first_input, flattened_gradient, preferred_element_type=jnp.float32
    )
    first_grad = jnp.einsum(
        "roxu,xcu->roc",
        flattened_gradient,
        query_key_value_weight,
        preferred_element_type=jnp.float32,
    )
    input_part, gain_one_grad, offset_one_grad, gain_two_grad, offset_two_grad = norm_back(
        (first_grad, second_grad)
    )
    input_grad = cotangent.astype(jnp.float32) + lax.psum(
        input_part.astype(jnp.bfloat16), "tp"
    ).astype(jnp.float32)
    owner_share = jnp.where(tensor_index == 0, 1.0, 0.0).astype(jnp.float32)
    bias_grad = jnp.sum(cotangent.astype(jnp.float32), axis=(0, 1)) * owner_share
    qkv_bias_grad = jnp.transpose(
        jnp.sum(projected_grad.astype(jnp.float32), axis=(0, 1)), (1, 0, 2)
    ).reshape(-1)
    unit_bias_grad = jnp.sum(hidden_gradient.astype(jnp.float32), axis=(0, 1)).reshape(-1)
    local_small = jnp.concatenate(
        [
            gain_one_grad,
            offset_one_grad,
            gain_two_grad,
            offset_two_grad,
            bias_grad,
            bias_grad,
            jnp.zeros((small.shape[0] - 6 * model_width,), jnp.float32),
        ]
    )
    local_small = lax.dynamic_update_slice_in_dim(local_small, qkv_bias_grad, qkv_start, 0)
    local_small = lax.dynamic_update_slice_in_dim(local_small, unit_bias_grad, unit_start, 0)
    small_grads = lax.psum(local_small, ("blk", "ctx", "tp"))
    local_grad = jnp.concatenate(
        [query_key_value_gradient, outproj_grad, in_grad, down_grad], axis=0
    ).reshape(per_group, -1)
    shares = lax.psum_scatter(
        local_grad.astype(jnp.bfloat16), "blk", scatter_dimension=1, tiled=True
    )
    matrix_grads = lax.psum(shares, "ctx").astype(jnp.float32)
    new_momenta = momentum_decay * momenta + matrix_grads
    update = matrix_grads + momentum_decay * new_momenta
    per_owner = per_group // cycle_size
    sectioned = update.reshape(cycle_size, per_owner, update.shape[1])
    pieces = lax.all_to_all(
        sectioned.astype(jnp.bfloat16), "blk", split_axis=0, concat_axis=2, tiled=True
    ).astype(sectioned.dtype)
    piece_count = pieces.shape[1]
    settled_blocks = newton_schulz(pieces.reshape(piece_count, MODEL_DIM, HD)).reshape(
        1, piece_count, MODEL_DIM * HD
    )
    settled = lax.all_to_all(
        as_sent(settled_blocks), "blk", split_axis=2, concat_axis=0, tiled=True
    ).astype(settled_blocks.dtype)
    orthogonal_all = settled.reshape(per_group, -1)
    muon_scale = max(1.0, MODEL_DIM / HD) ** 0.5
    new_matrices = matrices - muon_rate * (muon_scale * orthogonal_all + weight_decay * matrices)
    new_first = adam_first * small_first + (1.0 - adam_first) * small_grads
    new_second = adam_second * small_second + (1.0 - adam_second) * small_grads * small_grads
    corrected = new_first / (1.0 - adam_first**STEP)
    spread = jnp.sqrt(new_second / (1.0 - adam_second**STEP))
    new_small = small - small_rate * corrected / (spread + adam_epsilon)
    return (
        block_output,
        input_grad,
        matrix_grads,
        new_matrices,
        new_momenta,
        small_grads,
        new_first,
        new_second,
        new_small,
    )


def native_view(array):
    rows, columns = array.shape
    tiled = array.reshape(rows // 8, 8, columns // 128, 128).transpose(0, 2, 1, 3)
    return tiled.reshape(rows // 8, columns // 16, 128)


def native_back(array):
    groups, rows, _ = array.shape
    return array.reshape(groups, rows // 8, 8, 128).transpose(0, 2, 1, 3).reshape(groups * 8, rows * 16)


def members_of(head):
    if head:
        return lambda piece, j: (j // 2, 4 * (j % 2) + piece)
    return lambda piece, j: (piece // 2, 4 * (piece % 2) + j)


def mem(kind=pltpu.VMEM):
    return pl.BlockSpec(memory_space=kind)


def limits(mebibytes):
    return pltpu.CompilerParams(vmem_limit_bytes=mebibytes << 20)


def low_lanes(rows):
    return lax.broadcasted_iota(jnp.int32, (rows, 128), 1) < HD


def dot(a, b, dims=((1,), (0,)), precision=None):
    return lax.dot_general(
        a, b, (dims, ((), ())), precision=precision, preferred_element_type=jnp.float32
    )


NT = ((1,), (1,))
TN = ((0,), (0,))


def corner(array):
    block = (1,) * (array.ndim - 2) + (min(16, array.shape[-2]), 128)
    return pl.BlockSpec(block, lambda *_: (0,) * array.ndim)


def takes(microseconds):
    return pl.CostEstimate(
        flops=int(microseconds * 1.15e9), transcendentals=0, bytes_accessed=int(1e6)
    )


def in_hbm(array):
    if array.size * array.dtype.itemsize < 1 << 21:
        return array
    return pltpu.with_memory_space_constraint(array, pltpu.HBM)


def out_hbm(shape):
    if shape.size * shape.dtype.itemsize < 1 << 20:
        return shape
    return pltpu.HBM(shape.shape, shape.dtype)


def full(array):
    return pl.BlockSpec(array.shape, lambda *_: (0,) * array.ndim)


def launch(kernel, operands, out_shapes, name, specs=None, after=(), vmem=16, cost=3, **more):
    taken = len(operands)
    body = kernel
    if after:
        body = lambda *refs: kernel(*refs[:taken], *refs[taken + len(after) :])
    if specs is None:
        specs = [mem(pltpu.SMEM)] + [full(a) for a in operands[1:]]
    if "out_specs" not in more:
        more["out_specs"] = jax.tree.map(full, out_shapes)
    more.setdefault("grid", (1,))
    return pl.pallas_call(
        body,
        in_specs=list(specs) + [corner(a) for a in after],
        out_shape=jax.tree.map(out_hbm, out_shapes),
        compiler_params=limits(vmem),
        cost_estimate=takes(cost),
        name=name,
        **more,
    )(*map(in_hbm, operands), *map(in_hbm, after))


def relayout_kernel(n, first, count, scal, src, out, *refs):
    fetched, paired, packed, arrivals, departures = refs[-5:]
    low = low_lanes(n)
    place_of = members_of(first == 0)
    steps = [(k, i) for k in range(count) for i in range(256 // n)]

    def fetch(k, i, group):
        rows = pl.ds(i * 8 * n, 8 * n)
        return pltpu.make_async_copy(
            src.at[2 * first + 2 * k + group, rows],
            fetched.at[2 * k + group, rows],
            arrivals.at[2 * k + group, i],
        )

    def leave(k, i):
        rows = pl.ds(i * 2 * n, 2 * n)
        return pltpu.make_async_copy(
            packed.at[pl.ds(4 * k, 4), rows], out.at[pl.ds(4 * k, 4), rows], departures.at[k, i]
        )

    for k, i in steps:
        for group in range(2):
            fetch(k, i, group).start()
    for k, i in steps:
        for group in range(2):
            fetch(k, i, group).wait()
        for piece in range(4):
            for half in range(2):
                pair = []
                for j in (2 * half, 2 * half + 1):
                    group, line = place_of(piece, j)
                    rows = pl.ds(i * 8 * n + line, n, stride=8)
                    pair.append(fetched[2 * k + group, rows, :])
                a, b = pair
                at = 2 * piece + half
                paired[at, pl.ds(0, n, stride=2), :] = jnp.where(low, a, pltpu.roll(b, 64, 1))
                paired[at, pl.ds(1, n, stride=2), :] = jnp.where(low, pltpu.roll(a, 64, 1), b)
                lanes = slice(half * 128, (half + 1) * 128)
                rows = slice(i * 2 * n, (i + 1) * 2 * n)
                packed[4 * k + piece, rows, lanes] = paired[at].astype(packed.dtype)
        leave(k, i).start()
    if len(refs) == 6:
        for k in range(count):
            refs[0][k] = packed[4 * k + scal[1]]
    for k, i in steps:
        leave(k, i).wait()


def relayout(scal, array, dtype, first, count, mine=False, n=128, after=()):
    shapes = [jax.ShapeDtypeStruct((4 * count, 512, 256), dtype)]
    specs = [mem(pl.ANY)]
    if mine:
        shapes.append(jax.ShapeDtypeStruct((count, 512, 256), dtype))
        specs.append(full(shapes[1]))
    return launch(
        functools.partial(relayout_kernel, n, first, count),
        [scal, native_view(array)],
        shapes,
        "relayout",
        specs=[mem(pltpu.SMEM), mem(pl.ANY)],
        after=after,
        cost=0.2 * count,
        vmem=14,
        out_specs=specs,
        scratch_shapes=[
            pltpu.VMEM((2 * count, 2048, 128), jnp.float32),
            pltpu.VMEM((8, 2 * n, 128), jnp.float32),
            pltpu.VMEM((4 * count, 512, 256), dtype),
            pltpu.SemaphoreType.DMA((2 * count, 256 // n)),
            pltpu.SemaphoreType.DMA((count, 256 // n)),
        ],
    )


def add_up(groups):
    for parts, target in groups:
        values = [part[...].astype(jnp.float32) for part in parts]
        while len(values) > 1:
            values = [sum(values[i : i + 2]) for i in range(0, len(values), 2)]
        if isinstance(target, list):
            for i, part in enumerate(target):
                part[...] = values[0][i].astype(part.dtype)
        else:
            target[...] = values[0].astype(target.dtype)


def grouped(refs, counts, targets):
    refs = iter(refs)
    return [([next(refs) for _ in range(n)], target) for n, target in zip(counts, targets)]


def normalized(x):
    centred = x - jnp.mean(x, axis=-1, keepdims=True)
    spread = jnp.mean(centred * centred, axis=-1, keepdims=True)
    root = lax.rsqrt(spread + norm_epsilon)
    return centred * root, root


def halves(values, first):
    left, right = values[:, :512], values[:, 512:]
    return jnp.where(first, left, right), jnp.where(first, right, left)


def whole(own, other, first):
    return jnp.concatenate([jnp.where(first, own, other), jnp.where(first, other, own)], axis=1)


def norm_back(grad, hat, root, gain):
    scaled = grad * gain
    along = jnp.mean(scaled * hat, axis=-1, keepdims=True)
    return root * (scaled - jnp.mean(scaled, axis=-1, keepdims=True) - hat * along)


def turned(values, cosine, sine):
    lane = lax.broadcasted_iota(jnp.int32, values.shape, 1) % HD
    other = jnp.where(lane < 8, pltpu.roll(values, 120, 1), pltpu.roll(values, 8, 1))
    return values * cosine + other * sine


def project_kernel(scal, x, cot, norms, bias, cosine, sine, own, r0, r1, r2, r3, send):
    first = scal[0] == 0
    hat, _ = normalized(x[...].astype(jnp.float32))
    h = (hat * norms[0:1] + norms[1:2]).astype(jnp.bfloat16)
    h_own, h_other = halves(h, first)
    c_own, c_other = halves(cot[...], first)
    tokens = h.shape[0]
    low = low_lanes(tokens)
    for r, other in enumerate((r0, r1, r2, r3)):
        head = scal[1] ^ r
        mine = own[head]
        theirs = other[...]
        pre = dot(h_own, mine) + dot(h_other, theirs) + bias[pl.ds(head, 1), :]
        back = dot(c_own, mine[:, 128:]) + dot(c_other, theirs[:, 128:])
        left = turned(pre[:, :128], cosine[...], sine[...]).astype(jnp.bfloat16)
        right = jnp.where(low, pre[:, 128:], back).astype(jnp.bfloat16)
        for s in range(2):
            rows = slice(128 * s, 128 * s + 128)
            send[4 * s + head, :, :128] = left[rows]
            send[4 * s + head, :, 128:] = right[rows]


def attention_kernel(rows_ref, seg, out, key_total, value_total):
    key_total[...] = jnp.zeros_like(key_total)
    value_total[...] = jnp.zeros_like(value_total)
    step = 256
    for block in range(rows_ref.shape[0] // step):
        rows = slice(block * step, (block + 1) * step)
        n = (block + 1) * step
        query = rows_ref[rows, 0:HD] * jnp.bfloat16(0.125)
        grad = rows_ref[rows, 3 * HD : 4 * HD]
        keys = rows_ref[0:n, HD : 2 * HD]
        values = rows_ref[0:n, 2 * HD : 3 * HD]
        scores = dot(query, keys, NT)
        query_place = block * step + lax.broadcasted_iota(jnp.int32, (step, n), 0)
        key_place = lax.broadcasted_iota(jnp.int32, (step, n), 1)
        allowed = (key_place <= query_place) & (key_place >= seg[rows, :])
        scores = jnp.where(allowed, scores, masked_score)
        weights = jnp.exp(scores - jnp.max(scores, axis=-1, keepdims=True))
        weights = jnp.where(allowed, weights, 0.0)
        weights = weights * (1.0 / jnp.sum(weights, axis=-1, keepdims=True))
        short = weights.astype(jnp.bfloat16)
        attended = dot(short, values)
        weight_grad = dot(grad, values, NT)
        delta = jnp.sum(weights * weight_grad, axis=-1, keepdims=True)
        score_grad = (weights * (weight_grad - delta)).astype(jnp.bfloat16)
        query_grad = dot(score_grad, keys) * 0.125
        key_total[0:n, :] += dot(score_grad, query, TN)
        value_total[0:n, :] += dot(short, grad, TN)
        out[rows, 0:HD] = query_grad.astype(jnp.bfloat16)
        out[rows, 3 * HD : 4 * HD] = attended.astype(jnp.bfloat16)
    out[:, HD : 2 * HD] = key_total[...].astype(jnp.bfloat16)
    out[:, 2 * HD : 3 * HD] = value_total[...].astype(jnp.bfloat16)


def feed_forward_kernel(
    scal, x, cot, norms, bias, weights, r0, r1, r2, r3,
    branch, input_part, keep, send, hidden_sums, norm_grads, cot_sums,
):
    first = scal[0] == 0
    hat, root = normalized(x[...].astype(jnp.float32))
    h = (hat * norms[2:3] + norms[3:4]).astype(jnp.bfloat16)
    h_own, h_other = halves(h, first)
    c_own, c_other = halves(cot[...], first)
    cot_sums[...] = jnp.sum(cot[...].astype(jnp.float32), axis=0, keepdims=True)
    outs = [0.0] * 4
    for r, other in enumerate((r0, r1, r2, r3)):
        piece = scal[1] ^ r
        in_own, in_other = weights[piece], other[0]
        down_own, down_other = weights[4 + piece], other[1]
        pre = dot(h_own, in_own) + dot(h_other, in_other) + bias[pl.ds(piece, 1), :]
        cumulative = 0.5 * (1.0 + lax.erf(pre * 0.7071067811865476))
        slope = cumulative + pre * (0.3989422804014327 * jnp.exp(-0.5 * pre * pre))
        act = (pre * cumulative).astype(jnp.bfloat16)
        act_grad = dot(c_own, down_own) + dot(c_other, down_other)
        grad = (act_grad * slope).astype(jnp.bfloat16)
        hidden_sums[pl.ds(piece, 1), :] = jnp.sum(
            grad.astype(jnp.float32), axis=0, keepdims=True
        )
        outs[0] += dot(act, down_own, NT)
        outs[1] += dot(act, down_other, NT)
        outs[2] += dot(grad, in_own, NT)
        outs[3] += dot(grad, in_other, NT)
        target = send if r % 2 else keep
        target[r // 2, 0] = grad
        target[r // 2, 1] = act
    branch[...] = whole(outs[0], outs[1], first)
    second = whole(outs[2], outs[3], first)
    norm_grads[0:1] = jnp.sum(second * hat, axis=0, keepdims=True)
    norm_grads[1:2] = jnp.sum(second, axis=0, keepdims=True)
    input_part[...] = norm_back(second, hat, root, norms[2:3])


def both_cores(scal, x, x_beside, cot, cot_beside, norms, at):
    first = scal[0] == 0
    tokens = jnp.concatenate([x[...], x_beside[...]], axis=0).astype(jnp.float32)
    hat, _ = normalized(tokens)
    h = (hat * norms[at : at + 1] + norms[at + 1 : at + 2]).astype(jnp.bfloat16)
    c = jnp.concatenate([cot[...], cot_beside[...]], axis=0)
    return list(zip(halves(h, first), halves(c, first)))


def unit_grads_kernel(
    scal, x, x_beside, cot, cot_beside, norms, keep, came, in_keep, in_send, down_keep, down_send
):
    for side, (h, c) in enumerate(both_cores(scal, x, x_beside, cot, cot_beside, norms, 2)):
        for far in range(2):
            grad = jnp.concatenate([keep[far, 0], came[far, 0]], axis=0)
            act = jnp.concatenate([keep[far, 1], came[far, 1]], axis=0)
            (in_send if side else in_keep)[far] = dot(h, grad, TN).astype(jnp.bfloat16)
            (down_send if far else down_keep)[side] = dot(c, act, TN).astype(jnp.bfloat16)


def combine_kernel(in_keep, in_came, down_keep, down_came, own, in_send, down_send):
    pairs = ((in_keep, in_came, in_send), (down_keep, down_came, down_send))
    for k, (keep, came, send) in enumerate(pairs):
        total = keep[...].astype(jnp.float32) + came[...].astype(jnp.float32)
        own[k] = total[0].astype(jnp.bfloat16)
        send[0] = total[1].astype(jnp.bfloat16)


def turn_kernel(scal, cosine, sine, back, keep, send, sums):
    low = low_lanes(keep.shape[1])
    for r in range(4):
        head = scal[1] ^ r
        grads = jnp.concatenate([back[head], back[4 + head]], axis=0)
        left = turned(grads[:, :128].astype(jnp.float32), cosine[...], -sine[...])
        left = left.astype(jnp.bfloat16)
        right = grads[:, 128:]
        target = send if r % 2 else keep
        target[r // 2, :, :128] = left
        target[r // 2, :, 128:] = right
        right = jnp.where(low, right.astype(jnp.float32), 0.0)
        wide = jnp.concatenate([left.astype(jnp.float32), right], axis=1)
        sums[pl.ds(head, 1), :] = jnp.sum(wide, axis=0, keepdims=True)


def split_last(piece):
    wide = piece.astype(jnp.float32)
    lane = lax.broadcasted_iota(jnp.int32, (1, wide.shape[1]), 1)
    share = (lane < 3 * HD).astype(jnp.float32)
    pre_grad = (wide * share).astype(jnp.bfloat16)
    attended = (wide * (1.0 - share)).astype(jnp.bfloat16)
    return pre_grad, attended


def head_grads_kernel(
    scal, x, x_beside, cot, cot_beside, norms, keep, came, totals, totals_came, *outs
):
    add_up([((totals, totals_came), outs[4])])
    sides = both_cores(scal, x, x_beside, cot, cot_beside, norms, 0)
    a_keep, a_send, b_keep, b_send = outs[:4]
    for far in range(2):
        piece = jnp.concatenate([keep[far], came[far]], axis=0)
        pre_grad, attended = split_last(piece)
        for side, (h, c) in enumerate(sides):
            grad = (dot(h, pre_grad, TN) + dot(c, attended, TN)).astype(jnp.bfloat16)
            (a_send if side else a_keep)[far] = grad[0:256]
            (b_send if far else b_keep)[side] = grad[256:512]


def combine_heads_kernel(
    a_keep, a_came, b_keep, b_came, totals, totals_came, a_own, a_send, b_own, b_send, totals_sum
):
    add_up(
        [
            ((a_keep, a_came), [a_own, a_send]),
            ((b_keep, b_came), [b_own, b_send]),
            ((totals, totals_came), totals_sum),
        ]
    )


def add_kernel(near, came, kept, passed):
    add_up([((near, came), [kept, passed])])


def gather_kernel(
    scal, x, norms, keep, send, weights, r0, r1, r2, r3, ff_branch, ff_part,
    norm_two, cot_sums, unit_sums, qkv_sums, near, far, totals, parts,
):
    first = scal[0] == 0
    hat, root = normalized(x[...].astype(jnp.float32))
    outs = [0.0] * 4
    for r, other in enumerate((r0, r1, r2, r3)):
        mine, theirs = weights[scal[1] ^ r], other[0]
        pre_grad, attended = split_last((send if r % 2 else keep)[r // 2])
        outs[0] += dot(attended, mine, NT)
        outs[1] += dot(attended, theirs, NT)
        outs[2] += dot(pre_grad, mine, NT)
        outs[3] += dot(pre_grad, theirs, NT)
    branch = ff_branch[...] + whole(outs[0], outs[1], first)
    grad = whole(outs[2], outs[3], first)
    totals[...] = jnp.zeros_like(totals)
    rows = [jnp.sum(grad * hat, axis=0, keepdims=True), jnp.sum(grad, axis=0, keepdims=True)]
    rows += [norm_two[0:1], norm_two[1:2], cot_sums[...]]
    for i, row in enumerate(rows):
        for q in range(4):
            at = 4 * (i % 2) + q
            totals[i // 2, at : at + 1, :] = row[:, 256 * q : 256 * q + 256]
    totals[3 + scal[2], 0:4, :] = qkv_sums[...]
    totals[3 + scal[2], 4:8, :] = unit_sums[...]
    input_part = ff_part[...] + norm_back(grad, hat, root, norms[0:1])
    for q in range(4):
        parts[q, 0] = branch[64 * q : 64 * q + 64].astype(jnp.bfloat16)
        parts[q, 1] = input_part[64 * q : 64 * q + 64].astype(jnp.bfloat16)
    for r in range(4):
        (far if r % 2 else near)[r // 2] = parts[scal[2] ^ r]


def finish_rows_kernel(scal, x, cot, bias, r0, r1, r2, r3, block_output, input_grad):
    for r, piece in enumerate((r0, r1, r2, r3)):
        q = scal[2] ^ r
        block_output[q] = x[q].astype(jnp.float32) + piece[0].astype(jnp.float32) + bias[...]
        input_grad[q] = cot[q].astype(jnp.float32) + piece[1].astype(jnp.float32)


def gram_of_piece(total, momenta, grads, grams):
    short = total.astype(jnp.bfloat16)
    grads[0] = short
    update = 1.95 * short.astype(jnp.float32) + 0.9025 * momenta[0]
    gram = dot(update, update, TN, lax.Precision.HIGHEST)
    for j in range(4):
        cut = slice(j * HD, (j + 1) * HD)
        grams[0, j] = gram[cut, cut]


def unit_gram_kernel(place, own, in_came, down_came, momenta, *refs):
    grads, grams = refs[-2:]
    a = in_came[0].astype(jnp.float32)
    b = down_came[0].astype(jnp.float32)
    other = jnp.where(pl.program_id(0) == 0, a, b)
    gram_of_piece(own[0].astype(jnp.float32) + other, momenta, grads, grams)


def head_gram_kernel(place, a_own, a_came, b_own, b_came, momenta, totals, totals_came, *refs):
    grads, grams, totals_sum = refs[-3:]
    add_up([((totals, totals_came), totals_sum)])
    a = a_own[...].astype(jnp.float32) + a_came[...].astype(jnp.float32)
    b = b_own[...].astype(jnp.float32) + b_came[...].astype(jnp.float32)
    gram_of_piece(jnp.concatenate([a, b], axis=0), momenta, grads, grams)


def gram_of(kernel, first, others, momenta, place, more, shapes, after=()):
    chunks = momenta.shape[0] // 4
    piece = pl.BlockSpec((1, 512, 256), lambda i, s: (i, 0, 0))
    block = pl.BlockSpec((1, 512, 256), lambda i, s: (4 * i + s[1], 0, 0))
    return pl.pallas_call(
        kernel,
        grid_spec=pltpu.PrefetchScalarGridSpec(
            num_scalar_prefetch=1,
            grid=(chunks,),
            in_specs=[piece if first.ndim == 3 else full(first)]
            + [full(other) for other in others]
            + [block]
            + [full(part) for part in more]
            + [corner(a) for a in after],
            out_specs=[piece, pl.BlockSpec((1, 4, HD, HD), lambda i, s: (i, 0, 0, 0))]
            + [full(shape) for shape in shapes],
        ),
        out_shape=[
            jax.ShapeDtypeStruct((chunks, 512, 256), jnp.bfloat16),
            jax.ShapeDtypeStruct((chunks, 4, HD, HD), jnp.float32),
            *map(out_hbm, shapes),
        ],
        compiler_params=limits(12),
        cost_estimate=takes(2.5),
        name="gram",
    )(place, *map(in_hbm, [first, *others, momenta, *more, *after]))


def newton_kernel(counts, mine, theirs, *refs):
    taken = sum(counts)
    out = refs[taken]
    add_up(grouped(refs, counts, refs[taken + 1 :]))
    linear, square, cubic = quintic
    shape = (HD, HD)
    eye = lax.broadcasted_iota(jnp.int32, shape, 0) == lax.broadcasted_iota(jnp.int32, shape, 1)
    full = lax.Precision.HIGHEST
    chunks = mine.shape[0]
    places = [(i, j) for i in range(chunks) for j in range(4)]
    states = []
    for i, j in places:
        gram = mine[i, j] + theirs[i, j]
        trace = jnp.sum(jnp.where(eye, gram, 0.0), axis=(0, 1), keepdims=True)
        scale = 1.0 / (jnp.sqrt(trace) + muon_epsilon)
        states.append([gram * scale * scale, None, scale])
    for iteration in range(NEWTON):
        squares = [dot(s[0], s[0], precision=full) for s in states]
        steps = [
            jnp.where(eye, linear, 0.0) + square * s[0] + cubic * sq
            for s, sq in zip(states, squares)
        ]
        if iteration == 0:
            halfway = [dot(s[0], m, precision=full) for s, m in zip(states, steps)]
            for s, m in zip(states, steps):
                s[1] = m
        elif iteration < NEWTON - 1:
            both = [
                dot(jnp.concatenate([s[0], s[1]], axis=0), m, precision=full)
                for s, m in zip(states, steps)
            ]
            halfway = [x[:HD] for x in both]
            for s, x in zip(states, both):
                s[1] = x[HD:]
        else:
            for s, m in zip(states, steps):
                s[1] = dot(s[1], m, precision=full)
        if iteration < NEWTON - 1:
            for s, x, m in zip(states, halfway, steps):
                s[0] = dot(x, m, precision=full)
    for (i, j), s in zip(places, states):
        mix = s[1] * s[2]
        coarse = mix.astype(jnp.bfloat16)
        fine = (mix - coarse.astype(jnp.float32)).astype(jnp.bfloat16)
        rows, lanes = slice(64 * (j // 2), 64 * (j // 2) + 64), slice(128 * (j % 2), 128 * (j % 2) + 128)
        out[i, rows, lanes] = jnp.concatenate([coarse, fine], axis=1)


def newton(mine, theirs, sums, after=()):
    flat = [part for group in sums for part in group]
    operands = [mine, theirs, *flat]
    return launch(
        functools.partial(newton_kernel, [len(group) for group in sums]),
        operands,
        [jax.ShapeDtypeStruct((mine.shape[0], 2 * HD, 256), jnp.bfloat16)]
        + [jax.ShapeDtypeStruct(group[0].shape, group[0].dtype) for group in sums],
        "newton",
        cost=3.5,
        specs=[full(a) for a in operands],
        after=after,
    )


def update_kernel(
    n, head, scal, g0, g1, g2, g3, q0, q1, q2, q3, momenta, native_momenta, native, *refs
):
    grads, weights, moved, mixing, first, second, steps = refs[-7:]
    place_of = members_of(head)

    @pl.when((pl.program_id(0) == 0) & (pl.program_id(1) == 0))
    def _():
        mixing[...] = jnp.zeros_like(mixing)

    @pl.when(pl.program_id(1) == 0)
    def _():
        for r, q in enumerate((q0, q1, q2, q3)):
            for j in range(4):
                at = slice(HD * (j // 2), HD * (j // 2) + HD), slice(128 * (j % 2), 128 * (j % 2) + 128)
                wide = q[(0,) * (len(q.shape) - 2) + at].astype(jnp.float32)
                other = pltpu.roll(wide, HD, 1)
                below = low_lanes(HD) == (j % 2 == 0)
                rows = slice(j * HD, (j + 1) * HD)
                lanes = slice(128 * (j // 2), 128 * (j // 2) + 128)
                pair = (wide, other) if j % 2 == 0 else (other, wide)
                for level in range(2):
                    part = jnp.where(below, pair[level], 0.0)
                    mixing[r, level, rows, lanes] = part.astype(jnp.bfloat16)

    low = low_lanes(n)
    for r, piece in enumerate((g0, g1, g2, g3)):
        place = scal[1] ^ r
        grad = piece[(0,) * (len(piece.shape) - 2)].astype(jnp.float32)
        update = 1.95 * grad + 0.9025 * momenta[place]
        coarse = update.astype(jnp.bfloat16)
        fine = (update - coarse.astype(jnp.float32)).astype(jnp.bfloat16)
        settled = dot(coarse, mixing[r, 0]) + dot(coarse, mixing[r, 1]) + dot(fine, mixing[r, 0])
        for half in range(2):
            k = 2 * r + half
            first[k] = grad[:, half * 128 : (half + 1) * 128]
            second[k] = settled[:, half * 128 : (half + 1) * 128]
            for source, target in ((first, grads), (second, steps)):
                even = source[k, pl.ds(0, n, stride=2), :]
                odd = source[k, pl.ds(1, n, stride=2), :]
                lines = (
                    jnp.where(low, even, pltpu.roll(odd, 64, 1)),
                    jnp.where(low, pltpu.roll(even, 64, 1), odd),
                )
                for w in range(2):
                    group, line = place_of(place, 2 * half + w)
                    target[group, pl.ds(line, n, stride=8), :] = lines[w]
    moved[...] = momentum_decay * native_momenta[...] + grads[...]
    weight = native[...]
    weights[...] = weight - muon_rate * (4.0 * steps[...] + weight_decay * weight)


def update(
    first, scal, own, far, mix, mix_far, beside, momenta, native_momenta, native, before=(), after=(), n=128
):
    chunks = own.shape[0]
    block = pl.BlockSpec((2, 8 * n, 128), lambda k, i: (first + k, i, 0))
    piece = pl.BlockSpec((1, 2 * n, 256), lambda k, i: (k, i, 0))
    factor = pl.BlockSpec((1, 2 * HD, 256), lambda k, i: (k, 0, 0))
    pieces, factors = [piece, None, piece, None], [factor, None, factor, None]
    for r in (0, 1):
        pieces[2 * r + 1] = pl.BlockSpec((1, 1, 2 * n, 256), lambda k, i, r=r: (r, k, i, 0))
        factors[2 * r + 1] = pl.BlockSpec((1, 1, 2 * HD, 256), lambda k, i, r=r: (r, k, 4, 0))
    grads, mixes = [own, beside, far, beside], [mix, beside, mix_far, beside]
    return launch(
        functools.partial(update_kernel, n, first == 0),
        [scal, *grads, *mixes, momenta, native_view(native_momenta), native_view(native), *before],
        [jax.ShapeDtypeStruct((6, 2048, 128), jnp.float32)] * 3,
        "update",
        specs=[mem(pltpu.SMEM)]
        + pieces
        + factors
        + [pl.BlockSpec((4, 2 * n, 256), lambda k, i: (k, i, 0)), block, block]
        + [mem(pl.ANY)] * len(before),
        after=after,
        vmem=24,
        cost=0.5 * chunks,
        grid=(chunks, 256 // n),
        out_specs=[block] * 3,
        scratch_shapes=[
            pltpu.VMEM((4, 2, 256, 256), jnp.bfloat16),
            pltpu.VMEM((8, 2 * n, 128), jnp.float32),
            pltpu.VMEM((8, 2 * n, 128), jnp.float32),
            pltpu.VMEM((2, 8 * n, 128), jnp.float32),
        ],
        input_output_aliases={12 + i: i for i in range(len(before))},
    )


def whole_device(
    inputs, cotangent, matrices, momenta, small, small_first, small_second, segments, positions
):
    blk_at = lax.axis_index("blk")
    ctx_at = lax.axis_index("ctx")
    tp_at = lax.axis_index("tp")
    scal = jnp.stack([blk_at, ctx_at, tp_at]).astype(jnp.int32)
    sequences, local_rows, width = inputs.shape
    tokens = sequences * local_rows
    both = ("blk", "ctx")
    f32, bf16 = jnp.float32, jnp.bfloat16
    shaped = jax.ShapeDtypeStruct

    def hop(values, by):
        return lax.ppermute(values, both, [(i, i ^ by) for i in range(8)])

    def hop_tp(values, by):
        return lax.ppermute(values, "tp", [(i, i ^ by) for i in range(4)])

    def tied(values, *results):
        return lax.optimization_barrier((values, *results))[0]

    def spread(piece):
        c = hop(piece, 2)
        return [piece, hop(piece, 1), c, hop(c, 1)]

    x = inputs.reshape(tokens, width)
    cot = cotangent.reshape(tokens, width)
    norms = small[: 4 * width].reshape(4, width)
    qkv_start = 6 * width + tp_at * 4 * 3 * HD
    qkv_bias = lax.dynamic_slice_in_dim(small, qkv_start, 4 * 3 * HD).reshape(4, 3 * HD)
    qkv_bias = jnp.pad(qkv_bias, ((0, 0), (0, HD)))
    unit_start = 6 * width + H * 3 * HD + tp_at * 1024
    unit_bias = lax.dynamic_slice_in_dim(small, unit_start, 1024).reshape(4, 256)
    lane = jnp.arange(128) % HD
    frequency = rope_base ** (-2.0 * (lane % 8).astype(f32) / ROTARY)
    angles = positions.astype(f32).reshape(tokens, 1) * frequency
    cosine = jnp.where(lane < ROTARY, jnp.cos(angles), 1.0)
    sign = jnp.where(lane < 8, -1.0, jnp.where(lane < ROTARY, 1.0, 0.0))
    sine = jnp.sin(angles) * sign

    head_weights, mine = relayout(scal, matrices, bf16, 0, 1, mine=True)
    first_hop = hop(mine, 4)
    unit_weights, mine_units = relayout(scal, matrices, bf16, 1, 2, mine=True, after=(mine,))
    first_hop = tied(first_hop, mine_units)
    other_heads = spread(first_hop)
    units_near = hop(tied(mine_units, first_hop), 4)
    x_beside = hop(x, 1)
    cot_beside = hop(cot, 1)

    send = launch(
        project_kernel,
        [scal, x, cot, norms, qkv_bias, cosine, sine, head_weights]
        + [piece[0] for piece in other_heads],
        shaped((8, local_rows, 256), bf16),
        "project",
    )
    arrived = lax.all_to_all(send, both, split_axis=0, concat_axis=0, tiled=True)
    (piled_heads,) = relayout(scal, momenta, f32, 0, 1, after=(send,))
    units_near = tied(units_near, piled_heads)
    units_far = hop(units_near, 2)
    units_beside = hop(units_near, 1)
    documents = lax.dynamic_index_in_dim(segments, blk_at, 0, keepdims=False)
    length = documents.shape[0]
    attended = launch(
        attention_kernel,
        [arrived.reshape(length, 256), documents.reshape(length, 1)],
        shaped((length, 256), bf16),
        "attention",
        vmem=20,
        cost=6,
        specs=[full(arrived.reshape(length, 256)), pl.BlockSpec((length, 1), lambda *_: (0, 0))],
        after=(piled_heads,),
        scratch_shapes=[pltpu.VMEM((length, HD), f32)] * 2,
    )
    back = lax.all_to_all(
        attended.reshape(8, local_rows, 256), both, split_axis=0, concat_axis=0, tiled=True
    )

    units_far = tied(units_far, attended)
    other_units = [units_near, units_beside, units_far, hop(units_far, 1)]
    ff_branch, ff_part, unit_keep, unit_send, unit_sums, norm_two, cot_sums = launch(
        feed_forward_kernel,
        [scal, x, cot, norms, unit_bias, unit_weights, *other_units],
        [
            shaped((tokens, width), f32),
            shaped((tokens, width), f32),
            shaped((2, 2, tokens, 256), bf16),
            shaped((2, 2, tokens, 256), bf16),
            shaped((4, 256), f32),
            shaped((2, width), f32),
            shaped((1, width), f32),
        ],
        "feed_forward",
        vmem=20,
        cost=0.3,
        after=(attended,),
    )
    head_keep, head_send, qkv_sums = launch(
        turn_kernel,
        [scal, cosine, sine, back],
        [shaped((2, tokens, 256), bf16)] * 2 + [shaped((4, 256), f32)],
        "turn",
        cost=2,
        after=(unit_sums,),
    )
    in_keep, in_send, down_keep, down_send = launch(
        unit_grads_kernel,
        [scal, x, x_beside, cot, cot_beside, norms, unit_keep, hop(unit_send, 1)],
        [shaped((2, 512, 256), bf16)] * 4,
        "unit_grads",
        cost=3.5,
        after=(qkv_sums,),
    )
    sums = [norm_two, cot_sums, unit_sums, qkv_sums]
    near, far, totals = launch(
        gather_kernel,
        [scal, x, norms, head_keep, head_send, head_weights, *other_heads, ff_branch, ff_part, *sums],
        [shaped((2, 2, 64, width), bf16)] * 2 + [shaped((8, 8, 256), f32)],
        "gather",
        cost=0.5,
        after=(in_keep,),
        scratch_shapes=[pltpu.VMEM((4, 2, 64, width), bf16)],
    )
    came = hop_tp(far, 1)
    totals_shape = shaped((8, 8, 256), f32)
    a_keep, a_send, b_keep, b_send, totals = launch(
        head_grads_kernel,
        [
            scal, x, x_beside, cot, cot_beside, norms, head_keep, hop(head_send, 1),
            totals, hop(totals, 1),
        ],
        [shaped((2, 256, 256), bf16)] * 4 + [totals_shape],
        "head_grads",
        cost=0.5,
    )
    a_came, b_came = hop(a_send, 4), hop(b_send, 2)
    operands = [in_keep, hop(in_send, 4), down_keep, hop(down_send, 2)]
    own, in_send, down_send = launch(
        combine_kernel,
        operands,
        [shaped((2, 512, 256), bf16)] + [shaped((1, 512, 256), bf16)] * 2,
        "combine",
        specs=[full(a) for a in operands],
        cost=2,
        after=(a_keep,),
    )
    in_came, down_came = hop(in_send, 2), hop(down_send, 4)
    kept, passed = launch(
        add_kernel,
        [near, came],
        [shaped((2, 64, width), bf16)] * 2,
        "add",
        specs=[full(near)] * 2,
        cost=1,
        after=(in_send,),
    )
    passed = hop_tp(passed, 2)
    operands = [a_keep, a_came, b_keep, b_came, totals, hop(totals, 4)]
    a_own, a_send, b_own, b_send, totals = launch(
        combine_heads_kernel,
        operands,
        [shaped((256, 256), bf16)] * 4 + [totals_shape],
        "combine_heads",
        specs=[full(a) for a in operands],
        after=(kept,),
    )
    a_came, b_came = hop(a_send, 2), hop(b_send, 4)
    (piled_units,) = relayout(scal, momenta, f32, 1, 2, after=(a_own,))
    unit_sum, unit_grams = gram_of(
        unit_gram_kernel,
        own,
        [in_came, down_came],
        piled_units,
        scal,
        [],
        [],
        after=(a_own,),
    )
    unit_theirs = hop(unit_grams, 4)
    unit_far = hop(unit_sum, 2)
    head_sum, head_grams, totals = gram_of(
        head_gram_kernel,
        a_own,
        [a_came, b_own, b_came],
        piled_heads,
        scal,
        [totals, hop(totals, 2)],
        [totals_shape],
        after=(unit_sum,),
    )
    head_theirs = hop(head_grams, 4)
    head_far = hop(head_sum, 2)
    unit_mix, total = newton(unit_grams, unit_theirs, [(kept, passed)], after=(head_sum,))
    total_far, total_beside = hop_tp(total, 2), hop_tp(total, 1)
    unit_mix_far = hop(unit_mix, 2)
    head_mix, totals = newton(
        head_grams, head_theirs, [(totals, hop_tp(totals, 1))], after=(unit_mix, unit_far)
    )
    head_mix_far = hop(head_mix, 2)

    def to_beside(*pieces):
        return hop(jnp.stack([jnp.concatenate(pair, axis=1) for pair in pieces]), 1)

    beside = to_beside((unit_sum, unit_mix), (unit_far, tied(unit_mix_far, head_mix)))
    before = update(
        1, scal, unit_sum, unit_far, unit_mix, unit_mix_far, beside, piled_units, momenta, matrices,
        after=(head_mix,),
    )
    head_far, head_mix_far = tied((head_far, head_mix_far), before[0])
    beside = to_beside((head_sum, head_mix), (head_far, head_mix_far))
    outs = update(
        0, scal, head_sum, head_far, head_mix, head_mix_far, beside, piled_heads, momenta, matrices,
        before,
    )
    total_far = tied(total_far, before[0])
    bias = (small[4 * width : 5 * width] + small[5 * width : 6 * width]).reshape(1, width)
    block_output, input_grad = launch(
        finish_rows_kernel,
        [
            scal,
            x.reshape(4, 64, width),
            cot.reshape(4, 64, width),
            bias,
            total,
            total_beside,
            total_far,
            hop_tp(total_far, 1),
        ],
        [shaped((4, 64, width), f32)] * 2,
        "finish_rows",
        cost=2,
        after=(outs[0],),
    )
    totals = totals + tied(hop_tp(totals, 2), before[0])
    cot_total = totals[2, :4].reshape(-1) * 0.25
    small_grads = jnp.concatenate(
        [
            totals[:2].reshape(-1),
            cot_total,
            cot_total,
            totals[3:7, :4, : 3 * HD].reshape(-1),
            totals[3:7, 4:].reshape(-1),
        ]
    )
    return (
        block_output.reshape(inputs.shape),
        input_grad.reshape(inputs.shape),
        native_back(outs[0]),
        native_back(outs[1]),
        native_back(outs[2]),
        small_grads,
        *small_step(small, small_first, small_second, small_grads),
    )


def small_step(small, small_first, small_second, small_grads):
    new_first = adam_first * small_first + (1.0 - adam_first) * small_grads
    new_second = adam_second * small_second + (1.0 - adam_second) * small_grads * small_grads
    corrected = new_first / (1.0 - adam_first**STEP)
    spread = jnp.sqrt(new_second / (1.0 - adam_second**STEP))
    new_small = small - small_rate * corrected / (spread + adam_epsilon)
    return new_first, new_second, new_small


def solution(mesh):
    in_specs = (
        P(None, ("blk", "ctx"), None),
        P(None, ("blk", "ctx"), None),
        P("tp", "blk"),
        P("tp", "blk"),
        P(),
        P(),
        P(),
        P(),
        P(None, ("blk", "ctx")),
    )
    out_specs = (
        P(None, ("blk", "ctx"), None),
        P(None, ("blk", "ctx"), None),
        P("tp", "blk"),
        P("tp", "blk"),
        P("tp", "blk"),
        P(),
        P(),
        P(),
        P(),
    )
    one_each = mesh.shape["blk"] == SEQS and mesh.shape["ctx"] * mesh.shape["tp"] == H
    one_each = one_each and mesh.shape["tp"] == 4
    return jax.shard_map(
        whole_device if one_each else on_device, mesh=mesh, in_specs=in_specs, out_specs=out_specs, check_vma=False
    )
```
